32 devices in a mesh: gauss: 8 (over z, x), view: 4 (over y, core).
Axes of the slice: x: 2, y: 2, z: 4, core: 2. Of those that a mesh axis runs over, the one named last changes fastest.
Arguments:
- params: bfloat16 [64, 8192], P(None, 'gauss'), may hold values from -5 to 2, as said below
- lists: int32 [128, 128], P(('gauss', 'view')), may hold values from -1 to 8191, as said below
- tile_pos: int32 [128], P(('gauss', 'view')), may hold values from 0 to 255
- cam_index: int32 [128], P(('gauss', 'view')), may hold values from 0 to 15
- cams: float32 [28, 16], replicated, may hold values from -1 to 1100, as said below
- targets: float32 [3, 128, 256], P(None, ('gauss', 'view')), may hold values from 0 to 1
Outputs:
- rendered: float32 [3, 128, 256], P(None, ('gauss', 'view'))
- grads: float32 [64, 8192], P(None, 'gauss')
The draws below stay inside these ranges and needn't reach their ends.
Inputs may be any that keep to these rules, and one draw needn't show every extreme that they name: `lists`: within each tile the entries that are not -1 come first. The entries of one device's 4 tiles that are not -1 name at most 64 times Gaussians of one gauss index (blocks of 1024 consecutive Gaussians), and in every draw some gauss index is named exactly 64 times by the tiles of every device; the number of entries that are not -1 differs from device to device. `cams`: columns are cameras: rows 0-8 a rotation matrix, 9-11 a translation putting every Gaussian mean at depth 2.4 or more, row 12 the focal length, rows 13-27 appearance weights. `params`: rows 6-9 are quaternions whose first component is 1 or more.
All inputs are finite; a program needn't handle non-finite values.
Results may differ from the reference program's by a relative error of at most 0.0003.
Values may be sent and summed in bfloat16 or wider, within the bound.
No kernel may reach another device: no remote copies, remote signals or barrier semaphores. Data moves between devices by JAX's collectives and lax.ppermute only.
A program may use at most 64 MiB of HBM per device.

```python
import jax
import jax.numpy as jnp
from jax import lax

G_DEV = 1024
TILES_DEV = 4
LIST = 128
VIEWS = 16
WIN = 16
NG = 8192
TILES = 128
CAP = 64


def tile_positions(key):
    return jax.random.randint(jax.random.fold_in(key, 7), (TILES,), 0, WIN * WIN).astype(jnp.int32)


def draw_tile_pos(key, part):
    return tile_positions(key)


def draw_params(key, part):
    keys = jax.random.split(key, 8)
    count = NG
    gauss_ids = jnp.arange(count)
    home = gauss_ids % (WIN * WIN)
    home_x = (home % WIN - WIN // 2).astype(jnp.float32)
    home_y = (home // WIN - WIN // 2).astype(jnp.float32)
    offsets = jax.random.uniform(keys[0], (2, count), jnp.float32, 0.0, 16.0)
    mean_z = jax.random.uniform(keys[1], (1, count), jnp.float32, -1.0, 1.0)
    screen_x = 16.0 * home_x[None, :] + offsets[0:1]
    screen_y = 16.0 * home_y[None, :] + offsets[1:2]
    mean_x = screen_x * (4.0 + mean_z) / 1000.0
    mean_y = screen_y * (4.0 + mean_z) / 1000.0
    scales = jax.random.uniform(keys[2], (3, count), jnp.float32, -4.5, -3.0)
    quat_w = jax.random.uniform(keys[3], (1, count), jnp.float32, 1.0, 2.0)
    quat_v = jax.random.uniform(keys[4], (3, count), jnp.float32, -0.5, 0.5)
    opacity = jax.random.uniform(keys[5], (1, count), jnp.float32, -5.0, -2.5)
    shade = jax.random.uniform(keys[6], (48, count), jnp.float32, -0.25, 0.25)
    first = (jnp.arange(48) % 16 == 0).astype(jnp.float32)[:, None]
    shade = shade * (1.0 + first)
    features = jax.random.uniform(keys[7], (5, count), jnp.float32, -0.5, 0.5)
    whole = jnp.concatenate([mean_x, mean_y, mean_z, scales, quat_w, quat_v, opacity, shade, features], axis=0)
    return whole.astype(jnp.bfloat16)


def draw_cams(key, part):
    keys = jax.random.split(key, 5)
    angles = jax.random.uniform(keys[0], (3, VIEWS), jnp.float32, -0.01, 0.01)
    depth = jax.random.uniform(keys[1], (1, VIEWS), jnp.float32, 3.9, 4.1)
    shift_xy = jax.random.uniform(keys[2], (2, VIEWS), jnp.float32, -0.02, 0.02)
    cos_a, sin_a = (jnp.cos(angles[0]), jnp.sin(angles[0]))
    cos_b, sin_b = (jnp.cos(angles[1]), jnp.sin(angles[1]))
    cos_c, sin_c = (jnp.cos(angles[2]), jnp.sin(angles[2]))
    rotation = jnp.stack([cos_b * cos_c, sin_a * sin_b * cos_c - cos_a * sin_c, cos_a * sin_b * cos_c + sin_a * sin_c, cos_b * sin_c, sin_a * sin_b * sin_c + cos_a * cos_c, cos_a * sin_b * sin_c - sin_a * cos_c, -sin_b, sin_a * cos_b, cos_a * cos_b])
    focal = jax.random.uniform(keys[3], (1, VIEWS), jnp.float32, 980.0, 1020.0)
    appear = jax.random.uniform(keys[4], (15, VIEWS), jnp.float32, -0.6, 0.6)
    return jnp.concatenate([rotation, shift_xy, depth, focal, appear], axis=0)


def neighbour_step(step_key, shape):
    pick = jax.random.randint(step_key, shape, 0, 4)
    return jnp.where(pick == 2, -1, jnp.where(pick == 3, 1, 0))


def draw_lists(key, part):
    owners = NG // G_DEV
    blocks = TILES // TILES_DEV
    slots = TILES_DEV * LIST
    per_home = G_DEV // (WIN * WIN)
    hottest = jax.random.randint(jax.random.fold_in(key, 1), (), 0, owners)
    block_positions = tile_positions(key).reshape(blocks, TILES_DEV)

    def one_block(block_key, block_pos):
        keys = jax.random.split(block_key, 7)
        lowest = jax.random.randint(keys[0], (), 0, CAP * 3 // 4 + 1)
        counts = jax.random.randint(keys[1], (owners,), lowest, CAP)
        counts = jnp.where(jnp.arange(owners) == hottest, CAP, counts)
        bounds = jnp.cumsum(counts)
        positions = jnp.arange(slots)
        owner_idx = jnp.searchsorted(bounds, positions, side='right').astype(jnp.int32)
        owner_slots = jnp.where(positions < bounds[-1], owner_idx, -1)
        owner_slots = owner_slots[jax.random.permutation(keys[3], slots)].reshape(TILES_DEV, LIST)
        order = jnp.argsort((owner_slots < 0).astype(jnp.int32), axis=1, stable=True)
        owner_slots = jnp.take_along_axis(owner_slots, order, axis=1)
        near_x = jnp.clip(block_pos[:, None] % WIN + neighbour_step(keys[4], (TILES_DEV, LIST)), 0, WIN - 1)
        near_y = jnp.clip(block_pos[:, None] // WIN + neighbour_step(keys[5], (TILES_DEV, LIST)), 0, WIN - 1)
        layer = jax.random.randint(keys[6], (TILES_DEV, LIST), 0, per_home)
        local_idx = layer * (WIN * WIN) + near_y * WIN + near_x
        return jnp.where(owner_slots >= 0, owner_slots * G_DEV + local_idx, -1)
    block_keys = jax.random.split(jax.random.fold_in(key, 2), blocks)
    return jax.vmap(one_block)(block_keys, block_positions).reshape(TILES, LIST).astype(jnp.int32)


def plant(values, rng, least, high):
    longest = values.shape.index(max(values.shape))
    spots = []
    for shift in (0, 1):
        where = [jax.random.randint(jax.random.fold_in(rng, axis), (), 0, length) for axis, length in enumerate(values.shape)]
        where[longest] = (where[longest] + shift) % values.shape[longest]
        spots.append(tuple(where))
    return values.at[spots[0]].set(least).at[spots[1]].set(high)


def shard_levels(key, dims, pieces, low, high):
    level, own = 1.0, jax.random.fold_in(key, 6)
    for dim, parts in pieces:
        heights = jnp.exp(jax.random.uniform(jax.random.fold_in(own, dim), (parts,), jnp.float32, low / len(pieces), high / len(pieces)))
        level = level * jnp.repeat(heights, dims[dim] // parts).reshape([-1 if axis == dim else 1 for axis in range(len(dims))])
    return level


def setup_inputs(seed: int = 0) -> dict:
    arg_keys = jax.random.split(jax.random.key(seed), 7)
    return {
        "params": draw_params(jax.random.fold_in(arg_keys[6], 71), 0),
        "lists": draw_lists(jax.random.fold_in(arg_keys[6], 71), 0),
        "tile_pos": draw_tile_pos(jax.random.fold_in(arg_keys[6], 71), 0),
        "cam_index": plant(jax.random.randint(arg_keys[3], (TILES,), 0, VIEWS), jax.random.fold_in(arg_keys[3], 1), 0, VIEWS - 1).astype(jnp.int32),
        "cams": draw_cams(jax.random.fold_in(arg_keys[6], 71), 0),
        "targets": jnp.clip(1.0 * jax.random.uniform(arg_keys[5], (3, TILES, 256), jnp.float32) ** shard_levels(arg_keys[5], (3, TILES, 256), ((1, 32),), -0.2, 0.2), 0.0, 1.0),
    }


HIGH = lax.Precision.HIGHEST

def sh_terms(dir_x, dir_y, dir_z):
    return [jnp.ones_like(dir_x), dir_x, dir_y, dir_z, dir_x * dir_y, dir_y * dir_z, dir_x * dir_z, dir_x * dir_x - dir_y * dir_y, 3.0 * dir_z * dir_z - 1.0, dir_x * (dir_x * dir_x - 3.0 * dir_y * dir_y), dir_x * dir_y * dir_z, dir_y * (3.0 * dir_x * dir_x - dir_y * dir_y), dir_z * (dir_x * dir_x - dir_y * dir_y), dir_x * (5.0 * dir_z * dir_z - 1.0), dir_y * (5.0 * dir_z * dir_z - 1.0), dir_z * (5.0 * dir_z * dir_z - 3.0)]

def fix_rows(row_vals, is_live):
    return row_vals.at[6].set(jnp.where(is_live, row_vals[6], 1.0))

def project(row_vals, camcols):
    mean_x, mean_y, mean_z = (row_vals[0], row_vals[1], row_vals[2])
    cam_rot = [camcols[index] for index in range(9)]
    focal = camcols[12]
    cam_x = cam_rot[0] * mean_x + cam_rot[1] * mean_y + cam_rot[2] * mean_z + camcols[9]
    cam_y = cam_rot[3] * mean_x + cam_rot[4] * mean_y + cam_rot[5] * mean_z + camcols[10]
    cam_z = cam_rot[6] * mean_x + cam_rot[7] * mean_y + cam_rot[8] * mean_z + camcols[11]
    inv_z = 1.0 / cam_z
    quaternion = row_vals[6:10]
    q_norm = jnp.sqrt(lax.optimization_barrier(jnp.sum(quaternion * quaternion, axis=0)))
    unit_w = quaternion[0] / q_norm
    unit_x = quaternion[1] / q_norm
    unit_y = quaternion[2] / q_norm
    unit_z = quaternion[3] / q_norm
    rotation = [[1.0 - 2.0 * (unit_y * unit_y + unit_z * unit_z), 2.0 * (unit_x * unit_y - unit_w * unit_z), 2.0 * (unit_x * unit_z + unit_w * unit_y)], [2.0 * (unit_x * unit_y + unit_w * unit_z), 1.0 - 2.0 * (unit_x * unit_x + unit_z * unit_z), 2.0 * (unit_y * unit_z - unit_w * unit_x)], [2.0 * (unit_x * unit_z - unit_w * unit_y), 2.0 * (unit_y * unit_z + unit_w * unit_x), 1.0 - 2.0 * (unit_x * unit_x + unit_y * unit_y)]]
    mixed = [[cam_rot[3 * row_i] * rotation[0][col_k] + cam_rot[3 * row_i + 1] * rotation[1][col_k] + cam_rot[3 * row_i + 2] * rotation[2][col_k] for col_k in range(3)] for row_i in range(3)]
    jac_scale = focal * inv_z
    proj_u = [jac_scale * mixed[0][col_k] - jac_scale * cam_x * inv_z * mixed[2][col_k] for col_k in range(3)]
    proj_v = [jac_scale * mixed[1][col_k] - jac_scale * cam_y * inv_z * mixed[2][col_k] for col_k in range(3)]
    var_diag = jnp.exp(2.0 * row_vals[3:6])
    cov_a = proj_u[0] * proj_u[0] * var_diag[0] + proj_u[1] * proj_u[1] * var_diag[1] + proj_u[2] * proj_u[2] * var_diag[2] + 0.3
    cov_b = proj_u[0] * proj_v[0] * var_diag[0] + proj_u[1] * proj_v[1] * var_diag[1] + proj_u[2] * proj_v[2] * var_diag[2]
    cov_c = proj_v[0] * proj_v[0] * var_diag[0] + proj_v[1] * proj_v[1] * var_diag[1] + proj_v[2] * proj_v[2] * var_diag[2] + 0.3
    determinant = cov_a * cov_c - cov_b * cov_b
    opacity = jax.nn.sigmoid(row_vals[10])
    distance = jnp.sqrt(cam_x * cam_x + cam_y * cam_y + cam_z * cam_z)
    terms = sh_terms(cam_x / distance, cam_y / distance, cam_z / distance)
    colors = []
    for chan in range(3):
        shade = 0.5 + sum((row_vals[11 + 16 * chan + basis_b] * terms[basis_b] for basis_b in range(16)))
        shade = shade + sum((row_vals[59 + feat_j] * camcols[13 + 3 * feat_j + chan] for feat_j in range(5)))
        colors.append(shade)
    centre_u = focal * cam_x * inv_z
    centre_v = focal * cam_y * inv_z
    return jnp.stack([centre_u, centre_v, cov_c / determinant, -cov_b / determinant, cov_a / determinant, opacity, colors[0], colors[1], colors[2]])

def render(attrs, is_live, pixel_x, pixel_y):
    diff_x = pixel_x[None, :] - attrs[0][:, None]
    diff_y = pixel_y[None, :] - attrs[1][:, None]
    power = -0.5 * (attrs[2][:, None] * diff_x * diff_x + 2.0 * attrs[3][:, None] * diff_x * diff_y + attrs[4][:, None] * diff_y * diff_y)
    alpha = jnp.where(is_live[:, None], attrs[5][:, None] * jnp.exp(power), 0.0)
    keeping = jnp.cumprod(1.0 - alpha, axis=0)
    transmit = jnp.concatenate([jnp.ones((1, alpha.shape[1]), alpha.dtype), keeping[:-1]], axis=0)
    return jnp.dot(attrs[6:9], alpha * transmit, precision=HIGH)

def pixels(position):
    pixel_idx = jnp.arange(256)
    pixel_x = (16 * (position % WIN - WIN // 2) + pixel_idx % 16).astype(jnp.float32) + 0.5
    pixel_y = (16 * (position // WIN - WIN // 2) + pixel_idx // 16).astype(jnp.float32) + 0.5
    return (pixel_x, pixel_y)

def tile_grads(row_vals, camcol, is_live, pixel_x, pixel_y, target):

    def loss_of(params_in):
        picture = render(project(params_in, camcol[:, None]), is_live, pixel_x, pixel_y)
        return (0.5 * jnp.sum((picture - target) ** 2), picture)
    loss_val, pullback, picture = jax.vjp(loss_of, row_vals, has_aux=True)
    return (picture, pullback(jnp.ones_like(loss_val))[0])

def reference(params, lists, tile_pos, cam_index, cams, targets):
    num_gauss = params.shape[1]

    def one_tile(packed):
        ids, position, camera, target = packed
        is_live = ids >= 0
        row_vals = fix_rows(params[:, jnp.maximum(ids, 0)].astype(jnp.float32), is_live)
        camcol = cams[:, camera]
        pixel_x, pixel_y = pixels(position)
        return tile_grads(row_vals, camcol, is_live, pixel_x, pixel_y, target)
    pictures, tile_g = lax.map(one_tile, (lists, tile_pos, cam_index, jnp.transpose(targets, (1, 0, 2))), batch_size=64)
    flat_ids = jnp.where(lists >= 0, lists, num_gauss).reshape(-1)
    slot_g = jnp.transpose(tile_g, (1, 0, 2)).reshape(params.shape[0], -1)
    summed = jnp.zeros((params.shape[0], num_gauss), jnp.float32).at[:, flat_ids].add(slot_g, mode='drop')
    return (jnp.transpose(pictures, (1, 0, 2)), summed)
```

```python
import functools
import math

import jax
import jax.numpy as jnp
from jax import lax
from jax.experimental import pallas as pl
from jax.experimental.pallas import tpu as pltpu
from jax.sharding import PartitionSpec as P

WIN = 16
SIDE = 16
LANES = 128
LOG2E = math.log2(math.e)
F32 = jnp.float32
BF16 = jnp.bfloat16
VMEM_LIMIT = 24 * 2**20


def sh_terms(x, y, z):
    xx, yy, zz = x * x, y * y, z * z
    xy = x * y
    diff = xx - yy
    five = 5.0 * zz - 1.0
    return [
        x,
        y,
        z,
        xy,
        y * z,
        x * z,
        diff,
        3.0 * zz - 1.0,
        x * (xx - 3.0 * yy),
        xy * z,
        y * (3.0 * xx - yy),
        z * diff,
        x * five,
        y * five,
        z * (5.0 * zz - 3.0),
    ]


def project(rows, cam, live):
    mx, my, mz = rows[0], rows[1], rows[2]
    cam_x = cam[0] * mx + cam[1] * my + cam[2] * mz + cam[9]
    cam_y = cam[3] * mx + cam[4] * my + cam[5] * mz + cam[10]
    cam_z = cam[6] * mx + cam[7] * my + cam[8] * mz + cam[11]
    cam_z = jnp.where(live, cam_z, 1.0)
    inv_z = 1.0 / cam_z
    qw, qx, qy, qz = rows[6], rows[7], rows[8], rows[9]
    qw = jnp.where(live, qw, 1.0)
    inv_q = lax.rsqrt(qw * qw + qx * qx + qy * qy + qz * qz)
    qw, qx, qy, qz = qw * inv_q, qx * inv_q, qy * inv_q, qz * inv_q
    rot = [
        [
            1.0 - 2.0 * (qy * qy + qz * qz),
            2.0 * (qx * qy - qw * qz),
            2.0 * (qx * qz + qw * qy),
        ],
        [
            2.0 * (qx * qy + qw * qz),
            1.0 - 2.0 * (qx * qx + qz * qz),
            2.0 * (qy * qz - qw * qx),
        ],
        [
            2.0 * (qx * qz - qw * qy),
            2.0 * (qy * qz + qw * qx),
            1.0 - 2.0 * (qx * qx + qy * qy),
        ],
    ]
    mixed = [
        [
            cam[3 * i] * rot[0][k] + cam[3 * i + 1] * rot[1][k] + cam[3 * i + 2] * rot[2][k]
            for k in range(3)
        ]
        for i in range(3)
    ]
    scale = cam[12] * inv_z
    ray_x, ray_y = cam_x * inv_z, cam_y * inv_z
    proj_u = [scale * (mixed[0][k] - ray_x * mixed[2][k]) for k in range(3)]
    proj_v = [scale * (mixed[1][k] - ray_y * mixed[2][k]) for k in range(3)]
    var = [jnp.exp(2.0 * rows[3 + k]) for k in range(3)]
    uv = [proj_u[k] * var[k] for k in range(3)]
    cov_a = sum(uv[k] * proj_u[k] for k in range(3)) + 0.3
    cov_b = sum(uv[k] * proj_v[k] for k in range(3))
    cov_c = sum(proj_v[k] * proj_v[k] * var[k] for k in range(3)) + 0.3
    inv_det = 1.0 / (cov_a * cov_c - cov_b * cov_b)
    inv_dist = lax.rsqrt(cam_x * cam_x + cam_y * cam_y + cam_z * cam_z)
    terms = sh_terms(cam_x * inv_dist, cam_y * inv_dist, cam_z * inv_dist)
    geometry = [cam_x * scale, cam_y * scale, cov_c * inv_det, -cov_b * inv_det, cov_a * inv_det]
    return geometry + terms


def iota(shape, dim):
    return lax.broadcasted_iota(jnp.int32, shape, dim)


def one_hot(mask):
    return jnp.where(mask, 1.0, 0.0).astype(BF16)


def dot(lhs, rhs, lhs_dim=1, rhs_dim=0):
    return lax.dot_general(
        lhs, rhs, (((lhs_dim,), (rhs_dim,)), ((), ())), preferred_element_type=F32
    )


def split(x, parts):
    out = []
    for _ in range(parts):
        head = x.astype(BF16)
        out.append(head)
        x = x - head.astype(F32)
    return out


def ranks(mask, tiles):
    rows, length = mask.shape
    bits = one_hot(mask)
    earlier = one_hot(iota((length, length), 0) < iota((length, length), 1))
    within = dot(bits, earlier)
    count = dot(bits, jnp.ones((length, length), BF16)).astype(BF16)
    here, there = iota((rows, rows), 0), iota((rows, rows), 1)
    above = one_hot((there < here) & (there >= here - lax.rem(here, tiles)))
    return (within + dot(above, count)).astype(jnp.int32)


def pick_kernel(tiles, cap, me_ref, lists_ref, params_ref, picked_ref, hot_ref):
    ids = lists_ref[...]
    width, g_dev = params_ref.shape
    local = ids - me_ref[0] * g_dev
    mine = (local >= 0) & (local < g_dev)
    key = jnp.where(mine, ranks(mine, tiles), -1)
    length = ids.shape[1]
    renderers = ids.shape[0] // tiles
    slot = iota((cap, length), 0)
    found = []
    for r in range(renderers):
        total = jnp.zeros((cap, length), jnp.int32)
        for t in range(r * tiles, (r + 1) * tiles):
            total = total + jnp.where(key[t : t + 1, :] == slot, local[t : t + 1, :], 0)
        found.append(jnp.sum(total, axis=1, keepdims=True))
    where = jnp.concatenate(found, axis=0)
    hot = one_hot(where == iota((where.shape[0], g_dev), 1))
    hot_ref[...] = hot
    wide = jnp.concatenate([params_ref[...], jnp.zeros((LANES - width, g_dev), BF16)], axis=0)
    picked_ref[...] = dot(hot, wide, 1, 1).astype(BF16)


def render_kernel(
    owners,
    g_dev,
    tile_pos_ref,
    cam_index_ref,
    cams_ref,
    recv_ref,
    lists_ref,
    targets_ref,
    pictures_ref,
    send_ref,
    rows_ref,
    table_ref,
    alpha_ref,
    weight_ref,
    part_ref,
):
    tiles, length = lists_ref.shape
    slots = tiles * length
    cap = slots // owners
    width = rows_ref.shape[0] // tiles
    share = LANES // tiles
    depth = SIDE * SIDE // share
    ids = lists_ref[...]
    live = ids >= 0

    masks = [(ids >= o * g_dev) & (ids < (o + 1) * g_dev) for o in range(owners)]
    rank = ranks(jnp.concatenate([m.astype(jnp.int32) for m in masks], axis=0) > 0, tiles)
    place = jnp.full((tiles, length), -1, jnp.int32)
    for o in range(owners):
        place = jnp.where(masks[o], rank[o * tiles : (o + 1) * tiles] + o * cap, place)
    slot_iota = iota((slots, length), 0)
    hot = jnp.concatenate(
        [one_hot(slot_iota == place[t : t + 1, :]) for t in range(tiles)], axis=1
    )
    listed = dot(recv_ref[...], hot, 0, 0)
    for t in range(tiles):
        rows_ref[t * width : (t + 1) * width, :] = listed[
            :width, t * length : (t + 1) * length
        ]
    rows = [rows_ref[pl.ds(f, tiles, stride=width), :] for f in range(width)]

    tile_row = iota((tiles, length), 0)

    def by_tile(values, row):
        out = jnp.full(row.shape, values[tiles - 1])
        for t in range(tiles - 1):
            out = jnp.where(row == t, values[t], out)
        return out

    cam_ids = [cam_index_ref[t] for t in range(tiles)]
    cam = [
        by_tile([cams_ref[j, cam_ids[t]] for t in range(tiles)], tile_row)
        for j in range(cams_ref.shape[0])
    ]

    outs, pullback = jax.vjp(lambda r: project(r, cam, live), rows[:10])
    terms = outs[5:]
    colors = []
    for k in range(3):
        base = 11 + 16 * k
        shade = 0.5 + rows[base]
        for b in range(15):
            shade = shade + rows[base + 1 + b] * terms[b]
        for j in range(5):
            shade = shade + rows[59 + j] * cam[13 + 3 * j + k]
        colors.append(shade)
    opacity = jax.nn.sigmoid(rows[10])
    con_a, con_b, con_c = outs[2], outs[3], outs[4]

    attrs = [
        outs[0],
        outs[1],
        (-0.5 * LOG2E) * con_a,
        -LOG2E * con_b,
        (-0.5 * LOG2E) * con_c,
        jnp.where(live, opacity, 0.0),
    ] + colors
    count = len(attrs)
    blocks = []
    for value in attrs:
        pieces = [p.astype(F32) for p in split(value, 3)]
        pieces.append(jnp.zeros((16 - 3 * tiles, length), F32))
        blocks.append(jnp.concatenate(pieces, axis=0))
    stacked = jnp.concatenate(blocks, axis=1)
    lane_tile = iota((16, LANES), 1) // share
    row_index = iota((16, LANES), 0)
    spread = one_hot((row_index % tiles == lane_tile) & (row_index < 3 * tiles))
    table = dot(stacked.T.astype(BF16), spread)
    pos = [tile_pos_ref[t] for t in range(tiles)]
    lane_row = iota((1, LANES), 1)
    origin_x = [(SIDE * (lax.rem(p, WIN) - WIN // 2)).astype(F32) + 0.5 for p in pos]
    pixel_x = by_tile(origin_x, lane_row // share) + (lane_row % SIDE).astype(F32)
    dx = pixel_x - table[:length]
    table_ref[0:length, :] = table[2 * length : 3 * length] * dx * dx
    table_ref[length : 2 * length, :] = table[3 * length : 4 * length] * dx
    table_ref[2 * length : 3 * length, :] = table[length : 2 * length]
    table_ref[3 * length :, :] = table[4 * length :]

    lane = iota((depth, LANES), 1)
    origin_y = [(SIDE * (lax.div(p, WIN) - WIN // 2)).astype(F32) + 0.5 for p in pos]
    pixel_row = iota((depth, LANES), 0) * (share // SIDE) + (lane % share) // SIDE
    pixel_y = by_tile(origin_y, lane // share) + pixel_row.astype(F32)

    def row(index, l):
        return table_ref[pl.ds(index * length + l, 1), :]

    group = 16
    zero = jnp.zeros((depth, LANES), F32)

    def forward(chunk, carry):
        through, red, green, blue = carry
        for i in range(group):
            l = chunk * group + i
            dy = pixel_y - row(2, l)
            power = row(0, l) + dy * (row(1, l) + row(3, l) * dy)
            alpha = row(4, l) * jnp.exp2(power)
            weight = through * alpha
            red = red + weight * row(5, l)
            green = green + weight * row(6, l)
            blue = blue + weight * row(7, l)
            through = through - weight
            at = pl.ds(pl.multiple_of(l * depth, depth), depth)
            alpha_ref[at, :] = alpha
            weight_ref[at, :] = weight
        return through, red, green, blue

    start = (jnp.ones((depth, LANES), F32), zero, zero, zero)
    _, red, green, blue = lax.fori_loop(0, length // group, forward, start)
    pictures_ref[0] = red
    pictures_ref[1] = green
    pictures_ref[2] = blue
    res = [red - targets_ref[0], green - targets_ref[1], blue - targets_ref[2]]

    def backward(step, behind):
        chunk = length // group - 1 - step
        for i in reversed(range(group)):
            l = chunk * group + i
            at = pl.ds(pl.multiple_of(l * depth, depth), depth)
            alpha = alpha_ref[at, :]
            weight = weight_ref[at, :]
            dy = pixel_y - row(2, l)
            seen = row(5, l) * res[0] + row(6, l) * res[1] + row(7, l) * res[2]
            gap = seen - behind
            behind = behind + alpha * gap
            g = weight * gap
            gy = g * dy
            part_ref[0, at, :] = g
            part_ref[1, at, :] = gy
            part_ref[2, at, :] = gy * dy
            for k in range(3):
                part_ref[3 + k, at, :] = weight * res[k]
        return behind

    lax.fori_loop(0, length // group, backward, zero)

    def down(index):
        blocks = []
        for first in range(0, length, 8):
            pieces = [
                part_ref[index, pl.ds(first * depth + s, 8, stride=depth), :] for s in range(depth)
            ]
            while len(pieces) > 1:
                pieces = [a + b for a, b in zip(pieces[::2], pieces[1::2])]
            blocks.append(pieces[0])
        return jnp.concatenate(blocks, axis=0)

    sums = [down(index) for index in range(6)]
    g_x = sums[0] * dx
    sums = sums + [g_x, g_x * dx, sums[1] * dx]
    wide = jnp.concatenate([jnp.concatenate(split(s, 3), axis=1) for s in sums], axis=0)
    gather = one_hot(iota((8, 3 * LANES), 0) == (iota((8, 3 * LANES), 1) % LANES) // share)
    reduced = dot(gather, wide, 1, 1)
    g_0, g_y, g_yy, s_0, s_1, s_2, g_x, g_xx, g_xy = [
        reduced[:tiles, q * length : (q + 1) * length] for q in range(len(sums))
    ]

    d_colors = [s_0, s_1, s_2]
    d_terms = []
    for b in range(15):
        d_terms.append(sum(d_colors[k] * rows[12 + 16 * k + b] for k in range(3)))
    d_geometry = [
        con_a * g_x + con_b * g_y,
        con_b * g_x + con_c * g_y,
        -0.5 * g_xx,
        -g_xy,
        -0.5 * g_yy,
    ]
    (d_rows,) = pullback(d_geometry + d_terms)
    d_rows = list(d_rows)
    d_rows.append(g_0 * (1.0 - opacity))
    for k in range(3):
        d_rows.append(d_colors[k])
        d_rows.extend(d_colors[k] * terms[b] for b in range(15))
    for j in range(5):
        d_rows.append(sum(d_colors[k] * cam[13 + 3 * j + k] for k in range(3)))
    for f in range(width):
        rows_ref[pl.ds(f, tiles, stride=width), :] = d_rows[f]
    sent = jnp.concatenate(
        [
            jnp.concatenate(split(rows_ref[t * width : (t + 1) * width, :], 2), axis=0)
            for t in range(tiles)
        ],
        axis=1,
    )
    send_ref[...] = dot(hot, sent, 1, 1).astype(BF16)


def scatter_kernel(hot_ref, recv_ref, out_ref):
    width = out_ref.shape[0]
    total = dot(recv_ref[...], hot_ref[...], 0, 0)
    out_ref[...] = total[:width] + total[width : 2 * width]


def call(kernel, out_shape, args, scalars=0, scratch=()):
    in_specs = [pl.BlockSpec(memory_space=pltpu.SMEM)] * scalars
    in_specs += [pl.BlockSpec(memory_space=pltpu.VMEM)] * (len(args) - scalars)
    many = isinstance(out_shape, (list, tuple))
    spec = pl.BlockSpec(memory_space=pltpu.VMEM)
    return pl.pallas_call(
        kernel,
        out_shape=out_shape,
        in_specs=in_specs,
        out_specs=[spec] * len(out_shape) if many else spec,
        scratch_shapes=list(scratch),
        compiler_params=pltpu.CompilerParams(vmem_limit_bytes=VMEM_LIMIT),
    )(*args)


def exchange(x, owners):
    blocks = x.reshape(owners, x.shape[0] // owners, *x.shape[1:])
    moved = lax.all_to_all(blocks, "gauss", split_axis=0, concat_axis=0, tiled=True)
    return moved.reshape(x.shape)


def on_device(params, lists, tile_pos, cam_index, cams, targets):
    owners = lax.axis_size("gauss")
    views = lax.axis_size("view")
    width, g_dev = params.shape
    tiles, length = lists.shape
    slots = tiles * length
    cap = slots // owners
    share = LANES // tiles
    depth = SIDE * SIDE // share
    me = lax.axis_index("gauss").reshape(1)

    all_lists = exchange(
        jnp.broadcast_to(lists[None], (owners, tiles, length)).reshape(owners * tiles, length),
        owners,
    )
    picked, hot = call(
        functools.partial(pick_kernel, tiles, cap),
        [
            jax.ShapeDtypeStruct((slots, LANES), BF16),
            jax.ShapeDtypeStruct((slots, g_dev), BF16),
        ],
        (me, all_lists, params),
        scalars=1,
    )
    returned = exchange(picked, owners)
    spread_targets = (
        targets.reshape(3, tiles, depth, share).transpose(0, 2, 1, 3).reshape(3, depth, LANES)
    )
    pictures, sent = call(
        functools.partial(render_kernel, owners, g_dev),
        [
            jax.ShapeDtypeStruct((3, depth, LANES), F32),
            jax.ShapeDtypeStruct((slots, LANES), BF16),
        ],
        (tile_pos, cam_index, cams, returned, lists, spread_targets),
        scalars=3,
        scratch=(
            pltpu.VMEM((tiles * width, length), F32),
            pltpu.VMEM((8 * length, LANES), F32),
            pltpu.VMEM((length * depth, LANES), F32),
            pltpu.VMEM((length * depth, LANES), F32),
            pltpu.VMEM((6, length * depth, LANES), F32),
        ),
    )
    pictures = (
        pictures.reshape(3, depth, tiles, share)
        .transpose(0, 2, 1, 3)
        .reshape(3, tiles, SIDE * SIDE)
    )
    row_g = exchange(sent, owners)
    grads = call(scatter_kernel, jax.ShapeDtypeStruct((width, g_dev), F32), (hot, row_g))
    step = 1
    while step < views:
        grads = grads + lax.ppermute(grads, "view", [(i, i ^ step) for i in range(views)])
        step *= 2
    return (pictures, grads)


def solution(mesh):
    return jax.shard_map(
        on_device,
        mesh=mesh,
        in_specs=(
            P(None, "gauss"),
            P(("gauss", "view"), None),
            P(("gauss", "view")),
            P(("gauss", "view")),
            P(),
            P(None, ("gauss", "view"), None),
        ),
        out_specs=(P(None, ("gauss", "view"), None), P(None, "gauss")),
        check_vma=False,
    )
```

```python
import functools
import math

import jax
import jax.numpy as jnp
from jax import lax
from jax.experimental import pallas as pl
from jax.experimental.pallas import tpu as pltpu
from jax.sharding import PartitionSpec as P

WIN = 16
SIDE = 16
LANES = 128
LOG2E = math.log2(math.e)
F32 = jnp.float32
BF16 = jnp.bfloat16
VMEM_LIMIT = 24 * 2**20


def sh_terms(x, y, z):
    xx, yy, zz = x * x, y * y, z * z
    xy = x * y
    diff = xx - yy
    five = 5.0 * zz - 1.0
    return [
        x,
        y,
        z,
        xy,
        y * z,
        x * z,
        diff,
        3.0 * zz - 1.0,
        x * (xx - 3.0 * yy),
        xy * z,
        y * (3.0 * xx - yy),
        z * diff,
        x * five,
        y * five,
        z * (5.0 * zz - 3.0),
    ]


def project(rows, cam, live):
    mx, my, mz = rows[0], rows[1], rows[2]
    cam_x = cam[0] * mx + cam[1] * my + cam[2] * mz + cam[9]
    cam_y = cam[3] * mx + cam[4] * my + cam[5] * mz + cam[10]
    cam_z = cam[6] * mx + cam[7] * my + cam[8] * mz + cam[11]
    cam_z = jnp.where(live, cam_z, 1.0)
    inv_z = 1.0 / cam_z
    qw, qx, qy, qz = rows[6], rows[7], rows[8], rows[9]
    qw = jnp.where(live, qw, 1.0)
    inv_q = lax.rsqrt(qw * qw + qx * qx + qy * qy + qz * qz)
    qw, qx, qy, qz = qw * inv_q, qx * inv_q, qy * inv_q, qz * inv_q
    rot = [
        [
            1.0 - 2.0 * (qy * qy + qz * qz),
            2.0 * (qx * qy - qw * qz),
            2.0 * (qx * qz + qw * qy),
        ],
        [
            2.0 * (qx * qy + qw * qz),
            1.0 - 2.0 * (qx * qx + qz * qz),
            2.0 * (qy * qz - qw * qx),
        ],
        [
            2.0 * (qx * qz - qw * qy),
            2.0 * (qy * qz + qw * qx),
            1.0 - 2.0 * (qx * qx + qy * qy),
        ],
    ]
    mixed = [
        [
            cam[3 * i] * rot[0][k] + cam[3 * i + 1] * rot[1][k] + cam[3 * i + 2] * rot[2][k]
            for k in range(3)
        ]
        for i in range(3)
    ]
    scale = cam[12] * inv_z
    ray_x, ray_y = cam_x * inv_z, cam_y * inv_z
    proj_u = [scale * (mixed[0][k] - ray_x * mixed[2][k]) for k in range(3)]
    proj_v = [scale * (mixed[1][k] - ray_y * mixed[2][k]) for k in range(3)]
    var = [jnp.exp(2.0 * rows[3 + k]) for k in range(3)]
    uv = [proj_u[k] * var[k] for k in range(3)]
    cov_a = sum(uv[k] * proj_u[k] for k in range(3)) + 0.3
    cov_b = sum(uv[k] * proj_v[k] for k in range(3))
    cov_c = sum(proj_v[k] * proj_v[k] * var[k] for k in range(3)) + 0.3
    inv_det = 1.0 / (cov_a * cov_c - cov_b * cov_b)
    inv_dist = lax.rsqrt(cam_x * cam_x + cam_y * cam_y + cam_z * cam_z)
    terms = sh_terms(cam_x * inv_dist, cam_y * inv_dist, cam_z * inv_dist)
    geometry = [cam_x * scale, cam_y * scale, cov_c * inv_det, -cov_b * inv_det, cov_a * inv_det]
    return geometry + terms


def iota(shape, dim):
    return lax.broadcasted_iota(jnp.int32, shape, dim)


def one_hot(mask):
    return jnp.where(mask, 1.0, 0.0).astype(BF16)


def dot(lhs, rhs, lhs_dim=1, rhs_dim=0):
    return lax.dot_general(
        lhs, rhs, (((lhs_dim,), (rhs_dim,)), ((), ())), preferred_element_type=F32
    )


def split(x, parts):
    out = []
    for _ in range(parts):
        head = x.astype(BF16)
        out.append(head)
        x = x - head.astype(F32)
    return out


def ranks(mask, tiles):
    rows, length = mask.shape
    bits = one_hot(mask)
    earlier = one_hot(iota((length, length), 0) < iota((length, length), 1))
    within = dot(bits, earlier)
    count = dot(bits, jnp.ones((length, length), BF16)).astype(BF16)
    here, there = iota((rows, rows), 0), iota((rows, rows), 1)
    above = one_hot((there < here) & (there >= here - lax.rem(here, tiles)))
    return (within + dot(above, count)).astype(jnp.int32)


def pick_kernel(tiles, cap, pieces, me_ref, *refs):
    lists_refs, params_ref, picked_refs, hot_ref = (
        refs[:pieces],
        refs[pieces],
        refs[pieces + 1 : 2 * pieces + 1],
        refs[-1],
    )
    ids = jnp.concatenate([ref[...] for ref in lists_refs], axis=0)
    width, g_dev = params_ref.shape
    local = ids - me_ref[0] * g_dev
    mine = (local >= 0) & (local < g_dev)
    key = jnp.where(mine, ranks(mine, tiles), -1)
    length = ids.shape[1]
    renderers = ids.shape[0] // tiles
    slot = iota((cap, length), 0)
    found = []
    for r in range(renderers):
        total = jnp.zeros((cap, length), jnp.int32)
        for t in range(r * tiles, (r + 1) * tiles):
            total = total + jnp.where(key[t : t + 1, :] == slot, local[t : t + 1, :], 0)
        found.append(jnp.sum(total, axis=1, keepdims=True))
    where = jnp.concatenate(found, axis=0)
    hot = one_hot(where == iota((where.shape[0], g_dev), 1))
    hot_ref[...] = hot
    wide = jnp.concatenate([params_ref[...], jnp.zeros((LANES - width, g_dev), BF16)], axis=0)
    picked = dot(hot, wide, 1, 1).astype(BF16)
    block = picked.shape[0] // pieces
    for k in range(pieces):
        picked_refs[k][...] = picked[k * block : (k + 1) * block]


def render_kernel(owners, g_dev, pieces, me_ref, tile_pos_ref, cam_index_ref, cams_ref, *refs):
    recv_refs, refs = refs[:pieces], refs[pieces:]
    lists_ref, targets_ref, pictures_ref = refs[:3]
    send_refs, refs = refs[3 : 3 + pieces], refs[3 + pieces :]
    rows_ref, table_ref, alpha_ref, weight_ref, part_ref = refs
    tiles, length = lists_ref.shape
    slots = tiles * length
    cap = slots // owners
    width = rows_ref.shape[0] // tiles
    share = LANES // tiles
    depth = SIDE * SIDE // share
    ids = lists_ref[...]
    live = ids >= 0

    peers = [o if pieces == 1 else me_ref[0] ^ o for o in range(owners)]
    masks = [(ids >= o * g_dev) & (ids < (o + 1) * g_dev) for o in peers]
    rank = ranks(jnp.concatenate([m.astype(jnp.int32) for m in masks], axis=0) > 0, tiles)
    place = jnp.full((tiles, length), -1, jnp.int32)
    for o in range(owners):
        place = jnp.where(masks[o], rank[o * tiles : (o + 1) * tiles] + o * cap, place)
    slot_iota = iota((slots, length), 0)
    hot = jnp.concatenate(
        [one_hot(slot_iota == place[t : t + 1, :]) for t in range(tiles)], axis=1
    )
    received = jnp.concatenate([ref[...] for ref in recv_refs], axis=0)
    listed = dot(received, hot, 0, 0)
    for t in range(tiles):
        rows_ref[t * width : (t + 1) * width, :] = listed[
            :width, t * length : (t + 1) * length
        ]
    rows = [rows_ref[pl.ds(f, tiles, stride=width), :] for f in range(width)]

    tile_row = iota((tiles, length), 0)

    def by_tile(values, row):
        out = jnp.full(row.shape, values[tiles - 1])
        for t in range(tiles - 1):
            out = jnp.where(row == t, values[t], out)
        return out

    cam_ids = [cam_index_ref[t] for t in range(tiles)]
    cam = [
        by_tile([cams_ref[j, cam_ids[t]] for t in range(tiles)], tile_row)
        for j in range(cams_ref.shape[0])
    ]

    outs, pullback = jax.vjp(lambda r: project(r, cam, live), rows[:10])
    terms = outs[5:]
    colors = []
    for k in range(3):
        base = 11 + 16 * k
        shade = 0.5 + rows[base]
        for b in range(15):
            shade = shade + rows[base + 1 + b] * terms[b]
        for j in range(5):
            shade = shade + rows[59 + j] * cam[13 + 3 * j + k]
        colors.append(shade)
    opacity = jax.nn.sigmoid(rows[10])
    con_a, con_b, con_c = outs[2], outs[3], outs[4]

    attrs = [
        outs[0],
        outs[1],
        (-0.5 * LOG2E) * con_a,
        -LOG2E * con_b,
        (-0.5 * LOG2E) * con_c,
        jnp.where(live, opacity, 0.0),
    ] + colors
    count = len(attrs)
    blocks = []
    for value in attrs:
        parts = [p.astype(F32) for p in split(value, 3)]
        parts.append(jnp.zeros((16 - 3 * tiles, length), F32))
        blocks.append(jnp.concatenate(parts, axis=0))
    stacked = jnp.concatenate(blocks, axis=1)
    lane_tile = iota((16, LANES), 1) // share
    row_index = iota((16, LANES), 0)
    spread = one_hot((row_index % tiles == lane_tile) & (row_index < 3 * tiles))
    table = dot(stacked.T.astype(BF16), spread)
    pos = [tile_pos_ref[t] for t in range(tiles)]
    lane_row = iota((1, LANES), 1)
    origin_x = [(SIDE * (lax.rem(p, WIN) - WIN // 2)).astype(F32) + 0.5 for p in pos]
    pixel_x = by_tile(origin_x, lane_row // share) + (lane_row % SIDE).astype(F32)
    dx = pixel_x - table[:length]
    table_ref[0:length, :] = table[2 * length : 3 * length] * dx * dx
    table_ref[length : 2 * length, :] = table[3 * length : 4 * length] * dx
    table_ref[2 * length : 3 * length, :] = table[length : 2 * length]
    table_ref[3 * length :, :] = table[4 * length :]

    lane = iota((depth, LANES), 1)
    origin_y = [(SIDE * (lax.div(p, WIN) - WIN // 2)).astype(F32) + 0.5 for p in pos]
    pixel_row = iota((depth, LANES), 0) * (share // SIDE) + (lane % share) // SIDE
    pixel_y = by_tile(origin_y, lane // share) + pixel_row.astype(F32)

    def row(index, l):
        return table_ref[pl.ds(index * length + l, 1), :]

    group = 16
    zero = jnp.zeros((depth, LANES), F32)

    def forward(chunk, carry):
        through, red, green, blue = carry
        for i in range(group):
            l = chunk * group + i
            dy = pixel_y - row(2, l)
            power = row(0, l) + dy * (row(1, l) + row(3, l) * dy)
            alpha = row(4, l) * jnp.exp2(power)
            weight = through * alpha
            red = red + weight * row(5, l)
            green = green + weight * row(6, l)
            blue = blue + weight * row(7, l)
            through = through - weight
            at = pl.ds(pl.multiple_of(l * depth, depth), depth)
            alpha_ref[at, :] = alpha
            weight_ref[at, :] = weight
        return through, red, green, blue

    start = (jnp.ones((depth, LANES), F32), zero, zero, zero)
    _, red, green, blue = lax.fori_loop(0, length // group, forward, start)
    pictures_ref[0] = red
    pictures_ref[1] = green
    pictures_ref[2] = blue
    res = [red - targets_ref[0], green - targets_ref[1], blue - targets_ref[2]]

    def backward(step, behind):
        chunk = length // group - 1 - step
        for i in reversed(range(group)):
            l = chunk * group + i
            at = pl.ds(pl.multiple_of(l * depth, depth), depth)
            alpha = alpha_ref[at, :]
            weight = weight_ref[at, :]
            dy = pixel_y - row(2, l)
            seen = row(5, l) * res[0] + row(6, l) * res[1] + row(7, l) * res[2]
            gap = seen - behind
            behind = behind + alpha * gap
            g = weight * gap
            gy = g * dy
            part_ref[0, at, :] = g
            part_ref[1, at, :] = gy
            part_ref[2, at, :] = gy * dy
            for k in range(3):
                part_ref[3 + k, at, :] = weight * res[k]
        return behind

    lax.fori_loop(0, length // group, backward, zero)

    def down(index):
        blocks = []
        for first in range(0, length, 8):
            parts = [
                part_ref[index, pl.ds(first * depth + s, 8, stride=depth), :] for s in range(depth)
            ]
            while len(parts) > 1:
                parts = [a + b for a, b in zip(parts[::2], parts[1::2])]
            blocks.append(parts[0])
        return jnp.concatenate(blocks, axis=0)

    sums = [down(index) for index in range(6)]
    g_x = sums[0] * dx
    sums = sums + [g_x, g_x * dx, sums[1] * dx]
    wide = jnp.concatenate([jnp.concatenate(split(s, 3), axis=1) for s in sums], axis=0)
    gather = one_hot(iota((8, 3 * LANES), 0) == (iota((8, 3 * LANES), 1) % LANES) // share)
    reduced = dot(gather, wide, 1, 1)
    g_0, g_y, g_yy, s_0, s_1, s_2, g_x, g_xx, g_xy = [
        reduced[:tiles, q * length : (q + 1) * length] for q in range(len(sums))
    ]

    d_colors = [s_0, s_1, s_2]
    d_terms = []
    for b in range(15):
        d_terms.append(sum(d_colors[k] * rows[12 + 16 * k + b] for k in range(3)))
    d_geometry = [
        con_a * g_x + con_b * g_y,
        con_b * g_x + con_c * g_y,
        -0.5 * g_xx,
        -g_xy,
        -0.5 * g_yy,
    ]
    (d_rows,) = pullback(d_geometry + d_terms)
    d_rows = list(d_rows)
    d_rows.append(g_0 * (1.0 - opacity))
    for k in range(3):
        d_rows.append(d_colors[k])
        d_rows.extend(d_colors[k] * terms[b] for b in range(15))
    for j in range(5):
        d_rows.append(sum(d_colors[k] * cam[13 + 3 * j + k] for k in range(3)))
    for f in range(width):
        rows_ref[pl.ds(f, tiles, stride=width), :] = d_rows[f]
    sent = jnp.concatenate(
        [
            jnp.concatenate(split(rows_ref[t * width : (t + 1) * width, :], 2), axis=0)
            for t in range(tiles)
        ],
        axis=1,
    )
    sorted_g = dot(hot, sent, 1, 1).astype(BF16)
    block = slots // pieces
    for k in range(pieces):
        send_refs[k][...] = sorted_g[k * block : (k + 1) * block]


def scatter_kernel(halves, bit_ref, hot_ref, *refs):
    recv_refs, out_refs = refs[:-halves], refs[-halves:]
    received = jnp.concatenate([ref[...] for ref in recv_refs], axis=0)
    total = dot(received, hot_ref[...], 0, 0)
    width = total.shape[0] // 2
    total = total[:width] + total[width:]
    if halves == 1:
        out_refs[0][...] = total
        return
    low, high = total[: width // 2], total[width // 2 :]
    first = bit_ref[0] == 0
    out_refs[0][...] = jnp.where(first, low, high)
    out_refs[1][...] = jnp.where(first, high, low)


def call(kernel, out_shape, args, scalars=0, scratch=()):
    in_specs = [pl.BlockSpec(memory_space=pltpu.SMEM)] * scalars
    in_specs += [pl.BlockSpec(memory_space=pltpu.VMEM)] * (len(args) - scalars)
    many = isinstance(out_shape, (list, tuple))
    spec = pl.BlockSpec(memory_space=pltpu.VMEM)
    return pl.pallas_call(
        kernel,
        out_shape=out_shape,
        in_specs=in_specs,
        out_specs=[spec] * len(out_shape) if many else spec,
        scratch_shapes=list(scratch),
        compiler_params=pltpu.CompilerParams(vmem_limit_bytes=VMEM_LIMIT),
    )(*args)


def swap(x, axis, k):
    return lax.ppermute(x, axis, [(i, i ^ k) for i in range(lax.axis_size(axis))])


def exchange(blocks):
    owners = lax.axis_size("gauss")
    if len(blocks) == owners:
        return [b if k == 0 else swap(b, "gauss", k) for k, b in enumerate(blocks)]
    (x,) = blocks
    parts = x.reshape(owners, x.shape[0] // owners, *x.shape[1:])
    moved = lax.all_to_all(parts, "gauss", split_axis=0, concat_axis=0, tiled=True)
    return [moved.reshape(x.shape)]


def power_of_two(n):
    return n & (n - 1) == 0


def on_device(params, lists, tile_pos, cam_index, cams, targets):
    owners = lax.axis_size("gauss")
    views = lax.axis_size("view")
    width, g_dev = params.shape
    tiles, length = lists.shape
    slots = tiles * length
    cap = slots // owners
    share = LANES // tiles
    depth = SIDE * SIDE // share
    me = lax.axis_index("gauss").reshape(1)
    pieces = owners if owners <= 16 and power_of_two(owners) else 1
    block = slots // pieces

    if pieces == 1:
        mine = jnp.broadcast_to(lists[None], (owners, tiles, length))
        all_lists = exchange([mine.reshape(owners * tiles, length)])
    else:
        all_lists = exchange([lists] * pieces)
    outs = call(
        functools.partial(pick_kernel, tiles, cap, pieces),
        [jax.ShapeDtypeStruct((block, LANES), BF16)] * pieces
        + [jax.ShapeDtypeStruct((slots, g_dev), BF16)],
        (me, *all_lists, params),
        scalars=1,
    )
    picked, hot = outs[:pieces], outs[pieces]
    returned = exchange(picked)
    spread_targets = (
        targets.reshape(3, tiles, depth, share).transpose(0, 2, 1, 3).reshape(3, depth, LANES)
    )
    pictures, *sent = call(
        functools.partial(render_kernel, owners, g_dev, pieces),
        [jax.ShapeDtypeStruct((3, depth, LANES), F32)]
        + [jax.ShapeDtypeStruct((block, LANES), BF16)] * pieces,
        (me, tile_pos, cam_index, cams, *returned, lists, spread_targets),
        scalars=4,
        scratch=(
            pltpu.VMEM((tiles * width, length), F32),
            pltpu.VMEM((8 * length, LANES), F32),
            pltpu.VMEM((length * depth, LANES), F32),
            pltpu.VMEM((length * depth, LANES), F32),
            pltpu.VMEM((6, length * depth, LANES), F32),
        ),
    )
    pictures = (
        pictures.reshape(3, depth, tiles, share)
        .transpose(0, 2, 1, 3)
        .reshape(3, tiles, SIDE * SIDE)
    )
    row_g = exchange(sent)
    halves = 2 if views > 1 and power_of_two(views) else 1
    bit = (lax.axis_index("view") % 2).reshape(1)
    totals = call(
        functools.partial(scatter_kernel, halves),
        [jax.ShapeDtypeStruct((width // halves, g_dev), F32)] * halves,
        (bit, hot, *row_g),
        scalars=1,
    )
    if halves == 1:
        return (pictures, lax.psum(totals[0], "view"))
    kept, given = totals
    kept = kept + swap(given, "view", 1)
    step = 2
    while step < views:
        kept = kept + swap(kept, "view", step)
        step *= 2
    other = swap(kept, "view", 1)
    first = bit[0] == 0
    grads = jnp.concatenate(
        [jnp.where(first, kept, other), jnp.where(first, other, kept)], axis=0
    )
    return (pictures, grads)


def solution(mesh):
    return jax.shard_map(
        on_device,
        mesh=mesh,
        in_specs=(
            P(None, "gauss"),
            P(("gauss", "view"), None),
            P(("gauss", "view")),
            P(("gauss", "view")),
            P(),
            P(None, ("gauss", "view"), None),
        ),
        out_specs=(P(None, ("gauss", "view"), None), P(None, "gauss")),
        check_vma=False,
    )
```

```python
import functools
import math

import jax
import jax.numpy as jnp
from jax import lax
from jax.experimental import pallas as pl
from jax.experimental.pallas import tpu as pltpu
from jax.sharding import PartitionSpec as P

WIN = 16
SIDE = 16
LANES = 128
LOG2E = math.log2(math.e)
F32 = jnp.float32
BF16 = jnp.bfloat16
VMEM_LIMIT = 24 * 2**20


def sh_terms(x, y, z):
    xx, yy, zz = x * x, y * y, z * z
    xy = x * y
    diff = xx - yy
    five = 5.0 * zz - 1.0
    return [
        x,
        y,
        z,
        xy,
        y * z,
        x * z,
        diff,
        3.0 * zz - 1.0,
        x * (xx - 3.0 * yy),
        xy * z,
        y * (3.0 * xx - yy),
        z * diff,
        x * five,
        y * five,
        z * (5.0 * zz - 3.0),
    ]


def project(rows, cam, live):
    mx, my, mz = rows[0], rows[1], rows[2]
    cam_x = cam[0] * mx + cam[1] * my + cam[2] * mz + cam[9]
    cam_y = cam[3] * mx + cam[4] * my + cam[5] * mz + cam[10]
    cam_z = cam[6] * mx + cam[7] * my + cam[8] * mz + cam[11]
    cam_z = jnp.where(live, cam_z, 1.0)
    inv_z = 1.0 / cam_z
    qw, qx, qy, qz = rows[6], rows[7], rows[8], rows[9]
    qw = jnp.where(live, qw, 1.0)
    inv_q = lax.rsqrt(qw * qw + qx * qx + qy * qy + qz * qz)
    qw, qx, qy, qz = qw * inv_q, qx * inv_q, qy * inv_q, qz * inv_q
    rot = [
        [
            1.0 - 2.0 * (qy * qy + qz * qz),
            2.0 * (qx * qy - qw * qz),
            2.0 * (qx * qz + qw * qy),
        ],
        [
            2.0 * (qx * qy + qw * qz),
            1.0 - 2.0 * (qx * qx + qz * qz),
            2.0 * (qy * qz - qw * qx),
        ],
        [
            2.0 * (qx * qz - qw * qy),
            2.0 * (qy * qz + qw * qx),
            1.0 - 2.0 * (qx * qx + qy * qy),
        ],
    ]
    mixed = [
        [
            cam[3 * i] * rot[0][k] + cam[3 * i + 1] * rot[1][k] + cam[3 * i + 2] * rot[2][k]
            for k in range(3)
        ]
        for i in range(3)
    ]
    scale = cam[12] * inv_z
    ray_x, ray_y = cam_x * inv_z, cam_y * inv_z
    proj_u = [scale * (mixed[0][k] - ray_x * mixed[2][k]) for k in range(3)]
    proj_v = [scale * (mixed[1][k] - ray_y * mixed[2][k]) for k in range(3)]
    var = [jnp.exp(2.0 * rows[3 + k]) for k in range(3)]
    uv = [proj_u[k] * var[k] for k in range(3)]
    cov_a = sum(uv[k] * proj_u[k] for k in range(3)) + 0.3
    cov_b = sum(uv[k] * proj_v[k] for k in range(3))
    cov_c = sum(proj_v[k] * proj_v[k] * var[k] for k in range(3)) + 0.3
    inv_det = 1.0 / (cov_a * cov_c - cov_b * cov_b)
    inv_dist = lax.rsqrt(cam_x * cam_x + cam_y * cam_y + cam_z * cam_z)
    terms = sh_terms(cam_x * inv_dist, cam_y * inv_dist, cam_z * inv_dist)
    geometry = [cam_x * scale, cam_y * scale, cov_c * inv_det, -cov_b * inv_det, cov_a * inv_det]
    return geometry + terms


def iota(shape, dim):
    return lax.broadcasted_iota(jnp.int32, shape, dim)


def one_hot(mask):
    return jnp.where(mask, 1.0, 0.0).astype(BF16)


def dot(lhs, rhs, lhs_dim=1, rhs_dim=0):
    return lax.dot_general(
        lhs, rhs, (((lhs_dim,), (rhs_dim,)), ((), ())), preferred_element_type=F32
    )


def split(x, parts):
    out = []
    for _ in range(parts):
        head = x.astype(BF16)
        out.append(head)
        x = x - head.astype(F32)
    return out


def ranks(mask, tiles):
    rows, length = mask.shape
    bits = one_hot(mask)
    earlier = one_hot(iota((length, length), 0) < iota((length, length), 1))
    within = dot(bits, earlier)
    count = dot(bits, jnp.ones((length, length), BF16)).astype(BF16)
    here, there = iota((rows, rows), 0), iota((rows, rows), 1)
    above = one_hot((there < here) & (there >= here - lax.rem(here, tiles)))
    return (within + dot(above, count)).astype(jnp.int32)


def find(ids, base, tiles, cap, g_dev):
    local = ids - base
    mine = (local >= 0) & (local < g_dev)
    key = jnp.where(mine, ranks(mine, tiles), -1)
    rows, length = ids.shape
    slot = iota((cap, length), 0)
    found = []
    for r in range(0, rows, tiles):
        total = jnp.zeros((cap, length), jnp.int32)
        for t in range(r, r + tiles):
            total = total + jnp.where(key[t : t + 1, :] == slot, local[t : t + 1, :], 0)
        found.append(jnp.sum(total, axis=1, keepdims=True))
    return jnp.concatenate(found, axis=0)


def as_rows(column):
    wide = jnp.broadcast_to(column.astype(F32), (column.shape[0], LANES))
    return wide.T[:8].astype(jnp.int32)


def pick_kernel(tiles, cap, me_ref, lists_ref, params_ref, picked_ref, where_ref):
    width, g_dev = params_ref.shape
    where = find(lists_ref[...], me_ref[0] * g_dev, tiles, cap, g_dev)
    hot = one_hot(where == iota((where.shape[0], g_dev), 1))
    wide = jnp.concatenate([params_ref[...], jnp.zeros((LANES - width, g_dev), BF16)], axis=0)
    picked_ref[...] = dot(hot, wide, 1, 1).astype(BF16)
    where_ref[...] = as_rows(where)


def pick_pair_kernel(cap, peers, me_ref, *refs):
    lists_refs, refs = refs[:peers], refs[peers:]
    own_ref, other_ref = refs[:2]
    picked_refs, refs = refs[2 : 2 + peers], refs[2 + peers :]
    where_own_ref, where_other_ref, lists_scratch, picked_scratch = refs
    tiles, length = lists_refs[0].shape
    width, g_dev = own_ref.shape
    me = me_ref[0]
    first = me % 2 == 0
    for k in range(peers):
        lists_scratch[(me // 2) ^ k] = lists_refs[k][...]
    ids = lists_scratch[...].reshape(peers * tiles, length)
    where_own = find(ids, me * g_dev, tiles, cap, g_dev)
    where_other = find(ids, (me ^ 1) * g_dev, tiles, cap, g_dev)
    own, other = own_ref[...], other_ref[...]
    blank = jnp.zeros((width, g_dev), BF16)
    lanes = iota((peers * cap, g_dev), 1)
    picked = dot(
        one_hot(where_own == lanes),
        jnp.concatenate([jnp.where(first, own, blank), jnp.where(first, blank, own)], axis=0),
        1,
        1,
    ) + dot(
        one_hot(where_other == lanes),
        jnp.concatenate([jnp.where(first, blank, other), jnp.where(first, other, blank)], axis=0),
        1,
        1,
    )
    picked_scratch[...] = picked.astype(BF16).reshape(peers, cap, 2 * width)
    for k in range(peers):
        picked_refs[k][...] = picked_scratch[(me // 2) ^ k]
    where_own_ref[...] = as_rows(where_own)
    where_other_ref[...] = as_rows(where_other)


def prepare_kernel(owners, g_dev, lists_ref, params_ref, hot_ref, copy_ref):
    tiles, length = lists_ref.shape
    slots = tiles * length
    cap = slots // owners
    ids = lists_ref[...]
    masks = [(ids >= o * g_dev) & (ids < (o + 1) * g_dev) for o in range(owners)]
    rank = ranks(jnp.concatenate([m.astype(jnp.int32) for m in masks], axis=0) > 0, tiles)
    place = jnp.full((tiles, length), -1, jnp.int32)
    for o in range(owners):
        place = jnp.where(masks[o], rank[o * tiles : (o + 1) * tiles] + o * cap, place)
    slot_iota = iota((slots, length), 0)
    hot_ref[...] = jnp.concatenate(
        [one_hot(slot_iota == place[t : t + 1, :]) for t in range(tiles)], axis=1
    )
    copy_ref[...] = params_ref[...]


def render_kernel(pieces, width, me_ref, tile_pos_ref, cam_index_ref, cams_ref, *refs):
    recv_refs, refs = refs[:pieces], refs[pieces:]
    lists_ref, hot_ref, targets_ref, pictures_ref, send_ref = refs[:5]
    rows_ref, table_ref, alpha_ref, weight_ref, part_ref = refs[5:10]
    tiles, length = lists_ref.shape
    share = LANES // tiles
    depth = SIDE * SIDE // share
    live = lists_ref[...] >= 0
    hot = hot_ref[...]

    if pieces == 1:
        listed = dot(recv_refs[0][...], hot, 0, 0)[:width]
    else:
        (recv_scratch,) = refs[10:]
        cap = recv_refs[0].shape[0]
        for k in range(pieces):
            recv_scratch[(me_ref[0] // 2) ^ k] = recv_refs[k][...]
        received = recv_scratch[...].reshape(pieces * cap, 2 * width)
        halves = [
            jnp.concatenate(
                [hot[(2 * p + j) * cap : (2 * p + j + 1) * cap] for p in range(pieces)], axis=0
            )
            for j in range(2)
        ]
        listed = dot(received, halves[0], 0, 0)[:width] + dot(received, halves[1], 0, 0)[width:]
    for t in range(tiles):
        rows_ref[t * width : (t + 1) * width, :] = listed[:, t * length : (t + 1) * length]
    rows = [rows_ref[pl.ds(f, tiles, stride=width), :] for f in range(width)]

    tile_row = iota((tiles, length), 0)

    def by_tile(values, row):
        out = jnp.full(row.shape, values[tiles - 1])
        for t in range(tiles - 1):
            out = jnp.where(row == t, values[t], out)
        return out

    cam_ids = [cam_index_ref[t] for t in range(tiles)]
    cam = [
        by_tile([cams_ref[j, cam_ids[t]] for t in range(tiles)], tile_row)
        for j in range(cams_ref.shape[0])
    ]

    outs, pullback = jax.vjp(lambda r: project(r, cam, live), rows[:10])
    terms = outs[5:]
    colors = []
    for k in range(3):
        base = 11 + 16 * k
        shade = 0.5 + rows[base]
        for b in range(15):
            shade = shade + rows[base + 1 + b] * terms[b]
        for j in range(5):
            shade = shade + rows[59 + j] * cam[13 + 3 * j + k]
        colors.append(shade)
    opacity = jax.nn.sigmoid(rows[10])
    con_a, con_b, con_c = outs[2], outs[3], outs[4]

    attrs = [
        outs[0],
        outs[1],
        (-0.5 * LOG2E) * con_a,
        -LOG2E * con_b,
        (-0.5 * LOG2E) * con_c,
        jnp.where(live, opacity, 0.0),
    ] + colors
    count = len(attrs)
    blocks = []
    for value in attrs:
        parts = [p.astype(F32) for p in split(value, 3)]
        parts.append(jnp.zeros((16 - 3 * tiles, length), F32))
        blocks.append(jnp.concatenate(parts, axis=0))
    stacked = jnp.concatenate(blocks, axis=1)
    lane_tile = iota((16, LANES), 1) // share
    row_index = iota((16, LANES), 0)
    spread = one_hot((row_index % tiles == lane_tile) & (row_index < 3 * tiles))
    table = dot(stacked.T.astype(BF16), spread)
    pos = [tile_pos_ref[t] for t in range(tiles)]
    lane_row = iota((1, LANES), 1)
    origin_x = [(SIDE * (lax.rem(p, WIN) - WIN // 2)).astype(F32) + 0.5 for p in pos]
    pixel_x = by_tile(origin_x, lane_row // share) + (lane_row % SIDE).astype(F32)
    dx = pixel_x - table[:length]
    table_ref[0:length, :] = table[2 * length : 3 * length] * dx * dx
    table_ref[length : 2 * length, :] = table[3 * length : 4 * length] * dx
    table_ref[2 * length : 3 * length, :] = table[length : 2 * length]
    table_ref[3 * length :, :] = table[4 * length :]

    lane = iota((depth, LANES), 1)
    origin_y = [(SIDE * (lax.div(p, WIN) - WIN // 2)).astype(F32) + 0.5 for p in pos]
    pixel_row = iota((depth, LANES), 0) * (share // SIDE) + (lane % share) // SIDE
    pixel_y = by_tile(origin_y, lane // share) + pixel_row.astype(F32)

    def row(index, l):
        return table_ref[pl.ds(index * length + l, 1), :]

    group = 16
    zero = jnp.zeros((depth, LANES), F32)

    def forward(chunk, carry):
        through, red, green, blue = carry
        for i in range(group):
            l = chunk * group + i
            dy = pixel_y - row(2, l)
            power = row(0, l) + dy * (row(1, l) + row(3, l) * dy)
            alpha = row(4, l) * jnp.exp2(power)
            weight = through * alpha
            red = red + weight * row(5, l)
            green = green + weight * row(6, l)
            blue = blue + weight * row(7, l)
            through = through - weight
            at = pl.ds(pl.multiple_of(l * depth, depth), depth)
            alpha_ref[at, :] = alpha
            weight_ref[at, :] = weight
        return through, red, green, blue

    start = (jnp.ones((depth, LANES), F32), zero, zero, zero)
    _, red, green, blue = lax.fori_loop(0, length // group, forward, start)
    pictures_ref[0] = red
    pictures_ref[1] = green
    pictures_ref[2] = blue
    res = [red - targets_ref[0], green - targets_ref[1], blue - targets_ref[2]]

    def backward(step, behind):
        chunk = length // group - 1 - step
        for i in reversed(range(group)):
            l = chunk * group + i
            at = pl.ds(pl.multiple_of(l * depth, depth), depth)
            alpha = alpha_ref[at, :]
            weight = weight_ref[at, :]
            dy = pixel_y - row(2, l)
            seen = row(5, l) * res[0] + row(6, l) * res[1] + row(7, l) * res[2]
            gap = seen - behind
            behind = behind + alpha * gap
            g = weight * gap
            gy = g * dy
            part_ref[0, at, :] = g
            part_ref[1, at, :] = gy
            part_ref[2, at, :] = gy * dy
            for k in range(3):
                part_ref[3 + k, at, :] = weight * res[k]
        return behind

    lax.fori_loop(0, length // group, backward, zero)

    def down(index):
        blocks = []
        for first in range(0, length, 8):
            parts = [
                part_ref[index, pl.ds(first * depth + s, 8, stride=depth), :] for s in range(depth)
            ]
            while len(parts) > 1:
                parts = [a + b for a, b in zip(parts[::2], parts[1::2])]
            blocks.append(parts[0])
        return jnp.concatenate(blocks, axis=0)

    sums = [down(index) for index in range(6)]
    g_x = sums[0] * dx
    sums = sums + [g_x, g_x * dx, sums[1] * dx]
    wide = jnp.concatenate([jnp.concatenate(split(s, 3), axis=1) for s in sums], axis=0)
    gather = one_hot(iota((8, 3 * LANES), 0) == (iota((8, 3 * LANES), 1) % LANES) // share)
    reduced = dot(gather, wide, 1, 1)
    g_0, g_y, g_yy, s_0, s_1, s_2, g_x, g_xx, g_xy = [
        reduced[:tiles, q * length : (q + 1) * length] for q in range(len(sums))
    ]

    d_colors = [s_0, s_1, s_2]
    d_terms = []
    for b in range(15):
        d_terms.append(sum(d_colors[k] * rows[12 + 16 * k + b] for k in range(3)))
    d_geometry = [
        con_a * g_x + con_b * g_y,
        con_b * g_x + con_c * g_y,
        -0.5 * g_xx,
        -g_xy,
        -0.5 * g_yy,
    ]
    (d_rows,) = pullback(d_geometry + d_terms)
    d_rows = list(d_rows)
    d_rows.append(g_0 * (1.0 - opacity))
    for k in range(3):
        d_rows.append(d_colors[k])
        d_rows.extend(d_colors[k] * terms[b] for b in range(15))
    for j in range(5):
        d_rows.append(sum(d_colors[k] * cam[13 + 3 * j + k] for k in range(3)))
    for f in range(width):
        rows_ref[pl.ds(f, tiles, stride=width), :] = d_rows[f]
    sent = jnp.concatenate(
        [
            jnp.concatenate(split(rows_ref[t * width : (t + 1) * width, :], 2), axis=0)
            for t in range(tiles)
        ],
        axis=1,
    )
    send_ref[...] = dot(hot, sent, 1, 1).astype(BF16)


def scatter_kernel(halves, pairs, me_ref, bit_ref, recv_ref, *refs):
    where_refs, out_refs = refs[:-halves], refs[-halves:]
    g_dev = out_refs[0].shape[1]

    def spread(where, received):
        hot = one_hot(iota((g_dev, where.shape[1]), 0) == where)
        return dot(received, hot, 0, 1)

    if pairs == 0:
        total = spread(where_refs[0][:1, :], recv_ref[...])
    else:
        slots, lanes = recv_ref.shape
        blocks = recv_ref[...].reshape(pairs, 2, slots // (2 * pairs), lanes)
        even = blocks[:, 0].reshape(slots // 2, lanes)
        odd = blocks[:, 1].reshape(slots // 2, lanes)
        first = me_ref[0] % 2 == 0
        own, other = where_refs[0][:1, :], where_refs[1][:1, :]
        total = spread(jnp.where(first, own, other), even) + spread(
            jnp.where(first, other, own), odd
        )
    width = total.shape[0] // 2
    total = total[:width] + total[width:]
    if halves == 1:
        out_refs[0][...] = total
        return
    low, high = total[: width // 2], total[width // 2 :]
    first = bit_ref[0] == 0
    out_refs[0][...] = jnp.where(first, low, high)
    out_refs[1][...] = jnp.where(first, high, low)


def call(kernel, out_shape, args, scalars=0, scratch=()):
    in_specs = [pl.BlockSpec(memory_space=pltpu.SMEM)] * scalars
    in_specs += [pl.BlockSpec(memory_space=pltpu.VMEM)] * (len(args) - scalars)
    many = isinstance(out_shape, (list, tuple))
    spec = pl.BlockSpec(memory_space=pltpu.VMEM)
    return pl.pallas_call(
        kernel,
        out_shape=out_shape,
        in_specs=in_specs,
        out_specs=[spec] * len(out_shape) if many else spec,
        scratch_shapes=list(scratch),
        compiler_params=pltpu.CompilerParams(vmem_limit_bytes=VMEM_LIMIT),
    )(*args)


def swap(x, axis, k):
    return lax.ppermute(x, axis, [(i, i ^ k) for i in range(lax.axis_size(axis))])


def exchange(x):
    owners = lax.axis_size("gauss")
    parts = x.reshape(owners, x.shape[0] // owners, *x.shape[1:])
    moved = lax.all_to_all(parts, "gauss", split_axis=0, concat_axis=0, tiled=True)
    return moved.reshape(x.shape)


def power_of_two(n):
    return n & (n - 1) == 0


def shape(dims, dtype):
    return jax.ShapeDtypeStruct(dims, dtype)


def on_device(params, lists, tile_pos, cam_index, cams, targets):
    owners = lax.axis_size("gauss")
    views = lax.axis_size("view")
    width, g_dev = params.shape
    tiles, length = lists.shape
    slots = tiles * length
    cap = slots // owners
    share = LANES // tiles
    depth = SIDE * SIDE // share
    me = lax.axis_index("gauss").reshape(1)
    paired = 2 <= owners <= 16 and power_of_two(owners)
    peers = owners // 2 if paired else 1

    if paired:
        other = swap(params, "gauss", 1)
        all_lists = [lists] + [swap(lists, "gauss", 2 * k) for k in range(1, peers)]
    hot, params_copy = call(
        functools.partial(prepare_kernel, owners, g_dev),
        [shape((slots, slots), BF16), shape((width, g_dev), BF16)],
        (lists, params),
    )
    if paired:
        *picked, where, where_other = call(
            functools.partial(pick_pair_kernel, cap, peers),
            [shape((cap, 2 * width), BF16)] * peers + [shape((8, slots // 2), jnp.int32)] * 2,
            (me, *all_lists, params_copy, other),
            scalars=1,
            scratch=(
                pltpu.VMEM((peers, tiles, length), jnp.int32),
                pltpu.VMEM((peers, cap, 2 * width), BF16),
            ),
        )
        returned = [picked[0]] + [swap(picked[k], "gauss", 2 * k) for k in range(1, peers)]
        wheres = [where, swap(where_other, "gauss", 1)]
        recv_scratch = (pltpu.VMEM((peers, cap, 2 * width), BF16),)
    else:
        mine = jnp.broadcast_to(lists[None], (owners, tiles, length))
        all_lists = exchange(mine.reshape(owners * tiles, length))
        picked, where = call(
            functools.partial(pick_kernel, tiles, cap),
            [shape((slots, LANES), BF16), shape((8, slots), jnp.int32)],
            (me, all_lists, params_copy),
            scalars=1,
        )
        returned = [exchange(picked)]
        wheres = [where]
        recv_scratch = ()
    spread_targets = (
        targets.reshape(3, tiles, depth, share).transpose(0, 2, 1, 3).reshape(3, depth, LANES)
    )
    pictures, sent = call(
        functools.partial(render_kernel, peers, width),
        [shape((3, depth, LANES), F32), shape((slots, LANES), BF16)],
        (me, tile_pos, cam_index, cams, *returned, lists, hot, spread_targets),
        scalars=4,
        scratch=(
            pltpu.VMEM((tiles * width, length), F32),
            pltpu.VMEM((8 * length, LANES), F32),
            pltpu.VMEM((length * depth, LANES), F32),
            pltpu.VMEM((length * depth, LANES), F32),
            pltpu.VMEM((6, length * depth, LANES), F32),
        )
        + recv_scratch,
    )
    pictures = (
        pictures.reshape(3, depth, tiles, share)
        .transpose(0, 2, 1, 3)
        .reshape(3, tiles, SIDE * SIDE)
    )
    row_g = exchange(sent)
    halves = 2 if views > 1 and power_of_two(views) else 1
    bit = (lax.axis_index("view") % 2).reshape(1)
    totals = call(
        functools.partial(scatter_kernel, halves, peers if paired else 0),
        [shape((width // halves, g_dev), F32)] * halves,
        (me, bit, row_g, *wheres),
        scalars=2,
    )
    if halves == 1:
        return (pictures, lax.psum(totals[0], "view"))
    kept, given = totals
    kept = kept + swap(given, "view", 1)
    step = 2
    while step < views:
        kept = kept + swap(kept, "view", step)
        step *= 2
    other = swap(kept, "view", 1)
    first = bit[0] == 0
    grads = jnp.concatenate(
        [jnp.where(first, kept, other), jnp.where(first, other, kept)], axis=0
    )
    return (pictures, grads)


def solution(mesh):
    return jax.shard_map(
        on_device,
        mesh=mesh,
        in_specs=(
            P(None, "gauss"),
            P(("gauss", "view"), None),
            P(("gauss", "view")),
            P(("gauss", "view")),
            P(),
            P(None, ("gauss", "view"), None),
        ),
        out_specs=(P(None, ("gauss", "view"), None), P(None, "gauss")),
        check_vma=False,
    )
```

```python
import functools
import math

import jax
import jax.numpy as jnp
from jax import lax
from jax.experimental import pallas as pl
from jax.experimental.pallas import tpu as pltpu
from jax.sharding import PartitionSpec as P

WIN = 16
SIDE = 16
LANES = 128
LOG2E = math.log2(math.e)
F32 = jnp.float32
BF16 = jnp.bfloat16
VMEM_LIMIT = 24 * 2**20
EXTRA = 16
PART_BITS = 5


def sh_terms(x, y, z):
    xx, yy, zz = x * x, y * y, z * z
    xy = x * y
    diff = xx - yy
    five = 5.0 * zz - 1.0
    return [
        x,
        y,
        z,
        xy,
        y * z,
        x * z,
        diff,
        3.0 * zz - 1.0,
        x * (xx - 3.0 * yy),
        xy * z,
        y * (3.0 * xx - yy),
        z * diff,
        x * five,
        y * five,
        z * (5.0 * zz - 3.0),
    ]


def project(rows, cam, live):
    mx, my, mz = rows[0], rows[1], rows[2]
    cam_x = cam[0] * mx + cam[1] * my + cam[2] * mz + cam[9]
    cam_y = cam[3] * mx + cam[4] * my + cam[5] * mz + cam[10]
    cam_z = cam[6] * mx + cam[7] * my + cam[8] * mz + cam[11]
    cam_z = jnp.where(live, cam_z, 1.0)
    inv_z = 1.0 / cam_z
    qw, qx, qy, qz = rows[6], rows[7], rows[8], rows[9]
    qw = jnp.where(live, qw, 1.0)
    inv_q = lax.rsqrt(qw * qw + qx * qx + qy * qy + qz * qz)
    qw, qx, qy, qz = qw * inv_q, qx * inv_q, qy * inv_q, qz * inv_q
    rot = [
        [
            1.0 - 2.0 * (qy * qy + qz * qz),
            2.0 * (qx * qy - qw * qz),
            2.0 * (qx * qz + qw * qy),
        ],
        [
            2.0 * (qx * qy + qw * qz),
            1.0 - 2.0 * (qx * qx + qz * qz),
            2.0 * (qy * qz - qw * qx),
        ],
        [
            2.0 * (qx * qz - qw * qy),
            2.0 * (qy * qz + qw * qx),
            1.0 - 2.0 * (qx * qx + qy * qy),
        ],
    ]
    mixed = [
        [
            cam[3 * i] * rot[0][k] + cam[3 * i + 1] * rot[1][k] + cam[3 * i + 2] * rot[2][k]
            for k in range(3)
        ]
        for i in range(3)
    ]
    scale = cam[12] * inv_z
    ray_x, ray_y = cam_x * inv_z, cam_y * inv_z
    proj_u = [scale * (mixed[0][k] - ray_x * mixed[2][k]) for k in range(3)]
    proj_v = [scale * (mixed[1][k] - ray_y * mixed[2][k]) for k in range(3)]
    var = [jnp.exp(2.0 * rows[3 + k]) for k in range(3)]
    uv = [proj_u[k] * var[k] for k in range(3)]
    cov_a = sum(uv[k] * proj_u[k] for k in range(3)) + 0.3
    cov_b = sum(uv[k] * proj_v[k] for k in range(3))
    cov_c = sum(proj_v[k] * proj_v[k] * var[k] for k in range(3)) + 0.3
    inv_det = 1.0 / (cov_a * cov_c - cov_b * cov_b)
    inv_dist = lax.rsqrt(cam_x * cam_x + cam_y * cam_y + cam_z * cam_z)
    terms = sh_terms(cam_x * inv_dist, cam_y * inv_dist, cam_z * inv_dist)
    geometry = [cam_x * scale, cam_y * scale, cov_c * inv_det, -cov_b * inv_det, cov_a * inv_det]
    return geometry + terms


def iota(shape, dim):
    return lax.broadcasted_iota(jnp.int32, shape, dim)


def one_hot(mask):
    return jnp.where(mask, 1.0, 0.0).astype(BF16)


def dot(lhs, rhs, lhs_dim=1, rhs_dim=0):
    return lax.dot_general(
        lhs, rhs, (((lhs_dim,), (rhs_dim,)), ((), ())), preferred_element_type=F32
    )


def split(x, parts):
    out = []
    for _ in range(parts):
        head = x.astype(BF16)
        out.append(head)
        x = x - head.astype(F32)
    return out


def ranks(mask, tiles):
    rows, length = mask.shape
    bits = one_hot(mask)
    earlier = one_hot(iota((length, length), 0) < iota((length, length), 1))
    within = dot(bits, earlier)
    count = dot(bits, jnp.ones((length, length), BF16)).astype(BF16)
    here, there = iota((rows, rows), 0), iota((rows, rows), 1)
    above = one_hot((there < here) & (there >= here - lax.rem(here, tiles)))
    return (within + dot(above, count)).astype(jnp.int32)


def find(ids, base, tiles, cap, g_dev):
    local = ids - base
    mine = (local >= 0) & (local < g_dev)
    key = jnp.where(mine, ranks(mine, tiles), -1)
    rows, length = ids.shape
    slot = iota((cap, length), 0)
    found = []
    for r in range(0, rows, tiles):
        total = jnp.zeros((cap, length), jnp.int32)
        for t in range(r, r + tiles):
            total = total + jnp.where(key[t : t + 1, :] == slot, local[t : t + 1, :], 0)
        found.append(jnp.sum(total, axis=1, keepdims=True))
    return jnp.concatenate(found, axis=0)


def pick_kernel(tiles, cap, me_ref, lists_ref, params_ref, picked_ref):
    width, g_dev = params_ref.shape
    where = find(lists_ref[...], me_ref[0] * g_dev, tiles, cap, g_dev)
    hot = one_hot(where == iota((where.shape[0], g_dev), 1))
    wide = jnp.concatenate([params_ref[...], jnp.zeros((LANES - width, g_dev), BF16)], axis=0)
    picked_ref[...] = dot(hot, wide, 1, 1).astype(BF16)


def pick_pair_kernel(cap, peers, me_ref, *refs):
    lists_refs, refs = refs[:peers], refs[peers:]
    own_ref, other_ref = refs[:2]
    picked_refs, refs = refs[2 : 2 + peers], refs[2 + peers :]
    lists_scratch, picked_scratch = refs
    tiles, length = lists_refs[0].shape
    width, g_dev = own_ref.shape
    me = me_ref[0]
    first = me % 2 == 0
    for k in range(peers):
        lists_scratch[(me // 2) ^ k] = lists_refs[k][...]
    ids = lists_scratch[...].reshape(peers * tiles, length)
    where_own = find(ids, me * g_dev, tiles, cap, g_dev)
    where_other = find(ids, (me ^ 1) * g_dev, tiles, cap, g_dev)
    own, other = own_ref[...], other_ref[...]
    blank = jnp.zeros((width, g_dev), BF16)
    lanes = iota((peers * cap, g_dev), 1)
    picked = dot(
        one_hot(where_own == lanes),
        jnp.concatenate([jnp.where(first, own, blank), jnp.where(first, blank, own)], axis=0),
        1,
        1,
    ) + dot(
        one_hot(where_other == lanes),
        jnp.concatenate([jnp.where(first, blank, other), jnp.where(first, other, blank)], axis=0),
        1,
        1,
    )
    picked_scratch[...] = picked.astype(BF16).reshape(peers, cap, 2 * width)
    for k in range(peers):
        picked_refs[k][...] = picked_scratch[(me // 2) ^ k]


def prepare_kernel(owners, cap, g_dev, lists_ref, params_ref, hot_ref, names_ref, copy_ref):
    tiles, length = lists_ref.shape
    slots = owners * cap
    ids = lists_ref[...]
    masks = [(ids >= o * g_dev) & (ids < (o + 1) * g_dev) for o in range(owners)]
    rank = ranks(jnp.concatenate([m.astype(jnp.int32) for m in masks], axis=0) > 0, tiles)
    place = jnp.full((tiles, length), -1, jnp.int32)
    local = jnp.zeros((tiles, length), jnp.int32)
    for o in range(owners):
        place = jnp.where(masks[o], rank[o * tiles : (o + 1) * tiles] + o * cap, place)
        local = jnp.where(masks[o], ids - o * g_dev, local)
    slot_iota = iota((slots, length), 0)
    hot = jnp.concatenate(
        [one_hot(slot_iota == place[t : t + 1, :]) for t in range(tiles)], axis=1
    )
    hot_ref[...] = hot

    def along(values):
        values = values.astype(F32)
        return jnp.concatenate([values[t : t + 1, :] for t in range(tiles)], axis=1)

    parts = jnp.concatenate(
        [
            along(lax.shift_right_logical(local, PART_BITS)),
            along(local & (2**PART_BITS - 1)),
            jnp.zeros((EXTRA - 2, tiles * length), F32),
        ],
        axis=0,
    )
    names = dot(parts.astype(BF16), hot, 1, 1)
    for o in range(owners):
        names_ref[o, :, :cap] = names[:, o * cap : (o + 1) * cap].astype(BF16)
        names_ref[o, :, cap:] = jnp.zeros((EXTRA, LANES - cap), BF16)
    copy_ref[...] = params_ref[...]


def render_kernel(pieces, width, me_ref, tile_pos_ref, cam_index_ref, cams_ref, *refs):
    recv_refs, refs = refs[:pieces], refs[pieces:]
    lists_ref, hot_ref, names_ref, targets_ref, pictures_ref, send_ref = refs[:6]
    rows_ref, table_ref, alpha_ref, weight_ref, part_ref = refs[6:11]
    tiles, length = lists_ref.shape
    share = LANES // tiles
    depth = SIDE * SIDE // share
    live = lists_ref[...] >= 0
    hot = hot_ref[...]

    if pieces == 1:
        listed = dot(recv_refs[0][...], hot, 0, 0)[:width]
    else:
        (recv_scratch,) = refs[11:]
        cap = recv_refs[0].shape[0]
        for k in range(pieces):
            recv_scratch[(me_ref[0] // 2) ^ k] = recv_refs[k][...]
        received = recv_scratch[...].reshape(pieces * cap, 2 * width)
        halves = [
            jnp.concatenate(
                [hot[(2 * p + j) * cap : (2 * p + j + 1) * cap] for p in range(pieces)], axis=0
            )
            for j in range(2)
        ]
        listed = dot(received, halves[0], 0, 0)[:width] + dot(received, halves[1], 0, 0)[width:]
    for t in range(tiles):
        rows_ref[t * width : (t + 1) * width, :] = listed[:, t * length : (t + 1) * length]
    rows = [rows_ref[pl.ds(f, tiles, stride=width), :] for f in range(width)]

    tile_row = iota((tiles, length), 0)

    def by_tile(values, row):
        out = jnp.full(row.shape, values[tiles - 1])
        for t in range(tiles - 1):
            out = jnp.where(row == t, values[t], out)
        return out

    cam_ids = [cam_index_ref[t] for t in range(tiles)]
    cam = [
        by_tile([cams_ref[j, cam_ids[t]] for t in range(tiles)], tile_row)
        for j in range(cams_ref.shape[0])
    ]

    outs, pullback = jax.vjp(lambda r: project(r, cam, live), rows[:10])
    terms = outs[5:]
    colors = []
    for k in range(3):
        base = 11 + 16 * k
        shade = 0.5 + rows[base]
        for b in range(15):
            shade = shade + rows[base + 1 + b] * terms[b]
        for j in range(5):
            shade = shade + rows[59 + j] * cam[13 + 3 * j + k]
        colors.append(shade)
    opacity = jax.nn.sigmoid(rows[10])
    con_a, con_b, con_c = outs[2], outs[3], outs[4]

    attrs = [
        outs[0],
        outs[1],
        (-0.5 * LOG2E) * con_a,
        -LOG2E * con_b,
        (-0.5 * LOG2E) * con_c,
        jnp.where(live, opacity, 0.0),
    ] + colors
    count = len(attrs)
    blocks = []
    for value in attrs:
        parts = [p.astype(F32) for p in split(value, 3)]
        parts.append(jnp.zeros((16 - 3 * tiles, length), F32))
        blocks.append(jnp.concatenate(parts, axis=0))
    stacked = jnp.concatenate(blocks, axis=1)
    lane_tile = iota((16, LANES), 1) // share
    row_index = iota((16, LANES), 0)
    spread = one_hot((row_index % tiles == lane_tile) & (row_index < 3 * tiles))
    table = dot(stacked.T.astype(BF16), spread)
    pos = [tile_pos_ref[t] for t in range(tiles)]
    lane_row = iota((1, LANES), 1)
    origin_x = [(SIDE * (lax.rem(p, WIN) - WIN // 2)).astype(F32) + 0.5 for p in pos]
    pixel_x = by_tile(origin_x, lane_row // share) + (lane_row % SIDE).astype(F32)
    dx = pixel_x - table[:length]
    table_ref[0:length, :] = table[2 * length : 3 * length] * dx * dx
    table_ref[length : 2 * length, :] = table[3 * length : 4 * length] * dx
    table_ref[2 * length : 3 * length, :] = table[length : 2 * length]
    table_ref[3 * length :, :] = table[4 * length :]

    lane = iota((depth, LANES), 1)
    origin_y = [(SIDE * (lax.div(p, WIN) - WIN // 2)).astype(F32) + 0.5 for p in pos]
    pixel_row = iota((depth, LANES), 0) * (share // SIDE) + (lane % share) // SIDE
    pixel_y = by_tile(origin_y, lane // share) + pixel_row.astype(F32)

    def row(index, l):
        return table_ref[pl.ds(index * length + l, 1), :]

    group = 16
    zero = jnp.zeros((depth, LANES), F32)

    def forward(chunk, carry):
        through, red, green, blue = carry
        for i in range(group):
            l = chunk * group + i
            dy = pixel_y - row(2, l)
            power = row(0, l) + dy * (row(1, l) + row(3, l) * dy)
            alpha = row(4, l) * jnp.exp2(power)
            weight = through * alpha
            red = red + weight * row(5, l)
            green = green + weight * row(6, l)
            blue = blue + weight * row(7, l)
            through = through - weight
            at = pl.ds(pl.multiple_of(l * depth, depth), depth)
            alpha_ref[at, :] = alpha
            weight_ref[at, :] = weight
        return through, red, green, blue

    start = (jnp.ones((depth, LANES), F32), zero, zero, zero)
    _, red, green, blue = lax.fori_loop(0, length // group, forward, start)
    pictures_ref[0] = red
    pictures_ref[1] = green
    pictures_ref[2] = blue
    res = [red - targets_ref[0], green - targets_ref[1], blue - targets_ref[2]]

    def backward(step, behind):
        chunk = length // group - 1 - step
        for i in reversed(range(group)):
            l = chunk * group + i
            at = pl.ds(pl.multiple_of(l * depth, depth), depth)
            alpha = alpha_ref[at, :]
            weight = weight_ref[at, :]
            dy = pixel_y - row(2, l)
            seen = row(5, l) * res[0] + row(6, l) * res[1] + row(7, l) * res[2]
            gap = seen - behind
            behind = behind + alpha * gap
            g = weight * gap
            gy = g * dy
            part_ref[0, at, :] = g
            part_ref[1, at, :] = gy
            part_ref[2, at, :] = gy * dy
            for k in range(3):
                part_ref[3 + k, at, :] = weight * res[k]
        return behind

    lax.fori_loop(0, length // group, backward, zero)

    def down(index):
        blocks = []
        for first in range(0, length, 8):
            parts = [
                part_ref[index, pl.ds(first * depth + s, 8, stride=depth), :] for s in range(depth)
            ]
            while len(parts) > 1:
                parts = [a + b for a, b in zip(parts[::2], parts[1::2])]
            blocks.append(parts[0])
        return jnp.concatenate(blocks, axis=0)

    sums = [down(index) for index in range(6)]
    g_x = sums[0] * dx
    sums = sums + [g_x, g_x * dx, sums[1] * dx]
    wide = jnp.concatenate([jnp.concatenate(split(s, 3), axis=1) for s in sums], axis=0)
    gather = one_hot(iota((8, 3 * LANES), 0) == (iota((8, 3 * LANES), 1) % LANES) // share)
    reduced = dot(gather, wide, 1, 1)
    g_0, g_y, g_yy, s_0, s_1, s_2, g_x, g_xx, g_xy = [
        reduced[:tiles, q * length : (q + 1) * length] for q in range(len(sums))
    ]

    d_colors = [s_0, s_1, s_2]
    d_terms = []
    for b in range(15):
        d_terms.append(sum(d_colors[k] * rows[12 + 16 * k + b] for k in range(3)))
    d_geometry = [
        con_a * g_x + con_b * g_y,
        con_b * g_x + con_c * g_y,
        -0.5 * g_xx,
        -g_xy,
        -0.5 * g_yy,
    ]
    (d_rows,) = pullback(d_geometry + d_terms)
    d_rows = list(d_rows)
    d_rows.append(g_0 * (1.0 - opacity))
    for k in range(3):
        d_rows.append(d_colors[k])
        d_rows.extend(d_colors[k] * terms[b] for b in range(15))
    for j in range(5):
        d_rows.append(sum(d_colors[k] * cam[13 + 3 * j + k] for k in range(3)))
    for f in range(width):
        rows_ref[pl.ds(f, tiles, stride=width), :] = d_rows[f]
    sent = jnp.concatenate(
        [
            jnp.concatenate(split(rows_ref[t * width : (t + 1) * width, :], 2), axis=0)
            for t in range(tiles)
        ],
        axis=1,
    )
    owners, copies, _, _ = send_ref.shape
    cap = hot.shape[0] // owners
    sorted_g = dot(hot, sent, 1, 1).astype(BF16).reshape(owners, cap, 2 * width)
    for c in range(copies):
        send_ref[:, c, :cap, :] = sorted_g
        send_ref[:, c, cap:, :] = names_ref[...]


def scatter_kernel(recv_ref, out_ref):
    blocks, rows, lanes = recv_ref.shape
    cap = rows - EXTRA
    width, g_dev = out_ref.shape
    wheres = []
    for b in range(blocks):
        parts = recv_ref[b, cap:, :].astype(F32)
        wheres.append((parts[0:1, :cap] * 2**PART_BITS + parts[1:2, :cap]).astype(jnp.int32))
    where = jnp.concatenate(wheres, axis=1)
    received = recv_ref[:, :cap, :].reshape(blocks * cap, lanes)
    hot = one_hot(iota((g_dev, blocks * cap), 0) == where)
    total = dot(received, hot, 0, 1)
    out_ref[...] = total[:width] + total[width:]


def call(kernel, out_shape, args, scalars=0, scratch=()):
    in_specs = [pl.BlockSpec(memory_space=pltpu.SMEM)] * scalars
    in_specs += [pl.BlockSpec(memory_space=pltpu.VMEM)] * (len(args) - scalars)
    many = isinstance(out_shape, (list, tuple))
    spec = pl.BlockSpec(memory_space=pltpu.VMEM)
    return pl.pallas_call(
        kernel,
        out_shape=out_shape,
        in_specs=in_specs,
        out_specs=[spec] * len(out_shape) if many else spec,
        scratch_shapes=list(scratch),
        compiler_params=pltpu.CompilerParams(vmem_limit_bytes=VMEM_LIMIT),
    )(*args)


def swap(x, axis, k):
    return lax.ppermute(x, axis, [(i, i ^ k) for i in range(lax.axis_size(axis))])


def exchange(x):
    return lax.all_to_all(x, "gauss", split_axis=0, concat_axis=0, tiled=True)


def exchange_wide(x):
    owners, views = lax.axis_size("gauss"), lax.axis_size("view")
    blocks = x.reshape(owners * views // 2, *x.shape[2:])
    groups = [[i for i in range(owners * views) if i % 2 == c] for c in range(2)]
    return lax.all_to_all(
        blocks,
        ("gauss", "view"),
        split_axis=0,
        concat_axis=0,
        axis_index_groups=groups,
        tiled=True,
    )


def power_of_two(n):
    return n & (n - 1) == 0


def shape(dims, dtype):
    return jax.ShapeDtypeStruct(dims, dtype)


def on_device(params, lists, tile_pos, cam_index, cams, targets):
    owners = lax.axis_size("gauss")
    views = lax.axis_size("view")
    width, g_dev = params.shape
    tiles, length = lists.shape
    cap = max(tiles * length // owners, 16)
    slots = owners * cap
    share = LANES // tiles
    depth = SIDE * SIDE // share
    me = lax.axis_index("gauss").reshape(1)
    paired = 2 <= owners <= 16 and power_of_two(owners)
    peers = owners // 2 if paired else 1
    wide = views % 2 == 0 and owners * views <= 32

    if paired:
        other = swap(params, "gauss", 1)
        all_lists = [lists] + [swap(lists, "gauss", 2 * k) for k in range(1, peers)]
    hot, names, params_copy = call(
        functools.partial(prepare_kernel, owners, cap, g_dev),
        [
            shape((slots, tiles * length), BF16),
            shape((owners, EXTRA, LANES), BF16),
            shape((width, g_dev), BF16),
        ],
        (lists, params),
    )
    if paired:
        picked = call(
            functools.partial(pick_pair_kernel, cap, peers),
            [shape((cap, 2 * width), BF16)] * peers,
            (me, *all_lists, params_copy, other),
            scalars=1,
            scratch=(
                pltpu.VMEM((peers, tiles, length), jnp.int32),
                pltpu.VMEM((peers, cap, 2 * width), BF16),
            ),
        )
        returned = [picked[0]] + [swap(picked[k], "gauss", 2 * k) for k in range(1, peers)]
        recv_scratch = (pltpu.VMEM((peers, cap, 2 * width), BF16),)
    else:
        all_lists = exchange(jnp.broadcast_to(lists[None], (owners, tiles, length)))
        picked = call(
            functools.partial(pick_kernel, tiles, cap),
            shape((slots, LANES), BF16),
            (me, all_lists.reshape(owners * tiles, length), params_copy),
            scalars=1,
        )
        returned = [exchange(picked.reshape(owners, cap, LANES)).reshape(slots, LANES)]
        recv_scratch = ()
    spread_targets = (
        targets.reshape(3, tiles, depth, share).transpose(0, 2, 1, 3).reshape(3, depth, LANES)
    )
    copies = views // 2 if wide else 1
    pictures, sent = call(
        functools.partial(render_kernel, peers, width),
        [shape((3, depth, LANES), F32), shape((owners, copies, cap + EXTRA, 2 * width), BF16)],
        (me, tile_pos, cam_index, cams, *returned, lists, hot, names, spread_targets),
        scalars=4,
        scratch=(
            pltpu.VMEM((tiles * width, length), F32),
            pltpu.VMEM((8 * length, LANES), F32),
            pltpu.VMEM((length * depth, LANES), F32),
            pltpu.VMEM((length * depth, LANES), F32),
            pltpu.VMEM((6, length * depth, LANES), F32),
        )
        + recv_scratch,
    )
    pictures = (
        pictures.reshape(3, depth, tiles, share)
        .transpose(0, 2, 1, 3)
        .reshape(3, tiles, SIDE * SIDE)
    )
    received = exchange_wide(sent) if wide else exchange(sent[:, 0])
    grads = call(scatter_kernel, shape((width, g_dev), F32), (received,))
    if wide:
        grads = grads + swap(grads, "view", 1)
    else:
        grads = lax.psum(grads, "view")
    return (pictures, grads)


def solution(mesh):
    return jax.shard_map(
        on_device,
        mesh=mesh,
        in_specs=(
            P(None, "gauss"),
            P(("gauss", "view"), None),
            P(("gauss", "view")),
            P(("gauss", "view")),
            P(),
            P(None, ("gauss", "view"), None),
        ),
        out_specs=(P(None, ("gauss", "view"), None), P(None, "gauss")),
        check_vma=False,
    )
```

```python
import functools
import math

import jax
import jax.numpy as jnp
from jax import lax
from jax.experimental import pallas as pl
from jax.experimental.pallas import tpu as pltpu
from jax.sharding import PartitionSpec as P

WIN = 16
SIDE = 16
LANES = 128
LOG2E = math.log2(math.e)
F32 = jnp.float32
BF16 = jnp.bfloat16
VMEM_LIMIT = 24 * 2**20
EXTRA = 16
PART_BITS = 5


def sh_terms(x, y, z):
    xx, yy, zz = x * x, y * y, z * z
    xy = x * y
    diff = xx - yy
    five = 5.0 * zz - 1.0
    return [
        x,
        y,
        z,
        xy,
        y * z,
        x * z,
        diff,
        3.0 * zz - 1.0,
        x * (xx - 3.0 * yy),
        xy * z,
        y * (3.0 * xx - yy),
        z * diff,
        x * five,
        y * five,
        z * (5.0 * zz - 3.0),
    ]


def project(rows, cam, live):
    mx, my, mz = rows[0], rows[1], rows[2]
    cam_x = cam[0] * mx + cam[1] * my + cam[2] * mz + cam[9]
    cam_y = cam[3] * mx + cam[4] * my + cam[5] * mz + cam[10]
    cam_z = cam[6] * mx + cam[7] * my + cam[8] * mz + cam[11]
    cam_z = jnp.where(live, cam_z, 1.0)
    inv_z = 1.0 / cam_z
    qw, qx, qy, qz = rows[6], rows[7], rows[8], rows[9]
    qw = jnp.where(live, qw, 1.0)
    inv_q = lax.rsqrt(qw * qw + qx * qx + qy * qy + qz * qz)
    qw, qx, qy, qz = qw * inv_q, qx * inv_q, qy * inv_q, qz * inv_q
    rot = [
        [
            1.0 - 2.0 * (qy * qy + qz * qz),
            2.0 * (qx * qy - qw * qz),
            2.0 * (qx * qz + qw * qy),
        ],
        [
            2.0 * (qx * qy + qw * qz),
            1.0 - 2.0 * (qx * qx + qz * qz),
            2.0 * (qy * qz - qw * qx),
        ],
        [
            2.0 * (qx * qz - qw * qy),
            2.0 * (qy * qz + qw * qx),
            1.0 - 2.0 * (qx * qx + qy * qy),
        ],
    ]
    mixed = [
        [
            cam[3 * i] * rot[0][k] + cam[3 * i + 1] * rot[1][k] + cam[3 * i + 2] * rot[2][k]
            for k in range(3)
        ]
        for i in range(3)
    ]
    scale = cam[12] * inv_z
    ray_x, ray_y = cam_x * inv_z, cam_y * inv_z
    proj_u = [scale * (mixed[0][k] - ray_x * mixed[2][k]) for k in range(3)]
    proj_v = [scale * (mixed[1][k] - ray_y * mixed[2][k]) for k in range(3)]
    var = [jnp.exp(2.0 * rows[3 + k]) for k in range(3)]
    uv = [proj_u[k] * var[k] for k in range(3)]
    cov_a = sum(uv[k] * proj_u[k] for k in range(3)) + 0.3
    cov_b = sum(uv[k] * proj_v[k] for k in range(3))
    cov_c = sum(proj_v[k] * proj_v[k] * var[k] for k in range(3)) + 0.3
    inv_det = 1.0 / (cov_a * cov_c - cov_b * cov_b)
    inv_dist = lax.rsqrt(cam_x * cam_x + cam_y * cam_y + cam_z * cam_z)
    terms = sh_terms(cam_x * inv_dist, cam_y * inv_dist, cam_z * inv_dist)
    geometry = [cam_x * scale, cam_y * scale, cov_c * inv_det, -cov_b * inv_det, cov_a * inv_det]
    return geometry + terms


def iota(shape, dim):
    return lax.broadcasted_iota(jnp.int32, shape, dim)


def one_hot(mask):
    return jnp.where(mask, 1.0, 0.0).astype(BF16)


def dot(lhs, rhs, lhs_dim=1, rhs_dim=0):
    return lax.dot_general(
        lhs, rhs, (((lhs_dim,), (rhs_dim,)), ((), ())), preferred_element_type=F32
    )


def split(x, parts):
    out = []
    for _ in range(parts):
        head = x.astype(BF16)
        out.append(head)
        x = x - head.astype(F32)
    return out


def ranks(mask, tiles):
    rows, length = mask.shape
    bits = one_hot(mask)
    earlier = one_hot(iota((length, length), 0) < iota((length, length), 1))
    within = dot(bits, earlier)
    count = dot(bits, jnp.ones((length, length), BF16)).astype(BF16)
    here, there = iota((rows, rows), 0), iota((rows, rows), 1)
    above = one_hot((there < here) & (there >= here - lax.rem(here, tiles)))
    return (within + dot(above, count)).astype(jnp.int32)


def find(ids, base, tiles, cap, g_dev):
    local = ids - base
    mine = (local >= 0) & (local < g_dev)
    key = jnp.where(mine, ranks(mine, tiles), -1)
    rows, length = ids.shape
    slot = iota((cap, length), 0)
    found = []
    for r in range(0, rows, tiles):
        total = jnp.zeros((cap, length), jnp.int32)
        for t in range(r, r + tiles):
            total = total + jnp.where(key[t : t + 1, :] == slot, local[t : t + 1, :], 0)
        found.append(jnp.sum(total, axis=1, keepdims=True))
    return jnp.concatenate(found, axis=0)


def pick_kernel(tiles, cap, lists_ref, params_ref, picked_ref):
    width, g_dev = params_ref.shape
    where = find(lists_ref[...], lax.axis_index("gauss") * g_dev, tiles, cap, g_dev)
    hot = one_hot(where == iota((where.shape[0], g_dev), 1))
    wide = jnp.concatenate([params_ref[...], jnp.zeros((LANES - width, g_dev), BF16)], axis=0)
    picked_ref[...] = dot(hot, wide, 1, 1).astype(BF16)


def pick_pair_kernel(cap, chip_ref, near_ref, far_ref, own_ref, other_ref, first_out, second_out):
    width, g_dev = own_ref.shape
    me = lax.axis_index("gauss")
    core_0 = lax.axis_index("view") % 2 == 0
    even = me % 2 == 0
    chip, near, far = chip_ref[...], near_ref[...], far_ref[...]
    ids = jnp.concatenate(
        [jnp.where(core_0, chip, near), jnp.where(core_0, near, far)], axis=0
    )
    rows, _ = ids.shape
    tiles = chip.shape[0] // 2
    where_own = find(ids, me * g_dev, tiles, cap, g_dev)
    where_other = find(ids, (me ^ 1) * g_dev, tiles, cap, g_dev)
    own, other = own_ref[...], other_ref[...]
    blank = jnp.zeros((width, g_dev), BF16)
    lanes = iota((where_own.shape[0], g_dev), 1)
    picked = dot(
        one_hot(where_own == lanes),
        jnp.concatenate([jnp.where(even, own, blank), jnp.where(even, blank, own)], axis=0),
        1,
        1,
    ) + dot(
        one_hot(where_other == lanes),
        jnp.concatenate([jnp.where(even, blank, other), jnp.where(even, other, blank)], axis=0),
        1,
        1,
    )
    picked = picked.astype(BF16)
    low, high = picked[: 2 * cap], picked[2 * cap :]
    first_out[...] = jnp.where(core_0, high, low)
    second_out[...] = jnp.where(core_0, low, high)


def by_tile(values, row):
    out = jnp.full(row.shape, values[-1])
    for t in range(len(values) - 1):
        out = jnp.where(row == t, values[t], out)
    return out


def prepare_kernel(
    owners,
    cap,
    g_dev,
    tile_pos_ref,
    cam_index_ref,
    cams_ref,
    lists_ref,
    params_ref,
    hot_ref,
    names_ref,
    copy_ref,
    cam_ref,
    pixel_ref,
):
    tiles, length = lists_ref.shape
    share = LANES // tiles
    depth = SIDE * SIDE // share
    cam_ids = [cam_index_ref[t] for t in range(tiles)]
    tile_row = iota((tiles, length), 0)
    for j in range(cams_ref.shape[0]):
        cam_ref[j] = by_tile([cams_ref[j, cam_ids[t]] for t in range(tiles)], tile_row)
    pos = [tile_pos_ref[t] for t in range(tiles)]
    lane = iota((depth, LANES), 1)
    origin_x = [(SIDE * (lax.rem(p, WIN) - WIN // 2)).astype(F32) + 0.5 for p in pos]
    pixel_ref[0] = by_tile(origin_x, lane // share) + (lane % SIDE).astype(F32)
    origin_y = [(SIDE * (lax.div(p, WIN) - WIN // 2)).astype(F32) + 0.5 for p in pos]
    pixel_row = iota((depth, LANES), 0) * (share // SIDE) + (lane % share) // SIDE
    pixel_ref[1] = by_tile(origin_y, lane // share) + pixel_row.astype(F32)

    slots = owners * cap
    ids = lists_ref[...]
    masks = [(ids >= o * g_dev) & (ids < (o + 1) * g_dev) for o in range(owners)]
    rank = ranks(jnp.concatenate([m.astype(jnp.int32) for m in masks], axis=0) > 0, tiles)
    place = jnp.full((tiles, length), -1, jnp.int32)
    local = jnp.zeros((tiles, length), jnp.int32)
    for o in range(owners):
        place = jnp.where(masks[o], rank[o * tiles : (o + 1) * tiles] + o * cap, place)
        local = jnp.where(masks[o], ids - o * g_dev, local)
    slot_iota = iota((slots, length), 0)
    hot = jnp.concatenate(
        [one_hot(slot_iota == place[t : t + 1, :]) for t in range(tiles)], axis=1
    )
    hot_ref[...] = hot

    def along(values):
        values = values.astype(F32)
        return jnp.concatenate([values[t : t + 1, :] for t in range(tiles)], axis=1)

    parts = jnp.concatenate(
        [
            along(lax.shift_right_logical(local, PART_BITS)),
            along(local & (2**PART_BITS - 1)),
            jnp.zeros((EXTRA - 2, tiles * length), F32),
        ],
        axis=0,
    )
    names = dot(parts.astype(BF16), hot, 1, 1)
    for o in range(owners):
        names_ref[o, :, :cap] = names[:, o * cap : (o + 1) * cap].astype(BF16)
        names_ref[o, :, cap:] = jnp.zeros((EXTRA, LANES - cap), BF16)
    copy_ref[...] = params_ref[...]


def render_kernel(shared, width, *refs):
    recv_refs, refs = (refs[:6], refs[6:]) if shared else (refs[:1], refs[1:])
    lists_ref, hot_ref, names_ref, cam_ref, pixel_ref, targets_ref = refs[:6]
    pictures_ref, send_ref, rows_ref, table_ref, alpha_ref, weight_ref, part_ref = refs[6:13]
    tiles, length = lists_ref.shape
    share = LANES // tiles
    depth = SIDE * SIDE // share
    live = lists_ref[...] >= 0
    hot = hot_ref[...]

    if shared:
        (recv_scratch,) = refs[13:]
        second, near, far, second_by, near_by, far_by = recv_refs
        cap = second.shape[0] // 2
        core_0 = lax.axis_index("view") % 2 == 0
        place = lax.axis_index("gauss") // 2
        for k, (ours, theirs) in enumerate(
            ((second, second_by), (near, near_by), (near_by, near), (far_by, far))
        ):
            one = ours[:cap] if k < 2 else ours[cap:]
            two = theirs[cap:] if k < 2 else theirs[:cap]
            recv_scratch[place ^ k] = jnp.where(core_0, one, two)
        received = recv_scratch[...].reshape(4 * cap, 2 * width)
        halves = [
            jnp.concatenate(
                [hot[(2 * p + j) * cap : (2 * p + j + 1) * cap] for p in range(4)], axis=0
            )
            for j in range(2)
        ]
        listed = dot(received, halves[0], 0, 0)[:width] + dot(received, halves[1], 0, 0)[width:]
    else:
        listed = dot(recv_refs[0][...], hot, 0, 0)[:width]
    for t in range(tiles):
        rows_ref[t * width : (t + 1) * width, :] = listed[:, t * length : (t + 1) * length]
    rows = [rows_ref[pl.ds(f, tiles, stride=width), :] for f in range(width)]

    cam = [cam_ref[j] for j in range(cam_ref.shape[0])]
    outs, pullback = jax.vjp(lambda r: project(r, cam, live), rows[:10])
    terms = outs[5:]
    colors = []
    for k in range(3):
        base = 11 + 16 * k
        shade = 0.5 + rows[base]
        for b in range(15):
            shade = shade + rows[base + 1 + b] * terms[b]
        for j in range(5):
            shade = shade + rows[59 + j] * cam[13 + 3 * j + k]
        colors.append(shade)
    opacity = jax.nn.sigmoid(rows[10])
    con_a, con_b, con_c = outs[2], outs[3], outs[4]

    attrs = [
        outs[0],
        outs[1],
        (-0.5 * LOG2E) * con_a,
        -LOG2E * con_b,
        (-0.5 * LOG2E) * con_c,
        jnp.where(live, opacity, 0.0),
    ] + colors
    count = len(attrs)
    blocks = []
    for value in attrs:
        parts = [p.astype(F32) for p in split(value, 3)]
        parts.append(jnp.zeros((16 - 3 * tiles, length), F32))
        blocks.append(jnp.concatenate(parts, axis=0))
    stacked = jnp.concatenate(blocks, axis=1)
    lane_tile = iota((16, LANES), 1) // share
    row_index = iota((16, LANES), 0)
    spread = one_hot((row_index % tiles == lane_tile) & (row_index < 3 * tiles))
    table = dot(stacked.T.astype(BF16), spread)
    pixel_x, pixel_y = pixel_ref[0, :1, :], pixel_ref[1]
    dx = pixel_x - table[:length]
    table_ref[0:length, :] = table[2 * length : 3 * length] * dx * dx
    table_ref[length : 2 * length, :] = table[3 * length : 4 * length] * dx
    table_ref[2 * length : 3 * length, :] = table[length : 2 * length]
    table_ref[3 * length :, :] = table[4 * length :]

    def row(index, l):
        return table_ref[pl.ds(index * length + l, 1), :]

    group = 16
    zero = jnp.zeros((depth, LANES), F32)

    def forward(chunk, carry):
        through, red, green, blue = carry
        for i in range(group):
            l = chunk * group + i
            dy = pixel_y - row(2, l)
            power = row(0, l) + dy * (row(1, l) + row(3, l) * dy)
            alpha = row(4, l) * jnp.exp2(power)
            weight = through * alpha
            red = red + weight * row(5, l)
            green = green + weight * row(6, l)
            blue = blue + weight * row(7, l)
            through = through - weight
            at = pl.ds(pl.multiple_of(l * depth, depth), depth)
            alpha_ref[at, :] = alpha
            weight_ref[at, :] = weight
        return through, red, green, blue

    start = (jnp.ones((depth, LANES), F32), zero, zero, zero)
    _, red, green, blue = lax.fori_loop(0, length // group, forward, start)
    pictures_ref[0] = red
    pictures_ref[1] = green
    pictures_ref[2] = blue
    res = [red - targets_ref[0], green - targets_ref[1], blue - targets_ref[2]]

    def backward(step, behind):
        chunk = length // group - 1 - step
        for i in reversed(range(group)):
            l = chunk * group + i
            at = pl.ds(pl.multiple_of(l * depth, depth), depth)
            alpha = alpha_ref[at, :]
            weight = weight_ref[at, :]
            dy = pixel_y - row(2, l)
            seen = row(5, l) * res[0] + row(6, l) * res[1] + row(7, l) * res[2]
            gap = seen - behind
            behind = behind + alpha * gap
            g = weight * gap
            gy = g * dy
            part_ref[0, at, :] = g
            part_ref[1, at, :] = gy
            part_ref[2, at, :] = gy * dy
            for k in range(3):
                part_ref[3 + k, at, :] = weight * res[k]
        return behind

    lax.fori_loop(0, length // group, backward, zero)

    def down(index):
        blocks = []
        for first in range(0, length, 8):
            parts = [
                part_ref[index, pl.ds(first * depth + s, 8, stride=depth), :] for s in range(depth)
            ]
            while len(parts) > 1:
                parts = [a + b for a, b in zip(parts[::2], parts[1::2])]
            blocks.append(parts[0])
        return jnp.concatenate(blocks, axis=0)

    sums = [down(index) for index in range(6)]
    g_x = sums[0] * dx
    sums = sums + [g_x, g_x * dx, sums[1] * dx]
    wide = jnp.concatenate([jnp.concatenate(split(s, 3), axis=1) for s in sums], axis=0)
    gather = one_hot(iota((8, 3 * LANES), 0) == (iota((8, 3 * LANES), 1) % LANES) // share)
    reduced = dot(gather, wide, 1, 1)
    g_0, g_y, g_yy, s_0, s_1, s_2, g_x, g_xx, g_xy = [
        reduced[:tiles, q * length : (q + 1) * length] for q in range(len(sums))
    ]

    d_colors = [s_0, s_1, s_2]
    d_terms = []
    for b in range(15):
        d_terms.append(sum(d_colors[k] * rows[12 + 16 * k + b] for k in range(3)))
    d_geometry = [
        con_a * g_x + con_b * g_y,
        con_b * g_x + con_c * g_y,
        -0.5 * g_xx,
        -g_xy,
        -0.5 * g_yy,
    ]
    (d_rows,) = pullback(d_geometry + d_terms)
    d_rows = list(d_rows)
    d_rows.append(g_0 * (1.0 - opacity))
    for k in range(3):
        d_rows.append(d_colors[k])
        d_rows.extend(d_colors[k] * terms[b] for b in range(15))
    for j in range(5):
        d_rows.append(sum(d_colors[k] * cam[13 + 3 * j + k] for k in range(3)))
    for f in range(width):
        rows_ref[pl.ds(f, tiles, stride=width), :] = d_rows[f]
    sent = jnp.concatenate(
        [
            jnp.concatenate(split(rows_ref[t * width : (t + 1) * width, :], 2), axis=0)
            for t in range(tiles)
        ],
        axis=1,
    )
    owners, copies, _, _ = send_ref.shape
    cap = hot.shape[0] // owners
    sorted_g = dot(hot, sent, 1, 1).astype(BF16).reshape(owners, cap, 2 * width)
    for c in range(copies):
        send_ref[:, c, :cap, :] = sorted_g
        send_ref[:, c, cap:, :] = names_ref[...]


def scatter_kernel(recv_ref, out_ref):
    blocks, rows, lanes = recv_ref.shape
    cap = rows - EXTRA
    width, g_dev = out_ref.shape
    wheres = []
    for b in range(blocks):
        parts = recv_ref[b, cap:, :].astype(F32)
        wheres.append((parts[0:1, :cap] * 2**PART_BITS + parts[1:2, :cap]).astype(jnp.int32))
    where = jnp.concatenate(wheres, axis=1)
    received = recv_ref[:, :cap, :].reshape(blocks * cap, lanes)
    hot = one_hot(iota((g_dev, blocks * cap), 0) == where)
    total = dot(received, hot, 0, 1)
    out_ref[...] = total[:width] + total[width:]


def call(kernel, out_shape, args, scalars=0, scratch=()):
    in_specs = [pl.BlockSpec(memory_space=pltpu.SMEM)] * scalars
    in_specs += [pl.BlockSpec(memory_space=pltpu.VMEM)] * (len(args) - scalars)
    many = isinstance(out_shape, (list, tuple))
    spec = pl.BlockSpec(memory_space=pltpu.VMEM)
    return pl.pallas_call(
        kernel,
        out_shape=out_shape,
        in_specs=in_specs,
        out_specs=[spec] * len(out_shape) if many else spec,
        scratch_shapes=list(scratch),
        compiler_params=pltpu.CompilerParams(vmem_limit_bytes=VMEM_LIMIT),
    )(*args)


def swap(x, axis, k):
    return lax.ppermute(x, axis, [(i, i ^ k) for i in range(lax.axis_size(axis))])


def reach(x, steps):
    owners, views = lax.axis_size("gauss"), lax.axis_size("view")
    pairs = [
        (g * views + v, (g ^ 2 * steps[v % 2]) * views + v)
        for g in range(owners)
        for v in range(views)
        if steps[v % 2] is not None
    ]
    return lax.ppermute(x, ("gauss", "view"), pairs)


def exchange(x):
    return lax.all_to_all(x, "gauss", split_axis=0, concat_axis=0, tiled=True)


def exchange_wide(x):
    owners, views = lax.axis_size("gauss"), lax.axis_size("view")
    blocks = x.reshape(owners * views // 2, *x.shape[2:])
    groups = [[i for i in range(owners * views) if i % 2 == c] for c in range(2)]
    return lax.all_to_all(
        blocks,
        ("gauss", "view"),
        split_axis=0,
        concat_axis=0,
        axis_index_groups=groups,
        tiled=True,
    )


def shape(dims, dtype):
    return jax.ShapeDtypeStruct(dims, dtype)


def on_device(params, lists, tile_pos, cam_index, cams, targets):
    owners = lax.axis_size("gauss")
    views = lax.axis_size("view")
    width, g_dev = params.shape
    tiles, length = lists.shape
    cap = max(tiles * length // owners, 16)
    slots = owners * cap
    share = LANES // tiles
    depth = SIDE * SIDE // share
    shared = owners == 8 and views % 2 == 0
    wide = views % 2 == 0 and owners * views <= 32

    if shared:
        other_lists = swap(lists, "view", 1)
        other = swap(params, "gauss", 1)
        chip_lists = jnp.concatenate([lists, other_lists], axis=0)
        near_lists, far_lists = reach(chip_lists, (1, 2)), reach(chip_lists, (None, 3))
    hot, names, params_copy, cam, pixel = call(
        functools.partial(prepare_kernel, owners, cap, g_dev),
        [
            shape((slots, tiles * length), BF16),
            shape((owners, EXTRA, LANES), BF16),
            shape((width, g_dev), BF16),
            shape((cams.shape[0], tiles, length), F32),
            shape((2, depth, LANES), F32),
        ],
        (tile_pos, cam_index, cams, lists, params),
        scalars=3,
    )
    if shared:
        first, second = call(
            functools.partial(pick_pair_kernel, cap),
            [shape((2 * cap, 2 * width), BF16)] * 2,
            (chip_lists, near_lists, far_lists, params_copy, other),
        )
        near, far = reach(first, (1, 2)), reach(second, (None, 3))
        returned = [second, near, far] + [swap(x, "view", 1) for x in (second, near, far)]
        recv_scratch = (pltpu.VMEM((4, cap, 2 * width), BF16),)
    else:
        all_lists = exchange(jnp.broadcast_to(lists[None], (owners, tiles, length)))
        picked = call(
            functools.partial(pick_kernel, tiles, cap),
            shape((slots, LANES), BF16),
            (all_lists.reshape(owners * tiles, length), params_copy),
        )
        returned = [exchange(picked.reshape(owners, cap, LANES)).reshape(slots, LANES)]
        recv_scratch = ()
    spread_targets = (
        targets.reshape(3, tiles, depth, share).transpose(0, 2, 1, 3).reshape(3, depth, LANES)
    )
    copies = views // 2 if wide else 1
    pictures, sent = call(
        functools.partial(render_kernel, shared, width),
        [shape((3, depth, LANES), F32), shape((owners, copies, cap + EXTRA, 2 * width), BF16)],
        (*returned, lists, hot, names, cam, pixel, spread_targets),
        scratch=(
            pltpu.VMEM((tiles * width, length), F32),
            pltpu.VMEM((8 * length, LANES), F32),
            pltpu.VMEM((length * depth, LANES), F32),
            pltpu.VMEM((length * depth, LANES), F32),
            pltpu.VMEM((6, length * depth, LANES), F32),
        )
        + recv_scratch,
    )
    pictures = (
        pictures.reshape(3, depth, tiles, share)
        .transpose(0, 2, 1, 3)
        .reshape(3, tiles, SIDE * SIDE)
    )
    received = exchange_wide(sent) if wide else exchange(sent[:, 0])
    grads = call(scatter_kernel, shape((width, g_dev), F32), (received,))
    if wide:
        grads = grads + swap(grads, "view", 1)
    else:
        grads = lax.psum(grads, "view")
    return (pictures, grads)


def solution(mesh):
    return jax.shard_map(
        on_device,
        mesh=mesh,
        in_specs=(
            P(None, "gauss"),
            P(("gauss", "view"), None),
            P(("gauss", "view")),
            P(("gauss", "view")),
            P(),
            P(None, ("gauss", "view"), None),
        ),
        out_specs=(P(None, ("gauss", "view"), None), P(None, "gauss")),
        check_vma=False,
    )
```

```python
import functools
import math

import jax
import jax.numpy as jnp
from jax import lax
from jax.experimental import pallas as pl
from jax.experimental.pallas import tpu as pltpu
from jax.sharding import PartitionSpec as P

WIN = 16
SIDE = 16
LANES = 128
LOG2E = math.log2(math.e)
F32 = jnp.float32
BF16 = jnp.bfloat16
VMEM_LIMIT = 24 * 2**20
SENT = 32


def sh_terms(x, y, z):
    xx, yy, zz = x * x, y * y, z * z
    xy = x * y
    diff = xx - yy
    five = 5.0 * zz - 1.0
    return [
        x,
        y,
        z,
        xy,
        y * z,
        x * z,
        diff,
        3.0 * zz - 1.0,
        x * (xx - 3.0 * yy),
        xy * z,
        y * (3.0 * xx - yy),
        z * diff,
        x * five,
        y * five,
        z * (5.0 * zz - 3.0),
    ]


def project(rows, cam, live):
    mx, my, mz = rows[0], rows[1], rows[2]
    cam_x = cam[0] * mx + cam[1] * my + cam[2] * mz + cam[9]
    cam_y = cam[3] * mx + cam[4] * my + cam[5] * mz + cam[10]
    cam_z = cam[6] * mx + cam[7] * my + cam[8] * mz + cam[11]
    cam_z = jnp.where(live, cam_z, 1.0)
    inv_z = 1.0 / cam_z
    qw, qx, qy, qz = rows[6], rows[7], rows[8], rows[9]
    qw = jnp.where(live, qw, 1.0)
    inv_q = lax.rsqrt(qw * qw + qx * qx + qy * qy + qz * qz)
    qw, qx, qy, qz = qw * inv_q, qx * inv_q, qy * inv_q, qz * inv_q
    rot = [
        [
            1.0 - 2.0 * (qy * qy + qz * qz),
            2.0 * (qx * qy - qw * qz),
            2.0 * (qx * qz + qw * qy),
        ],
        [
            2.0 * (qx * qy + qw * qz),
            1.0 - 2.0 * (qx * qx + qz * qz),
            2.0 * (qy * qz - qw * qx),
        ],
        [
            2.0 * (qx * qz - qw * qy),
            2.0 * (qy * qz + qw * qx),
            1.0 - 2.0 * (qx * qx + qy * qy),
        ],
    ]
    mixed = [
        [
            cam[3 * i] * rot[0][k] + cam[3 * i + 1] * rot[1][k] + cam[3 * i + 2] * rot[2][k]
            for k in range(3)
        ]
        for i in range(3)
    ]
    scale = cam[12] * inv_z
    ray_x, ray_y = cam_x * inv_z, cam_y * inv_z
    proj_u = [scale * (mixed[0][k] - ray_x * mixed[2][k]) for k in range(3)]
    proj_v = [scale * (mixed[1][k] - ray_y * mixed[2][k]) for k in range(3)]
    var = [jnp.exp(2.0 * rows[3 + k]) for k in range(3)]
    uv = [proj_u[k] * var[k] for k in range(3)]
    cov_a = sum(uv[k] * proj_u[k] for k in range(3)) + 0.3
    cov_b = sum(uv[k] * proj_v[k] for k in range(3))
    cov_c = sum(proj_v[k] * proj_v[k] * var[k] for k in range(3)) + 0.3
    inv_det = 1.0 / (cov_a * cov_c - cov_b * cov_b)
    inv_dist = lax.rsqrt(cam_x * cam_x + cam_y * cam_y + cam_z * cam_z)
    terms = sh_terms(cam_x * inv_dist, cam_y * inv_dist, cam_z * inv_dist)
    geometry = [cam_x * scale, cam_y * scale, cov_c * inv_det, -cov_b * inv_det, cov_a * inv_det]
    return geometry + terms, (ray_x, ray_y)


def iota(shape, dim):
    return lax.broadcasted_iota(jnp.int32, shape, dim)


def one_hot(mask):
    return jnp.where(mask, 1.0, 0.0).astype(BF16)


def dot(lhs, rhs, lhs_dim=1, rhs_dim=0):
    return lax.dot_general(
        lhs, rhs, (((lhs_dim,), (rhs_dim,)), ((), ())), preferred_element_type=F32
    )


def split(x, parts):
    out = []
    for _ in range(parts):
        head = x.astype(BF16)
        out.append(head)
        x = x - head.astype(F32)
    return out


def ranks(mask, tiles):
    rows, length = mask.shape
    bits = one_hot(mask)
    earlier = one_hot(iota((length, length), 0) < iota((length, length), 1))
    within = dot(bits, earlier)
    count = dot(bits, jnp.ones((length, length), BF16)).astype(BF16)
    here, there = iota((rows, rows), 0), iota((rows, rows), 1)
    above = one_hot((there < here) & (there >= here - lax.rem(here, tiles)))
    return (within + dot(above, count)).astype(jnp.int32)


def find(ids, base, tiles, cap, g_dev):
    local = ids - base
    mine = (local >= 0) & (local < g_dev)
    key = jnp.where(mine, ranks(mine, tiles), -1)
    rows, length = ids.shape
    slot = iota((cap, length), 0)
    found = []
    for r in range(0, rows, tiles):
        total = jnp.zeros((cap, length), jnp.int32)
        for t in range(r, r + tiles):
            total = total + jnp.where(key[t : t + 1, :] == slot, local[t : t + 1, :], 0)
        found.append(jnp.sum(total, axis=1, keepdims=True))
    return jnp.concatenate(found, axis=0)


def pick_kernel(tiles, cap, lists_ref, params_ref, picked_ref):
    width, g_dev = params_ref.shape
    where = find(lists_ref[...], lax.axis_index("gauss") * g_dev, tiles, cap, g_dev)
    hot = one_hot(where == iota((where.shape[0], g_dev), 1))
    wide = jnp.concatenate([params_ref[...], jnp.zeros((LANES - width, g_dev), BF16)], axis=0)
    picked_ref[...] = dot(hot, wide, 1, 1).astype(BF16)


def pick_pair_kernel(cap, peers, *refs):
    lists_refs, refs = refs[:peers], refs[peers:]
    own_ref, other_ref = refs[:2]
    picked_refs, refs = refs[2 : 2 + peers], refs[2 + peers :]
    lists_scratch, picked_scratch = refs
    tiles, length = lists_refs[0].shape
    width, g_dev = own_ref.shape
    me = lax.axis_index("gauss")
    first = me % 2 == 0
    for k in range(peers):
        lists_scratch[(me // 2) ^ k] = lists_refs[k][...]
    ids = lists_scratch[...].reshape(peers * tiles, length)
    where_own = find(ids, me * g_dev, tiles, cap, g_dev)
    where_other = find(ids, (me ^ 1) * g_dev, tiles, cap, g_dev)
    own, other = own_ref[...], other_ref[...]
    blank = jnp.zeros((width, g_dev), BF16)
    lanes = iota((peers * cap, g_dev), 1)
    picked = dot(
        one_hot(where_own == lanes),
        jnp.concatenate([jnp.where(first, own, blank), jnp.where(first, blank, own)], axis=0),
        1,
        1,
    ) + dot(
        one_hot(where_other == lanes),
        jnp.concatenate([jnp.where(first, blank, other), jnp.where(first, other, blank)], axis=0),
        1,
        1,
    )
    picked_scratch[...] = picked.astype(BF16).reshape(peers, cap, 2 * width)
    for k in range(peers):
        picked_refs[k][...] = picked_scratch[(me // 2) ^ k]


def by_tile(values, row):
    out = jnp.full(row.shape, values[-1])
    for t in range(len(values) - 1):
        out = jnp.where(row == t, values[t], out)
    return out


def prepare_kernel(
    owners,
    cap,
    g_dev,
    tile_pos_ref,
    cam_index_ref,
    cams_ref,
    lists_ref,
    params_ref,
    hot_ref,
    local_ref,
    copy_ref,
    cam_ref,
    pixel_ref,
):
    tiles, length = lists_ref.shape
    share = LANES // tiles
    depth = SIDE * SIDE // share
    cam_ids = [cam_index_ref[t] for t in range(tiles)]
    tile_row = iota((tiles, length), 0)
    for j in range(cams_ref.shape[0]):
        cam_ref[j] = by_tile([cams_ref[j, cam_ids[t]] for t in range(tiles)], tile_row)
    pos = [tile_pos_ref[t] for t in range(tiles)]
    lane = iota((depth, LANES), 1)
    origin_x = [(SIDE * (lax.rem(p, WIN) - WIN // 2)).astype(F32) + 0.5 for p in pos]
    pixel_ref[0] = by_tile(origin_x, lane // share) + (lane % SIDE).astype(F32)
    origin_y = [(SIDE * (lax.div(p, WIN) - WIN // 2)).astype(F32) + 0.5 for p in pos]
    pixel_row = iota((depth, LANES), 0) * (share // SIDE) + (lane % share) // SIDE
    pixel_ref[1] = by_tile(origin_y, lane // share) + pixel_row.astype(F32)

    slots = owners * cap
    ids = lists_ref[...]
    masks = [(ids >= o * g_dev) & (ids < (o + 1) * g_dev) for o in range(owners)]
    rank = ranks(jnp.concatenate([m.astype(jnp.int32) for m in masks], axis=0) > 0, tiles)
    place = jnp.full((tiles, length), -1, jnp.int32)
    local = jnp.zeros((tiles, length), jnp.int32)
    for o in range(owners):
        place = jnp.where(masks[o], rank[o * tiles : (o + 1) * tiles] + o * cap, place)
        local = jnp.where(masks[o], ids - o * g_dev, local)
    slot_iota = iota((slots, length), 0)
    hot_ref[...] = jnp.concatenate(
        [one_hot(slot_iota == place[t : t + 1, :]) for t in range(tiles)], axis=1
    )
    local_ref[...] = local.astype(F32)
    copy_ref[...] = params_ref[...]


def render_kernel(pieces, width, *refs):
    recv_refs, refs = refs[:pieces], refs[pieces:]
    lists_ref, hot_ref, local_ref, cam_ref, pixel_ref, targets_ref = refs[:6]
    pictures_ref, send_ref, rows_ref, table_ref, alpha_ref, weight_ref, part_ref = refs[6:13]
    tiles, length = lists_ref.shape
    share = LANES // tiles
    depth = SIDE * SIDE // share
    live = lists_ref[...] >= 0
    hot = hot_ref[...]

    if pieces == 1:
        listed = dot(recv_refs[0][...], hot, 0, 0)[:width]
    else:
        (recv_scratch,) = refs[13:]
        cap = recv_refs[0].shape[0]
        place = lax.axis_index("gauss") // 2
        for k in range(pieces):
            recv_scratch[place ^ k] = recv_refs[k][...]
        received = recv_scratch[...].reshape(pieces * cap, 2 * width)
        halves = [
            jnp.concatenate(
                [hot[(2 * p + j) * cap : (2 * p + j + 1) * cap] for p in range(pieces)], axis=0
            )
            for j in range(2)
        ]
        listed = dot(received, halves[0], 0, 0)[:width] + dot(received, halves[1], 0, 0)[width:]
    for t in range(tiles):
        rows_ref[t * width : (t + 1) * width, :] = listed[:, t * length : (t + 1) * length]
    rows = [rows_ref[pl.ds(f, tiles, stride=width), :] for f in range(width)]

    cam = [cam_ref[j] for j in range(cam_ref.shape[0])]
    outs, pullback, rays = jax.vjp(lambda r: project(r, cam, live), rows[:10], has_aux=True)
    terms = outs[5:]
    colors = []
    for k in range(3):
        base = 11 + 16 * k
        shade = 0.5 + rows[base]
        for b in range(15):
            shade = shade + rows[base + 1 + b] * terms[b]
        for j in range(5):
            shade = shade + rows[59 + j] * cam[13 + 3 * j + k]
        colors.append(shade)
    opacity = jax.nn.sigmoid(rows[10])
    con_a, con_b, con_c = outs[2], outs[3], outs[4]

    attrs = [
        outs[0],
        outs[1],
        (-0.5 * LOG2E) * con_a,
        -LOG2E * con_b,
        (-0.5 * LOG2E) * con_c,
        jnp.where(live, opacity, 0.0),
    ] + colors
    count = len(attrs)
    blocks = []
    for value in attrs:
        parts = [p.astype(F32) for p in split(value, 3)]
        parts.append(jnp.zeros((16 - 3 * tiles, length), F32))
        blocks.append(jnp.concatenate(parts, axis=0))
    stacked = jnp.concatenate(blocks, axis=1)
    lane_tile = iota((16, LANES), 1) // share
    row_index = iota((16, LANES), 0)
    spread = one_hot((row_index % tiles == lane_tile) & (row_index < 3 * tiles))
    table = dot(stacked.T.astype(BF16), spread)
    pixel_x, pixel_y = pixel_ref[0, :1, :], pixel_ref[1]
    dx = pixel_x - table[:length]
    table_ref[0:length, :] = table[2 * length : 3 * length] * dx * dx
    table_ref[length : 2 * length, :] = table[3 * length : 4 * length] * dx
    table_ref[2 * length : 3 * length, :] = table[length : 2 * length]
    table_ref[3 * length :, :] = table[4 * length :]

    def row(index, l):
        return table_ref[pl.ds(index * length + l, 1), :]

    group = 16
    zero = jnp.zeros((depth, LANES), F32)

    def forward(chunk, carry):
        through, red, green, blue = carry
        for i in range(group):
            l = chunk * group + i
            dy = pixel_y - row(2, l)
            power = row(0, l) + dy * (row(1, l) + row(3, l) * dy)
            alpha = row(4, l) * jnp.exp2(power)
            weight = through * alpha
            red = red + weight * row(5, l)
            green = green + weight * row(6, l)
            blue = blue + weight * row(7, l)
            through = through - weight
            at = pl.ds(pl.multiple_of(l * depth, depth), depth)
            alpha_ref[at, :] = alpha
            weight_ref[at, :] = weight
        return through, red, green, blue

    start = (jnp.ones((depth, LANES), F32), zero, zero, zero)
    _, red, green, blue = lax.fori_loop(0, length // group, forward, start)
    pictures_ref[0] = red
    pictures_ref[1] = green
    pictures_ref[2] = blue
    res = [red - targets_ref[0], green - targets_ref[1], blue - targets_ref[2]]

    def backward(step, behind):
        chunk = length // group - 1 - step
        for i in reversed(range(group)):
            l = chunk * group + i
            at = pl.ds(pl.multiple_of(l * depth, depth), depth)
            alpha = alpha_ref[at, :]
            weight = weight_ref[at, :]
            dy = pixel_y - row(2, l)
            seen = row(5, l) * res[0] + row(6, l) * res[1] + row(7, l) * res[2]
            gap = seen - behind
            behind = behind + alpha * gap
            g = weight * gap
            gy = g * dy
            part_ref[0, at, :] = g
            part_ref[1, at, :] = gy
            part_ref[2, at, :] = gy * dy
            for k in range(3):
                part_ref[3 + k, at, :] = weight * res[k]
        return behind

    lax.fori_loop(0, length // group, backward, zero)

    def down(index):
        blocks = []
        for first in range(0, length, 8):
            parts = [
                part_ref[index, pl.ds(first * depth + s, 8, stride=depth), :] for s in range(depth)
            ]
            while len(parts) > 1:
                parts = [a + b for a, b in zip(parts[::2], parts[1::2])]
            blocks.append(parts[0])
        return jnp.concatenate(blocks, axis=0)

    sums = [down(index) for index in range(6)]
    g_x = sums[0] * dx
    sums = sums + [g_x, g_x * dx, sums[1] * dx]
    wide = jnp.concatenate([jnp.concatenate(split(s, 3), axis=1) for s in sums], axis=0)
    gather = one_hot(iota((8, 3 * LANES), 0) == (iota((8, 3 * LANES), 1) % LANES) // share)
    reduced = dot(gather, wide, 1, 1)
    g_0, g_y, g_yy, s_0, s_1, s_2, g_x, g_xx, g_xy = [
        reduced[:tiles, q * length : (q + 1) * length] for q in range(len(sums))
    ]

    d_colors = [s_0, s_1, s_2]
    d_terms = []
    for b in range(15):
        d_terms.append(sum(d_colors[k] * rows[12 + 16 * k + b] for k in range(3)))
    d_geometry = [
        con_a * g_x + con_b * g_y,
        con_b * g_x + con_c * g_y,
        -0.5 * g_xx,
        -g_xy,
        -0.5 * g_yy,
    ]
    (d_rows,) = pullback(d_geometry + d_terms)
    values = list(d_rows)
    values.append(g_0 * (1.0 - opacity))
    values.extend(d_colors)
    values.extend(rays)
    for j in range(5):
        values.append(sum(d_colors[k] * cam[13 + 3 * j + k] for k in range(3)))
    values.append(local_ref[...])
    values.extend([jnp.zeros((tiles, length), F32)] * (SENT - len(values)))
    for v in range(SENT):
        rows_ref[pl.ds(v, tiles, stride=width), :] = values[v]
    by_slot = jnp.concatenate(
        [
            jnp.concatenate(split(rows_ref[t * width : t * width + SENT, :], 3), axis=0)
            for t in range(tiles)
        ],
        axis=1,
    )
    by_slot = dot(by_slot, hot, 1, 1)
    by_slot = by_slot[:SENT] + by_slot[SENT : 2 * SENT] + by_slot[2 * SENT :]
    owners, copies, high, _ = send_ref.shape
    cap = hot.shape[0] // owners
    for o in range(owners):
        block = jnp.concatenate(
            [by_slot[r : r + high, o * cap : (o + 1) * cap] for r in range(0, SENT, high)], axis=1
        )
        for c in range(copies):
            send_ref[o, c] = block


def scatter_kernel(cap, recv_ref, out_ref, rows_ref):
    blocks, high, _ = recv_ref.shape
    width, g_dev = out_ref.shape

    def value(v):
        first = v // high * cap
        return recv_ref[:, v % high, first : first + cap]

    ray_x, ray_y = value(14), value(15)
    dir_z = lax.rsqrt(ray_x * ray_x + ray_y * ray_y + 1.0)
    terms = sh_terms(ray_x * dir_z, ray_y * dir_z, dir_z)
    features = [value(v) for v in range(11)]
    for k in range(3):
        color = value(11 + k)
        features.append(color)
        features.extend(color * term for term in terms)
    features.extend(value(v) for v in range(16, 21))
    for f in range(width):
        rows_ref[pl.ds(f, blocks, stride=width), :] = features[f]
    received = jnp.concatenate(
        [rows_ref[b * width : (b + 1) * width, :] for b in range(blocks)], axis=1
    )
    names = value(21).astype(jnp.int32)
    where = jnp.concatenate([names[b : b + 1, :] for b in range(blocks)], axis=1)
    hot = one_hot(iota((g_dev, blocks * cap), 0) == where)
    total = dot(jnp.concatenate(split(received, 2), axis=0), hot, 1, 1)
    out_ref[...] = total[:width] + total[width:]


def call(kernel, out_shape, args, scalars=0, scratch=()):
    in_specs = [pl.BlockSpec(memory_space=pltpu.SMEM)] * scalars
    in_specs += [pl.BlockSpec(memory_space=pltpu.VMEM)] * (len(args) - scalars)
    many = isinstance(out_shape, (list, tuple))
    spec = pl.BlockSpec(memory_space=pltpu.VMEM)
    return pl.pallas_call(
        kernel,
        out_shape=out_shape,
        in_specs=in_specs,
        out_specs=[spec] * len(out_shape) if many else spec,
        scratch_shapes=list(scratch),
        compiler_params=pltpu.CompilerParams(vmem_limit_bytes=VMEM_LIMIT),
    )(*args)


def swap(x, axis, k):
    return lax.ppermute(x, axis, [(i, i ^ k) for i in range(lax.axis_size(axis))])


def exchange(x):
    return lax.all_to_all(x, "gauss", split_axis=0, concat_axis=0, tiled=True)


def exchange_wide(x):
    owners, views = lax.axis_size("gauss"), lax.axis_size("view")
    blocks = x.reshape(owners * views // 2, *x.shape[2:])
    groups = [[i for i in range(owners * views) if i % 2 == c] for c in range(2)]
    return lax.all_to_all(
        blocks,
        ("gauss", "view"),
        split_axis=0,
        concat_axis=0,
        axis_index_groups=groups,
        tiled=True,
    )


def power_of_two(n):
    return n & (n - 1) == 0


def shape(dims, dtype):
    return jax.ShapeDtypeStruct(dims, dtype)


def on_device(params, lists, tile_pos, cam_index, cams, targets):
    owners = lax.axis_size("gauss")
    views = lax.axis_size("view")
    width, g_dev = params.shape
    tiles, length = lists.shape
    cap = max(tiles * length // owners, 16)
    slots = owners * cap
    share = LANES // tiles
    depth = SIDE * SIDE // share
    paired = 2 <= owners <= 16 and power_of_two(owners) and LANES == 2 * width
    peers = owners // 2 if paired else 1
    wide = views % 2 == 0 and owners * views <= 32

    if paired:
        other = swap(params, "gauss", 1)
        all_lists = [lists] + [swap(lists, "gauss", 2 * k) for k in range(1, peers)]
    hot, local, params_copy, cam, pixel = call(
        functools.partial(prepare_kernel, owners, cap, g_dev),
        [
            shape((slots, tiles * length), BF16),
            shape((tiles, length), F32),
            shape((width, g_dev), BF16),
            shape((cams.shape[0], tiles, length), F32),
            shape((2, depth, LANES), F32),
        ],
        (tile_pos, cam_index, cams, lists, params),
        scalars=3,
    )
    if paired:
        picked = call(
            functools.partial(pick_pair_kernel, cap, peers),
            [shape((cap, 2 * width), BF16)] * peers,
            (*all_lists, params_copy, other),
            scratch=(
                pltpu.VMEM((peers, tiles, length), jnp.int32),
                pltpu.VMEM((peers, cap, 2 * width), BF16),
            ),
        )
        returned = [picked[0]] + [swap(picked[k], "gauss", 2 * k) for k in range(1, peers)]
        recv_scratch = (pltpu.VMEM((peers, cap, 2 * width), BF16),)
    else:
        all_lists = exchange(jnp.broadcast_to(lists[None], (owners, tiles, length)))
        picked = call(
            functools.partial(pick_kernel, tiles, cap),
            shape((slots, LANES), BF16),
            (all_lists.reshape(owners * tiles, length), params_copy),
        )
        returned = [exchange(picked.reshape(owners, cap, LANES)).reshape(slots, LANES)]
        recv_scratch = ()
    spread_targets = (
        targets.reshape(3, tiles, depth, share).transpose(0, 2, 1, 3).reshape(3, depth, LANES)
    )
    copies = views // 2 if wide else 1
    high = SENT * cap // LANES
    pictures, sent = call(
        functools.partial(render_kernel, peers, width),
        [shape((3, depth, LANES), F32), shape((owners, copies, high, LANES), F32)],
        (*returned, lists, hot, local, cam, pixel, spread_targets),
        scratch=(
            pltpu.VMEM((tiles * width, length), F32),
            pltpu.VMEM((8 * length, LANES), F32),
            pltpu.VMEM((length * depth, LANES), F32),
            pltpu.VMEM((length * depth, LANES), F32),
            pltpu.VMEM((6, length * depth, LANES), F32),
        )
        + recv_scratch,
    )
    pictures = (
        pictures.reshape(3, depth, tiles, share)
        .transpose(0, 2, 1, 3)
        .reshape(3, tiles, SIDE * SIDE)
    )
    received = exchange_wide(sent) if wide else exchange(sent[:, 0])
    grads = call(
        functools.partial(scatter_kernel, cap),
        shape((width, g_dev), F32),
        (received,),
        scratch=(pltpu.VMEM((received.shape[0] * width, cap), F32),),
    )
    if wide:
        grads = grads + swap(grads, "view", 1)
    else:
        grads = lax.psum(grads, "view")
    return (pictures, grads)


def solution(mesh):
    return jax.shard_map(
        on_device,
        mesh=mesh,
        in_specs=(
            P(None, "gauss"),
            P(("gauss", "view"), None),
            P(("gauss", "view")),
            P(("gauss", "view")),
            P(),
            P(None, ("gauss", "view"), None),
        ),
        out_specs=(P(None, ("gauss", "view"), None), P(None, "gauss")),
        check_vma=False,
    )
```

```python
import functools
import math

import jax
import jax.numpy as jnp
from jax import lax
from jax.experimental import pallas as pl
from jax.experimental.pallas import tpu as pltpu
from jax.sharding import PartitionSpec as P

WIN = 16
SIDE = 16
LANES = 128
LOG2E = math.log2(math.e)
F32 = jnp.float32
BF16 = jnp.bfloat16
VMEM_LIMIT = 24 * 2**20
SENT = 32


def sh_terms(x, y, z):
    xx, yy, zz = x * x, y * y, z * z
    xy = x * y
    diff = xx - yy
    five = 5.0 * zz - 1.0
    return [
        x,
        y,
        z,
        xy,
        y * z,
        x * z,
        diff,
        3.0 * zz - 1.0,
        x * (xx - 3.0 * yy),
        xy * z,
        y * (3.0 * xx - yy),
        z * diff,
        x * five,
        y * five,
        z * (5.0 * zz - 3.0),
    ]


def project(rows, cam, live):
    mx, my, mz = rows[0], rows[1], rows[2]
    cam_x = cam[0] * mx + cam[1] * my + cam[2] * mz + cam[9]
    cam_y = cam[3] * mx + cam[4] * my + cam[5] * mz + cam[10]
    cam_z = cam[6] * mx + cam[7] * my + cam[8] * mz + cam[11]
    cam_z = jnp.where(live, cam_z, 1.0)
    inv_z = 1.0 / cam_z
    qw, qx, qy, qz = rows[6], rows[7], rows[8], rows[9]
    qw = jnp.where(live, qw, 1.0)
    inv_q = lax.rsqrt(qw * qw + qx * qx + qy * qy + qz * qz)
    qw, qx, qy, qz = qw * inv_q, qx * inv_q, qy * inv_q, qz * inv_q
    rot = [
        [
            1.0 - 2.0 * (qy * qy + qz * qz),
            2.0 * (qx * qy - qw * qz),
            2.0 * (qx * qz + qw * qy),
        ],
        [
            2.0 * (qx * qy + qw * qz),
            1.0 - 2.0 * (qx * qx + qz * qz),
            2.0 * (qy * qz - qw * qx),
        ],
        [
            2.0 * (qx * qz - qw * qy),
            2.0 * (qy * qz + qw * qx),
            1.0 - 2.0 * (qx * qx + qy * qy),
        ],
    ]
    mixed = [
        [
            cam[3 * i] * rot[0][k] + cam[3 * i + 1] * rot[1][k] + cam[3 * i + 2] * rot[2][k]
            for k in range(3)
        ]
        for i in range(3)
    ]
    scale = cam[12] * inv_z
    ray_x, ray_y = cam_x * inv_z, cam_y * inv_z
    proj_u = [scale * (mixed[0][k] - ray_x * mixed[2][k]) for k in range(3)]
    proj_v = [scale * (mixed[1][k] - ray_y * mixed[2][k]) for k in range(3)]
    var = [jnp.exp(2.0 * rows[3 + k]) for k in range(3)]
    uv = [proj_u[k] * var[k] for k in range(3)]
    cov_a = sum(uv[k] * proj_u[k] for k in range(3)) + 0.3
    cov_b = sum(uv[k] * proj_v[k] for k in range(3))
    cov_c = sum(proj_v[k] * proj_v[k] * var[k] for k in range(3)) + 0.3
    inv_det = 1.0 / (cov_a * cov_c - cov_b * cov_b)
    inv_dist = lax.rsqrt(cam_x * cam_x + cam_y * cam_y + cam_z * cam_z)
    terms = sh_terms(cam_x * inv_dist, cam_y * inv_dist, cam_z * inv_dist)
    geometry = [cam_x * scale, cam_y * scale, cov_c * inv_det, -cov_b * inv_det, cov_a * inv_det]
    return geometry + terms, (ray_x, ray_y)


def iota(shape, dim):
    return lax.broadcasted_iota(jnp.int32, shape, dim)


def one_hot(mask):
    return jnp.where(mask, 1.0, 0.0).astype(BF16)


def dot(lhs, rhs, lhs_dim=1, rhs_dim=0):
    return lax.dot_general(
        lhs, rhs, (((lhs_dim,), (rhs_dim,)), ((), ())), preferred_element_type=F32
    )


def split(x, parts):
    out = []
    for _ in range(parts):
        head = x.astype(BF16)
        out.append(head)
        x = x - head.astype(F32)
    return out


def ranks(mask, tiles):
    rows, length = mask.shape
    bits = one_hot(mask)
    earlier = one_hot(iota((length, length), 0) < iota((length, length), 1))
    within = dot(bits, earlier)
    count = dot(bits, jnp.ones((length, length), BF16)).astype(BF16)
    here, there = iota((rows, rows), 0), iota((rows, rows), 1)
    above = one_hot((there < here) & (there >= here - lax.rem(here, tiles)))
    return (within + dot(above, count)).astype(jnp.int32)


def find(ids, base, tiles, cap, g_dev):
    local = ids - base
    mine = (local >= 0) & (local < g_dev)
    key = jnp.where(mine, ranks(mine, tiles), -1)
    rows, length = ids.shape
    slot = iota((cap, length), 0)
    found = []
    for r in range(0, rows, tiles):
        total = jnp.zeros((cap, length), jnp.int32)
        for t in range(r, r + tiles):
            total = total + jnp.where(key[t : t + 1, :] == slot, local[t : t + 1, :], 0)
        found.append(jnp.sum(total, axis=1, keepdims=True))
    return jnp.concatenate(found, axis=0)


def pick_kernel(tiles, cap, lists_ref, params_ref, picked_ref):
    width, g_dev = params_ref.shape
    where = find(lists_ref[...], lax.axis_index("gauss") * g_dev, tiles, cap, g_dev)
    hot = one_hot(where == iota((where.shape[0], g_dev), 1))
    wide = jnp.concatenate([params_ref[...], jnp.zeros((LANES - width, g_dev), BF16)], axis=0)
    picked_ref[...] = dot(hot, wide, 1, 1).astype(BF16)


def pick_pair_kernel(cap, peers, *refs):
    lists_refs, refs = refs[:peers], refs[peers:]
    own_ref, other_ref, picked_ref, lists_scratch = refs
    tiles, length = lists_refs[0].shape
    width, g_dev = own_ref.shape
    me = lax.axis_index("gauss")
    first = me % 2 == 0
    for k in range(peers):
        lists_scratch[(me // 2) ^ k] = lists_refs[k][...]
    ids = lists_scratch[...].reshape(peers * tiles, length)
    where_own = find(ids, me * g_dev, tiles, cap, g_dev)
    where_other = find(ids, (me ^ 1) * g_dev, tiles, cap, g_dev)
    own, other = own_ref[...], other_ref[...]
    blank = jnp.zeros((width, g_dev), BF16)
    lanes = iota((peers * cap, g_dev), 1)
    picked = dot(
        one_hot(where_own == lanes),
        jnp.concatenate([jnp.where(first, own, blank), jnp.where(first, blank, own)], axis=0),
        1,
        1,
    ) + dot(
        one_hot(where_other == lanes),
        jnp.concatenate([jnp.where(first, blank, other), jnp.where(first, other, blank)], axis=0),
        1,
        1,
    )
    picked_ref[...] = picked.astype(BF16).reshape(peers, cap, 2 * width)


def by_tile(values, row):
    out = jnp.full(row.shape, values[-1])
    for t in range(len(values) - 1):
        out = jnp.where(row == t, values[t], out)
    return out


def prepare_kernel(
    owners,
    cap,
    g_dev,
    tile_pos_ref,
    cam_index_ref,
    cams_ref,
    lists_ref,
    params_ref,
    hot_ref,
    local_ref,
    copy_ref,
    cam_ref,
    pixel_ref,
):
    tiles, length = lists_ref.shape
    share = LANES // tiles
    depth = SIDE * SIDE // share
    cam_ids = [cam_index_ref[t] for t in range(tiles)]
    tile_row = iota((tiles, length), 0)
    for j in range(cams_ref.shape[0]):
        cam_ref[j] = by_tile([cams_ref[j, cam_ids[t]] for t in range(tiles)], tile_row)
    pos = [tile_pos_ref[t] for t in range(tiles)]
    lane = iota((depth, LANES), 1)
    origin_x = [(SIDE * (lax.rem(p, WIN) - WIN // 2)).astype(F32) + 0.5 for p in pos]
    pixel_ref[0] = by_tile(origin_x, lane // share) + (lane % SIDE).astype(F32)
    origin_y = [(SIDE * (lax.div(p, WIN) - WIN // 2)).astype(F32) + 0.5 for p in pos]
    pixel_row = iota((depth, LANES), 0) * (share // SIDE) + (lane % share) // SIDE
    pixel_ref[1] = by_tile(origin_y, lane // share) + pixel_row.astype(F32)

    slots = owners * cap
    ids = lists_ref[...]
    masks = [(ids >= o * g_dev) & (ids < (o + 1) * g_dev) for o in range(owners)]
    rank = ranks(jnp.concatenate([m.astype(jnp.int32) for m in masks], axis=0) > 0, tiles)
    place = jnp.full((tiles, length), -1, jnp.int32)
    local = jnp.zeros((tiles, length), jnp.int32)
    for o in range(owners):
        place = jnp.where(masks[o], rank[o * tiles : (o + 1) * tiles] + o * cap, place)
        local = jnp.where(masks[o], ids - o * g_dev, local)
    slot_iota = iota((slots, length), 0)
    hot_ref[...] = jnp.concatenate(
        [one_hot(slot_iota == place[t : t + 1, :]) for t in range(tiles)], axis=1
    )
    local_ref[...] = local.astype(F32)
    copy_ref[...] = params_ref[...]


def render_kernel(
    paired,
    width,
    recv_ref,
    lists_ref,
    hot_ref,
    local_ref,
    cam_ref,
    pixel_ref,
    targets_ref,
    pictures_ref,
    send_ref,
    rows_ref,
    table_ref,
    alpha_ref,
    weight_ref,
    part_ref,
):
    tiles, length = lists_ref.shape
    share = LANES // tiles
    depth = SIDE * SIDE // share
    live = lists_ref[...] >= 0
    hot = hot_ref[...]
    blocks, cap, lanes = recv_ref.shape
    received = recv_ref[...].reshape(blocks * cap, lanes)
    if paired:
        halves = [
            jnp.concatenate(
                [hot[(2 * p + j) * cap : (2 * p + j + 1) * cap] for p in range(blocks)], axis=0
            )
            for j in range(2)
        ]
        listed = dot(received, halves[0], 0, 0)[:width] + dot(received, halves[1], 0, 0)[width:]
    else:
        listed = dot(received, hot, 0, 0)[:width]
    for t in range(tiles):
        rows_ref[t * width : (t + 1) * width, :] = listed[:, t * length : (t + 1) * length]
    rows = [rows_ref[pl.ds(f, tiles, stride=width), :] for f in range(width)]

    cam = [cam_ref[j] for j in range(cam_ref.shape[0])]
    outs, pullback, rays = jax.vjp(lambda r: project(r, cam, live), rows[:10], has_aux=True)
    terms = outs[5:]
    colors = []
    for k in range(3):
        base = 11 + 16 * k
        shade = 0.5 + rows[base]
        for b in range(15):
            shade = shade + rows[base + 1 + b] * terms[b]
        for j in range(5):
            shade = shade + rows[59 + j] * cam[13 + 3 * j + k]
        colors.append(shade)
    opacity = jax.nn.sigmoid(rows[10])
    con_a, con_b, con_c = outs[2], outs[3], outs[4]

    attrs = [
        outs[0],
        outs[1],
        (-0.5 * LOG2E) * con_a,
        -LOG2E * con_b,
        (-0.5 * LOG2E) * con_c,
        jnp.where(live, opacity, 0.0),
    ] + colors
    count = len(attrs)
    blocks = []
    for value in attrs:
        parts = [p.astype(F32) for p in split(value, 3)]
        parts.append(jnp.zeros((16 - 3 * tiles, length), F32))
        blocks.append(jnp.concatenate(parts, axis=0))
    stacked = jnp.concatenate(blocks, axis=1)
    lane_tile = iota((16, LANES), 1) // share
    row_index = iota((16, LANES), 0)
    spread = one_hot((row_index % tiles == lane_tile) & (row_index < 3 * tiles))
    table = dot(stacked.T.astype(BF16), spread)
    pixel_x, pixel_y = pixel_ref[0, :1, :], pixel_ref[1]
    dx = pixel_x - table[:length]
    table_ref[0:length, :] = table[2 * length : 3 * length] * dx * dx
    table_ref[length : 2 * length, :] = table[3 * length : 4 * length] * dx
    table_ref[2 * length : 3 * length, :] = table[length : 2 * length]
    table_ref[3 * length :, :] = table[4 * length :]

    def row(index, l):
        return table_ref[pl.ds(index * length + l, 1), :]

    group = 16
    zero = jnp.zeros((depth, LANES), F32)

    def forward(chunk, carry):
        through, red, green, blue = carry
        for i in range(group):
            l = chunk * group + i
            dy = pixel_y - row(2, l)
            power = row(0, l) + dy * (row(1, l) + row(3, l) * dy)
            alpha = row(4, l) * jnp.exp2(power)
            weight = through * alpha
            red = red + weight * row(5, l)
            green = green + weight * row(6, l)
            blue = blue + weight * row(7, l)
            through = through - weight
            at = pl.ds(pl.multiple_of(l * depth, depth), depth)
            alpha_ref[at, :] = alpha
            weight_ref[at, :] = weight
        return through, red, green, blue

    start = (jnp.ones((depth, LANES), F32), zero, zero, zero)
    _, red, green, blue = lax.fori_loop(0, length // group, forward, start)
    pictures_ref[0] = red
    pictures_ref[1] = green
    pictures_ref[2] = blue
    res = [red - targets_ref[0], green - targets_ref[1], blue - targets_ref[2]]

    def backward(step, behind):
        chunk = length // group - 1 - step
        for i in reversed(range(group)):
            l = chunk * group + i
            at = pl.ds(pl.multiple_of(l * depth, depth), depth)
            alpha = alpha_ref[at, :]
            weight = weight_ref[at, :]
            dy = pixel_y - row(2, l)
            seen = row(5, l) * res[0] + row(6, l) * res[1] + row(7, l) * res[2]
            gap = seen - behind
            behind = behind + alpha * gap
            g = weight * gap
            gy = g * dy
            part_ref[0, at, :] = g
            part_ref[1, at, :] = gy
            part_ref[2, at, :] = gy * dy
            for k in range(3):
                part_ref[3 + k, at, :] = weight * res[k]
        return behind

    lax.fori_loop(0, length // group, backward, zero)

    def down(index):
        blocks = []
        for first in range(0, length, 8):
            parts = [
                part_ref[index, pl.ds(first * depth + s, 8, stride=depth), :] for s in range(depth)
            ]
            while len(parts) > 1:
                parts = [a + b for a, b in zip(parts[::2], parts[1::2])]
            blocks.append(parts[0])
        return jnp.concatenate(blocks, axis=0)

    sums = [down(index) for index in range(6)]
    g_x = sums[0] * dx
    sums = sums + [g_x, g_x * dx, sums[1] * dx]
    wide = jnp.concatenate([jnp.concatenate(split(s, 3), axis=1) for s in sums], axis=0)
    gather = one_hot(iota((8, 3 * LANES), 0) == (iota((8, 3 * LANES), 1) % LANES) // share)
    reduced = dot(gather, wide, 1, 1)
    g_0, g_y, g_yy, s_0, s_1, s_2, g_x, g_xx, g_xy = [
        reduced[:tiles, q * length : (q + 1) * length] for q in range(len(sums))
    ]

    d_colors = [s_0, s_1, s_2]
    d_terms = []
    for b in range(15):
        d_terms.append(sum(d_colors[k] * rows[12 + 16 * k + b] for k in range(3)))
    d_geometry = [
        con_a * g_x + con_b * g_y,
        con_b * g_x + con_c * g_y,
        -0.5 * g_xx,
        -g_xy,
        -0.5 * g_yy,
    ]
    (d_rows,) = pullback(d_geometry + d_terms)
    values = list(d_rows)
    values.append(g_0 * (1.0 - opacity))
    values.extend(d_colors)
    values.extend(rays)
    for j in range(5):
        values.append(sum(d_colors[k] * cam[13 + 3 * j + k] for k in range(3)))
    values.append(local_ref[...])
    values.extend([jnp.zeros((tiles, length), F32)] * (SENT - len(values)))
    for v in range(SENT):
        rows_ref[pl.ds(v, tiles, stride=width), :] = values[v]
    by_slot = jnp.concatenate(
        [
            jnp.concatenate(split(rows_ref[t * width : t * width + SENT, :], 3), axis=0)
            for t in range(tiles)
        ],
        axis=1,
    )
    by_slot = dot(by_slot, hot, 1, 1)
    by_slot = by_slot[:SENT] + by_slot[SENT : 2 * SENT] + by_slot[2 * SENT :]
    owners, copies, high, _ = send_ref.shape
    cap = hot.shape[0] // owners
    for o in range(owners):
        block = jnp.concatenate(
            [by_slot[r : r + high, o * cap : (o + 1) * cap] for r in range(0, SENT, high)], axis=1
        )
        for c in range(copies):
            send_ref[o, c] = block


def scatter_kernel(cap, recv_ref, out_ref):
    blocks, high, lanes = recv_ref.shape
    g_dev = out_ref.shape[1]
    values = jnp.concatenate(
        [
            jnp.concatenate(
                [recv_ref[b, :, first : first + cap] for b in range(blocks)], axis=1
            )
            for first in range(0, SENT * cap // high, cap)
        ],
        axis=0,
    )
    ray_x, ray_y = values[14:15], values[15:16]
    dir_z = lax.rsqrt(ray_x * ray_x + ray_y * ray_y + 1.0)
    terms = sh_terms(ray_x * dir_z, ray_y * dir_z, dir_z)
    terms = jnp.concatenate([jnp.ones_like(dir_z)] + terms, axis=0)
    rows = [values] + [terms * values[11 + k : 12 + k] for k in range(3)]
    hot = one_hot(iota((g_dev, blocks * cap), 0) == values[21:22].astype(jnp.int32))
    parts = split(jnp.concatenate(rows, axis=0), 2)
    total = dot(jnp.concatenate(parts, axis=0), hot, 1, 1)
    count = total.shape[0] // 2
    total = total[:count] + total[count:]
    out_ref[:11, :] = total[:11]
    out_ref[11:59, :] = total[SENT:]
    out_ref[59:, :] = total[16:21]


def call(kernel, out_shape, args, scalars=0, scratch=()):
    in_specs = [pl.BlockSpec(memory_space=pltpu.SMEM)] * scalars
    in_specs += [pl.BlockSpec(memory_space=pltpu.VMEM)] * (len(args) - scalars)
    many = isinstance(out_shape, (list, tuple))
    spec = pl.BlockSpec(memory_space=pltpu.VMEM)
    return pl.pallas_call(
        kernel,
        out_shape=out_shape,
        in_specs=in_specs,
        out_specs=[spec] * len(out_shape) if many else spec,
        scratch_shapes=list(scratch),
        compiler_params=pltpu.CompilerParams(vmem_limit_bytes=VMEM_LIMIT),
    )(*args)


def swap(x, axis, k):
    return lax.ppermute(x, axis, [(i, i ^ k) for i in range(lax.axis_size(axis))])


def exchange(x, groups=None):
    return lax.all_to_all(
        x, "gauss", split_axis=0, concat_axis=0, axis_index_groups=groups, tiled=True
    )


def exchange_wide(x):
    owners, views = lax.axis_size("gauss"), lax.axis_size("view")
    blocks = x.reshape(owners * views // 2, *x.shape[2:])
    groups = [[i for i in range(owners * views) if i % 2 == c] for c in range(2)]
    return lax.all_to_all(
        blocks,
        ("gauss", "view"),
        split_axis=0,
        concat_axis=0,
        axis_index_groups=groups,
        tiled=True,
    )


def power_of_two(n):
    return n & (n - 1) == 0


def shape(dims, dtype):
    return jax.ShapeDtypeStruct(dims, dtype)


def on_device(params, lists, tile_pos, cam_index, cams, targets):
    owners = lax.axis_size("gauss")
    views = lax.axis_size("view")
    width, g_dev = params.shape
    tiles, length = lists.shape
    cap = max(tiles * length // owners, 16)
    slots = owners * cap
    share = LANES // tiles
    depth = SIDE * SIDE // share
    paired = 2 <= owners <= 16 and power_of_two(owners) and LANES == 2 * width
    peers = owners // 2 if paired else 1
    wide = views % 2 == 0 and owners * views <= 32

    if paired:
        other = swap(params, "gauss", 1)
        all_lists = [lists] + [swap(lists, "gauss", 2 * k) for k in range(1, peers)]
    hot, local, params_copy, cam, pixel = call(
        functools.partial(prepare_kernel, owners, cap, g_dev),
        [
            shape((slots, tiles * length), BF16),
            shape((tiles, length), F32),
            shape((width, g_dev), BF16),
            shape((cams.shape[0], tiles, length), F32),
            shape((2, depth, LANES), F32),
        ],
        (tile_pos, cam_index, cams, lists, params),
        scalars=3,
    )
    if paired:
        picked = call(
            functools.partial(pick_pair_kernel, cap, peers),
            shape((peers, cap, 2 * width), BF16),
            (*all_lists, params_copy, other),
            scratch=(pltpu.VMEM((peers, tiles, length), jnp.int32),),
        )
        returned = exchange(picked, [[i for i in range(owners) if i % 2 == c] for c in range(2)])
    else:
        all_lists = exchange(jnp.broadcast_to(lists[None], (owners, tiles, length)))
        picked = call(
            functools.partial(pick_kernel, tiles, cap),
            shape((slots, LANES), BF16),
            (all_lists.reshape(owners * tiles, length), params_copy),
        )
        returned = exchange(picked.reshape(owners, cap, LANES))
    spread_targets = (
        targets.reshape(3, tiles, depth, share).transpose(0, 2, 1, 3).reshape(3, depth, LANES)
    )
    copies = views // 2 if wide else 1
    high = SENT * cap // LANES
    pictures, sent = call(
        functools.partial(render_kernel, paired, width),
        [shape((3, depth, LANES), F32), shape((owners, copies, high, LANES), F32)],
        (returned, lists, hot, local, cam, pixel, spread_targets),
        scratch=(
            pltpu.VMEM((tiles * width, length), F32),
            pltpu.VMEM((8 * length, LANES), F32),
            pltpu.VMEM((length * depth, LANES), F32),
            pltpu.VMEM((length * depth, LANES), F32),
            pltpu.VMEM((6, length * depth, LANES), F32),
        ),
    )
    pictures = (
        pictures.reshape(3, depth, tiles, share)
        .transpose(0, 2, 1, 3)
        .reshape(3, tiles, SIDE * SIDE)
    )
    received = exchange_wide(sent) if wide else exchange(sent[:, 0])
    grads = call(
        functools.partial(scatter_kernel, cap),
        shape((width, g_dev), F32),
        (received,),
    )
    if wide:
        grads = grads + swap(grads, "view", 1)
    else:
        grads = lax.psum(grads, "view")
    return (pictures, grads)


def solution(mesh):
    return jax.shard_map(
        on_device,
        mesh=mesh,
        in_specs=(
            P(None, "gauss"),
            P(("gauss", "view"), None),
            P(("gauss", "view")),
            P(("gauss", "view")),
            P(),
            P(None, ("gauss", "view"), None),
        ),
        out_specs=(P(None, ("gauss", "view"), None), P(None, "gauss")),
        check_vma=False,
    )
```

```python
import functools
import math

import jax
import jax.numpy as jnp
from jax import lax
from jax.experimental import pallas as pl
from jax.experimental.pallas import tpu as pltpu
from jax.sharding import PartitionSpec as P

WIN = 16
SIDE = 16
LANES = 128
LOG2E = math.log2(math.e)
F32 = jnp.float32
BF16 = jnp.bfloat16
VMEM_LIMIT = 24 * 2**20
SENT = 32


def sh_terms(x, y, z):
    xx, yy, zz = x * x, y * y, z * z
    xy = x * y
    diff = xx - yy
    five = 5.0 * zz - 1.0
    return [
        x,
        y,
        z,
        xy,
        y * z,
        x * z,
        diff,
        3.0 * zz - 1.0,
        x * (xx - 3.0 * yy),
        xy * z,
        y * (3.0 * xx - yy),
        z * diff,
        x * five,
        y * five,
        z * (5.0 * zz - 3.0),
    ]


def project(rows, cam, live):
    mx, my, mz = rows[0], rows[1], rows[2]
    cam_x = cam[0] * mx + cam[1] * my + cam[2] * mz + cam[9]
    cam_y = cam[3] * mx + cam[4] * my + cam[5] * mz + cam[10]
    cam_z = cam[6] * mx + cam[7] * my + cam[8] * mz + cam[11]
    cam_z = jnp.where(live, cam_z, 1.0)
    inv_z = 1.0 / cam_z
    qw, qx, qy, qz = rows[6], rows[7], rows[8], rows[9]
    qw = jnp.where(live, qw, 1.0)
    inv_q = lax.rsqrt(qw * qw + qx * qx + qy * qy + qz * qz)
    qw, qx, qy, qz = qw * inv_q, qx * inv_q, qy * inv_q, qz * inv_q
    rot = [
        [
            1.0 - 2.0 * (qy * qy + qz * qz),
            2.0 * (qx * qy - qw * qz),
            2.0 * (qx * qz + qw * qy),
        ],
        [
            2.0 * (qx * qy + qw * qz),
            1.0 - 2.0 * (qx * qx + qz * qz),
            2.0 * (qy * qz - qw * qx),
        ],
        [
            2.0 * (qx * qz - qw * qy),
            2.0 * (qy * qz + qw * qx),
            1.0 - 2.0 * (qx * qx + qy * qy),
        ],
    ]
    mixed = [
        [
            cam[3 * i] * rot[0][k] + cam[3 * i + 1] * rot[1][k] + cam[3 * i + 2] * rot[2][k]
            for k in range(3)
        ]
        for i in range(3)
    ]
    scale = cam[12] * inv_z
    ray_x, ray_y = cam_x * inv_z, cam_y * inv_z
    proj_u = [scale * (mixed[0][k] - ray_x * mixed[2][k]) for k in range(3)]
    proj_v = [scale * (mixed[1][k] - ray_y * mixed[2][k]) for k in range(3)]
    var = [jnp.exp(2.0 * rows[3 + k]) for k in range(3)]
    uv = [proj_u[k] * var[k] for k in range(3)]
    cov_a = sum(uv[k] * proj_u[k] for k in range(3)) + 0.3
    cov_b = sum(uv[k] * proj_v[k] for k in range(3))
    cov_c = sum(proj_v[k] * proj_v[k] * var[k] for k in range(3)) + 0.3
    inv_det = 1.0 / (cov_a * cov_c - cov_b * cov_b)
    inv_dist = lax.rsqrt(cam_x * cam_x + cam_y * cam_y + cam_z * cam_z)
    terms = sh_terms(cam_x * inv_dist, cam_y * inv_dist, cam_z * inv_dist)
    geometry = [cam_x * scale, cam_y * scale, cov_c * inv_det, -cov_b * inv_det, cov_a * inv_det]
    return geometry + terms, (ray_x, ray_y)


def iota(shape, dim):
    return lax.broadcasted_iota(jnp.int32, shape, dim)


def one_hot(mask):
    return jnp.where(mask, 1.0, 0.0).astype(BF16)


def dot(lhs, rhs, lhs_dim=1, rhs_dim=0):
    return lax.dot_general(
        lhs, rhs, (((lhs_dim,), (rhs_dim,)), ((), ())), preferred_element_type=F32
    )


def split(x, parts):
    out = []
    for _ in range(parts):
        head = x.astype(BF16)
        out.append(head)
        x = x - head.astype(F32)
    return out


def ranks(mask, tiles):
    rows, length = mask.shape
    bits = one_hot(mask)
    earlier = one_hot(iota((length, length), 0) < iota((length, length), 1))
    within = dot(bits, earlier)
    count = dot(bits, jnp.ones((length, length), BF16)).astype(BF16)
    here, there = iota((rows, rows), 0), iota((rows, rows), 1)
    above = one_hot((there < here) & (there >= here - lax.rem(here, tiles)))
    return (within + dot(above, count)).astype(jnp.int32)


def find(ids, base, tiles, cap, g_dev):
    local = ids - base
    mine = (local >= 0) & (local < g_dev)
    key = jnp.where(mine, ranks(mine, tiles), -1)
    rows, length = ids.shape
    slot = iota((cap, length), 0)
    found = []
    for r in range(0, rows, tiles):
        total = jnp.zeros((cap, length), jnp.int32)
        for t in range(r, r + tiles):
            total = total + jnp.where(key[t : t + 1, :] == slot, local[t : t + 1, :], 0)
        found.append(jnp.sum(total, axis=1, keepdims=True))
    return jnp.concatenate(found, axis=0)


def pick_kernel(tiles, cap, lists_ref, params_ref, picked_ref):
    width, g_dev = params_ref.shape
    where = find(lists_ref[...], lax.axis_index("gauss") * g_dev, tiles, cap, g_dev)
    hot = one_hot(where == iota((where.shape[0], g_dev), 1))
    wide = jnp.concatenate([params_ref[...], jnp.zeros((LANES - width, g_dev), BF16)], axis=0)
    picked_ref[...] = dot(hot, wide, 1, 1).astype(BF16)


def pick_pair_kernel(cap, peers, *refs):
    lists_refs, refs = refs[:peers], refs[peers:]
    own_ref, other_ref = refs[:2]
    picked_refs, refs = refs[2 : 2 + peers], refs[2 + peers :]
    lists_scratch, picked_scratch = refs
    tiles, length = lists_refs[0].shape
    width, g_dev = own_ref.shape
    me = lax.axis_index("gauss")
    first = me % 2 == 0
    for k in range(peers):
        lists_scratch[(me // 2) ^ k] = lists_refs[peers - 1 - k][...]
    ids = lists_scratch[...].reshape(peers * tiles, length)
    where_own = find(ids, me * g_dev, tiles, cap, g_dev)
    where_other = find(ids, (me ^ 1) * g_dev, tiles, cap, g_dev)
    own, other = own_ref[...], other_ref[...]
    blank = jnp.zeros((width, g_dev), BF16)
    lanes = iota((peers * cap, g_dev), 1)
    picked = dot(
        one_hot(where_own == lanes),
        jnp.concatenate([jnp.where(first, own, blank), jnp.where(first, blank, own)], axis=0),
        1,
        1,
    ) + dot(
        one_hot(where_other == lanes),
        jnp.concatenate([jnp.where(first, blank, other), jnp.where(first, other, blank)], axis=0),
        1,
        1,
    )
    picked_scratch[...] = picked.astype(BF16).reshape(peers, cap, 2 * width)
    for k in range(peers):
        picked_refs[peers - 1 - k][...] = picked_scratch[(me // 2) ^ k]


def by_tile(values, row):
    out = jnp.full(row.shape, values[-1])
    for t in range(len(values) - 1):
        out = jnp.where(row == t, values[t], out)
    return out


def prepare_kernel(
    owners,
    cap,
    g_dev,
    tile_pos_ref,
    cam_index_ref,
    cams_ref,
    lists_ref,
    params_ref,
    hot_ref,
    local_ref,
    copy_ref,
    cam_ref,
    pixel_ref,
):
    tiles, length = lists_ref.shape
    share = LANES // tiles
    depth = SIDE * SIDE // share
    cam_ids = [cam_index_ref[t] for t in range(tiles)]
    tile_row = iota((tiles, length), 0)
    for j in range(cams_ref.shape[0]):
        cam_ref[j] = by_tile([cams_ref[j, cam_ids[t]] for t in range(tiles)], tile_row)
    pos = [tile_pos_ref[t] for t in range(tiles)]
    lane = iota((depth, LANES), 1)
    origin_x = [(SIDE * (lax.rem(p, WIN) - WIN // 2)).astype(F32) + 0.5 for p in pos]
    pixel_ref[0] = by_tile(origin_x, lane // share) + (lane % SIDE).astype(F32)
    origin_y = [(SIDE * (lax.div(p, WIN) - WIN // 2)).astype(F32) + 0.5 for p in pos]
    pixel_row = iota((depth, LANES), 0) * (share // SIDE) + (lane % share) // SIDE
    pixel_ref[1] = by_tile(origin_y, lane // share) + pixel_row.astype(F32)

    slots = owners * cap
    ids = lists_ref[...]
    masks = [(ids >= o * g_dev) & (ids < (o + 1) * g_dev) for o in range(owners)]
    rank = ranks(jnp.concatenate([m.astype(jnp.int32) for m in masks], axis=0) > 0, tiles)
    place = jnp.full((tiles, length), -1, jnp.int32)
    local = jnp.zeros((tiles, length), jnp.int32)
    for o in range(owners):
        place = jnp.where(masks[o], rank[o * tiles : (o + 1) * tiles] + o * cap, place)
        local = jnp.where(masks[o], ids - o * g_dev, local)
    slot_iota = iota((slots, length), 0)
    hot_ref[...] = jnp.concatenate(
        [one_hot(slot_iota == place[t : t + 1, :]) for t in range(tiles)], axis=1
    )
    local_ref[...] = local.astype(F32)
    copy_ref[...] = params_ref[...]


def render_kernel(pieces, width, *refs):
    recv_refs, refs = refs[:pieces], refs[pieces:]
    lists_ref, hot_ref, local_ref, cam_ref, pixel_ref, targets_ref = refs[:6]
    pictures_ref, send_ref, rows_ref, table_ref, alpha_ref, weight_ref, part_ref = refs[6:13]
    tiles, length = lists_ref.shape
    share = LANES // tiles
    depth = SIDE * SIDE // share
    live = lists_ref[...] >= 0
    hot = hot_ref[...]

    if pieces == 1:
        listed = dot(recv_refs[0][...].reshape(-1, LANES), hot, 0, 0)[:width]
    else:
        (recv_scratch,) = refs[13:]
        cap = recv_refs[0].shape[0]
        place = lax.axis_index("gauss") // 2
        for k in range(pieces):
            recv_scratch[place ^ k] = recv_refs[pieces - 1 - k][...]
        received = recv_scratch[...].reshape(pieces * cap, 2 * width)
        halves = [
            jnp.concatenate(
                [hot[(2 * p + j) * cap : (2 * p + j + 1) * cap] for p in range(pieces)], axis=0
            )
            for j in range(2)
        ]
        listed = dot(received, halves[0], 0, 0)[:width] + dot(received, halves[1], 0, 0)[width:]
    for t in range(tiles):
        rows_ref[t * width : (t + 1) * width, :] = listed[:, t * length : (t + 1) * length]
    rows = [rows_ref[pl.ds(f, tiles, stride=width), :] for f in range(width)]

    cam = [cam_ref[j] for j in range(cam_ref.shape[0])]
    outs, pullback, rays = jax.vjp(lambda r: project(r, cam, live), rows[:10], has_aux=True)
    terms = outs[5:]
    colors = []
    for k in range(3):
        base = 11 + 16 * k
        shade = 0.5 + rows[base]
        for b in range(15):
            shade = shade + rows[base + 1 + b] * terms[b]
        for j in range(5):
            shade = shade + rows[59 + j] * cam[13 + 3 * j + k]
        colors.append(shade)
    opacity = jax.nn.sigmoid(rows[10])
    con_a, con_b, con_c = outs[2], outs[3], outs[4]

    attrs = [
        outs[0],
        outs[1],
        (-0.5 * LOG2E) * con_a,
        -LOG2E * con_b,
        (-0.5 * LOG2E) * con_c,
        jnp.where(live, opacity, 0.0),
    ] + colors
    count = len(attrs)
    blocks = []
    for value in attrs:
        parts = [p.astype(F32) for p in split(value, 3)]
        parts.append(jnp.zeros((16 - 3 * tiles, length), F32))
        blocks.append(jnp.concatenate(parts, axis=0))
    stacked = jnp.concatenate(blocks, axis=1)
    lane_tile = iota((16, LANES), 1) // share
    row_index = iota((16, LANES), 0)
    spread = one_hot((row_index % tiles == lane_tile) & (row_index < 3 * tiles))
    table = dot(stacked.T.astype(BF16), spread)
    pixel_x, pixel_y = pixel_ref[0, :1, :], pixel_ref[1]
    dx = pixel_x - table[:length]
    table_ref[0:length, :] = table[2 * length : 3 * length] * dx * dx
    table_ref[length : 2 * length, :] = table[3 * length : 4 * length] * dx
    table_ref[2 * length : 3 * length, :] = table[length : 2 * length]
    table_ref[3 * length :, :] = table[4 * length :]

    def row(index, l):
        return table_ref[pl.ds(index * length + l, 1), :]

    group = 16
    zero = jnp.zeros((depth, LANES), F32)

    def forward(chunk, carry):
        through, red, green, blue = carry
        for i in range(group):
            l = chunk * group + i
            dy = pixel_y - row(2, l)
            power = row(0, l) + dy * (row(1, l) + row(3, l) * dy)
            alpha = row(4, l) * jnp.exp2(power)
            weight = through * alpha
            red = red + weight * row(5, l)
            green = green + weight * row(6, l)
            blue = blue + weight * row(7, l)
            through = through - weight
            at = pl.ds(pl.multiple_of(l * depth, depth), depth)
            alpha_ref[at, :] = alpha
            weight_ref[at, :] = weight
        return through, red, green, blue

    start = (jnp.ones((depth, LANES), F32), zero, zero, zero)
    _, red, green, blue = lax.fori_loop(0, length // group, forward, start)
    pictures_ref[0] = red
    pictures_ref[1] = green
    pictures_ref[2] = blue
    res = [red - targets_ref[0], green - targets_ref[1], blue - targets_ref[2]]

    def backward(step, behind):
        chunk = length // group - 1 - step
        for i in reversed(range(group)):
            l = chunk * group + i
            at = pl.ds(pl.multiple_of(l * depth, depth), depth)
            alpha = alpha_ref[at, :]
            weight = weight_ref[at, :]
            dy = pixel_y - row(2, l)
            seen = row(5, l) * res[0] + row(6, l) * res[1] + row(7, l) * res[2]
            gap = seen - behind
            behind = behind + alpha * gap
            g = weight * gap
            gy = g * dy
            part_ref[0, at, :] = g
            part_ref[1, at, :] = gy
            part_ref[2, at, :] = gy * dy
            for k in range(3):
                part_ref[3 + k, at, :] = weight * res[k]
        return behind

    lax.fori_loop(0, length // group, backward, zero)

    def down(index):
        blocks = []
        for first in range(0, length, 8):
            parts = [
                part_ref[index, pl.ds(first * depth + s, 8, stride=depth), :] for s in range(depth)
            ]
            while len(parts) > 1:
                parts = [a + b for a, b in zip(parts[::2], parts[1::2])]
            blocks.append(parts[0])
        return jnp.concatenate(blocks, axis=0)

    sums = [down(index) for index in range(6)]
    g_x = sums[0] * dx
    sums = sums + [g_x, g_x * dx, sums[1] * dx]
    wide = jnp.concatenate([jnp.concatenate(split(s, 3), axis=1) for s in sums], axis=0)
    gather = one_hot(iota((8, 3 * LANES), 0) == (iota((8, 3 * LANES), 1) % LANES) // share)
    reduced = dot(gather, wide, 1, 1)
    g_0, g_y, g_yy, s_0, s_1, s_2, g_x, g_xx, g_xy = [
        reduced[:tiles, q * length : (q + 1) * length] for q in range(len(sums))
    ]

    d_colors = [s_0, s_1, s_2]
    d_terms = []
    for b in range(15):
        d_terms.append(sum(d_colors[k] * rows[12 + 16 * k + b] for k in range(3)))
    d_geometry = [
        con_a * g_x + con_b * g_y,
        con_b * g_x + con_c * g_y,
        -0.5 * g_xx,
        -g_xy,
        -0.5 * g_yy,
    ]
    (d_rows,) = pullback(d_geometry + d_terms)
    values = list(d_rows)
    values.append(g_0 * (1.0 - opacity))
    values.extend(d_colors)
    values.extend(rays)
    for j in range(5):
        values.append(sum(d_colors[k] * cam[13 + 3 * j + k] for k in range(3)))
    values.append(local_ref[...])
    values.extend([jnp.zeros((tiles, length), F32)] * (SENT - len(values)))
    for v in range(SENT):
        rows_ref[pl.ds(v, tiles, stride=width), :] = values[v]
    by_slot = jnp.concatenate(
        [
            jnp.concatenate(split(rows_ref[t * width : t * width + SENT, :], 3), axis=0)
            for t in range(tiles)
        ],
        axis=1,
    )
    by_slot = dot(by_slot, hot, 1, 1)
    by_slot = by_slot[:SENT] + by_slot[SENT : 2 * SENT] + by_slot[2 * SENT :]
    owners, copies, high, _ = send_ref.shape
    cap = hot.shape[0] // owners
    for o in range(owners):
        block = jnp.concatenate(
            [by_slot[r : r + high, o * cap : (o + 1) * cap] for r in range(0, SENT, high)], axis=1
        )
        for c in range(copies):
            send_ref[o, c] = block


def scatter_kernel(cap, recv_ref, out_ref):
    blocks, high, lanes = recv_ref.shape
    g_dev = out_ref.shape[1]
    values = jnp.concatenate(
        [
            jnp.concatenate(
                [recv_ref[b, :, first : first + cap] for b in range(blocks)], axis=1
            )
            for first in range(0, SENT * cap // high, cap)
        ],
        axis=0,
    )
    ray_x, ray_y = values[14:15], values[15:16]
    dir_z = lax.rsqrt(ray_x * ray_x + ray_y * ray_y + 1.0)
    terms = sh_terms(ray_x * dir_z, ray_y * dir_z, dir_z)
    terms = jnp.concatenate([jnp.ones_like(dir_z)] + terms, axis=0)
    rows = [values] + [terms * values[11 + k : 12 + k] for k in range(3)]
    hot = one_hot(iota((g_dev, blocks * cap), 0) == values[21:22].astype(jnp.int32))
    parts = split(jnp.concatenate(rows, axis=0), 2)
    total = dot(jnp.concatenate(parts, axis=0), hot, 1, 1)
    count = total.shape[0] // 2
    total = total[:count] + total[count:]
    out_ref[:11, :] = total[:11]
    out_ref[11:59, :] = total[SENT:]
    out_ref[59:, :] = total[16:21]


def call(kernel, out_shape, args, scalars=0, scratch=()):
    in_specs = [pl.BlockSpec(memory_space=pltpu.SMEM)] * scalars
    in_specs += [pl.BlockSpec(memory_space=pltpu.VMEM)] * (len(args) - scalars)
    many = isinstance(out_shape, (list, tuple))
    spec = pl.BlockSpec(memory_space=pltpu.VMEM)
    return pl.pallas_call(
        kernel,
        out_shape=out_shape,
        in_specs=in_specs,
        out_specs=[spec] * len(out_shape) if many else spec,
        scratch_shapes=list(scratch),
        compiler_params=pltpu.CompilerParams(vmem_limit_bytes=VMEM_LIMIT),
    )(*args)


def swap(x, axis, k):
    return lax.ppermute(x, axis, [(i, i ^ k) for i in range(lax.axis_size(axis))])


def far_first(blocks):
    last = len(blocks) - 1
    return [swap(b, "gauss", 2 * (last - i)) if i < last else b for i, b in enumerate(blocks)]


def exchange(x):
    return lax.all_to_all(x, "gauss", split_axis=0, concat_axis=0, tiled=True)


def exchange_wide(x):
    owners, views = lax.axis_size("gauss"), lax.axis_size("view")
    blocks = x.reshape(owners * views // 2, *x.shape[2:])
    groups = [[i for i in range(owners * views) if i % 2 == c] for c in range(2)]
    return lax.all_to_all(
        blocks,
        ("gauss", "view"),
        split_axis=0,
        concat_axis=0,
        axis_index_groups=groups,
        tiled=True,
    )


def power_of_two(n):
    return n & (n - 1) == 0


def shape(dims, dtype):
    return jax.ShapeDtypeStruct(dims, dtype)


def on_device(params, lists, tile_pos, cam_index, cams, targets):
    owners = lax.axis_size("gauss")
    views = lax.axis_size("view")
    width, g_dev = params.shape
    tiles, length = lists.shape
    cap = max(tiles * length // owners, 16)
    slots = owners * cap
    share = LANES // tiles
    depth = SIDE * SIDE // share
    paired = 2 <= owners <= 16 and power_of_two(owners) and LANES == 2 * width
    peers = owners // 2 if paired else 1
    wide = views % 2 == 0 and owners * views <= 32

    if paired:
        other = swap(params, "gauss", 1)
        all_lists = far_first([lists] * peers)
    hot, local, params_copy, cam, pixel = call(
        functools.partial(prepare_kernel, owners, cap, g_dev),
        [
            shape((slots, tiles * length), BF16),
            shape((tiles, length), F32),
            shape((width, g_dev), BF16),
            shape((cams.shape[0], tiles, length), F32),
            shape((2, depth, LANES), F32),
        ],
        (tile_pos, cam_index, cams, lists, params),
        scalars=3,
    )
    if paired:
        picked = call(
            functools.partial(pick_pair_kernel, cap, peers),
            [shape((cap, 2 * width), BF16)] * peers,
            (*all_lists, params_copy, other),
            scratch=(
                pltpu.VMEM((peers, tiles, length), jnp.int32),
                pltpu.VMEM((peers, cap, 2 * width), BF16),
            ),
        )
        returned = far_first(picked)
    else:
        all_lists = exchange(jnp.broadcast_to(lists[None], (owners, tiles, length)))
        picked = call(
            functools.partial(pick_kernel, tiles, cap),
            shape((slots, LANES), BF16),
            (all_lists.reshape(owners * tiles, length), params_copy),
        )
        returned = [exchange(picked.reshape(owners, cap, LANES))]
    spread_targets = (
        targets.reshape(3, tiles, depth, share).transpose(0, 2, 1, 3).reshape(3, depth, LANES)
    )
    copies = views // 2 if wide else 1
    high = SENT * cap // LANES
    pictures, sent = call(
        functools.partial(render_kernel, peers, width),
        [shape((3, depth, LANES), F32), shape((owners, copies, high, LANES), F32)],
        (*returned, lists, hot, local, cam, pixel, spread_targets),
        scratch=(
            pltpu.VMEM((tiles * width, length), F32),
            pltpu.VMEM((8 * length, LANES), F32),
            pltpu.VMEM((length * depth, LANES), F32),
            pltpu.VMEM((length * depth, LANES), F32),
            pltpu.VMEM((6, length * depth, LANES), F32),
            pltpu.VMEM((peers, *returned[0].shape[-2:]), BF16),
        ),
    )
    pictures = (
        pictures.reshape(3, depth, tiles, share)
        .transpose(0, 2, 1, 3)
        .reshape(3, tiles, SIDE * SIDE)
    )
    received = exchange_wide(sent) if wide else exchange(sent[:, 0])
    grads = call(
        functools.partial(scatter_kernel, cap),
        shape((width, g_dev), F32),
        (received,),
    )
    if wide:
        grads = grads + swap(grads, "view", 1)
    else:
        grads = lax.psum(grads, "view")
    return (pictures, grads)


def solution(mesh):
    return jax.shard_map(
        on_device,
        mesh=mesh,
        in_specs=(
            P(None, "gauss"),
            P(("gauss", "view"), None),
            P(("gauss", "view")),
            P(("gauss", "view")),
            P(),
            P(None, ("gauss", "view"), None),
        ),
        out_specs=(P(None, ("gauss", "view"), None), P(None, "gauss")),
        check_vma=False,
    )
```

```python
import functools
import math

import jax
import jax.numpy as jnp
from jax import lax
from jax.experimental import pallas as pl
from jax.experimental.pallas import tpu as pltpu
from jax.sharding import PartitionSpec as P

WIN = 16
SIDE = 16
LANES = 128
LOG2E = math.log2(math.e)
F32 = jnp.float32
BF16 = jnp.bfloat16
VMEM_LIMIT = 24 * 2**20
SENT = 32


def sh_terms(x, y, z):
    xx, yy, zz = x * x, y * y, z * z
    xy = x * y
    diff = xx - yy
    five = 5.0 * zz - 1.0
    return [
        x,
        y,
        z,
        xy,
        y * z,
        x * z,
        diff,
        3.0 * zz - 1.0,
        x * (xx - 3.0 * yy),
        xy * z,
        y * (3.0 * xx - yy),
        z * diff,
        x * five,
        y * five,
        z * (5.0 * zz - 3.0),
    ]


def project(rows, cam, live):
    mx, my, mz = rows[0], rows[1], rows[2]
    cam_x = cam[0] * mx + cam[1] * my + cam[2] * mz + cam[9]
    cam_y = cam[3] * mx + cam[4] * my + cam[5] * mz + cam[10]
    cam_z = cam[6] * mx + cam[7] * my + cam[8] * mz + cam[11]
    cam_z = jnp.where(live, cam_z, 1.0)
    inv_z = 1.0 / cam_z
    qw, qx, qy, qz = rows[6], rows[7], rows[8], rows[9]
    qw = jnp.where(live, qw, 1.0)
    inv_q = lax.rsqrt(qw * qw + qx * qx + qy * qy + qz * qz)
    qw, qx, qy, qz = qw * inv_q, qx * inv_q, qy * inv_q, qz * inv_q
    rot = [
        [
            1.0 - 2.0 * (qy * qy + qz * qz),
            2.0 * (qx * qy - qw * qz),
            2.0 * (qx * qz + qw * qy),
        ],
        [
            2.0 * (qx * qy + qw * qz),
            1.0 - 2.0 * (qx * qx + qz * qz),
            2.0 * (qy * qz - qw * qx),
        ],
        [
            2.0 * (qx * qz - qw * qy),
            2.0 * (qy * qz + qw * qx),
            1.0 - 2.0 * (qx * qx + qy * qy),
        ],
    ]
    mixed = [
        [
            cam[3 * i] * rot[0][k] + cam[3 * i + 1] * rot[1][k] + cam[3 * i + 2] * rot[2][k]
            for k in range(3)
        ]
        for i in range(3)
    ]
    scale = cam[12] * inv_z
    ray_x, ray_y = cam_x * inv_z, cam_y * inv_z
    proj_u = [scale * (mixed[0][k] - ray_x * mixed[2][k]) for k in range(3)]
    proj_v = [scale * (mixed[1][k] - ray_y * mixed[2][k]) for k in range(3)]
    var = [jnp.exp(2.0 * rows[3 + k]) for k in range(3)]
    uv = [proj_u[k] * var[k] for k in range(3)]
    cov_a = sum(uv[k] * proj_u[k] for k in range(3)) + 0.3
    cov_b = sum(uv[k] * proj_v[k] for k in range(3))
    cov_c = sum(proj_v[k] * proj_v[k] * var[k] for k in range(3)) + 0.3
    inv_det = 1.0 / (cov_a * cov_c - cov_b * cov_b)
    inv_dist = lax.rsqrt(cam_x * cam_x + cam_y * cam_y + cam_z * cam_z)
    terms = sh_terms(cam_x * inv_dist, cam_y * inv_dist, cam_z * inv_dist)
    geometry = [cam_x * scale, cam_y * scale, cov_c * inv_det, -cov_b * inv_det, cov_a * inv_det]
    return geometry + terms, (ray_x, ray_y)


def iota(shape, dim):
    return lax.broadcasted_iota(jnp.int32, shape, dim)


def one_hot(mask):
    return jnp.where(mask, 1.0, 0.0).astype(BF16)


def dot(lhs, rhs, lhs_dim=1, rhs_dim=0):
    return lax.dot_general(
        lhs, rhs, (((lhs_dim,), (rhs_dim,)), ((), ())), preferred_element_type=F32
    )


def split(x, parts):
    out = []
    for _ in range(parts):
        head = x.astype(BF16)
        out.append(head)
        x = x - head.astype(F32)
    return out


def ranks(mask, tiles):
    rows, length = mask.shape
    bits = one_hot(mask)
    earlier = one_hot(iota((length, length), 0) < iota((length, length), 1))
    within = dot(bits, earlier)
    count = dot(bits, jnp.ones((length, length), BF16)).astype(BF16)
    here, there = iota((rows, rows), 0), iota((rows, rows), 1)
    above = one_hot((there < here) & (there >= here - lax.rem(here, tiles)))
    return (within + dot(above, count)).astype(jnp.int32)


def find(ids, base, tiles, cap, g_dev):
    local = ids - base
    mine = (local >= 0) & (local < g_dev)
    key = jnp.where(mine, ranks(mine, tiles), -1)
    rows, length = ids.shape
    slot = iota((cap, length), 0)
    found = []
    for r in range(0, rows, tiles):
        total = jnp.zeros((cap, length), jnp.int32)
        for t in range(r, r + tiles):
            total = total + jnp.where(key[t : t + 1, :] == slot, local[t : t + 1, :], 0)
        found.append(jnp.sum(total, axis=1, keepdims=True))
    return jnp.concatenate(found, axis=0)


def pick_kernel(tiles, cap, lists_ref, params_ref, picked_ref):
    width, g_dev = params_ref.shape
    where = find(lists_ref[...], lax.axis_index("gauss") * g_dev, tiles, cap, g_dev)
    hot = one_hot(where == iota((where.shape[0], g_dev), 1))
    wide = jnp.concatenate([params_ref[...], jnp.zeros((LANES - width, g_dev), BF16)], axis=0)
    picked_ref[...] = dot(hot, wide, 1, 1).astype(BF16)


def pick_pair_kernel(cap, peers, *refs):
    lists_refs, refs = refs[:peers], refs[peers:]
    own_ref, other_ref = refs[:2]
    picked_refs, refs = refs[2 : 2 + peers], refs[2 + peers :]
    lists_scratch, picked_scratch = refs
    tiles, length = lists_refs[0].shape
    g_dev = own_ref.shape[1]
    me = lax.axis_index("gauss")
    first = me % 2 == 0
    for k in range(peers):
        lists_scratch[(me // 2) ^ k] = lists_refs[peers - 1 - k][...]
    ids = lists_scratch[...].reshape(peers * tiles, length)
    where_own = find(ids, me * g_dev, tiles, cap, g_dev)
    where_other = find(ids, (me ^ 1) * g_dev, tiles, cap, g_dev)
    lanes = iota((peers * cap, g_dev), 1)
    of_own = dot(own_ref[...], one_hot(where_own == lanes), 1, 1)
    of_other = dot(other_ref[...], one_hot(where_other == lanes), 1, 1)
    of_even = jnp.where(first, of_own, of_other)
    of_odd = jnp.where(first, of_other, of_own)
    for p in range(peers):
        block = slice(p * cap, (p + 1) * cap)
        picked_scratch[p] = jnp.concatenate(
            [of_even[:, block], of_odd[:, block]], axis=1
        ).astype(BF16)
    for k in range(peers):
        picked_refs[peers - 1 - k][...] = picked_scratch[(me // 2) ^ k]


def by_tile(values, row):
    out = jnp.full(row.shape, values[-1])
    for t in range(len(values) - 1):
        out = jnp.where(row == t, values[t], out)
    return out


def prepare_kernel(
    owners,
    cap,
    g_dev,
    tile_pos_ref,
    cam_index_ref,
    cams_ref,
    lists_ref,
    params_ref,
    hot_ref,
    local_ref,
    copy_ref,
    cam_ref,
    pixel_ref,
):
    tiles, length = lists_ref.shape
    share = LANES // tiles
    depth = SIDE * SIDE // share
    cam_ids = [cam_index_ref[t] for t in range(tiles)]
    tile_row = iota((tiles, length), 0)
    for j in range(cams_ref.shape[0]):
        cam_ref[j] = by_tile([cams_ref[j, cam_ids[t]] for t in range(tiles)], tile_row)
    pos = [tile_pos_ref[t] for t in range(tiles)]
    lane = iota((depth, LANES), 1)
    origin_x = [(SIDE * (lax.rem(p, WIN) - WIN // 2)).astype(F32) + 0.5 for p in pos]
    pixel_ref[0] = by_tile(origin_x, lane // share) + (lane % SIDE).astype(F32)
    origin_y = [(SIDE * (lax.div(p, WIN) - WIN // 2)).astype(F32) + 0.5 for p in pos]
    pixel_row = iota((depth, LANES), 0) * (share // SIDE) + (lane % share) // SIDE
    pixel_ref[1] = by_tile(origin_y, lane // share) + pixel_row.astype(F32)

    slots = owners * cap
    ids = lists_ref[...]
    masks = [(ids >= o * g_dev) & (ids < (o + 1) * g_dev) for o in range(owners)]
    rank = ranks(jnp.concatenate([m.astype(jnp.int32) for m in masks], axis=0) > 0, tiles)
    place = jnp.full((tiles, length), -1, jnp.int32)
    local = jnp.zeros((tiles, length), jnp.int32)
    for o in range(owners):
        place = jnp.where(masks[o], rank[o * tiles : (o + 1) * tiles] + o * cap, place)
        local = jnp.where(masks[o], ids - o * g_dev, local)
    slot_iota = iota((slots, length), 0)
    hot_ref[...] = jnp.concatenate(
        [one_hot(slot_iota == place[t : t + 1, :]) for t in range(tiles)], axis=1
    )
    local_ref[...] = local.astype(F32)
    copy_ref[...] = params_ref[...]


def render_kernel(pieces, width, *refs):
    recv_refs, refs = refs[:pieces], refs[pieces:]
    lists_ref, hot_ref, local_ref, cam_ref, pixel_ref, targets_ref = refs[:6]
    pictures_ref, send_ref, rows_ref, table_ref, alpha_ref, weight_ref, part_ref = refs[6:13]
    tiles, length = lists_ref.shape
    share = LANES // tiles
    depth = SIDE * SIDE // share
    live = lists_ref[...] >= 0
    hot = hot_ref[...]

    if pieces == 1:
        listed = dot(recv_refs[0][...].reshape(-1, LANES), hot, 0, 0)[:width]
    else:
        (recv_scratch,) = refs[13:]
        place = lax.axis_index("gauss") // 2
        for k in range(pieces):
            recv_scratch[place ^ k] = recv_refs[pieces - 1 - k][...]
        received = jnp.concatenate([recv_scratch[p] for p in range(pieces)], axis=1)
        listed = dot(received, hot)
    for t in range(tiles):
        rows_ref[t * width : (t + 1) * width, :] = listed[:, t * length : (t + 1) * length]
    rows = [rows_ref[pl.ds(f, tiles, stride=width), :] for f in range(width)]

    cam = [cam_ref[j] for j in range(cam_ref.shape[0])]
    outs, pullback, rays = jax.vjp(lambda r: project(r, cam, live), rows[:10], has_aux=True)
    terms = outs[5:]
    colors = []
    for k in range(3):
        base = 11 + 16 * k
        shade = 0.5 + rows[base]
        for b in range(15):
            shade = shade + rows[base + 1 + b] * terms[b]
        for j in range(5):
            shade = shade + rows[59 + j] * cam[13 + 3 * j + k]
        colors.append(shade)
    opacity = jax.nn.sigmoid(rows[10])
    con_a, con_b, con_c = outs[2], outs[3], outs[4]

    attrs = [
        outs[0],
        outs[1],
        (-0.5 * LOG2E) * con_a,
        -LOG2E * con_b,
        (-0.5 * LOG2E) * con_c,
        jnp.where(live, opacity, 0.0),
    ] + colors
    count = len(attrs)
    blocks = []
    for value in attrs:
        parts = [p.astype(F32) for p in split(value, 3)]
        parts.append(jnp.zeros((16 - 3 * tiles, length), F32))
        blocks.append(jnp.concatenate(parts, axis=0))
    stacked = jnp.concatenate(blocks, axis=1)
    lane_tile = iota((16, LANES), 1) // share
    row_index = iota((16, LANES), 0)
    spread = one_hot((row_index % tiles == lane_tile) & (row_index < 3 * tiles))
    table = dot(stacked.T.astype(BF16), spread)
    pixel_x, pixel_y = pixel_ref[0, :1, :], pixel_ref[1]
    dx = pixel_x - table[:length]
    table_ref[0:length, :] = table[2 * length : 3 * length] * dx * dx
    table_ref[length : 2 * length, :] = table[3 * length : 4 * length] * dx
    table_ref[2 * length : 3 * length, :] = table[length : 2 * length]
    table_ref[3 * length :, :] = table[4 * length :]

    def row(index, l):
        return table_ref[pl.ds(index * length + l, 1), :]

    group = 16
    zero = jnp.zeros((depth, LANES), F32)

    def forward(chunk, carry):
        through, red, green, blue = carry
        for i in range(group):
            l = chunk * group + i
            dy = pixel_y - row(2, l)
            power = row(0, l) + dy * (row(1, l) + row(3, l) * dy)
            alpha = row(4, l) * jnp.exp2(power)
            weight = through * alpha
            red = red + weight * row(5, l)
            green = green + weight * row(6, l)
            blue = blue + weight * row(7, l)
            through = through - weight
            at = pl.ds(pl.multiple_of(l * depth, depth), depth)
            alpha_ref[at, :] = alpha
            weight_ref[at, :] = weight
        return through, red, green, blue

    start = (jnp.ones((depth, LANES), F32), zero, zero, zero)
    _, red, green, blue = lax.fori_loop(0, length // group, forward, start)
    pictures_ref[0] = red
    pictures_ref[1] = green
    pictures_ref[2] = blue
    res = [red - targets_ref[0], green - targets_ref[1], blue - targets_ref[2]]

    def backward(step, behind):
        chunk = length // group - 1 - step
        for i in reversed(range(group)):
            l = chunk * group + i
            at = pl.ds(pl.multiple_of(l * depth, depth), depth)
            alpha = alpha_ref[at, :]
            weight = weight_ref[at, :]
            dy = pixel_y - row(2, l)
            seen = row(5, l) * res[0] + row(6, l) * res[1] + row(7, l) * res[2]
            gap = seen - behind
            behind = behind + alpha * gap
            g = weight * gap
            gy = g * dy
            part_ref[0, at, :] = g
            part_ref[1, at, :] = gy
            part_ref[2, at, :] = gy * dy
            for k in range(3):
                part_ref[3 + k, at, :] = weight * res[k]
        return behind

    lax.fori_loop(0, length // group, backward, zero)

    def down(index):
        blocks = []
        for first in range(0, length, 8):
            parts = [
                part_ref[index, pl.ds(first * depth + s, 8, stride=depth), :] for s in range(depth)
            ]
            while len(parts) > 1:
                parts = [a + b for a, b in zip(parts[::2], parts[1::2])]
            blocks.append(parts[0])
        return jnp.concatenate(blocks, axis=0)

    sums = [down(index) for index in range(6)]
    g_x = sums[0] * dx
    sums = sums + [g_x, g_x * dx, sums[1] * dx]
    wide = jnp.concatenate([jnp.concatenate(split(s, 3), axis=1) for s in sums], axis=0)
    gather = one_hot(iota((8, 3 * LANES), 0) == (iota((8, 3 * LANES), 1) % LANES) // share)
    reduced = dot(gather, wide, 1, 1)
    g_0, g_y, g_yy, s_0, s_1, s_2, g_x, g_xx, g_xy = [
        reduced[:tiles, q * length : (q + 1) * length] for q in range(len(sums))
    ]

    d_colors = [s_0, s_1, s_2]
    d_terms = []
    for b in range(15):
        d_terms.append(sum(d_colors[k] * rows[12 + 16 * k + b] for k in range(3)))
    d_geometry = [
        con_a * g_x + con_b * g_y,
        con_b * g_x + con_c * g_y,
        -0.5 * g_xx,
        -g_xy,
        -0.5 * g_yy,
    ]
    (d_rows,) = pullback(d_geometry + d_terms)
    values = list(d_rows)
    values.append(g_0 * (1.0 - opacity))
    values.extend(d_colors)
    values.extend(rays)
    for j in range(5):
        values.append(sum(d_colors[k] * cam[13 + 3 * j + k] for k in range(3)))
    values.append(local_ref[...])
    values.extend([jnp.zeros((tiles, length), F32)] * (SENT - len(values)))
    for v in range(SENT):
        rows_ref[pl.ds(v, tiles, stride=width), :] = values[v]
    by_slot = jnp.concatenate(
        [
            jnp.concatenate(split(rows_ref[t * width : t * width + SENT, :], 3), axis=0)
            for t in range(tiles)
        ],
        axis=1,
    )
    by_slot = dot(by_slot, hot, 1, 1)
    by_slot = by_slot[:SENT] + by_slot[SENT : 2 * SENT] + by_slot[2 * SENT :]
    owners, copies, high, _ = send_ref.shape
    cap = hot.shape[0] // owners
    for o in range(owners):
        block = jnp.concatenate(
            [by_slot[r : r + high, o * cap : (o + 1) * cap] for r in range(0, SENT, high)], axis=1
        )
        for c in range(copies):
            send_ref[o, c] = block


def scatter(cap, recv_ref, g_dev):
    blocks, high, _ = recv_ref.shape
    values = jnp.concatenate(
        [
            jnp.concatenate(
                [recv_ref[b, :, first : first + cap] for b in range(blocks)], axis=1
            )
            for first in range(0, SENT * cap // high, cap)
        ],
        axis=0,
    )
    ray_x, ray_y = values[14:15], values[15:16]
    dir_z = lax.rsqrt(ray_x * ray_x + ray_y * ray_y + 1.0)
    terms = sh_terms(ray_x * dir_z, ray_y * dir_z, dir_z)
    terms = jnp.concatenate([jnp.ones_like(dir_z)] + terms, axis=0)
    rows = [values] + [terms * values[11 + k : 12 + k] for k in range(3)]
    hot = one_hot(iota((g_dev, blocks * cap), 0) == values[21:22].astype(jnp.int32))
    parts = split(jnp.concatenate(rows, axis=0), 2)
    total = dot(jnp.concatenate(parts, axis=0), hot, 1, 1)
    count = total.shape[0] // 2
    return total[:count] + total[count:]


def in_order(total, out_ref):
    out_ref[:11, :] = total[:11]
    out_ref[11:59, :] = total[SENT:]
    out_ref[59:, :] = total[16:21]


def scatter_kernel(cap, recv_ref, out_ref):
    in_order(scatter(cap, recv_ref, out_ref.shape[1]), out_ref)


def first_kernel(cap, recv_ref, out_ref):
    out_ref[...] = scatter(cap, recv_ref, out_ref.shape[1])


def last_kernel(cap, recv_ref, sum_ref, spread_ref, out_ref, pictures_ref):
    in_order(sum_ref[...] + scatter(cap, recv_ref, out_ref.shape[1]), out_ref)
    _, tiles, _ = pictures_ref.shape
    depth = spread_ref.shape[1]
    share = LANES // tiles
    for k in range(3):
        for t in range(tiles):
            pictures_ref[k, t : t + 1, :] = jnp.concatenate(
                [
                    spread_ref[k, s : s + 1, t * share : (t + 1) * share]
                    for s in range(depth)
                ],
                axis=1,
            )


def call(kernel, out_shape, args, scalars=0, scratch=()):
    in_specs = [pl.BlockSpec(memory_space=pltpu.SMEM)] * scalars
    in_specs += [pl.BlockSpec(memory_space=pltpu.VMEM)] * (len(args) - scalars)
    many = isinstance(out_shape, (list, tuple))
    spec = pl.BlockSpec(memory_space=pltpu.VMEM)
    return pl.pallas_call(
        kernel,
        out_shape=out_shape,
        in_specs=in_specs,
        out_specs=[spec] * len(out_shape) if many else spec,
        scratch_shapes=list(scratch),
        compiler_params=pltpu.CompilerParams(vmem_limit_bytes=VMEM_LIMIT),
    )(*args)


def swap(x, axis, k):
    return lax.ppermute(x, axis, [(i, i ^ k) for i in range(lax.axis_size(axis))])


def far_first(blocks):
    last = len(blocks) - 1
    return [swap(b, "gauss", 2 * (last - i)) if i < last else b for i, b in enumerate(blocks)]


def exchange(x):
    return lax.all_to_all(x, "gauss", split_axis=0, concat_axis=0, tiled=True)


def exchange_wide(x):
    owners, views = lax.axis_size("gauss"), lax.axis_size("view")
    blocks = x.reshape(owners * views // 2, *x.shape[2:])
    groups = [[i for i in range(owners * views) if i % 2 == c] for c in range(2)]
    return lax.all_to_all(
        blocks,
        ("gauss", "view"),
        split_axis=0,
        concat_axis=0,
        axis_index_groups=groups,
        tiled=True,
    )


def power_of_two(n):
    return n & (n - 1) == 0


def shape(dims, dtype):
    return jax.ShapeDtypeStruct(dims, dtype)


def on_device(params, lists, tile_pos, cam_index, cams, targets):
    owners = lax.axis_size("gauss")
    views = lax.axis_size("view")
    width, g_dev = params.shape
    tiles, length = lists.shape
    cap = max(tiles * length // owners, 16)
    slots = owners * cap
    share = LANES // tiles
    depth = SIDE * SIDE // share
    paired = 2 <= owners <= 16 and power_of_two(owners) and LANES == 2 * width
    peers = owners // 2 if paired else 1
    wide = views % 2 == 0 and owners * views <= 32

    if paired:
        other = swap(params, "gauss", 1)
        all_lists = far_first([lists] * peers)
    hot, local, params_copy, cam, pixel = call(
        functools.partial(prepare_kernel, owners, cap, g_dev),
        [
            shape((slots, tiles * length), BF16),
            shape((tiles, length), F32),
            shape((width, g_dev), BF16),
            shape((cams.shape[0], tiles, length), F32),
            shape((2, depth, LANES), F32),
        ],
        (tile_pos, cam_index, cams, lists, params),
        scalars=3,
    )
    if paired:
        picked = call(
            functools.partial(pick_pair_kernel, cap, peers),
            [shape((width, 2 * cap), BF16)] * peers,
            (*all_lists, params_copy, other),
            scratch=(
                pltpu.VMEM((peers, tiles, length), jnp.int32),
                pltpu.VMEM((peers, width, 2 * cap), BF16),
            ),
        )
        returned = far_first(picked)
    else:
        all_lists = exchange(jnp.broadcast_to(lists[None], (owners, tiles, length)))
        picked = call(
            functools.partial(pick_kernel, tiles, cap),
            shape((slots, LANES), BF16),
            (all_lists.reshape(owners * tiles, length), params_copy),
        )
        returned = [exchange(picked.reshape(owners, cap, LANES))]
    spread_targets = (
        targets.reshape(3, tiles, depth, share).transpose(0, 2, 1, 3).reshape(3, depth, LANES)
    )
    copies = views // 2 if wide else 1
    high = SENT * cap // LANES
    pictures, sent = call(
        functools.partial(render_kernel, peers, width),
        [shape((3, depth, LANES), F32), shape((owners, copies, high, LANES), F32)],
        (*returned, lists, hot, local, cam, pixel, spread_targets),
        scratch=(
            pltpu.VMEM((tiles * width, length), F32),
            pltpu.VMEM((8 * length, LANES), F32),
            pltpu.VMEM((length * depth, LANES), F32),
            pltpu.VMEM((length * depth, LANES), F32),
            pltpu.VMEM((6, length * depth, LANES), F32),
            pltpu.VMEM((peers, *returned[0].shape[-2:]), BF16),
        ),
    )
    if wide:
        received = exchange_wide(sent)
        other = swap(received, "view", 1)
        total = call(
            functools.partial(first_kernel, cap), shape((SENT + 48, g_dev), F32), (received,)
        )
        grads, pictures = call(
            functools.partial(last_kernel, cap),
            [shape((width, g_dev), F32), shape(targets.shape, F32)],
            (other, total, pictures),
        )
        return (pictures, grads)
    pictures = (
        pictures.reshape(3, depth, tiles, share)
        .transpose(0, 2, 1, 3)
        .reshape(3, tiles, SIDE * SIDE)
    )
    received = exchange(sent[:, 0])
    grads = call(
        functools.partial(scatter_kernel, cap), shape((width, g_dev), F32), (received,)
    )
    return (pictures, lax.psum(grads, "view"))


def solution(mesh):
    return jax.shard_map(
        on_device,
        mesh=mesh,
        in_specs=(
            P(None, "gauss"),
            P(("gauss", "view"), None),
            P(("gauss", "view")),
            P(("gauss", "view")),
            P(),
            P(None, ("gauss", "view"), None),
        ),
        out_specs=(P(None, ("gauss", "view"), None), P(None, "gauss")),
        check_vma=False,
    )
```

```python
import functools
import math

import jax
import jax.numpy as jnp
from jax import lax
from jax.experimental import pallas as pl
from jax.experimental.pallas import tpu as pltpu
from jax.sharding import PartitionSpec as P

WIN = 16
SIDE = 16
LANES = 128
LOG2E = math.log2(math.e)
F32 = jnp.float32
BF16 = jnp.bfloat16
VMEM_LIMIT = 24 * 2**20
SENT = 32


def sh_terms(x, y, z):
    xx, yy, zz = x * x, y * y, z * z
    xy = x * y
    diff = xx - yy
    five = 5.0 * zz - 1.0
    return [
        x,
        y,
        z,
        xy,
        y * z,
        x * z,
        diff,
        3.0 * zz - 1.0,
        x * (xx - 3.0 * yy),
        xy * z,
        y * (3.0 * xx - yy),
        z * diff,
        x * five,
        y * five,
        z * (5.0 * zz - 3.0),
    ]


def project(rows, cam, live):
    mx, my, mz = rows[0], rows[1], rows[2]
    cam_x = cam[0] * mx + cam[1] * my + cam[2] * mz + cam[9]
    cam_y = cam[3] * mx + cam[4] * my + cam[5] * mz + cam[10]
    cam_z = cam[6] * mx + cam[7] * my + cam[8] * mz + cam[11]
    cam_z = jnp.where(live, cam_z, 1.0)
    inv_z = 1.0 / cam_z
    qw, qx, qy, qz = rows[6], rows[7], rows[8], rows[9]
    qw = jnp.where(live, qw, 1.0)
    inv_q = lax.rsqrt(qw * qw + qx * qx + qy * qy + qz * qz)
    qw, qx, qy, qz = qw * inv_q, qx * inv_q, qy * inv_q, qz * inv_q
    rot = [
        [
            1.0 - 2.0 * (qy * qy + qz * qz),
            2.0 * (qx * qy - qw * qz),
            2.0 * (qx * qz + qw * qy),
        ],
        [
            2.0 * (qx * qy + qw * qz),
            1.0 - 2.0 * (qx * qx + qz * qz),
            2.0 * (qy * qz - qw * qx),
        ],
        [
            2.0 * (qx * qz - qw * qy),
            2.0 * (qy * qz + qw * qx),
            1.0 - 2.0 * (qx * qx + qy * qy),
        ],
    ]
    mixed = [
        [
            cam[3 * i] * rot[0][k] + cam[3 * i + 1] * rot[1][k] + cam[3 * i + 2] * rot[2][k]
            for k in range(3)
        ]
        for i in range(3)
    ]
    scale = cam[12] * inv_z
    ray_x, ray_y = cam_x * inv_z, cam_y * inv_z
    proj_u = [scale * (mixed[0][k] - ray_x * mixed[2][k]) for k in range(3)]
    proj_v = [scale * (mixed[1][k] - ray_y * mixed[2][k]) for k in range(3)]
    var = [jnp.exp(2.0 * rows[3 + k]) for k in range(3)]
    uv = [proj_u[k] * var[k] for k in range(3)]
    cov_a = sum(uv[k] * proj_u[k] for k in range(3)) + 0.3
    cov_b = sum(uv[k] * proj_v[k] for k in range(3))
    cov_c = sum(proj_v[k] * proj_v[k] * var[k] for k in range(3)) + 0.3
    inv_det = 1.0 / (cov_a * cov_c - cov_b * cov_b)
    inv_dist = lax.rsqrt(cam_x * cam_x + cam_y * cam_y + cam_z * cam_z)
    terms = sh_terms(cam_x * inv_dist, cam_y * inv_dist, cam_z * inv_dist)
    geometry = [cam_x * scale, cam_y * scale, cov_c * inv_det, -cov_b * inv_det, cov_a * inv_det]
    return geometry + terms, (ray_x, ray_y)


def iota(shape, dim):
    return lax.broadcasted_iota(jnp.int32, shape, dim)


def one_hot(mask):
    return jnp.where(mask, 1.0, 0.0).astype(BF16)


def dot(lhs, rhs, lhs_dim=1, rhs_dim=0):
    return lax.dot_general(
        lhs, rhs, (((lhs_dim,), (rhs_dim,)), ((), ())), preferred_element_type=F32
    )


def split(x, parts):
    out = []
    for _ in range(parts):
        head = x.astype(BF16)
        out.append(head)
        x = x - head.astype(F32)
    return out


def ranks(mask, tiles):
    rows, length = mask.shape
    bits = one_hot(mask)
    earlier = one_hot(iota((length, length), 0) < iota((length, length), 1))
    within = dot(bits, earlier)
    count = dot(bits, jnp.ones((length, length), BF16)).astype(BF16)
    here, there = iota((rows, rows), 0), iota((rows, rows), 1)
    above = one_hot((there < here) & (there >= here - lax.rem(here, tiles)))
    return (within + dot(above, count)).astype(jnp.int32)


def find(ids, base, tiles, cap, g_dev):
    local = ids - base
    mine = (local >= 0) & (local < g_dev)
    key = jnp.where(mine, ranks(mine, tiles), -1)
    rows, length = ids.shape
    slot = iota((cap, length), 0)
    found = []
    for r in range(0, rows, tiles):
        total = jnp.zeros((cap, length), jnp.int32)
        for t in range(r, r + tiles):
            total = total + jnp.where(key[t : t + 1, :] == slot, local[t : t + 1, :], 0)
        found.append(jnp.sum(total, axis=1, keepdims=True))
    return jnp.concatenate(found, axis=0)


def pick_kernel(tiles, cap, lists_ref, params_ref, picked_ref):
    width, g_dev = params_ref.shape
    where = find(lists_ref[...], lax.axis_index("gauss") * g_dev, tiles, cap, g_dev)
    hot = one_hot(where == iota((where.shape[0], g_dev), 1))
    wide = jnp.concatenate([params_ref[...], jnp.zeros((LANES - width, g_dev), BF16)], axis=0)
    picked_ref[...] = dot(hot, wide, 1, 1).astype(BF16)


def pick_pair_kernel(cap, peers, *refs):
    lists_refs, refs = refs[:peers], refs[peers:]
    own_ref, other_ref = refs[:2]
    picked_refs, refs = refs[2 : 2 + peers], refs[2 + peers :]
    lists_scratch, picked_scratch = refs
    tiles, length = lists_refs[0].shape
    g_dev = own_ref.shape[1]
    me = lax.axis_index("gauss")
    first = me % 2 == 0
    for k in range(peers):
        lists_scratch[(me // 2) ^ k] = lists_refs[k][...]
    ids = lists_scratch[...].reshape(peers * tiles, length)
    where_own = find(ids, me * g_dev, tiles, cap, g_dev)
    where_other = find(ids, (me ^ 1) * g_dev, tiles, cap, g_dev)
    lanes = iota((peers * cap, g_dev), 1)
    of_own = dot(own_ref[...], one_hot(where_own == lanes), 1, 1)
    of_other = dot(other_ref[...], one_hot(where_other == lanes), 1, 1)
    of_even = jnp.where(first, of_own, of_other)
    of_odd = jnp.where(first, of_other, of_own)
    for p in range(peers):
        block = slice(p * cap, (p + 1) * cap)
        picked_scratch[p] = jnp.concatenate(
            [of_even[:, block], of_odd[:, block]], axis=1
        ).astype(BF16)
    for k in range(peers):
        picked_refs[peers - 1 - k][...] = picked_scratch[(me // 2) ^ k]


def by_tile(values, row):
    out = jnp.full(row.shape, values[-1])
    for t in range(len(values) - 1):
        out = jnp.where(row == t, values[t], out)
    return out


def prepare_kernel(
    tile_pos_ref, cam_index_ref, cams_ref, params_ref, copy_ref, cam_ref, pixel_ref
):
    copy_ref[...] = params_ref[...]
    values, tiles, length = cam_ref.shape
    share = LANES // tiles
    depth = SIDE * SIDE // share
    cam_ids = [cam_index_ref[t] for t in range(tiles)]
    tile_row = iota((tiles, length), 0)
    for j in range(values):
        cam_ref[j] = by_tile([cams_ref[cam_ids[t], j] for t in range(tiles)], tile_row)
    pos = [tile_pos_ref[t] for t in range(tiles)]
    lane = iota((depth, LANES), 1)
    origin_x = [(SIDE * (lax.rem(p, WIN) - WIN // 2)).astype(F32) + 0.5 for p in pos]
    pixel_ref[0] = by_tile(origin_x, lane // share) + (lane % SIDE).astype(F32)
    origin_y = [(SIDE * (lax.div(p, WIN) - WIN // 2)).astype(F32) + 0.5 for p in pos]
    pixel_row = iota((depth, LANES), 0) * (share // SIDE) + (lane % share) // SIDE
    pixel_ref[1] = by_tile(origin_y, lane // share) + pixel_row.astype(F32)


def place_kernel(owners, cap, g_dev, lists_ref, after_ref, hot_ref, local_ref):
    tiles, length = lists_ref.shape
    slots = owners * cap
    ids = lists_ref[...]
    masks = [(ids >= o * g_dev) & (ids < (o + 1) * g_dev) for o in range(owners)]
    rank = ranks(jnp.concatenate([m.astype(jnp.int32) for m in masks], axis=0) > 0, tiles)
    place = jnp.full((tiles, length), -1, jnp.int32)
    local = jnp.zeros((tiles, length), jnp.int32)
    for o in range(owners):
        place = jnp.where(masks[o], rank[o * tiles : (o + 1) * tiles] + o * cap, place)
        local = jnp.where(masks[o], ids - o * g_dev, local)
    slot_iota = iota((slots, length), 0)
    hot_ref[...] = jnp.concatenate(
        [one_hot(slot_iota == place[t : t + 1, :]) for t in range(tiles)], axis=1
    )
    local_ref[...] = local.astype(F32)


def render_kernel(pieces, width, *refs):
    recv_refs, refs = refs[:pieces], refs[pieces:]
    lists_ref, hot_ref, local_ref, cam_ref, pixel_ref, targets_ref = refs[:6]
    pictures_ref, send_ref, rows_ref, table_ref, alpha_ref, weight_ref, part_ref = refs[6:13]
    tiles, length = lists_ref.shape
    share = LANES // tiles
    depth = SIDE * SIDE // share
    live = lists_ref[...] >= 0
    hot = hot_ref[...]

    if pieces == 1:
        listed = dot(recv_refs[0][...].reshape(-1, LANES), hot, 0, 0)[:width]
    else:
        (recv_scratch,) = refs[13:]
        place = lax.axis_index("gauss") // 2
        for k in range(pieces):
            recv_scratch[place ^ k] = recv_refs[pieces - 1 - k][...]
        received = jnp.concatenate([recv_scratch[p] for p in range(pieces)], axis=1)
        listed = dot(received, hot)
    for t in range(tiles):
        rows_ref[t * width : (t + 1) * width, :] = listed[:, t * length : (t + 1) * length]
    rows = [rows_ref[pl.ds(f, tiles, stride=width), :] for f in range(width)]

    cam = [cam_ref[j] for j in range(cam_ref.shape[0])]
    outs, pullback, rays = jax.vjp(lambda r: project(r, cam, live), rows[:10], has_aux=True)
    terms = outs[5:]
    colors = []
    for k in range(3):
        base = 11 + 16 * k
        shade = 0.5 + rows[base]
        for b in range(15):
            shade = shade + rows[base + 1 + b] * terms[b]
        for j in range(5):
            shade = shade + rows[59 + j] * cam[13 + 3 * j + k]
        colors.append(shade)
    opacity = jax.nn.sigmoid(rows[10])
    con_a, con_b, con_c = outs[2], outs[3], outs[4]

    attrs = [
        outs[0],
        outs[1],
        (-0.5 * LOG2E) * con_a,
        -LOG2E * con_b,
        (-0.5 * LOG2E) * con_c,
        jnp.where(live, opacity, 0.0),
    ] + colors
    count = len(attrs)
    blocks = []
    for value in attrs:
        parts = [p.astype(F32) for p in split(value, 3)]
        parts.append(jnp.zeros((16 - 3 * tiles, length), F32))
        blocks.append(jnp.concatenate(parts, axis=0))
    stacked = jnp.concatenate(blocks, axis=1)
    lane_tile = iota((16, LANES), 1) // share
    row_index = iota((16, LANES), 0)
    spread = one_hot((row_index % tiles == lane_tile) & (row_index < 3 * tiles))
    table = dot(stacked.T.astype(BF16), spread)
    pixel_x, pixel_y = pixel_ref[0, :1, :], pixel_ref[1]
    dx = pixel_x - table[:length]
    table_ref[0:length, :] = table[2 * length : 3 * length] * dx * dx
    table_ref[length : 2 * length, :] = table[3 * length : 4 * length] * dx
    table_ref[2 * length : 3 * length, :] = table[length : 2 * length]
    table_ref[3 * length :, :] = table[4 * length :]

    def row(index, l):
        return table_ref[pl.ds(index * length + l, 1), :]

    group = 16
    zero = jnp.zeros((depth, LANES), F32)

    def forward(chunk, carry):
        through, red, green, blue = carry
        for i in range(group):
            l = chunk * group + i
            dy = pixel_y - row(2, l)
            power = row(0, l) + dy * (row(1, l) + row(3, l) * dy)
            alpha = row(4, l) * jnp.exp2(power)
            weight = through * alpha
            red = red + weight * row(5, l)
            green = green + weight * row(6, l)
            blue = blue + weight * row(7, l)
            through = through - weight
            at = pl.ds(pl.multiple_of(l * depth, depth), depth)
            alpha_ref[at, :] = alpha
            weight_ref[at, :] = weight
        return through, red, green, blue

    start = (jnp.ones((depth, LANES), F32), zero, zero, zero)
    _, red, green, blue = lax.fori_loop(0, length // group, forward, start)
    pictures_ref[0] = red
    pictures_ref[1] = green
    pictures_ref[2] = blue
    res = [red - targets_ref[0], green - targets_ref[1], blue - targets_ref[2]]

    def backward(step, behind):
        chunk = length // group - 1 - step
        for i in reversed(range(group)):
            l = chunk * group + i
            at = pl.ds(pl.multiple_of(l * depth, depth), depth)
            alpha = alpha_ref[at, :]
            weight = weight_ref[at, :]
            dy = pixel_y - row(2, l)
            seen = row(5, l) * res[0] + row(6, l) * res[1] + row(7, l) * res[2]
            gap = seen - behind
            behind = behind + alpha * gap
            g = weight * gap
            gy = g * dy
            part_ref[0, at, :] = g
            part_ref[1, at, :] = gy
            part_ref[2, at, :] = gy * dy
            for k in range(3):
                part_ref[3 + k, at, :] = weight * res[k]
        return behind

    lax.fori_loop(0, length // group, backward, zero)

    def down(index):
        blocks = []
        for first in range(0, length, 8):
            parts = [
                part_ref[index, pl.ds(first * depth + s, 8, stride=depth), :] for s in range(depth)
            ]
            while len(parts) > 1:
                parts = [a + b for a, b in zip(parts[::2], parts[1::2])]
            blocks.append(parts[0])
        return jnp.concatenate(blocks, axis=0)

    sums = [down(index) for index in range(6)]
    g_x = sums[0] * dx
    sums = sums + [g_x, g_x * dx, sums[1] * dx]
    wide = jnp.concatenate([jnp.concatenate(split(s, 3), axis=1) for s in sums], axis=0)
    gather = one_hot(iota((8, 3 * LANES), 0) == (iota((8, 3 * LANES), 1) % LANES) // share)
    reduced = dot(gather, wide, 1, 1)
    g_0, g_y, g_yy, s_0, s_1, s_2, g_x, g_xx, g_xy = [
        reduced[:tiles, q * length : (q + 1) * length] for q in range(len(sums))
    ]

    d_colors = [s_0, s_1, s_2]
    d_terms = []
    for b in range(15):
        d_terms.append(sum(d_colors[k] * rows[12 + 16 * k + b] for k in range(3)))
    d_geometry = [
        con_a * g_x + con_b * g_y,
        con_b * g_x + con_c * g_y,
        -0.5 * g_xx,
        -g_xy,
        -0.5 * g_yy,
    ]
    (d_rows,) = pullback(d_geometry + d_terms)
    values = list(d_rows)
    values.append(g_0 * (1.0 - opacity))
    values.extend(d_colors)
    values.extend(rays)
    for j in range(5):
        values.append(sum(d_colors[k] * cam[13 + 3 * j + k] for k in range(3)))
    values.append(local_ref[...])
    values.extend([jnp.zeros((tiles, length), F32)] * (SENT - len(values)))
    for v in range(SENT):
        rows_ref[pl.ds(v, tiles, stride=width), :] = values[v]
    by_slot = jnp.concatenate(
        [
            jnp.concatenate(split(rows_ref[t * width : t * width + SENT, :], 3), axis=0)
            for t in range(tiles)
        ],
        axis=1,
    )
    by_slot = dot(by_slot, hot, 1, 1)
    by_slot = by_slot[:SENT] + by_slot[SENT : 2 * SENT] + by_slot[2 * SENT :]
    owners, copies, high, _ = send_ref.shape
    cap = hot.shape[0] // owners
    for o in range(owners):
        block = jnp.concatenate(
            [by_slot[r : r + high, o * cap : (o + 1) * cap] for r in range(0, SENT, high)], axis=1
        )
        for c in range(copies):
            send_ref[o, c] = block


def scatter(cap, recv_ref, g_dev):
    blocks, high, _ = recv_ref.shape
    values = jnp.concatenate(
        [
            jnp.concatenate(
                [recv_ref[b, :, first : first + cap] for b in range(blocks)], axis=1
            )
            for first in range(0, SENT * cap // high, cap)
        ],
        axis=0,
    )
    ray_x, ray_y = values[14:15], values[15:16]
    dir_z = lax.rsqrt(ray_x * ray_x + ray_y * ray_y + 1.0)
    terms = sh_terms(ray_x * dir_z, ray_y * dir_z, dir_z)
    terms = jnp.concatenate([jnp.ones_like(dir_z)] + terms, axis=0)
    rows = [values] + [terms * values[11 + k : 12 + k] for k in range(3)]
    hot = one_hot(iota((g_dev, blocks * cap), 0) == values[21:22].astype(jnp.int32))
    parts = split(jnp.concatenate(rows, axis=0), 2)
    total = dot(jnp.concatenate(parts, axis=0), hot, 1, 1)
    count = total.shape[0] // 2
    return total[:count] + total[count:]


def in_order(total, out_ref):
    out_ref[:11, :] = total[:11]
    out_ref[11:59, :] = total[SENT:]
    out_ref[59:, :] = total[16:21]


def scatter_kernel(cap, recv_ref, out_ref):
    in_order(scatter(cap, recv_ref, out_ref.shape[1]), out_ref)


def first_kernel(cap, recv_ref, out_ref):
    out_ref[...] = scatter(cap, recv_ref, out_ref.shape[1])


def last_kernel(cap, recv_ref, sum_ref, spread_ref, out_ref, pictures_ref):
    in_order(sum_ref[...] + scatter(cap, recv_ref, out_ref.shape[1]), out_ref)
    _, tiles, _ = pictures_ref.shape
    depth = spread_ref.shape[1]
    share = LANES // tiles
    for k in range(3):
        for t in range(tiles):
            pictures_ref[k, t : t + 1, :] = jnp.concatenate(
                [
                    spread_ref[k, s : s + 1, t * share : (t + 1) * share]
                    for s in range(depth)
                ],
                axis=1,
            )


def call(kernel, out_shape, args, scalars=0, left=0, scratch=()):
    in_specs = [pl.BlockSpec(memory_space=pltpu.SMEM)] * scalars
    in_specs += [pl.BlockSpec(memory_space=pltpu.VMEM)] * (len(args) - scalars - left)
    in_specs += [pl.BlockSpec(memory_space=pl.ANY)] * left
    many = isinstance(out_shape, (list, tuple))
    spec = pl.BlockSpec(memory_space=pltpu.VMEM)
    return pl.pallas_call(
        kernel,
        out_shape=out_shape,
        in_specs=in_specs,
        out_specs=[spec] * len(out_shape) if many else spec,
        scratch_shapes=list(scratch),
        compiler_params=pltpu.CompilerParams(vmem_limit_bytes=VMEM_LIMIT),
    )(*args)


def swap(x, axis, k):
    return lax.ppermute(x, axis, [(i, i ^ k) for i in range(lax.axis_size(axis))])


def crossed(owner, owners):
    return int(owner >= owners // 2)


def far_first(blocks):
    owners, views = lax.axis_size("gauss"), lax.axis_size("view")
    last = len(blocks) - 1
    out = []
    for i, block in enumerate(blocks):
        k = 2 * (last - i)
        pairs = []
        for g in range(owners):
            flip = crossed(g, owners) ^ crossed(g ^ k, owners) if views % 2 == 0 else 0
            pairs += [(g * views + v, (g ^ k) * views + (v ^ flip)) for v in range(views)]
        out.append(lax.ppermute(block, ("gauss", "view"), pairs) if k else block)
    return out


def exchange(x):
    return lax.all_to_all(x, "gauss", split_axis=0, concat_axis=0, tiled=True)


def exchange_wide(x):
    owners, views = lax.axis_size("gauss"), lax.axis_size("view")
    blocks = x.reshape(owners * views // 2, *x.shape[2:])
    groups = [
        [
            g * views + v
            for g in range(owners)
            for v in range(views)
            if v % 2 == c ^ crossed(g, owners)
        ]
        for c in range(2)
    ]
    return lax.all_to_all(
        blocks,
        ("gauss", "view"),
        split_axis=0,
        concat_axis=0,
        axis_index_groups=groups,
        tiled=True,
    )


def power_of_two(n):
    return n & (n - 1) == 0


def shape(dims, dtype):
    return jax.ShapeDtypeStruct(dims, dtype)


def on_device(params, lists, tile_pos, cam_index, cams, targets):
    owners = lax.axis_size("gauss")
    views = lax.axis_size("view")
    width, g_dev = params.shape
    tiles, length = lists.shape
    cap = max(tiles * length // owners, 16)
    slots = owners * cap
    share = LANES // tiles
    depth = SIDE * SIDE // share
    paired = 2 <= owners <= 16 and power_of_two(owners) and LANES == 2 * width
    peers = owners // 2 if paired else 1
    wide = views % 2 == 0 and owners * views <= 32

    if paired:
        other = swap(params, "gauss", 1)
        all_lists = far_first([lists] * peers)
    params_copy, cam, pixel = call(
        prepare_kernel,
        [
            shape((width, g_dev), BF16),
            shape((cams.shape[0], tiles, length), F32),
            shape((2, depth, LANES), F32),
        ],
        (tile_pos, cam_index, cams.T, params),
        scalars=3,
    )
    if paired:
        picked = call(
            functools.partial(pick_pair_kernel, cap, peers),
            [shape((width, 2 * cap), BF16)] * peers,
            (*all_lists[::-1], params_copy, other),
            scratch=(
                pltpu.VMEM((peers, tiles, length), jnp.int32),
                pltpu.VMEM((peers, width, 2 * cap), BF16),
            ),
        )
        returned = far_first(picked)
        after = picked[-1]
    else:
        all_lists = exchange(jnp.broadcast_to(lists[None], (owners, tiles, length)))
        picked = call(
            functools.partial(pick_kernel, tiles, cap),
            shape((slots, LANES), BF16),
            (all_lists.reshape(owners * tiles, length), params_copy),
        )
        returned = [exchange(picked.reshape(owners, cap, LANES))]
        after = picked
    hot, local = call(
        functools.partial(place_kernel, owners, cap, g_dev),
        [shape((slots, tiles * length), BF16), shape((tiles, length), F32)],
        (lists, after),
        left=1,
    )
    spread_targets = (
        targets.reshape(3, tiles, depth, share).transpose(0, 2, 1, 3).reshape(3, depth, LANES)
    )
    copies = views // 2 if wide else 1
    high = SENT * cap // LANES
    pictures, sent = call(
        functools.partial(render_kernel, peers, width),
        [shape((3, depth, LANES), F32), shape((owners, copies, high, LANES), F32)],
        (*returned, lists, hot, local, cam, pixel, spread_targets),
        scratch=(
            pltpu.VMEM((tiles * width, length), F32),
            pltpu.VMEM((8 * length, LANES), F32),
            pltpu.VMEM((length * depth, LANES), F32),
            pltpu.VMEM((length * depth, LANES), F32),
            pltpu.VMEM((6, length * depth, LANES), F32),
            pltpu.VMEM((peers, *returned[0].shape[-2:]), BF16),
        ),
    )
    if wide:
        received = exchange_wide(sent)
        other = swap(received, "view", 1)
        total = call(
            functools.partial(first_kernel, cap), shape((SENT + 48, g_dev), F32), (received,)
        )
        grads, pictures = call(
            functools.partial(last_kernel, cap),
            [shape((width, g_dev), F32), shape(targets.shape, F32)],
            (other, total, pictures),
        )
        return (pictures, grads)
    pictures = (
        pictures.reshape(3, depth, tiles, share)
        .transpose(0, 2, 1, 3)
        .reshape(3, tiles, SIDE * SIDE)
    )
    received = exchange(sent[:, 0])
    grads = call(
        functools.partial(scatter_kernel, cap), shape((width, g_dev), F32), (received,)
    )
    return (pictures, lax.psum(grads, "view"))


def solution(mesh):
    return jax.shard_map(
        on_device,
        mesh=mesh,
        in_specs=(
            P(None, "gauss"),
            P(("gauss", "view"), None),
            P(("gauss", "view")),
            P(("gauss", "view")),
            P(),
            P(None, ("gauss", "view"), None),
        ),
        out_specs=(P(None, ("gauss", "view"), None), P(None, "gauss")),
        check_vma=False,
    )
```

```python
import functools
import math

import jax
import jax.numpy as jnp
from jax import lax
from jax.experimental import pallas as pl
from jax.experimental.pallas import tpu as pltpu
from jax.sharding import PartitionSpec as P

WIN = 16
SIDE = 16
LANES = 128
LOG2E = math.log2(math.e)
F32 = jnp.float32
BF16 = jnp.bfloat16
VMEM_LIMIT = 24 * 2**20
SENT = 32


def sh_terms(x, y, z):
    xx, yy, zz = x * x, y * y, z * z
    xy = x * y
    diff = xx - yy
    five = 5.0 * zz - 1.0
    return [
        x,
        y,
        z,
        xy,
        y * z,
        x * z,
        diff,
        3.0 * zz - 1.0,
        x * (xx - 3.0 * yy),
        xy * z,
        y * (3.0 * xx - yy),
        z * diff,
        x * five,
        y * five,
        z * (5.0 * zz - 3.0),
    ]


def project(rows, cam, live):
    mx, my, mz = rows[0], rows[1], rows[2]
    cam_x = cam[0] * mx + cam[1] * my + cam[2] * mz + cam[9]
    cam_y = cam[3] * mx + cam[4] * my + cam[5] * mz + cam[10]
    cam_z = cam[6] * mx + cam[7] * my + cam[8] * mz + cam[11]
    cam_z = jnp.where(live, cam_z, 1.0)
    inv_z = 1.0 / cam_z
    qw, qx, qy, qz = rows[6], rows[7], rows[8], rows[9]
    qw = jnp.where(live, qw, 1.0)
    inv_q = lax.rsqrt(qw * qw + qx * qx + qy * qy + qz * qz)
    qw, qx, qy, qz = qw * inv_q, qx * inv_q, qy * inv_q, qz * inv_q
    rot = [
        [
            1.0 - 2.0 * (qy * qy + qz * qz),
            2.0 * (qx * qy - qw * qz),
            2.0 * (qx * qz + qw * qy),
        ],
        [
            2.0 * (qx * qy + qw * qz),
            1.0 - 2.0 * (qx * qx + qz * qz),
            2.0 * (qy * qz - qw * qx),
        ],
        [
            2.0 * (qx * qz - qw * qy),
            2.0 * (qy * qz + qw * qx),
            1.0 - 2.0 * (qx * qx + qy * qy),
        ],
    ]
    mixed = [
        [
            cam[3 * i] * rot[0][k] + cam[3 * i + 1] * rot[1][k] + cam[3 * i + 2] * rot[2][k]
            for k in range(3)
        ]
        for i in range(3)
    ]
    scale = cam[12] * inv_z
    ray_x, ray_y = cam_x * inv_z, cam_y * inv_z
    proj_u = [scale * (mixed[0][k] - ray_x * mixed[2][k]) for k in range(3)]
    proj_v = [scale * (mixed[1][k] - ray_y * mixed[2][k]) for k in range(3)]
    var = [jnp.exp(2.0 * rows[3 + k]) for k in range(3)]
    uv = [proj_u[k] * var[k] for k in range(3)]
    cov_a = sum(uv[k] * proj_u[k] for k in range(3)) + 0.3
    cov_b = sum(uv[k] * proj_v[k] for k in range(3))
    cov_c = sum(proj_v[k] * proj_v[k] * var[k] for k in range(3)) + 0.3
    inv_det = 1.0 / (cov_a * cov_c - cov_b * cov_b)
    inv_dist = lax.rsqrt(cam_x * cam_x + cam_y * cam_y + cam_z * cam_z)
    terms = sh_terms(cam_x * inv_dist, cam_y * inv_dist, cam_z * inv_dist)
    geometry = [cam_x * scale, cam_y * scale, cov_c * inv_det, -cov_b * inv_det, cov_a * inv_det]
    return geometry + terms, (ray_x, ray_y)


def iota(shape, dim):
    return lax.broadcasted_iota(jnp.int32, shape, dim)


def one_hot(mask):
    return jnp.where(mask, 1.0, 0.0).astype(BF16)


def dot(lhs, rhs, lhs_dim=1, rhs_dim=0):
    return lax.dot_general(
        lhs, rhs, (((lhs_dim,), (rhs_dim,)), ((), ())), preferred_element_type=F32
    )


def split(x, parts):
    out = []
    for _ in range(parts):
        head = x.astype(BF16)
        out.append(head)
        x = x - head.astype(F32)
    return out


def ranks(mask, tiles):
    rows, length = mask.shape
    bits = one_hot(mask)
    earlier = one_hot(iota((length, length), 0) < iota((length, length), 1))
    within = dot(bits, earlier)
    count = dot(bits, jnp.ones((length, length), BF16)).astype(BF16)
    here, there = iota((rows, rows), 0), iota((rows, rows), 1)
    above = one_hot((there < here) & (there >= here - lax.rem(here, tiles)))
    return (within + dot(above, count)).astype(jnp.int32)


def find(ids, base, tiles, cap, g_dev):
    local = ids - base
    mine = (local >= 0) & (local < g_dev)
    key = jnp.where(mine, ranks(mine, tiles), -1)
    rows, length = ids.shape
    slot = iota((cap, length), 0)
    found = []
    for r in range(0, rows, tiles):
        total = jnp.zeros((cap, length), jnp.int32)
        for t in range(r, r + tiles):
            total = total + jnp.where(key[t : t + 1, :] == slot, local[t : t + 1, :], 0)
        found.append(jnp.sum(total, axis=1, keepdims=True))
    return jnp.concatenate(found, axis=0)


def pick_kernel(tiles, cap, lists_ref, params_ref, picked_ref):
    width, g_dev = params_ref.shape
    where = find(lists_ref[...], lax.axis_index("gauss") * g_dev, tiles, cap, g_dev)
    hot = one_hot(where == iota((where.shape[0], g_dev), 1))
    wide = jnp.concatenate([params_ref[...], jnp.zeros((LANES - width, g_dev), BF16)], axis=0)
    picked_ref[...] = dot(hot, wide, 1, 1).astype(BF16)


def pick_pair_kernel(cap, peers, *refs):
    lists_refs, refs = refs[:peers], refs[peers:]
    own_ref, other_ref = refs[:2]
    picked_refs, refs = refs[2 : 2 + peers], refs[2 + peers :]
    lists_scratch, picked_scratch = refs
    tiles, length = lists_refs[0].shape
    g_dev = own_ref.shape[1]
    me = lax.axis_index("gauss")
    first = me % 2 == 0
    for k in range(peers):
        lists_scratch[(me // 2) ^ k] = lists_refs[k][...]
    ids = lists_scratch[...].reshape(peers * tiles, length)
    where_own = find(ids, me * g_dev, tiles, cap, g_dev)
    where_other = find(ids, (me ^ 1) * g_dev, tiles, cap, g_dev)
    lanes = iota((peers * cap, g_dev), 1)
    of_own = dot(own_ref[...], one_hot(where_own == lanes), 1, 1)
    of_other = dot(other_ref[...], one_hot(where_other == lanes), 1, 1)
    of_even = jnp.where(first, of_own, of_other)
    of_odd = jnp.where(first, of_other, of_own)
    for p in range(peers):
        block = slice(p * cap, (p + 1) * cap)
        picked_scratch[p] = jnp.concatenate(
            [of_even[:, block], of_odd[:, block]], axis=1
        ).astype(BF16)
    for k in range(peers):
        picked_refs[peers - 1 - k][...] = picked_scratch[(me // 2) ^ k]


def by_tile(values, row):
    out = jnp.full(row.shape, values[-1])
    for t in range(len(values) - 1):
        out = jnp.where(row == t, values[t], out)
    return out


def prepare_kernel(params_ref, copy_ref):
    copy_ref[...] = params_ref[...]


def place_kernel(
    owners,
    cap,
    g_dev,
    tile_pos_ref,
    cam_index_ref,
    cams_ref,
    lists_ref,
    after_ref,
    hot_ref,
    local_ref,
    cam_ref,
    pixel_ref,
):
    values, tiles, length = cam_ref.shape
    share = LANES // tiles
    depth = SIDE * SIDE // share
    cam_ids = [cam_index_ref[t] for t in range(tiles)]
    tile_row = iota((tiles, length), 0)
    for j in range(values):
        cam_ref[j] = by_tile([cams_ref[cam_ids[t], j] for t in range(tiles)], tile_row)
    pos = [tile_pos_ref[t] for t in range(tiles)]
    lane = iota((depth, LANES), 1)
    origin_x = [(SIDE * (lax.rem(p, WIN) - WIN // 2)).astype(F32) + 0.5 for p in pos]
    pixel_ref[0] = by_tile(origin_x, lane // share) + (lane % SIDE).astype(F32)
    origin_y = [(SIDE * (lax.div(p, WIN) - WIN // 2)).astype(F32) + 0.5 for p in pos]
    pixel_row = iota((depth, LANES), 0) * (share // SIDE) + (lane % share) // SIDE
    pixel_ref[1] = by_tile(origin_y, lane // share) + pixel_row.astype(F32)
    slots = owners * cap
    ids = lists_ref[...]
    masks = [(ids >= o * g_dev) & (ids < (o + 1) * g_dev) for o in range(owners)]
    rank = ranks(jnp.concatenate([m.astype(jnp.int32) for m in masks], axis=0) > 0, tiles)
    place = jnp.full((tiles, length), -1, jnp.int32)
    local = jnp.zeros((tiles, length), jnp.int32)
    for o in range(owners):
        place = jnp.where(masks[o], rank[o * tiles : (o + 1) * tiles] + o * cap, place)
        local = jnp.where(masks[o], ids - o * g_dev, local)
    slot_iota = iota((slots, length), 0)
    hot_ref[...] = jnp.concatenate(
        [one_hot(slot_iota == place[t : t + 1, :]) for t in range(tiles)], axis=1
    )
    local_ref[...] = local.astype(F32)


def render_kernel(pieces, width, *refs):
    recv_refs, refs = refs[:pieces], refs[pieces:]
    lists_ref, hot_ref, local_ref, cam_ref, pixel_ref, targets_ref = refs[:6]
    pictures_ref, send_ref, rows_ref, table_ref, alpha_ref, weight_ref, part_ref = refs[6:13]
    tiles, length = lists_ref.shape
    share = LANES // tiles
    depth = SIDE * SIDE // share
    live = lists_ref[...] >= 0
    hot = hot_ref[...]

    if pieces == 1:
        listed = dot(recv_refs[0][...].reshape(-1, LANES), hot, 0, 0)[:width]
    else:
        (recv_scratch,) = refs[13:]
        place = lax.axis_index("gauss") // 2
        for k in range(pieces):
            recv_scratch[place ^ k] = recv_refs[pieces - 1 - k][...]
        received = jnp.concatenate([recv_scratch[p] for p in range(pieces)], axis=1)
        listed = dot(received, hot)
    for t in range(tiles):
        rows_ref[t * width : (t + 1) * width, :] = listed[:, t * length : (t + 1) * length]
    rows = [rows_ref[pl.ds(f, tiles, stride=width), :] for f in range(width)]

    cam = [cam_ref[j] for j in range(cam_ref.shape[0])]
    outs, pullback, rays = jax.vjp(lambda r: project(r, cam, live), rows[:10], has_aux=True)
    terms = outs[5:]
    colors = []
    for k in range(3):
        base = 11 + 16 * k
        shade = 0.5 + rows[base]
        for b in range(15):
            shade = shade + rows[base + 1 + b] * terms[b]
        for j in range(5):
            shade = shade + rows[59 + j] * cam[13 + 3 * j + k]
        colors.append(shade)
    opacity = jax.nn.sigmoid(rows[10])
    con_a, con_b, con_c = outs[2], outs[3], outs[4]

    attrs = [
        outs[0],
        outs[1],
        (-0.5 * LOG2E) * con_a,
        -LOG2E * con_b,
        (-0.5 * LOG2E) * con_c,
        jnp.where(live, opacity, 0.0),
    ] + colors
    count = len(attrs)
    blocks = []
    for value in attrs:
        parts = [p.astype(F32) for p in split(value, 3)]
        parts.append(jnp.zeros((16 - 3 * tiles, length), F32))
        blocks.append(jnp.concatenate(parts, axis=0))
    stacked = jnp.concatenate(blocks, axis=1)
    lane_tile = iota((16, LANES), 1) // share
    row_index = iota((16, LANES), 0)
    spread = one_hot((row_index % tiles == lane_tile) & (row_index < 3 * tiles))
    table = dot(stacked.T.astype(BF16), spread)
    pixel_x, pixel_y = pixel_ref[0, :1, :], pixel_ref[1]
    dx = pixel_x - table[:length]
    table_ref[0:length, :] = table[2 * length : 3 * length] * dx * dx
    table_ref[length : 2 * length, :] = table[3 * length : 4 * length] * dx
    table_ref[2 * length : 3 * length, :] = table[length : 2 * length]
    table_ref[3 * length :, :] = table[4 * length :]

    def row(index, l):
        return table_ref[pl.ds(index * length + l, 1), :]

    group = 16
    zero = jnp.zeros((depth, LANES), F32)

    def forward(chunk, carry):
        through, red, green, blue = carry
        for i in range(group):
            l = chunk * group + i
            dy = pixel_y - row(2, l)
            power = row(0, l) + dy * (row(1, l) + row(3, l) * dy)
            alpha = row(4, l) * jnp.exp2(power)
            weight = through * alpha
            red = red + weight * row(5, l)
            green = green + weight * row(6, l)
            blue = blue + weight * row(7, l)
            through = through - weight
            at = pl.ds(pl.multiple_of(l * depth, depth), depth)
            alpha_ref[at, :] = alpha
            weight_ref[at, :] = weight
        return through, red, green, blue

    start = (jnp.ones((depth, LANES), F32), zero, zero, zero)
    _, red, green, blue = lax.fori_loop(0, length // group, forward, start)
    pictures_ref[0] = red
    pictures_ref[1] = green
    pictures_ref[2] = blue
    res = [red - targets_ref[0], green - targets_ref[1], blue - targets_ref[2]]

    def backward(step, behind):
        chunk = length // group - 1 - step
        for i in reversed(range(group)):
            l = chunk * group + i
            at = pl.ds(pl.multiple_of(l * depth, depth), depth)
            alpha = alpha_ref[at, :]
            weight = weight_ref[at, :]
            dy = pixel_y - row(2, l)
            seen = row(5, l) * res[0] + row(6, l) * res[1] + row(7, l) * res[2]
            gap = seen - behind
            behind = behind + alpha * gap
            g = weight * gap
            gy = g * dy
            part_ref[0, at, :] = g
            part_ref[1, at, :] = gy
            part_ref[2, at, :] = gy * dy
            for k in range(3):
                part_ref[3 + k, at, :] = weight * res[k]
        return behind

    lax.fori_loop(0, length // group, backward, zero)

    def down(index):
        blocks = []
        for first in range(0, length, 8):
            parts = [
                part_ref[index, pl.ds(first * depth + s, 8, stride=depth), :] for s in range(depth)
            ]
            while len(parts) > 1:
                parts = [a + b for a, b in zip(parts[::2], parts[1::2])]
            blocks.append(parts[0])
        return jnp.concatenate(blocks, axis=0)

    sums = [down(index) for index in range(6)]
    g_x = sums[0] * dx
    sums = sums + [g_x, g_x * dx, sums[1] * dx]
    wide = jnp.concatenate([jnp.concatenate(split(s, 3), axis=1) for s in sums], axis=0)
    gather = one_hot(iota((8, 3 * LANES), 0) == (iota((8, 3 * LANES), 1) % LANES) // share)
    reduced = dot(gather, wide, 1, 1)
    g_0, g_y, g_yy, s_0, s_1, s_2, g_x, g_xx, g_xy = [
        reduced[:tiles, q * length : (q + 1) * length] for q in range(len(sums))
    ]

    d_colors = [s_0, s_1, s_2]
    d_terms = []
    for b in range(15):
        d_terms.append(sum(d_colors[k] * rows[12 + 16 * k + b] for k in range(3)))
    d_geometry = [
        con_a * g_x + con_b * g_y,
        con_b * g_x + con_c * g_y,
        -0.5 * g_xx,
        -g_xy,
        -0.5 * g_yy,
    ]
    (d_rows,) = pullback(d_geometry + d_terms)
    values = list(d_rows)
    values.append(g_0 * (1.0 - opacity))
    values.extend(d_colors)
    values.extend(rays)
    for j in range(5):
        values.append(sum(d_colors[k] * cam[13 + 3 * j + k] for k in range(3)))
    values.append(local_ref[...])
    values.extend([jnp.zeros((tiles, length), F32)] * (SENT - len(values)))
    for v in range(SENT):
        rows_ref[pl.ds(v, tiles, stride=width), :] = values[v]
    by_slot = jnp.concatenate(
        [
            jnp.concatenate(split(rows_ref[t * width : t * width + SENT, :], 3), axis=0)
            for t in range(tiles)
        ],
        axis=1,
    )
    by_slot = dot(by_slot, hot, 1, 1)
    by_slot = by_slot[:SENT] + by_slot[SENT : 2 * SENT] + by_slot[2 * SENT :]
    owners, copies, high, _ = send_ref.shape
    cap = hot.shape[0] // owners
    for o in range(owners):
        block = jnp.concatenate(
            [by_slot[r : r + high, o * cap : (o + 1) * cap] for r in range(0, SENT, high)], axis=1
        )
        for c in range(copies):
            send_ref[o, c] = block


def entry_rows(cap, recv_ref):
    blocks, high, _ = recv_ref.shape
    values = jnp.concatenate(
        [
            jnp.concatenate(
                [recv_ref[b, :, first : first + cap] for b in range(blocks)], axis=1
            )
            for first in range(0, SENT * cap // high, cap)
        ],
        axis=0,
    )
    ray_x, ray_y = values[14:15], values[15:16]
    dir_z = lax.rsqrt(ray_x * ray_x + ray_y * ray_y + 1.0)
    terms = sh_terms(ray_x * dir_z, ray_y * dir_z, dir_z)
    terms = jnp.concatenate([jnp.ones_like(dir_z)] + terms, axis=0)
    rows = [values] + [terms * values[11 + k : 12 + k] for k in range(3)]
    parts = split(jnp.concatenate(rows, axis=0), 2)
    return jnp.concatenate(parts, axis=0), values[21:22].astype(jnp.int32)


def scatter(rows, where, first, count):
    hot = one_hot(iota((count, where.shape[1]), 0) + first == where)
    total = dot(rows, hot, 1, 1)
    half = total.shape[0] // 2
    return total[:half] + total[half:]


def in_order(total):
    return jnp.concatenate([total[:11], total[SENT:], total[16:21]], axis=0)


def scatter_kernel(cap, recv_ref, out_ref):
    rows, where = entry_rows(cap, recv_ref)
    out_ref[...] = in_order(scatter(rows, where, 0, out_ref.shape[1]))


def first_kernel(cap, recv_ref, out_ref):
    rows, where = entry_rows(cap, recv_ref)
    out_ref[...] = scatter(rows, where, 0, out_ref.shape[1])


def last_kernel(
    cap, recv_ref, sum_ref, spread_ref, out_ref, pictures_ref, sums, pictures, out_sem, picture_sem
):
    _, tiles, _ = pictures.shape
    depth = spread_ref.shape[1]
    share = LANES // tiles
    for k in range(3):
        for t in range(tiles):
            pictures[k, t : t + 1, :] = jnp.concatenate(
                [
                    spread_ref[k, s : s + 1, t * share : (t + 1) * share]
                    for s in range(depth)
                ],
                axis=1,
            )
    copies = [pltpu.make_async_copy(pictures, pictures_ref, picture_sem)]
    copies[0].start()
    rows, where = entry_rows(cap, recv_ref)
    blocks, _, count = sums.shape
    for b in range(blocks):
        columns = slice(b * count, (b + 1) * count)
        sums[b] = in_order(sum_ref[:, columns] + scatter(rows, where, b * count, count))
        copies.append(
            pltpu.make_async_copy(
                sums.at[b], out_ref.at[:, pl.ds(b * count, count)], out_sem.at[b]
            )
        )
        copies[-1].start()
    for copy in copies:
        copy.wait()


def call(kernel, out_shape, args, scalars=0, left=0, out_left=False, scratch=()):
    in_specs = [pl.BlockSpec(memory_space=pltpu.SMEM)] * scalars
    in_specs += [pl.BlockSpec(memory_space=pltpu.VMEM)] * (len(args) - scalars - left)
    in_specs += [pl.BlockSpec(memory_space=pl.ANY)] * left
    many = isinstance(out_shape, (list, tuple))
    spec = pl.BlockSpec(memory_space=pl.ANY if out_left else pltpu.VMEM)
    return pl.pallas_call(
        kernel,
        out_shape=out_shape,
        in_specs=in_specs,
        out_specs=[spec] * len(out_shape) if many else spec,
        scratch_shapes=list(scratch),
        compiler_params=pltpu.CompilerParams(vmem_limit_bytes=VMEM_LIMIT),
    )(*args)


def swap(x, axis, k):
    return lax.ppermute(x, axis, [(i, i ^ k) for i in range(lax.axis_size(axis))])


def crossed(owner, owners):
    return int(owner >= owners // 2)


def far_first(blocks):
    owners, views = lax.axis_size("gauss"), lax.axis_size("view")
    last = len(blocks) - 1
    out = []
    for i, block in enumerate(blocks):
        k = 2 * (last - i)
        pairs = []
        for g in range(owners):
            flip = crossed(g, owners) ^ crossed(g ^ k, owners) if views % 2 == 0 else 0
            pairs += [(g * views + v, (g ^ k) * views + (v ^ flip)) for v in range(views)]
        out.append(lax.ppermute(block, ("gauss", "view"), pairs) if k else block)
    return out


def exchange(x):
    return lax.all_to_all(x, "gauss", split_axis=0, concat_axis=0, tiled=True)


def exchange_wide(x):
    owners, views = lax.axis_size("gauss"), lax.axis_size("view")
    blocks = x.reshape(owners * views // 2, *x.shape[2:])
    groups = [
        [
            g * views + v
            for g in range(owners)
            for v in range(views)
            if v % 2 == c ^ crossed(g, owners)
        ]
        for c in range(2)
    ]
    return lax.all_to_all(
        blocks,
        ("gauss", "view"),
        split_axis=0,
        concat_axis=0,
        axis_index_groups=groups,
        tiled=True,
    )


def power_of_two(n):
    return n & (n - 1) == 0


def shape(dims, dtype):
    return jax.ShapeDtypeStruct(dims, dtype)


def on_device(params, lists, tile_pos, cam_index, cams, targets):
    owners = lax.axis_size("gauss")
    views = lax.axis_size("view")
    width, g_dev = params.shape
    tiles, length = lists.shape
    cap = max(tiles * length // owners, 16)
    slots = owners * cap
    share = LANES // tiles
    depth = SIDE * SIDE // share
    paired = 2 <= owners <= 16 and power_of_two(owners) and LANES == 2 * width
    peers = owners // 2 if paired else 1
    wide = views % 2 == 0 and owners * views <= 32

    if paired:
        other = swap(params, "gauss", 1)
        all_lists = far_first([lists] * peers)
    params_copy = call(prepare_kernel, shape((width, g_dev), BF16), (params,))
    if paired:
        picked = call(
            functools.partial(pick_pair_kernel, cap, peers),
            [shape((width, 2 * cap), BF16)] * peers,
            (*all_lists[::-1], params_copy, other),
            scratch=(
                pltpu.VMEM((peers, tiles, length), jnp.int32),
                pltpu.VMEM((peers, width, 2 * cap), BF16),
            ),
        )
        returned = far_first(picked)
        after = picked[-1]
    else:
        all_lists = exchange(jnp.broadcast_to(lists[None], (owners, tiles, length)))
        picked = call(
            functools.partial(pick_kernel, tiles, cap),
            shape((slots, LANES), BF16),
            (all_lists.reshape(owners * tiles, length), params_copy),
        )
        returned = [exchange(picked.reshape(owners, cap, LANES))]
        after = picked
    hot, local, cam, pixel = call(
        functools.partial(place_kernel, owners, cap, g_dev),
        [
            shape((slots, tiles * length), BF16),
            shape((tiles, length), F32),
            shape((cams.shape[0], tiles, length), F32),
            shape((2, depth, LANES), F32),
        ],
        (tile_pos, cam_index, cams.T, lists, after),
        scalars=3,
        left=1,
    )
    spread_targets = (
        targets.reshape(3, tiles, depth, share).transpose(0, 2, 1, 3).reshape(3, depth, LANES)
    )
    copies = views // 2 if wide else 1
    high = SENT * cap // LANES
    pictures, sent = call(
        functools.partial(render_kernel, peers, width),
        [shape((3, depth, LANES), F32), shape((owners, copies, high, LANES), F32)],
        (*returned, lists, hot, local, cam, pixel, spread_targets),
        scratch=(
            pltpu.VMEM((tiles * width, length), F32),
            pltpu.VMEM((8 * length, LANES), F32),
            pltpu.VMEM((length * depth, LANES), F32),
            pltpu.VMEM((length * depth, LANES), F32),
            pltpu.VMEM((6, length * depth, LANES), F32),
            pltpu.VMEM((peers, *returned[0].shape[-2:]), BF16),
        ),
    )
    if wide:
        received = exchange_wide(sent)
        other = swap(received, "view", 1)
        total = call(
            functools.partial(first_kernel, cap), shape((SENT + 48, g_dev), F32), (received,)
        )
        parts = 4
        grads, pictures = call(
            functools.partial(last_kernel, cap),
            [shape((width, g_dev), F32), shape(targets.shape, F32)],
            (other, total, pictures),
            out_left=True,
            scratch=(
                pltpu.VMEM((parts, width, g_dev // parts), F32),
                pltpu.VMEM(targets.shape, F32),
                pltpu.SemaphoreType.DMA((parts,)),
                pltpu.SemaphoreType.DMA,
            ),
        )
        return (pictures, grads)
    pictures = (
        pictures.reshape(3, depth, tiles, share)
        .transpose(0, 2, 1, 3)
        .reshape(3, tiles, SIDE * SIDE)
    )
    received = exchange(sent[:, 0])
    grads = call(
        functools.partial(scatter_kernel, cap), shape((width, g_dev), F32), (received,)
    )
    return (pictures, lax.psum(grads, "view"))


def solution(mesh):
    return jax.shard_map(
        on_device,
        mesh=mesh,
        in_specs=(
            P(None, "gauss"),
            P(("gauss", "view"), None),
            P(("gauss", "view")),
            P(("gauss", "view")),
            P(),
            P(None, ("gauss", "view"), None),
        ),
        out_specs=(P(None, ("gauss", "view"), None), P(None, "gauss")),
        check_vma=False,
    )
```

```python
import functools
import math

import jax
import jax.numpy as jnp
from jax import lax
from jax.experimental import pallas as pl
from jax.experimental.pallas import tpu as pltpu
from jax.sharding import PartitionSpec as P

WIN = 16
SIDE = 16
LANES = 128
LOG2E = math.log2(math.e)
F32 = jnp.float32
BF16 = jnp.bfloat16
VMEM_LIMIT = 24 * 2**20
SENT = 32


def sh_terms(x, y, z):
    xx, yy, zz = x * x, y * y, z * z
    xy = x * y
    diff = xx - yy
    five = 5.0 * zz - 1.0
    return [
        x,
        y,
        z,
        xy,
        y * z,
        x * z,
        diff,
        3.0 * zz - 1.0,
        x * (xx - 3.0 * yy),
        xy * z,
        y * (3.0 * xx - yy),
        z * diff,
        x * five,
        y * five,
        z * (5.0 * zz - 3.0),
    ]


def project(rows, cam, live):
    mx, my, mz = rows[0], rows[1], rows[2]
    cam_x = cam[0] * mx + cam[1] * my + cam[2] * mz + cam[9]
    cam_y = cam[3] * mx + cam[4] * my + cam[5] * mz + cam[10]
    cam_z = cam[6] * mx + cam[7] * my + cam[8] * mz + cam[11]
    cam_z = jnp.where(live, cam_z, 1.0)
    inv_z = 1.0 / cam_z
    qw, qx, qy, qz = rows[6], rows[7], rows[8], rows[9]
    qw = jnp.where(live, qw, 1.0)
    inv_q = lax.rsqrt(qw * qw + qx * qx + qy * qy + qz * qz)
    qw, qx, qy, qz = qw * inv_q, qx * inv_q, qy * inv_q, qz * inv_q
    rot = [
        [
            1.0 - 2.0 * (qy * qy + qz * qz),
            2.0 * (qx * qy - qw * qz),
            2.0 * (qx * qz + qw * qy),
        ],
        [
            2.0 * (qx * qy + qw * qz),
            1.0 - 2.0 * (qx * qx + qz * qz),
            2.0 * (qy * qz - qw * qx),
        ],
        [
            2.0 * (qx * qz - qw * qy),
            2.0 * (qy * qz + qw * qx),
            1.0 - 2.0 * (qx * qx + qy * qy),
        ],
    ]
    mixed = [
        [
            cam[3 * i] * rot[0][k] + cam[3 * i + 1] * rot[1][k] + cam[3 * i + 2] * rot[2][k]
            for k in range(3)
        ]
        for i in range(3)
    ]
    scale = cam[12] * inv_z
    ray_x, ray_y = cam_x * inv_z, cam_y * inv_z
    proj_u = [scale * (mixed[0][k] - ray_x * mixed[2][k]) for k in range(3)]
    proj_v = [scale * (mixed[1][k] - ray_y * mixed[2][k]) for k in range(3)]
    var = [jnp.exp(2.0 * rows[3 + k]) for k in range(3)]
    uv = [proj_u[k] * var[k] for k in range(3)]
    cov_a = sum(uv[k] * proj_u[k] for k in range(3)) + 0.3
    cov_b = sum(uv[k] * proj_v[k] for k in range(3))
    cov_c = sum(proj_v[k] * proj_v[k] * var[k] for k in range(3)) + 0.3
    inv_det = 1.0 / (cov_a * cov_c - cov_b * cov_b)
    inv_dist = lax.rsqrt(cam_x * cam_x + cam_y * cam_y + cam_z * cam_z)
    terms = sh_terms(cam_x * inv_dist, cam_y * inv_dist, cam_z * inv_dist)
    geometry = [cam_x * scale, cam_y * scale, cov_c * inv_det, -cov_b * inv_det, cov_a * inv_det]
    return geometry + terms, (ray_x, ray_y)


def iota(shape, dim):
    return lax.broadcasted_iota(jnp.int32, shape, dim)


def one_hot(mask):
    return jnp.where(mask, 1.0, 0.0).astype(BF16)


def dot(lhs, rhs, lhs_dim=1, rhs_dim=0):
    return lax.dot_general(
        lhs, rhs, (((lhs_dim,), (rhs_dim,)), ((), ())), preferred_element_type=F32
    )


def split(x, parts):
    out = []
    for _ in range(parts):
        head = x.astype(BF16)
        out.append(head)
        x = x - head.astype(F32)
    return out


def ranks(mask, tiles):
    rows, length = mask.shape
    bits = jnp.where(mask, 1.0, 0.0)
    place = iota((rows, length), 0) % tiles
    shifted = [bits] + [
        jnp.where(place >= d, pltpu.roll(bits, d, 0), 0.0) for d in range(1, tiles)
    ]
    earlier = one_hot(iota((length, length), 0) < iota((length, length), 1))
    counted = jnp.concatenate([earlier] + [jnp.ones_like(earlier)] * (tiles - 1), axis=0)
    return dot(jnp.concatenate(shifted, axis=1).astype(BF16), counted).astype(jnp.int32)


def find(ids, base, tiles, cap, g_dev):
    local = ids - base
    mine = (local >= 0) & (local < g_dev)
    key = jnp.where(mine, ranks(mine, tiles), -1)
    rows, length = ids.shape
    slot = iota((cap, length), 0)
    found = []
    for r in range(0, rows, tiles):
        total = jnp.zeros((cap, length), jnp.int32)
        for t in range(r, r + tiles):
            total = total + jnp.where(key[t : t + 1, :] == slot, local[t : t + 1, :], 0)
        found.append(jnp.sum(total, axis=1, keepdims=True))
    return jnp.concatenate(found, axis=0)


def pick_kernel(tiles, cap, lists_ref, params_ref, picked_ref):
    width, g_dev = params_ref.shape
    where = find(lists_ref[...], lax.axis_index("gauss") * g_dev, tiles, cap, g_dev)
    hot = one_hot(where == iota((where.shape[0], g_dev), 1))
    wide = jnp.concatenate([params_ref[...], jnp.zeros((LANES - width, g_dev), BF16)], axis=0)
    picked_ref[...] = dot(hot, wide, 1, 1).astype(BF16)


def pick_pair_kernel(cap, peers, *refs):
    lists_refs, refs = refs[:peers], refs[peers:]
    own_ref, other_ref = refs[:2]
    picked_refs, refs = refs[2 : 2 + peers], refs[2 + peers :]
    lists_scratch, picked_scratch = refs
    tiles, length = lists_refs[0].shape
    g_dev = own_ref.shape[1]
    me = lax.axis_index("gauss")
    first = me % 2 == 0
    for k in range(peers):
        lists_scratch[(me // 2) ^ k] = lists_refs[k][...]
    ids = lists_scratch[...].reshape(peers * tiles, length)
    where_own = find(ids, me * g_dev, tiles, cap, g_dev)
    where_other = find(ids, (me ^ 1) * g_dev, tiles, cap, g_dev)
    lanes = iota((peers * cap, g_dev), 1)
    of_own = dot(own_ref[...], one_hot(where_own == lanes), 1, 1)
    of_other = dot(other_ref[...], one_hot(where_other == lanes), 1, 1)
    of_even = jnp.where(first, of_own, of_other)
    of_odd = jnp.where(first, of_other, of_own)
    for p in range(peers):
        block = slice(p * cap, (p + 1) * cap)
        picked_scratch[p] = jnp.concatenate(
            [of_even[:, block], of_odd[:, block]], axis=1
        ).astype(BF16)
    for k in range(peers):
        picked_refs[peers - 1 - k][...] = picked_scratch[(me // 2) ^ k]


def by_tile(values, row):
    out = jnp.full(row.shape, values[-1])
    for t in range(len(values) - 1):
        out = jnp.where(row == t, values[t], out)
    return out


def prepare_kernel(
    tile_pos_ref, cam_index_ref, cams_ref, params_ref, copy_ref, cam_ref, pixel_ref
):
    copy_ref[...] = params_ref[...]
    values, tiles, length = cam_ref.shape
    share = LANES // tiles
    depth = SIDE * SIDE // share
    cam_ids = [cam_index_ref[t] for t in range(tiles)]
    tile_row = iota((tiles, length), 0)
    for j in range(values):
        cam_ref[j] = by_tile([cams_ref[cam_ids[t], j] for t in range(tiles)], tile_row)
    pos = [tile_pos_ref[t] for t in range(tiles)]
    lane = iota((depth, LANES), 1)
    origin_x = [(SIDE * (lax.rem(p, WIN) - WIN // 2)).astype(F32) + 0.5 for p in pos]
    pixel_ref[0] = by_tile(origin_x, lane // share) + (lane % SIDE).astype(F32)
    origin_y = [(SIDE * (lax.div(p, WIN) - WIN // 2)).astype(F32) + 0.5 for p in pos]
    pixel_row = iota((depth, LANES), 0) * (share // SIDE) + (lane % share) // SIDE
    pixel_ref[1] = by_tile(origin_y, lane // share) + pixel_row.astype(F32)


def place_kernel(owners, cap, g_dev, lists_ref, after_ref, hot_ref, local_ref):
    tiles, length = lists_ref.shape
    slots = owners * cap
    ids = lists_ref[...]
    masks = [(ids >= o * g_dev) & (ids < (o + 1) * g_dev) for o in range(owners)]
    rank = ranks(jnp.concatenate([m.astype(jnp.int32) for m in masks], axis=0) > 0, tiles)
    place = jnp.full((tiles, length), -1, jnp.int32)
    local = jnp.zeros((tiles, length), jnp.int32)
    for o in range(owners):
        place = jnp.where(masks[o], rank[o * tiles : (o + 1) * tiles] + o * cap, place)
        local = jnp.where(masks[o], ids - o * g_dev, local)
    slot_iota = iota((slots, length), 0)
    hot_ref[...] = jnp.concatenate(
        [one_hot(slot_iota == place[t : t + 1, :]) for t in range(tiles)], axis=1
    )
    local_ref[...] = local.astype(F32)


def render_kernel(pieces, width, *refs):
    recv_refs, refs = refs[:pieces], refs[pieces:]
    lists_ref, hot_ref, local_ref, cam_ref, pixel_ref, targets_ref = refs[:6]
    pictures_ref, send_ref, rows_ref, table_ref, alpha_ref, weight_ref, part_ref = refs[6:13]
    tiles, length = lists_ref.shape
    share = LANES // tiles
    depth = SIDE * SIDE // share
    live = lists_ref[...] >= 0
    hot = hot_ref[...]

    if pieces == 1:
        listed = dot(recv_refs[0][...].reshape(-1, LANES), hot, 0, 0)[:width]
    else:
        (recv_scratch,) = refs[13:]
        place = lax.axis_index("gauss") // 2
        for k in range(pieces):
            recv_scratch[place ^ k] = recv_refs[pieces - 1 - k][...]
        received = jnp.concatenate([recv_scratch[p] for p in range(pieces)], axis=1)
        listed = dot(received, hot)
    for t in range(tiles):
        rows_ref[t * width : (t + 1) * width, :] = listed[:, t * length : (t + 1) * length]
    rows = [rows_ref[pl.ds(f, tiles, stride=width), :] for f in range(width)]

    cam = [cam_ref[j] for j in range(cam_ref.shape[0])]
    outs, pullback, rays = jax.vjp(lambda r: project(r, cam, live), rows[:10], has_aux=True)
    terms = outs[5:]
    colors = []
    for k in range(3):
        base = 11 + 16 * k
        shade = 0.5 + rows[base]
        for b in range(15):
            shade = shade + rows[base + 1 + b] * terms[b]
        for j in range(5):
            shade = shade + rows[59 + j] * cam[13 + 3 * j + k]
        colors.append(shade)
    opacity = jax.nn.sigmoid(rows[10])
    con_a, con_b, con_c = outs[2], outs[3], outs[4]

    attrs = [
        outs[0],
        outs[1],
        (-0.5 * LOG2E) * con_a,
        -LOG2E * con_b,
        (-0.5 * LOG2E) * con_c,
        jnp.where(live, opacity, 0.0),
    ] + colors
    count = len(attrs)
    blocks = []
    for value in attrs:
        parts = [p.astype(F32) for p in split(value, 3)]
        parts.append(jnp.zeros((16 - 3 * tiles, length), F32))
        blocks.append(jnp.concatenate(parts, axis=0))
    stacked = jnp.concatenate(blocks, axis=1)
    lane_tile = iota((16, LANES), 1) // share
    row_index = iota((16, LANES), 0)
    spread = one_hot((row_index % tiles == lane_tile) & (row_index < 3 * tiles))
    table = dot(stacked.T.astype(BF16), spread)
    pixel_x, pixel_y = pixel_ref[0, :1, :], pixel_ref[1]
    dx = pixel_x - table[:length]
    table_ref[0:length, :] = table[2 * length : 3 * length] * dx * dx
    table_ref[length : 2 * length, :] = table[3 * length : 4 * length] * dx
    table_ref[2 * length : 3 * length, :] = table[length : 2 * length]
    table_ref[3 * length :, :] = table[4 * length :]

    def row(index, l):
        return table_ref[index * length + l : index * length + l + 1, :]

    zero = jnp.zeros((depth, LANES), F32)
    through = jnp.ones((depth, LANES), F32)
    red, green, blue = zero, zero, zero
    for l in range(length):
        dy = pixel_y - row(2, l)
        power = row(0, l) + dy * (row(1, l) + row(3, l) * dy)
        alpha = row(4, l) * jnp.exp2(power)
        weight = through * alpha
        red = red + weight * row(5, l)
        green = green + weight * row(6, l)
        blue = blue + weight * row(7, l)
        through = through - weight
        at = slice(l * depth, (l + 1) * depth)
        alpha_ref[at, :] = alpha
        weight_ref[at, :] = weight
    pictures_ref[0] = red
    pictures_ref[1] = green
    pictures_ref[2] = blue
    res = [red - targets_ref[0], green - targets_ref[1], blue - targets_ref[2]]

    behind = zero
    for l in reversed(range(length)):
        at = slice(l * depth, (l + 1) * depth)
        alpha = alpha_ref[at, :]
        weight = weight_ref[at, :]
        dy = pixel_y - row(2, l)
        seen = row(5, l) * res[0] + row(6, l) * res[1] + row(7, l) * res[2]
        gap = seen - behind
        behind = behind + alpha * gap
        g = weight * gap
        gy = g * dy
        part_ref[0, at, :] = g
        part_ref[1, at, :] = gy
        part_ref[2, at, :] = gy * dy
        for k in range(3):
            part_ref[3 + k, at, :] = weight * res[k]

    def down(index):
        blocks = []
        for first in range(0, length, 8):
            parts = [
                part_ref[index, pl.ds(first * depth + s, 8, stride=depth), :] for s in range(depth)
            ]
            while len(parts) > 1:
                parts = [a + b for a, b in zip(parts[::2], parts[1::2])]
            blocks.append(parts[0])
        return jnp.concatenate(blocks, axis=0)

    sums = [down(index) for index in range(6)]
    g_x = sums[0] * dx
    sums = sums + [g_x, g_x * dx, sums[1] * dx]
    wide = jnp.concatenate([jnp.concatenate(split(s, 3), axis=1) for s in sums], axis=0)
    gather = one_hot(iota((8, 3 * LANES), 0) == (iota((8, 3 * LANES), 1) % LANES) // share)
    reduced = dot(gather, wide, 1, 1)
    g_0, g_y, g_yy, s_0, s_1, s_2, g_x, g_xx, g_xy = [
        reduced[:tiles, q * length : (q + 1) * length] for q in range(len(sums))
    ]

    d_colors = [s_0, s_1, s_2]
    d_terms = []
    for b in range(15):
        d_terms.append(sum(d_colors[k] * rows[12 + 16 * k + b] for k in range(3)))
    d_geometry = [
        con_a * g_x + con_b * g_y,
        con_b * g_x + con_c * g_y,
        -0.5 * g_xx,
        -g_xy,
        -0.5 * g_yy,
    ]
    (d_rows,) = pullback(d_geometry + d_terms)
    values = list(d_rows)
    values.append(g_0 * (1.0 - opacity))
    values.extend(d_colors)
    values.extend(rays)
    for j in range(5):
        values.append(sum(d_colors[k] * cam[13 + 3 * j + k] for k in range(3)))
    values.append(local_ref[...])
    values.extend([jnp.zeros((tiles, length), F32)] * (SENT - len(values)))
    for v in range(SENT):
        rows_ref[pl.ds(v, tiles, stride=width), :] = values[v]
    by_slot = jnp.concatenate(
        [
            jnp.concatenate(split(rows_ref[t * width : t * width + SENT, :], 3), axis=0)
            for t in range(tiles)
        ],
        axis=1,
    )
    by_slot = dot(by_slot, hot, 1, 1)
    by_slot = by_slot[:SENT] + by_slot[SENT : 2 * SENT] + by_slot[2 * SENT :]
    owners, copies, high, _ = send_ref.shape
    cap = hot.shape[0] // owners
    for o in range(owners):
        block = jnp.concatenate(
            [by_slot[r : r + high, o * cap : (o + 1) * cap] for r in range(0, SENT, high)], axis=1
        )
        for c in range(copies):
            send_ref[o, c] = block


def entry_rows(cap, recv_ref):
    blocks, high, _ = recv_ref.shape
    values = jnp.concatenate(
        [
            jnp.concatenate(
                [recv_ref[b, :, first : first + cap] for b in range(blocks)], axis=1
            )
            for first in range(0, SENT * cap // high, cap)
        ],
        axis=0,
    )
    ray_x, ray_y = values[14:15], values[15:16]
    dir_z = lax.rsqrt(ray_x * ray_x + ray_y * ray_y + 1.0)
    terms = sh_terms(ray_x * dir_z, ray_y * dir_z, dir_z)
    terms = jnp.concatenate([jnp.ones_like(dir_z)] + terms, axis=0)
    rows = [values] + [terms * values[11 + k : 12 + k] for k in range(3)]
    parts = split(jnp.concatenate(rows, axis=0), 2)
    return jnp.concatenate(parts, axis=0), values[21:22].astype(jnp.int32)


def scatter(rows, where, first, count):
    hot = one_hot(iota((count, where.shape[1]), 0) + first == where)
    total = dot(rows, hot, 1, 1)
    half = total.shape[0] // 2
    return total[:half] + total[half:]


def in_order(total):
    return jnp.concatenate([total[:11], total[SENT:], total[16:21]], axis=0)


def scatter_kernel(cap, recv_ref, out_ref):
    rows, where = entry_rows(cap, recv_ref)
    out_ref[...] = in_order(scatter(rows, where, 0, out_ref.shape[1]))


def first_kernel(cap, recv_ref, out_ref):
    rows, where = entry_rows(cap, recv_ref)
    out_ref[...] = scatter(rows, where, 0, out_ref.shape[1])


def last_kernel(
    cap, recv_ref, sum_ref, spread_ref, out_ref, pictures_ref, sums, pictures, out_sem, picture_sem
):
    _, tiles, _ = pictures.shape
    depth = spread_ref.shape[1]
    share = LANES // tiles
    lane_block = iota((depth, LANES), 1) // share
    row = iota((depth, LANES), 0) % tiles
    for k in range(3):
        spread = spread_ref[k]
        whole = spread
        for d in range(1, tiles):
            down = pltpu.roll(spread, d, 0)
            up = pltpu.roll(spread, depth + d - tiles, 0)
            moved = pltpu.roll(jnp.where(row >= d, down, up), LANES - d * share, 1)
            whole = jnp.where((row - lane_block) % tiles == d, moved, whole)
        for h in range(depth // tiles):
            pictures[k, :, h * LANES : (h + 1) * LANES] = whole[h * tiles : (h + 1) * tiles]
    copies = [pltpu.make_async_copy(pictures, pictures_ref, picture_sem)]
    copies[0].start()
    rows, where = entry_rows(cap, recv_ref)
    blocks, _, count = sums.shape
    for b in range(blocks):
        columns = slice(b * count, (b + 1) * count)
        sums[b] = in_order(sum_ref[:, columns] + scatter(rows, where, b * count, count))
        copies.append(
            pltpu.make_async_copy(
                sums.at[b], out_ref.at[:, pl.ds(b * count, count)], out_sem.at[b]
            )
        )
        copies[-1].start()
    for copy in copies:
        copy.wait()


def call(kernel, out_shape, args, scalars=0, left=0, out_left=False, scratch=()):
    in_specs = [pl.BlockSpec(memory_space=pltpu.SMEM)] * scalars
    in_specs += [pl.BlockSpec(memory_space=pltpu.VMEM)] * (len(args) - scalars - left)
    in_specs += [pl.BlockSpec(memory_space=pl.ANY)] * left
    many = isinstance(out_shape, (list, tuple))
    spec = pl.BlockSpec(memory_space=pl.ANY if out_left else pltpu.VMEM)
    return pl.pallas_call(
        kernel,
        out_shape=out_shape,
        in_specs=in_specs,
        out_specs=[spec] * len(out_shape) if many else spec,
        scratch_shapes=list(scratch),
        compiler_params=pltpu.CompilerParams(vmem_limit_bytes=VMEM_LIMIT),
    )(*args)


def swap(x, axis, k):
    return lax.ppermute(x, axis, [(i, i ^ k) for i in range(lax.axis_size(axis))])


def crossed(owner, owners):
    return int(owner >= owners // 2)


def far_first(blocks):
    owners, views = lax.axis_size("gauss"), lax.axis_size("view")
    last = len(blocks) - 1
    out = []
    for i, block in enumerate(blocks):
        k = 2 * (last - i)
        pairs = []
        for g in range(owners):
            flip = crossed(g, owners) ^ crossed(g ^ k, owners) if views % 2 == 0 else 0
            pairs += [(g * views + v, (g ^ k) * views + (v ^ flip)) for v in range(views)]
        out.append(lax.ppermute(block, ("gauss", "view"), pairs) if k else block)
    return out


def exchange(x):
    return lax.all_to_all(x, "gauss", split_axis=0, concat_axis=0, tiled=True)


def exchange_wide(x):
    owners, views = lax.axis_size("gauss"), lax.axis_size("view")
    blocks = x.reshape(owners * views // 2, *x.shape[2:])
    groups = [
        [
            g * views + v
            for g in range(owners)
            for v in range(views)
            if v % 2 == c ^ crossed(g, owners)
        ]
        for c in range(2)
    ]
    return lax.all_to_all(
        blocks,
        ("gauss", "view"),
        split_axis=0,
        concat_axis=0,
        axis_index_groups=groups,
        tiled=True,
    )


def power_of_two(n):
    return n & (n - 1) == 0


def shape(dims, dtype):
    return jax.ShapeDtypeStruct(dims, dtype)


def on_device(params, lists, tile_pos, cam_index, cams, targets):
    owners = lax.axis_size("gauss")
    views = lax.axis_size("view")
    width, g_dev = params.shape
    tiles, length = lists.shape
    cap = max(tiles * length // owners, 16)
    slots = owners * cap
    share = LANES // tiles
    depth = SIDE * SIDE // share
    paired = 2 <= owners <= 16 and power_of_two(owners) and LANES == 2 * width
    peers = owners // 2 if paired else 1
    wide = views % 2 == 0 and owners * views <= 32

    if paired:
        other = swap(params, "gauss", 1)
        all_lists = far_first([lists] * peers)
    params_copy, cam, pixel = call(
        prepare_kernel,
        [
            shape((width, g_dev), BF16),
            shape((cams.shape[0], tiles, length), F32),
            shape((2, depth, LANES), F32),
        ],
        (tile_pos, cam_index, cams.T, params),
        scalars=3,
    )
    if paired:
        picked = call(
            functools.partial(pick_pair_kernel, cap, peers),
            [shape((width, 2 * cap), BF16)] * peers,
            (*all_lists[::-1], params_copy, other),
            scratch=(
                pltpu.VMEM((peers, tiles, length), jnp.int32),
                pltpu.VMEM((peers, width, 2 * cap), BF16),
            ),
        )
        returned = far_first(picked)
        after = picked[-1]
    else:
        all_lists = exchange(jnp.broadcast_to(lists[None], (owners, tiles, length)))
        picked = call(
            functools.partial(pick_kernel, tiles, cap),
            shape((slots, LANES), BF16),
            (all_lists.reshape(owners * tiles, length), params_copy),
        )
        returned = [exchange(picked.reshape(owners, cap, LANES))]
        after = picked
    hot, local = call(
        functools.partial(place_kernel, owners, cap, g_dev),
        [shape((slots, tiles * length), BF16), shape((tiles, length), F32)],
        (lists, after),
        left=1,
    )
    spread_targets = (
        targets.reshape(3, tiles, depth, share).transpose(0, 2, 1, 3).reshape(3, depth, LANES)
    )
    copies = views // 2 if wide else 1
    high = SENT * cap // LANES
    pictures, sent = call(
        functools.partial(render_kernel, peers, width),
        [shape((3, depth, LANES), F32), shape((owners, copies, high, LANES), F32)],
        (*returned, lists, hot, local, cam, pixel, spread_targets),
        scratch=(
            pltpu.VMEM((tiles * width, length), F32),
            pltpu.VMEM((8 * length, LANES), F32),
            pltpu.VMEM((length * depth, LANES), F32),
            pltpu.VMEM((length * depth, LANES), F32),
            pltpu.VMEM((6, length * depth, LANES), F32),
            pltpu.VMEM((peers, *returned[0].shape[-2:]), BF16),
        ),
    )
    if wide:
        received = exchange_wide(sent)
        other = swap(received, "view", 1)
        total = call(
            functools.partial(first_kernel, cap), shape((SENT + 48, g_dev), F32), (received,)
        )
        parts = 4
        grads, pictures = call(
            functools.partial(last_kernel, cap),
            [shape((width, g_dev), F32), shape(targets.shape, F32)],
            (other, total, pictures),
            out_left=True,
            scratch=(
                pltpu.VMEM((parts, width, g_dev // parts), F32),
                pltpu.VMEM(targets.shape, F32),
                pltpu.SemaphoreType.DMA((parts,)),
                pltpu.SemaphoreType.DMA,
            ),
        )
        return (pictures, grads)
    pictures = (
        pictures.reshape(3, depth, tiles, share)
        .transpose(0, 2, 1, 3)
        .reshape(3, tiles, SIDE * SIDE)
    )
    received = exchange(sent[:, 0])
    grads = call(
        functools.partial(scatter_kernel, cap), shape((width, g_dev), F32), (received,)
    )
    return (pictures, lax.psum(grads, "view"))


def solution(mesh):
    return jax.shard_map(
        on_device,
        mesh=mesh,
        in_specs=(
            P(None, "gauss"),
            P(("gauss", "view"), None),
            P(("gauss", "view")),
            P(("gauss", "view")),
            P(),
            P(None, ("gauss", "view"), None),
        ),
        out_specs=(P(None, ("gauss", "view"), None), P(None, "gauss")),
        check_vma=False,
    )
```

```python
import functools
import math

import jax
import jax.numpy as jnp
from jax import lax
from jax.experimental import pallas as pl
from jax.experimental.pallas import tpu as pltpu
from jax.sharding import PartitionSpec as P

WIN = 16
SIDE = 16
LANES = 128
LOG2E = math.log2(math.e)
F32 = jnp.float32
BF16 = jnp.bfloat16
VMEM_LIMIT = 24 * 2**20
SENT = 32


def sh_terms(x, y, z):
    xx, yy, zz = x * x, y * y, z * z
    xy = x * y
    diff = xx - yy
    five = 5.0 * zz - 1.0
    return [
        x,
        y,
        z,
        xy,
        y * z,
        x * z,
        diff,
        3.0 * zz - 1.0,
        x * (xx - 3.0 * yy),
        xy * z,
        y * (3.0 * xx - yy),
        z * diff,
        x * five,
        y * five,
        z * (5.0 * zz - 3.0),
    ]


def project(rows, cam, live):
    mx, my, mz = rows[0], rows[1], rows[2]
    cam_x = cam[0] * mx + cam[1] * my + cam[2] * mz + cam[9]
    cam_y = cam[3] * mx + cam[4] * my + cam[5] * mz + cam[10]
    cam_z = cam[6] * mx + cam[7] * my + cam[8] * mz + cam[11]
    cam_z = jnp.where(live, cam_z, 1.0)
    inv_z = 1.0 / cam_z
    qw, qx, qy, qz = rows[6], rows[7], rows[8], rows[9]
    qw = jnp.where(live, qw, 1.0)
    inv_q = lax.rsqrt(qw * qw + qx * qx + qy * qy + qz * qz)
    qw, qx, qy, qz = qw * inv_q, qx * inv_q, qy * inv_q, qz * inv_q
    rot = [
        [
            1.0 - 2.0 * (qy * qy + qz * qz),
            2.0 * (qx * qy - qw * qz),
            2.0 * (qx * qz + qw * qy),
        ],
        [
            2.0 * (qx * qy + qw * qz),
            1.0 - 2.0 * (qx * qx + qz * qz),
            2.0 * (qy * qz - qw * qx),
        ],
        [
            2.0 * (qx * qz - qw * qy),
            2.0 * (qy * qz + qw * qx),
            1.0 - 2.0 * (qx * qx + qy * qy),
        ],
    ]
    mixed = [
        [
            cam[3 * i] * rot[0][k] + cam[3 * i + 1] * rot[1][k] + cam[3 * i + 2] * rot[2][k]
            for k in range(3)
        ]
        for i in range(3)
    ]
    scale = cam[12] * inv_z
    ray_x, ray_y = cam_x * inv_z, cam_y * inv_z
    proj_u = [scale * (mixed[0][k] - ray_x * mixed[2][k]) for k in range(3)]
    proj_v = [scale * (mixed[1][k] - ray_y * mixed[2][k]) for k in range(3)]
    var = [jnp.exp(2.0 * rows[3 + k]) for k in range(3)]
    uv = [proj_u[k] * var[k] for k in range(3)]
    cov_a = sum(uv[k] * proj_u[k] for k in range(3)) + 0.3
    cov_b = sum(uv[k] * proj_v[k] for k in range(3))
    cov_c = sum(proj_v[k] * proj_v[k] * var[k] for k in range(3)) + 0.3
    inv_det = 1.0 / (cov_a * cov_c - cov_b * cov_b)
    inv_dist = lax.rsqrt(cam_x * cam_x + cam_y * cam_y + cam_z * cam_z)
    terms = sh_terms(cam_x * inv_dist, cam_y * inv_dist, cam_z * inv_dist)
    geometry = [cam_x * scale, cam_y * scale, cov_c * inv_det, -cov_b * inv_det, cov_a * inv_det]
    return geometry + terms, (ray_x, ray_y)


def iota(shape, dim):
    return lax.broadcasted_iota(jnp.int32, shape, dim)


def one_hot(mask):
    return jnp.where(mask, 1.0, 0.0).astype(BF16)


def dot(lhs, rhs, lhs_dim=1, rhs_dim=0):
    return lax.dot_general(
        lhs, rhs, (((lhs_dim,), (rhs_dim,)), ((), ())), preferred_element_type=F32
    )


def split(x, parts):
    out = []
    for _ in range(parts):
        head = x.astype(BF16)
        out.append(head)
        x = x - head.astype(F32)
    return out


def ranks(mask, tiles):
    rows, length = mask.shape
    bits = jnp.where(mask, 1.0, 0.0)
    place = iota((rows, length), 0) % tiles
    shifted = [bits] + [
        jnp.where(place >= d, pltpu.roll(bits, d, 0), 0.0) for d in range(1, tiles)
    ]
    earlier = one_hot(iota((length, length), 0) < iota((length, length), 1))
    counted = jnp.concatenate([earlier] + [jnp.ones_like(earlier)] * (tiles - 1), axis=0)
    return dot(jnp.concatenate(shifted, axis=1).astype(BF16), counted).astype(jnp.int32)


def find(ids, base, tiles, cap, g_dev):
    local = ids - base
    mine = (local >= 0) & (local < g_dev)
    key = jnp.where(mine, ranks(mine, tiles), -1)
    rows, length = ids.shape
    slot = iota((cap, length), 0)
    found = []
    for r in range(0, rows, tiles):
        total = jnp.zeros((cap, length), jnp.int32)
        for t in range(r, r + tiles):
            total = total + jnp.where(key[t : t + 1, :] == slot, local[t : t + 1, :], 0)
        found.append(jnp.sum(total, axis=1, keepdims=True))
    return jnp.concatenate(found, axis=0)


def pick_kernel(tiles, cap, lists_ref, params_ref, picked_ref):
    width, g_dev = params_ref.shape
    where = find(lists_ref[...], lax.axis_index("gauss") * g_dev, tiles, cap, g_dev)
    hot = one_hot(where == iota((where.shape[0], g_dev), 1))
    wide = jnp.concatenate([params_ref[...], jnp.zeros((LANES - width, g_dev), BF16)], axis=0)
    picked_ref[...] = dot(hot, wide, 1, 1).astype(BF16)


def pick_near_kernel(
    cap,
    far_lists_ref,
    third_ref,
    second_ref,
    first_ref,
    own_ref,
    lists_ref,
    answer_ref,
    far_answer_ref,
    scratch,
):
    tiles, _ = lists_ref.shape
    g_dev = own_ref.shape[1]
    me = lax.axis_index("gauss")
    ids = jnp.concatenate([lists_ref[...], far_lists_ref[...]], axis=0)
    near = [own_ref, first_ref, second_ref, third_ref]
    lanes = iota((2 * cap, g_dev), 1)
    for r in range(4):
        where = find(ids, (me ^ r) * g_dev, tiles, cap, g_dev)
        scratch[(me % 4) ^ r] = dot(near[r][...], one_hot(where == lanes), 1, 1)
    for ref, block in ((answer_ref, slice(0, cap)), (far_answer_ref, slice(cap, 2 * cap))):
        ref[...] = jnp.concatenate([scratch[n][:, block] for n in range(4)], axis=1).astype(BF16)


def by_tile(values, row):
    out = jnp.full(row.shape, values[-1])
    for t in range(len(values) - 1):
        out = jnp.where(row == t, values[t], out)
    return out


def prepare_kernel(
    tile_pos_ref, cam_index_ref, cams_ref, params_ref, copy_ref, cam_ref, pixel_ref
):
    copy_ref[...] = params_ref[...]
    values, tiles, length = cam_ref.shape
    share = LANES // tiles
    depth = SIDE * SIDE // share
    cam_ids = [cam_index_ref[t] for t in range(tiles)]
    tile_row = iota((tiles, length), 0)
    for j in range(values):
        cam_ref[j] = by_tile([cams_ref[cam_ids[t], j] for t in range(tiles)], tile_row)
    pos = [tile_pos_ref[t] for t in range(tiles)]
    lane = iota((depth, LANES), 1)
    origin_x = [(SIDE * (lax.rem(p, WIN) - WIN // 2)).astype(F32) + 0.5 for p in pos]
    pixel_ref[0] = by_tile(origin_x, lane // share) + (lane % SIDE).astype(F32)
    origin_y = [(SIDE * (lax.div(p, WIN) - WIN // 2)).astype(F32) + 0.5 for p in pos]
    pixel_row = iota((depth, LANES), 0) * (share // SIDE) + (lane % share) // SIDE
    pixel_ref[1] = by_tile(origin_y, lane // share) + pixel_row.astype(F32)


def place_kernel(owners, cap, g_dev, lists_ref, after_ref, hot_ref, local_ref):
    tiles, length = lists_ref.shape
    slots = owners * cap
    ids = lists_ref[...]
    masks = [(ids >= o * g_dev) & (ids < (o + 1) * g_dev) for o in range(owners)]
    rank = ranks(jnp.concatenate([m.astype(jnp.int32) for m in masks], axis=0) > 0, tiles)
    place = jnp.full((tiles, length), -1, jnp.int32)
    local = jnp.zeros((tiles, length), jnp.int32)
    for o in range(owners):
        place = jnp.where(masks[o], rank[o * tiles : (o + 1) * tiles] + o * cap, place)
        local = jnp.where(masks[o], ids - o * g_dev, local)
    slot_iota = iota((slots, length), 0)
    hot_ref[...] = jnp.concatenate(
        [one_hot(slot_iota == place[t : t + 1, :]) for t in range(tiles)], axis=1
    )
    local_ref[...] = local.astype(F32)


def render_kernel(pieces, width, *refs):
    recv_refs, refs = refs[:pieces], refs[pieces:]
    lists_ref, hot_ref, local_ref, cam_ref, pixel_ref, targets_ref = refs[:6]
    pictures_ref, send_ref, rows_ref, table_ref, alpha_ref, weight_ref, part_ref = refs[6:13]
    tiles, length = lists_ref.shape
    share = LANES // tiles
    depth = SIDE * SIDE // share
    live = lists_ref[...] >= 0
    hot = hot_ref[...]

    if pieces == 1:
        listed = dot(recv_refs[0][...].reshape(-1, LANES), hot, 0, 0)[:width]
    else:
        own, far = recv_refs[0][...], recv_refs[1][...]
        low = lax.axis_index("gauss") < 4
        received = jnp.concatenate([jnp.where(low, own, far), jnp.where(low, far, own)], axis=1)
        listed = dot(received, hot)
    for t in range(tiles):
        rows_ref[t * width : (t + 1) * width, :] = listed[:, t * length : (t + 1) * length]
    rows = [rows_ref[pl.ds(f, tiles, stride=width), :] for f in range(width)]

    cam = [cam_ref[j] for j in range(cam_ref.shape[0])]
    outs, pullback, rays = jax.vjp(lambda r: project(r, cam, live), rows[:10], has_aux=True)
    terms = outs[5:]
    colors = []
    for k in range(3):
        base = 11 + 16 * k
        shade = 0.5 + rows[base]
        for b in range(15):
            shade = shade + rows[base + 1 + b] * terms[b]
        for j in range(5):
            shade = shade + rows[59 + j] * cam[13 + 3 * j + k]
        colors.append(shade)
    opacity = jax.nn.sigmoid(rows[10])
    con_a, con_b, con_c = outs[2], outs[3], outs[4]

    attrs = [
        outs[0],
        outs[1],
        (-0.5 * LOG2E) * con_a,
        -LOG2E * con_b,
        (-0.5 * LOG2E) * con_c,
        jnp.where(live, opacity, 0.0),
    ] + colors
    count = len(attrs)
    blocks = []
    for value in attrs:
        parts = [p.astype(F32) for p in split(value, 3)]
        parts.append(jnp.zeros((16 - 3 * tiles, length), F32))
        blocks.append(jnp.concatenate(parts, axis=0))
    stacked = jnp.concatenate(blocks, axis=1)
    lane_tile = iota((16, LANES), 1) // share
    row_index = iota((16, LANES), 0)
    spread = one_hot((row_index % tiles == lane_tile) & (row_index < 3 * tiles))
    table = dot(stacked.T.astype(BF16), spread)
    pixel_x, pixel_y = pixel_ref[0, :1, :], pixel_ref[1]
    dx = pixel_x - table[:length]
    table_ref[0:length, :] = table[2 * length : 3 * length] * dx * dx
    table_ref[length : 2 * length, :] = table[3 * length : 4 * length] * dx
    table_ref[2 * length : 3 * length, :] = table[length : 2 * length]
    table_ref[3 * length :, :] = table[4 * length :]

    def row(index, l):
        return table_ref[index * length + l : index * length + l + 1, :]

    zero = jnp.zeros((depth, LANES), F32)
    through = jnp.ones((depth, LANES), F32)
    red, green, blue = zero, zero, zero
    for l in range(length):
        dy = pixel_y - row(2, l)
        power = row(0, l) + dy * (row(1, l) + row(3, l) * dy)
        alpha = row(4, l) * jnp.exp2(power)
        weight = through * alpha
        red = red + weight * row(5, l)
        green = green + weight * row(6, l)
        blue = blue + weight * row(7, l)
        through = through - weight
        at = slice(l * depth, (l + 1) * depth)
        alpha_ref[at, :] = alpha
        weight_ref[at, :] = weight
    pictures_ref[0] = red
    pictures_ref[1] = green
    pictures_ref[2] = blue
    res = [red - targets_ref[0], green - targets_ref[1], blue - targets_ref[2]]

    behind = zero
    for l in reversed(range(length)):
        at = slice(l * depth, (l + 1) * depth)
        alpha = alpha_ref[at, :]
        weight = weight_ref[at, :]
        dy = pixel_y - row(2, l)
        seen = row(5, l) * res[0] + row(6, l) * res[1] + row(7, l) * res[2]
        gap = seen - behind
        behind = behind + alpha * gap
        g = weight * gap
        gy = g * dy
        part_ref[0, at, :] = g
        part_ref[1, at, :] = gy
        part_ref[2, at, :] = gy * dy
        for k in range(3):
            part_ref[3 + k, at, :] = weight * res[k]

    def down(index):
        blocks = []
        for first in range(0, length, 8):
            parts = [
                part_ref[index, pl.ds(first * depth + s, 8, stride=depth), :] for s in range(depth)
            ]
            while len(parts) > 1:
                parts = [a + b for a, b in zip(parts[::2], parts[1::2])]
            blocks.append(parts[0])
        return jnp.concatenate(blocks, axis=0)

    sums = [down(index) for index in range(6)]
    g_x = sums[0] * dx
    sums = sums + [g_x, g_x * dx, sums[1] * dx]
    wide = jnp.concatenate([jnp.concatenate(split(s, 3), axis=1) for s in sums], axis=0)
    gather = one_hot(iota((8, 3 * LANES), 0) == (iota((8, 3 * LANES), 1) % LANES) // share)
    reduced = dot(gather, wide, 1, 1)
    g_0, g_y, g_yy, s_0, s_1, s_2, g_x, g_xx, g_xy = [
        reduced[:tiles, q * length : (q + 1) * length] for q in range(len(sums))
    ]

    d_colors = [s_0, s_1, s_2]
    d_terms = []
    for b in range(15):
        d_terms.append(sum(d_colors[k] * rows[12 + 16 * k + b] for k in range(3)))
    d_geometry = [
        con_a * g_x + con_b * g_y,
        con_b * g_x + con_c * g_y,
        -0.5 * g_xx,
        -g_xy,
        -0.5 * g_yy,
    ]
    (d_rows,) = pullback(d_geometry + d_terms)
    values = list(d_rows)
    values.append(g_0 * (1.0 - opacity))
    values.extend(d_colors)
    values.extend(rays)
    for j in range(5):
        values.append(sum(d_colors[k] * cam[13 + 3 * j + k] for k in range(3)))
    values.append(local_ref[...])
    values.extend([jnp.zeros((tiles, length), F32)] * (SENT - len(values)))
    for v in range(SENT):
        rows_ref[pl.ds(v, tiles, stride=width), :] = values[v]
    by_slot = jnp.concatenate(
        [
            jnp.concatenate(split(rows_ref[t * width : t * width + SENT, :], 3), axis=0)
            for t in range(tiles)
        ],
        axis=1,
    )
    by_slot = dot(by_slot, hot, 1, 1)
    by_slot = by_slot[:SENT] + by_slot[SENT : 2 * SENT] + by_slot[2 * SENT :]
    owners, copies, high, _ = send_ref.shape
    cap = hot.shape[0] // owners
    for o in range(owners):
        block = jnp.concatenate(
            [by_slot[r : r + high, o * cap : (o + 1) * cap] for r in range(0, SENT, high)], axis=1
        )
        for c in range(copies):
            send_ref[o, c] = block


def entry_rows(cap, recv_ref):
    blocks, high, _ = recv_ref.shape
    values = jnp.concatenate(
        [
            jnp.concatenate(
                [recv_ref[b, :, first : first + cap] for b in range(blocks)], axis=1
            )
            for first in range(0, SENT * cap // high, cap)
        ],
        axis=0,
    )
    ray_x, ray_y = values[14:15], values[15:16]
    dir_z = lax.rsqrt(ray_x * ray_x + ray_y * ray_y + 1.0)
    terms = sh_terms(ray_x * dir_z, ray_y * dir_z, dir_z)
    terms = jnp.concatenate([jnp.ones_like(dir_z)] + terms, axis=0)
    rows = [values] + [terms * values[11 + k : 12 + k] for k in range(3)]
    parts = split(jnp.concatenate(rows, axis=0), 2)
    return jnp.concatenate(parts, axis=0), values[21:22].astype(jnp.int32)


def scatter(rows, where, first, count):
    hot = one_hot(iota((count, where.shape[1]), 0) + first == where)
    total = dot(rows, hot, 1, 1)
    half = total.shape[0] // 2
    return total[:half] + total[half:]


def in_order(total):
    return jnp.concatenate([total[:11], total[SENT:], total[16:21]], axis=0)


def scatter_kernel(cap, recv_ref, out_ref):
    rows, where = entry_rows(cap, recv_ref)
    out_ref[...] = in_order(scatter(rows, where, 0, out_ref.shape[1]))


def first_kernel(cap, recv_ref, out_ref):
    rows, where = entry_rows(cap, recv_ref)
    out_ref[...] = scatter(rows, where, 0, out_ref.shape[1])


def last_kernel(
    cap, recv_ref, sum_ref, spread_ref, out_ref, pictures_ref, sums, pictures, out_sem, picture_sem
):
    _, tiles, _ = pictures.shape
    depth = spread_ref.shape[1]
    share = LANES // tiles
    lane_block = iota((depth, LANES), 1) // share
    row = iota((depth, LANES), 0) % tiles
    for k in range(3):
        spread = spread_ref[k]
        whole = spread
        for d in range(1, tiles):
            down = pltpu.roll(spread, d, 0)
            up = pltpu.roll(spread, depth + d - tiles, 0)
            moved = pltpu.roll(jnp.where(row >= d, down, up), LANES - d * share, 1)
            whole = jnp.where((row - lane_block) % tiles == d, moved, whole)
        for h in range(depth // tiles):
            pictures[k, :, h * LANES : (h + 1) * LANES] = whole[h * tiles : (h + 1) * tiles]
    copies = [pltpu.make_async_copy(pictures, pictures_ref, picture_sem)]
    copies[0].start()
    rows, where = entry_rows(cap, recv_ref)
    blocks, _, count = sums.shape
    for b in range(blocks):
        columns = slice(b * count, (b + 1) * count)
        sums[b] = in_order(sum_ref[:, columns] + scatter(rows, where, b * count, count))
        copies.append(
            pltpu.make_async_copy(
                sums.at[b], out_ref.at[:, pl.ds(b * count, count)], out_sem.at[b]
            )
        )
        copies[-1].start()
    for copy in copies:
        copy.wait()


def call(kernel, out_shape, args, scalars=0, left=0, out_left=False, scratch=()):
    in_specs = [pl.BlockSpec(memory_space=pltpu.SMEM)] * scalars
    in_specs += [pl.BlockSpec(memory_space=pltpu.VMEM)] * (len(args) - scalars - left)
    in_specs += [pl.BlockSpec(memory_space=pl.ANY)] * left
    many = isinstance(out_shape, (list, tuple))
    spec = pl.BlockSpec(memory_space=pl.ANY if out_left else pltpu.VMEM)
    return pl.pallas_call(
        kernel,
        out_shape=out_shape,
        in_specs=in_specs,
        out_specs=[spec] * len(out_shape) if many else spec,
        scratch_shapes=list(scratch),
        compiler_params=pltpu.CompilerParams(vmem_limit_bytes=VMEM_LIMIT),
    )(*args)


def swap(x, axis, k):
    return lax.ppermute(x, axis, [(i, i ^ k) for i in range(lax.axis_size(axis))])


def crossed(owner, owners):
    return int(owner >= owners // 2)


def reach(x, step):
    owners, views = lax.axis_size("gauss"), lax.axis_size("view")
    flip = int(step > 1)
    pairs = [
        (g * views + v, (g ^ step) * views + (v ^ flip))
        for g in range(owners)
        for v in range(views)
    ]
    return lax.ppermute(x, ("gauss", "view"), pairs)


def exchange(x):
    return lax.all_to_all(x, "gauss", split_axis=0, concat_axis=0, tiled=True)


def exchange_wide(x):
    owners, views = lax.axis_size("gauss"), lax.axis_size("view")
    blocks = x.reshape(owners * views // 2, *x.shape[2:])
    groups = [
        [
            g * views + v
            for g in range(owners)
            for v in range(views)
            if v % 2 == c ^ crossed(g, owners)
        ]
        for c in range(2)
    ]
    return lax.all_to_all(
        blocks,
        ("gauss", "view"),
        split_axis=0,
        concat_axis=0,
        axis_index_groups=groups,
        tiled=True,
    )


def shape(dims, dtype):
    return jax.ShapeDtypeStruct(dims, dtype)


def on_device(params, lists, tile_pos, cam_index, cams, targets):
    owners = lax.axis_size("gauss")
    views = lax.axis_size("view")
    width, g_dev = params.shape
    tiles, length = lists.shape
    cap = max(tiles * length // owners, 16)
    slots = owners * cap
    share = LANES // tiles
    depth = SIDE * SIDE // share
    near = owners == 8 and views % 2 == 0
    wide = views % 2 == 0 and owners * views <= 32

    if near:
        third, second, first = [reach(params, step) for step in (3, 2, 1)]
        far_lists = reach(lists, 4)
    params_copy, cam, pixel = call(
        prepare_kernel,
        [
            shape((width, g_dev), BF16),
            shape((cams.shape[0], tiles, length), F32),
            shape((2, depth, LANES), F32),
        ],
        (tile_pos, cam_index, cams.T, params),
        scalars=3,
    )
    if near:
        answer, far_answer = call(
            functools.partial(pick_near_kernel, cap),
            [shape((width, 4 * cap), BF16)] * 2,
            (far_lists, third, second, first, params_copy, lists),
            scratch=(pltpu.VMEM((4, width, 2 * cap), F32),),
        )
        returned = [answer, reach(far_answer, 4)]
        after = answer
    else:
        all_lists = exchange(jnp.broadcast_to(lists[None], (owners, tiles, length)))
        picked = call(
            functools.partial(pick_kernel, tiles, cap),
            shape((slots, LANES), BF16),
            (all_lists.reshape(owners * tiles, length), params_copy),
        )
        returned = [exchange(picked.reshape(owners, cap, LANES))]
        after = picked
    hot, local = call(
        functools.partial(place_kernel, owners, cap, g_dev),
        [shape((slots, tiles * length), BF16), shape((tiles, length), F32)],
        (lists, after),
        left=1,
    )
    spread_targets = (
        targets.reshape(3, tiles, depth, share).transpose(0, 2, 1, 3).reshape(3, depth, LANES)
    )
    copies = views // 2 if wide else 1
    high = SENT * cap // LANES
    pictures, sent = call(
        functools.partial(render_kernel, len(returned), width),
        [shape((3, depth, LANES), F32), shape((owners, copies, high, LANES), F32)],
        (*returned, lists, hot, local, cam, pixel, spread_targets),
        scratch=(
            pltpu.VMEM((tiles * width, length), F32),
            pltpu.VMEM((8 * length, LANES), F32),
            pltpu.VMEM((length * depth, LANES), F32),
            pltpu.VMEM((length * depth, LANES), F32),
            pltpu.VMEM((6, length * depth, LANES), F32),
        ),
    )
    if wide:
        received = exchange_wide(sent)
        other = swap(received, "view", 1)
        total = call(
            functools.partial(first_kernel, cap), shape((SENT + 48, g_dev), F32), (received,)
        )
        parts = 4
        grads, pictures = call(
            functools.partial(last_kernel, cap),
            [shape((width, g_dev), F32), shape(targets.shape, F32)],
            (other, total, pictures),
            out_left=True,
            scratch=(
                pltpu.VMEM((parts, width, g_dev // parts), F32),
                pltpu.VMEM(targets.shape, F32),
                pltpu.SemaphoreType.DMA((parts,)),
                pltpu.SemaphoreType.DMA,
            ),
        )
        return (pictures, grads)
    pictures = (
        pictures.reshape(3, depth, tiles, share)
        .transpose(0, 2, 1, 3)
        .reshape(3, tiles, SIDE * SIDE)
    )
    received = exchange(sent[:, 0])
    grads = call(
        functools.partial(scatter_kernel, cap), shape((width, g_dev), F32), (received,)
    )
    return (pictures, lax.psum(grads, "view"))


def solution(mesh):
    return jax.shard_map(
        on_device,
        mesh=mesh,
        in_specs=(
            P(None, "gauss"),
            P(("gauss", "view"), None),
            P(("gauss", "view")),
            P(("gauss", "view")),
            P(),
            P(None, ("gauss", "view"), None),
        ),
        out_specs=(P(None, ("gauss", "view"), None), P(None, "gauss")),
        check_vma=False,
    )
```

```python
import functools
import math

import jax
import jax.numpy as jnp
from jax import lax
from jax.experimental import pallas as pl
from jax.experimental.pallas import tpu as pltpu
from jax.sharding import PartitionSpec as P

WIN = 16
SIDE = 16
LANES = 128
LOG2E = math.log2(math.e)
F32 = jnp.float32
BF16 = jnp.bfloat16
VMEM_LIMIT = 24 * 2**20
SENT = 32


def sh_terms(x, y, z):
    xx, yy, zz = x * x, y * y, z * z
    xy = x * y
    diff = xx - yy
    five = 5.0 * zz - 1.0
    return [
        x,
        y,
        z,
        xy,
        y * z,
        x * z,
        diff,
        3.0 * zz - 1.0,
        x * (xx - 3.0 * yy),
        xy * z,
        y * (3.0 * xx - yy),
        z * diff,
        x * five,
        y * five,
        z * (5.0 * zz - 3.0),
    ]


def project(rows, cam, live):
    mx, my, mz = rows[0], rows[1], rows[2]
    cam_x = cam[0] * mx + cam[1] * my + cam[2] * mz + cam[9]
    cam_y = cam[3] * mx + cam[4] * my + cam[5] * mz + cam[10]
    cam_z = cam[6] * mx + cam[7] * my + cam[8] * mz + cam[11]
    cam_z = jnp.where(live, cam_z, 1.0)
    inv_z = 1.0 / cam_z
    qw, qx, qy, qz = rows[6], rows[7], rows[8], rows[9]
    qw = jnp.where(live, qw, 1.0)
    inv_q = lax.rsqrt(qw * qw + qx * qx + qy * qy + qz * qz)
    qw, qx, qy, qz = qw * inv_q, qx * inv_q, qy * inv_q, qz * inv_q
    rot = [
        [
            1.0 - 2.0 * (qy * qy + qz * qz),
            2.0 * (qx * qy - qw * qz),
            2.0 * (qx * qz + qw * qy),
        ],
        [
            2.0 * (qx * qy + qw * qz),
            1.0 - 2.0 * (qx * qx + qz * qz),
            2.0 * (qy * qz - qw * qx),
        ],
        [
            2.0 * (qx * qz - qw * qy),
            2.0 * (qy * qz + qw * qx),
            1.0 - 2.0 * (qx * qx + qy * qy),
        ],
    ]
    mixed = [
        [
            cam[3 * i] * rot[0][k] + cam[3 * i + 1] * rot[1][k] + cam[3 * i + 2] * rot[2][k]
            for k in range(3)
        ]
        for i in range(3)
    ]
    scale = cam[12] * inv_z
    ray_x, ray_y = cam_x * inv_z, cam_y * inv_z
    proj_u = [scale * (mixed[0][k] - ray_x * mixed[2][k]) for k in range(3)]
    proj_v = [scale * (mixed[1][k] - ray_y * mixed[2][k]) for k in range(3)]
    var = [jnp.exp(2.0 * rows[3 + k]) for k in range(3)]
    uv = [proj_u[k] * var[k] for k in range(3)]
    cov_a = sum(uv[k] * proj_u[k] for k in range(3)) + 0.3
    cov_b = sum(uv[k] * proj_v[k] for k in range(3))
    cov_c = sum(proj_v[k] * proj_v[k] * var[k] for k in range(3)) + 0.3
    inv_det = 1.0 / (cov_a * cov_c - cov_b * cov_b)
    inv_dist = lax.rsqrt(cam_x * cam_x + cam_y * cam_y + cam_z * cam_z)
    terms = sh_terms(cam_x * inv_dist, cam_y * inv_dist, cam_z * inv_dist)
    geometry = [cam_x * scale, cam_y * scale, cov_c * inv_det, -cov_b * inv_det, cov_a * inv_det]
    return geometry + terms, (ray_x, ray_y)


def iota(shape, dim):
    return lax.broadcasted_iota(jnp.int32, shape, dim)


def one_hot(mask):
    return jnp.where(mask, 1.0, 0.0).astype(BF16)


def dot(lhs, rhs, lhs_dim=1, rhs_dim=0):
    return lax.dot_general(
        lhs, rhs, (((lhs_dim,), (rhs_dim,)), ((), ())), preferred_element_type=F32
    )


def split(x, parts):
    out = []
    for _ in range(parts):
        head = x.astype(BF16)
        out.append(head)
        x = x - head.astype(F32)
    return out


def ranks(mask, tiles):
    rows, length = mask.shape
    bits = jnp.where(mask, 1.0, 0.0)
    place = iota((rows, length), 0) % tiles
    shifted = [bits] + [
        jnp.where(place >= d, pltpu.roll(bits, d, 0), 0.0) for d in range(1, tiles)
    ]
    earlier = one_hot(iota((length, length), 0) < iota((length, length), 1))
    counted = jnp.concatenate([earlier] + [jnp.ones_like(earlier)] * (tiles - 1), axis=0)
    return dot(jnp.concatenate(shifted, axis=1).astype(BF16), counted).astype(jnp.int32)


def find(local, tiles, cap, g_dev):
    mine = (local >= 0) & (local < g_dev)
    key = jnp.where(mine, ranks(mine, tiles), -1)
    rows, length = local.shape
    slot = iota((cap, length), 0)
    found = []
    for r in range(0, rows, tiles):
        total = jnp.zeros((cap, length), jnp.int32)
        for t in range(r, r + tiles):
            total = total + jnp.where(key[t : t + 1, :] == slot, local[t : t + 1, :], 0)
        found.append(jnp.sum(total, axis=1, keepdims=True))
    return jnp.concatenate(found, axis=0)


def pick_kernel(tiles, cap, lists_ref, params_ref, picked_ref):
    width, g_dev = params_ref.shape
    where = find(lists_ref[...] - lax.axis_index("gauss") * g_dev, tiles, cap, g_dev)
    hot = one_hot(where == iota((where.shape[0], g_dev), 1))
    wide = jnp.concatenate([params_ref[...], jnp.zeros((LANES - width, g_dev), BF16)], axis=0)
    picked_ref[...] = dot(hot, wide, 1, 1).astype(BF16)


def pick_near_kernel(
    cap,
    far_lists_ref,
    got_ref,
    got_by_ref,
    third_ref,
    third_by_ref,
    own_ref,
    lists_ref,
    answer_ref,
    far_answer_ref,
    scratch,
):
    tiles, _ = lists_ref.shape
    g_dev = own_ref.shape[1]
    me = lax.axis_index("gauss")
    core_0 = lax.axis_index("view") % 2 == 0
    ids = jnp.concatenate([lists_ref[...], far_lists_ref[...]], axis=0)
    local = jnp.concatenate([ids - (me ^ r) * g_dev for r in range(4)], axis=0)
    where = find(local, tiles, cap, g_dev)
    got, got_by = got_ref[...], got_by_ref[...]
    near = [
        own_ref[...],
        jnp.where(core_0, got, got_by),
        jnp.where(core_0, got_by, got),
        jnp.where(core_0, third_by_ref[...], third_ref[...]),
    ]
    lanes = iota((2 * cap, g_dev), 1)
    for r in range(4):
        hot = one_hot(where[2 * r * cap : 2 * (r + 1) * cap] == lanes)
        scratch[(me % 4) ^ r] = dot(near[r], hot, 1, 1)
    for ref, block in ((answer_ref, slice(0, cap)), (far_answer_ref, slice(cap, 2 * cap))):
        ref[...] = jnp.concatenate([scratch[n][:, block] for n in range(4)], axis=1).astype(BF16)


def by_tile(values, row):
    out = jnp.full(row.shape, values[-1])
    for t in range(len(values) - 1):
        out = jnp.where(row == t, values[t], out)
    return out


def prepare_kernel(
    tile_pos_ref, cam_index_ref, cams_ref, params_ref, copy_ref, cam_ref, pixel_ref
):
    copy_ref[...] = params_ref[...]
    values, tiles, length = cam_ref.shape
    share = LANES // tiles
    depth = SIDE * SIDE // share
    cam_ids = [cam_index_ref[t] for t in range(tiles)]
    tile_row = iota((tiles, length), 0)
    for j in range(values):
        cam_ref[j] = by_tile([cams_ref[cam_ids[t], j] for t in range(tiles)], tile_row)
    pos = [tile_pos_ref[t] for t in range(tiles)]
    lane = iota((depth, LANES), 1)
    origin_x = [(SIDE * (lax.rem(p, WIN) - WIN // 2)).astype(F32) + 0.5 for p in pos]
    pixel_ref[0] = by_tile(origin_x, lane // share) + (lane % SIDE).astype(F32)
    origin_y = [(SIDE * (lax.div(p, WIN) - WIN // 2)).astype(F32) + 0.5 for p in pos]
    pixel_row = iota((depth, LANES), 0) * (share // SIDE) + (lane % share) // SIDE
    pixel_ref[1] = by_tile(origin_y, lane // share) + pixel_row.astype(F32)


def place_kernel(owners, cap, g_dev, lists_ref, after_ref, hot_ref, local_ref):
    tiles, length = lists_ref.shape
    slots = owners * cap
    ids = lists_ref[...]
    masks = [(ids >= o * g_dev) & (ids < (o + 1) * g_dev) for o in range(owners)]
    rank = ranks(jnp.concatenate([m.astype(jnp.int32) for m in masks], axis=0) > 0, tiles)
    place = jnp.full((tiles, length), -1, jnp.int32)
    local = jnp.zeros((tiles, length), jnp.int32)
    for o in range(owners):
        place = jnp.where(masks[o], rank[o * tiles : (o + 1) * tiles] + o * cap, place)
        local = jnp.where(masks[o], ids - o * g_dev, local)
    slot_iota = iota((slots, length), 0)
    hot_ref[...] = jnp.concatenate(
        [one_hot(slot_iota == place[t : t + 1, :]) for t in range(tiles)], axis=1
    )
    local_ref[...] = local.astype(F32)


def render_kernel(pieces, width, *refs):
    recv_refs, refs = refs[:pieces], refs[pieces:]
    lists_ref, hot_ref, local_ref, cam_ref, pixel_ref, targets_ref = refs[:6]
    pictures_ref, send_ref, rows_ref, table_ref, alpha_ref, weight_ref, part_ref = refs[6:13]
    tiles, length = lists_ref.shape
    share = LANES // tiles
    depth = SIDE * SIDE // share
    live = lists_ref[...] >= 0
    hot = hot_ref[...]

    if pieces == 1:
        listed = dot(recv_refs[0][...].reshape(-1, LANES), hot, 0, 0)[:width]
    else:
        own, far = recv_refs[0][...], recv_refs[1][...]
        low = lax.axis_index("gauss") < 4
        received = jnp.concatenate([jnp.where(low, own, far), jnp.where(low, far, own)], axis=1)
        listed = dot(received, hot)
    for t in range(tiles):
        rows_ref[t * width : (t + 1) * width, :] = listed[:, t * length : (t + 1) * length]
    rows = [rows_ref[pl.ds(f, tiles, stride=width), :] for f in range(width)]

    cam = [cam_ref[j] for j in range(cam_ref.shape[0])]
    outs, pullback, rays = jax.vjp(lambda r: project(r, cam, live), rows[:10], has_aux=True)
    terms = outs[5:]
    colors = []
    for k in range(3):
        base = 11 + 16 * k
        shade = 0.5 + rows[base]
        for b in range(15):
            shade = shade + rows[base + 1 + b] * terms[b]
        for j in range(5):
            shade = shade + rows[59 + j] * cam[13 + 3 * j + k]
        colors.append(shade)
    opacity = jax.nn.sigmoid(rows[10])
    con_a, con_b, con_c = outs[2], outs[3], outs[4]

    attrs = [
        outs[0],
        outs[1],
        (-0.5 * LOG2E) * con_a,
        -LOG2E * con_b,
        (-0.5 * LOG2E) * con_c,
        jnp.where(live, opacity, 0.0),
    ] + colors
    count = len(attrs)
    blocks = []
    for value in attrs:
        parts = [p.astype(F32) for p in split(value, 3)]
        parts.append(jnp.zeros((16 - 3 * tiles, length), F32))
        blocks.append(jnp.concatenate(parts, axis=0))
    stacked = jnp.concatenate(blocks, axis=1)
    lane_tile = iota((16, LANES), 1) // share
    row_index = iota((16, LANES), 0)
    spread = one_hot((row_index % tiles == lane_tile) & (row_index < 3 * tiles))
    table = dot(stacked.T.astype(BF16), spread)
    pixel_x, pixel_y = pixel_ref[0, :1, :], pixel_ref[1]
    dx = pixel_x - table[:length]
    table_ref[0:length, :] = table[2 * length : 3 * length] * dx * dx
    table_ref[length : 2 * length, :] = table[3 * length : 4 * length] * dx
    table_ref[2 * length : 3 * length, :] = table[length : 2 * length]
    table_ref[3 * length :, :] = table[4 * length :]

    def row(index, l):
        return table_ref[index * length + l : index * length + l + 1, :]

    zero = jnp.zeros((depth, LANES), F32)
    through = jnp.ones((depth, LANES), F32)
    red, green, blue = zero, zero, zero
    for l in range(length):
        dy = pixel_y - row(2, l)
        power = row(0, l) + dy * (row(1, l) + row(3, l) * dy)
        alpha = row(4, l) * jnp.exp2(power)
        weight = through * alpha
        red = red + weight * row(5, l)
        green = green + weight * row(6, l)
        blue = blue + weight * row(7, l)
        through = through - weight
        at = slice(l * depth, (l + 1) * depth)
        alpha_ref[at, :] = alpha
        weight_ref[at, :] = weight
    pictures_ref[0] = red
    pictures_ref[1] = green
    pictures_ref[2] = blue
    res = [red - targets_ref[0], green - targets_ref[1], blue - targets_ref[2]]

    behind = zero
    for l in reversed(range(length)):
        at = slice(l * depth, (l + 1) * depth)
        alpha = alpha_ref[at, :]
        weight = weight_ref[at, :]
        dy = pixel_y - row(2, l)
        seen = row(5, l) * res[0] + row(6, l) * res[1] + row(7, l) * res[2]
        gap = seen - behind
        behind = behind + alpha * gap
        g = weight * gap
        gy = g * dy
        part_ref[0, at, :] = g
        part_ref[1, at, :] = gy
        part_ref[2, at, :] = gy * dy
        for k in range(3):
            part_ref[3 + k, at, :] = weight * res[k]

    def down(index):
        blocks = []
        for first in range(0, length, 8):
            parts = [
                part_ref[index, pl.ds(first * depth + s, 8, stride=depth), :] for s in range(depth)
            ]
            while len(parts) > 1:
                parts = [a + b for a, b in zip(parts[::2], parts[1::2])]
            blocks.append(parts[0])
        return jnp.concatenate(blocks, axis=0)

    sums = [down(index) for index in range(6)]
    g_x = sums[0] * dx
    sums = sums + [g_x, g_x * dx, sums[1] * dx]
    wide = jnp.concatenate([jnp.concatenate(split(s, 3), axis=1) for s in sums], axis=0)
    gather = one_hot(iota((8, 3 * LANES), 0) == (iota((8, 3 * LANES), 1) % LANES) // share)
    reduced = dot(gather, wide, 1, 1)
    g_0, g_y, g_yy, s_0, s_1, s_2, g_x, g_xx, g_xy = [
        reduced[:tiles, q * length : (q + 1) * length] for q in range(len(sums))
    ]

    d_colors = [s_0, s_1, s_2]
    d_terms = []
    for b in range(15):
        d_terms.append(sum(d_colors[k] * rows[12 + 16 * k + b] for k in range(3)))
    d_geometry = [
        con_a * g_x + con_b * g_y,
        con_b * g_x + con_c * g_y,
        -0.5 * g_xx,
        -g_xy,
        -0.5 * g_yy,
    ]
    (d_rows,) = pullback(d_geometry + d_terms)
    values = list(d_rows)
    values.append(g_0 * (1.0 - opacity))
    values.extend(d_colors)
    values.extend(rays)
    for j in range(5):
        values.append(sum(d_colors[k] * cam[13 + 3 * j + k] for k in range(3)))
    values.append(local_ref[...])
    values.extend([jnp.zeros((tiles, length), F32)] * (SENT - len(values)))
    for v in range(SENT):
        rows_ref[pl.ds(v, tiles, stride=width), :] = values[v]
    by_slot = jnp.concatenate(
        [
            jnp.concatenate(split(rows_ref[t * width : t * width + SENT, :], 3), axis=0)
            for t in range(tiles)
        ],
        axis=1,
    )
    by_slot = dot(by_slot, hot, 1, 1)
    by_slot = by_slot[:SENT] + by_slot[SENT : 2 * SENT] + by_slot[2 * SENT :]
    owners, copies, high, _ = send_ref.shape
    cap = hot.shape[0] // owners
    for o in range(owners):
        block = jnp.concatenate(
            [by_slot[r : r + high, o * cap : (o + 1) * cap] for r in range(0, SENT, high)], axis=1
        )
        for c in range(copies):
            send_ref[o, c] = block


def entry_rows(cap, recv_ref):
    blocks, high, _ = recv_ref.shape
    values = jnp.concatenate(
        [
            jnp.concatenate(
                [recv_ref[b, :, first : first + cap] for b in range(blocks)], axis=1
            )
            for first in range(0, SENT * cap // high, cap)
        ],
        axis=0,
    )
    ray_x, ray_y = values[14:15], values[15:16]
    dir_z = lax.rsqrt(ray_x * ray_x + ray_y * ray_y + 1.0)
    terms = sh_terms(ray_x * dir_z, ray_y * dir_z, dir_z)
    terms = jnp.concatenate([jnp.ones_like(dir_z)] + terms, axis=0)
    rows = [values] + [terms * values[11 + k : 12 + k] for k in range(3)]
    parts = split(jnp.concatenate(rows, axis=0), 2)
    return jnp.concatenate(parts, axis=0), values[21:22].astype(jnp.int32)


def scatter(rows, where, first, count):
    hot = one_hot(iota((count, where.shape[1]), 0) + first == where)
    total = dot(rows, hot, 1, 1)
    half = total.shape[0] // 2
    return total[:half] + total[half:]


def in_order(total):
    return jnp.concatenate([total[:11], total[SENT:], total[16:21]], axis=0)


def scatter_kernel(cap, recv_ref, out_ref):
    rows, where = entry_rows(cap, recv_ref)
    out_ref[...] = in_order(scatter(rows, where, 0, out_ref.shape[1]))


def first_kernel(cap, recv_ref, out_ref):
    rows, where = entry_rows(cap, recv_ref)
    out_ref[...] = scatter(rows, where, 0, out_ref.shape[1])


def last_kernel(
    cap, recv_ref, sum_ref, spread_ref, out_ref, pictures_ref, sums, pictures, out_sem, picture_sem
):
    _, tiles, _ = pictures.shape
    depth = spread_ref.shape[1]
    share = LANES // tiles
    lane_block = iota((depth, LANES), 1) // share
    row = iota((depth, LANES), 0) % tiles
    for k in range(3):
        spread = spread_ref[k]
        whole = spread
        for d in range(1, tiles):
            down = pltpu.roll(spread, d, 0)
            up = pltpu.roll(spread, depth + d - tiles, 0)
            moved = pltpu.roll(jnp.where(row >= d, down, up), LANES - d * share, 1)
            whole = jnp.where((row - lane_block) % tiles == d, moved, whole)
        for h in range(depth // tiles):
            pictures[k, :, h * LANES : (h + 1) * LANES] = whole[h * tiles : (h + 1) * tiles]
    copies = [pltpu.make_async_copy(pictures, pictures_ref, picture_sem)]
    copies[0].start()
    rows, where = entry_rows(cap, recv_ref)
    blocks, _, count = sums.shape
    for b in range(blocks):
        columns = slice(b * count, (b + 1) * count)
        sums[b] = in_order(sum_ref[:, columns] + scatter(rows, where, b * count, count))
        copies.append(
            pltpu.make_async_copy(
                sums.at[b], out_ref.at[:, pl.ds(b * count, count)], out_sem.at[b]
            )
        )
        copies[-1].start()
    for copy in copies:
        copy.wait()


def call(kernel, out_shape, args, scalars=0, left=0, out_left=False, scratch=()):
    in_specs = [pl.BlockSpec(memory_space=pltpu.SMEM)] * scalars
    in_specs += [pl.BlockSpec(memory_space=pltpu.VMEM)] * (len(args) - scalars - left)
    in_specs += [pl.BlockSpec(memory_space=pl.ANY)] * left
    many = isinstance(out_shape, (list, tuple))
    spec = pl.BlockSpec(memory_space=pl.ANY if out_left else pltpu.VMEM)
    return pl.pallas_call(
        kernel,
        out_shape=out_shape,
        in_specs=in_specs,
        out_specs=[spec] * len(out_shape) if many else spec,
        scratch_shapes=list(scratch),
        compiler_params=pltpu.CompilerParams(vmem_limit_bytes=VMEM_LIMIT),
    )(*args)


def swap(x, axis, k):
    return lax.ppermute(x, axis, [(i, i ^ k) for i in range(lax.axis_size(axis))])


def crossed(owner, owners):
    return int(owner >= owners // 2)


def reach(x, steps):
    owners, views = lax.axis_size("gauss"), lax.axis_size("view")
    pairs = []
    for g in range(owners):
        for v in range(views):
            step = steps[v % 2]
            if step is not None:
                flip = crossed(g, owners) ^ crossed(g ^ step, owners)
                pairs.append((g * views + v, (g ^ step) * views + (v ^ flip)))
    return lax.ppermute(x, ("gauss", "view"), pairs)


def exchange(x):
    return lax.all_to_all(x, "gauss", split_axis=0, concat_axis=0, tiled=True)


def exchange_wide(x):
    owners, views = lax.axis_size("gauss"), lax.axis_size("view")
    blocks = x.reshape(owners * views // 2, *x.shape[2:])
    groups = [
        [
            g * views + v
            for g in range(owners)
            for v in range(views)
            if v % 2 == c ^ crossed(g, owners)
        ]
        for c in range(2)
    ]
    return lax.all_to_all(
        blocks,
        ("gauss", "view"),
        split_axis=0,
        concat_axis=0,
        axis_index_groups=groups,
        tiled=True,
    )


def shape(dims, dtype):
    return jax.ShapeDtypeStruct(dims, dtype)


def on_device(params, lists, tile_pos, cam_index, cams, targets):
    owners = lax.axis_size("gauss")
    views = lax.axis_size("view")
    width, g_dev = params.shape
    tiles, length = lists.shape
    cap = max(tiles * length // owners, 16)
    slots = owners * cap
    share = LANES // tiles
    depth = SIDE * SIDE // share
    near = owners == 8 and views % 2 == 0
    wide = views % 2 == 0 and owners * views <= 32

    if near:
        third = reach(params, (None, 3))
        got = reach(params, (1, 2))
        far_lists = reach(lists, (4, 4))
    params_copy, cam, pixel = call(
        prepare_kernel,
        [
            shape((width, g_dev), BF16),
            shape((cams.shape[0], tiles, length), F32),
            shape((2, depth, LANES), F32),
        ],
        (tile_pos, cam_index, cams.T, params),
        scalars=3,
    )
    if near:
        third, got, far_lists, params_copy = lax.optimization_barrier(
            (third, got, far_lists, params_copy)
        )
        got_by, third_by = swap(got, "view", 1), swap(third, "view", 1)
        answer, far_answer = call(
            functools.partial(pick_near_kernel, cap),
            [shape((width, 4 * cap), BF16)] * 2,
            (far_lists, got, got_by, third, third_by, params_copy, lists),
            scratch=(pltpu.VMEM((4, width, 2 * cap), F32),),
        )
        returned = [answer, reach(far_answer, (4, 4))]
        after = answer
    else:
        all_lists = exchange(jnp.broadcast_to(lists[None], (owners, tiles, length)))
        picked = call(
            functools.partial(pick_kernel, tiles, cap),
            shape((slots, LANES), BF16),
            (all_lists.reshape(owners * tiles, length), params_copy),
        )
        returned = [exchange(picked.reshape(owners, cap, LANES))]
        after = picked
    hot, local = call(
        functools.partial(place_kernel, owners, cap, g_dev),
        [shape((slots, tiles * length), BF16), shape((tiles, length), F32)],
        (lists, after),
        left=1,
    )
    spread_targets = (
        targets.reshape(3, tiles, depth, share).transpose(0, 2, 1, 3).reshape(3, depth, LANES)
    )
    copies = views // 2 if wide else 1
    high = SENT * cap // LANES
    pictures, sent = call(
        functools.partial(render_kernel, len(returned), width),
        [shape((3, depth, LANES), F32), shape((owners, copies, high, LANES), F32)],
        (*returned, lists, hot, local, cam, pixel, spread_targets),
        scratch=(
            pltpu.VMEM((tiles * width, length), F32),
            pltpu.VMEM((8 * length, LANES), F32),
            pltpu.VMEM((length * depth, LANES), F32),
            pltpu.VMEM((length * depth, LANES), F32),
            pltpu.VMEM((6, length * depth, LANES), F32),
        ),
    )
    if wide:
        received = exchange_wide(sent)
        other = swap(received, "view", 1)
        total = call(
            functools.partial(first_kernel, cap), shape((SENT + 48, g_dev), F32), (received,)
        )
        parts = 4
        grads, pictures = call(
            functools.partial(last_kernel, cap),
            [shape((width, g_dev), F32), shape(targets.shape, F32)],
            (other, total, pictures),
            out_left=True,
            scratch=(
                pltpu.VMEM((parts, width, g_dev // parts), F32),
                pltpu.VMEM(targets.shape, F32),
                pltpu.SemaphoreType.DMA((parts,)),
                pltpu.SemaphoreType.DMA,
            ),
        )
        return (pictures, grads)
    pictures = (
        pictures.reshape(3, depth, tiles, share)
        .transpose(0, 2, 1, 3)
        .reshape(3, tiles, SIDE * SIDE)
    )
    received = exchange(sent[:, 0])
    grads = call(
        functools.partial(scatter_kernel, cap), shape((width, g_dev), F32), (received,)
    )
    return (pictures, lax.psum(grads, "view"))


def solution(mesh):
    return jax.shard_map(
        on_device,
        mesh=mesh,
        in_specs=(
            P(None, "gauss"),
            P(("gauss", "view"), None),
            P(("gauss", "view")),
            P(("gauss", "view")),
            P(),
            P(None, ("gauss", "view"), None),
        ),
        out_specs=(P(None, ("gauss", "view"), None), P(None, "gauss")),
        check_vma=False,
    )
```

```python
import functools
import math

import jax
import jax.numpy as jnp
from jax import lax
from jax.experimental import pallas as pl
from jax.experimental.pallas import tpu as pltpu
from jax.sharding import PartitionSpec as P

WIN = 16
SIDE = 16
LANES = 128
LOG2E = math.log2(math.e)
F32 = jnp.float32
BF16 = jnp.bfloat16
VMEM_LIMIT = 24 * 2**20
SENT = 32


def sh_terms(x, y, z):
    xx, yy, zz = x * x, y * y, z * z
    xy = x * y
    diff = xx - yy
    five = 5.0 * zz - 1.0
    return [
        x,
        y,
        z,
        xy,
        y * z,
        x * z,
        diff,
        3.0 * zz - 1.0,
        x * (xx - 3.0 * yy),
        xy * z,
        y * (3.0 * xx - yy),
        z * diff,
        x * five,
        y * five,
        z * (5.0 * zz - 3.0),
    ]


def project(rows, cam, live):
    mx, my, mz = rows[0], rows[1], rows[2]
    cam_x = cam[0] * mx + cam[1] * my + cam[2] * mz + cam[9]
    cam_y = cam[3] * mx + cam[4] * my + cam[5] * mz + cam[10]
    cam_z = cam[6] * mx + cam[7] * my + cam[8] * mz + cam[11]
    cam_z = jnp.where(live, cam_z, 1.0)
    inv_z = 1.0 / cam_z
    qw, qx, qy, qz = rows[6], rows[7], rows[8], rows[9]
    qw = jnp.where(live, qw, 1.0)
    inv_q = lax.rsqrt(qw * qw + qx * qx + qy * qy + qz * qz)
    qw, qx, qy, qz = qw * inv_q, qx * inv_q, qy * inv_q, qz * inv_q
    rot = [
        [
            1.0 - 2.0 * (qy * qy + qz * qz),
            2.0 * (qx * qy - qw * qz),
            2.0 * (qx * qz + qw * qy),
        ],
        [
            2.0 * (qx * qy + qw * qz),
            1.0 - 2.0 * (qx * qx + qz * qz),
            2.0 * (qy * qz - qw * qx),
        ],
        [
            2.0 * (qx * qz - qw * qy),
            2.0 * (qy * qz + qw * qx),
            1.0 - 2.0 * (qx * qx + qy * qy),
        ],
    ]
    mixed = [
        [
            cam[3 * i] * rot[0][k] + cam[3 * i + 1] * rot[1][k] + cam[3 * i + 2] * rot[2][k]
            for k in range(3)
        ]
        for i in range(3)
    ]
    scale = cam[12] * inv_z
    ray_x, ray_y = cam_x * inv_z, cam_y * inv_z
    proj_u = [scale * (mixed[0][k] - ray_x * mixed[2][k]) for k in range(3)]
    proj_v = [scale * (mixed[1][k] - ray_y * mixed[2][k]) for k in range(3)]
    var = [jnp.exp(2.0 * rows[3 + k]) for k in range(3)]
    uv = [proj_u[k] * var[k] for k in range(3)]
    cov_a = sum(uv[k] * proj_u[k] for k in range(3)) + 0.3
    cov_b = sum(uv[k] * proj_v[k] for k in range(3))
    cov_c = sum(proj_v[k] * proj_v[k] * var[k] for k in range(3)) + 0.3
    inv_det = 1.0 / (cov_a * cov_c - cov_b * cov_b)
    inv_dist = lax.rsqrt(cam_x * cam_x + cam_y * cam_y + cam_z * cam_z)
    terms = sh_terms(cam_x * inv_dist, cam_y * inv_dist, cam_z * inv_dist)
    geometry = [cam_x * scale, cam_y * scale, cov_c * inv_det, -cov_b * inv_det, cov_a * inv_det]
    return geometry + terms, (ray_x, ray_y)


def iota(shape, dim):
    return lax.broadcasted_iota(jnp.int32, shape, dim)


def one_hot(mask):
    return jnp.where(mask, 1.0, 0.0).astype(BF16)


def dot(lhs, rhs, lhs_dim=1, rhs_dim=0):
    return lax.dot_general(
        lhs, rhs, (((lhs_dim,), (rhs_dim,)), ((), ())), preferred_element_type=F32
    )


def split(x, parts):
    out = []
    for _ in range(parts):
        head = x.astype(BF16)
        out.append(head)
        x = x - head.astype(F32)
    return out


def ranks(mask, tiles):
    rows, length = mask.shape
    bits = jnp.where(mask, 1.0, 0.0)
    place = iota((rows, length), 0) % tiles
    shifted = [bits] + [
        jnp.where(place >= d, pltpu.roll(bits, d, 0), 0.0) for d in range(1, tiles)
    ]
    earlier = one_hot(iota((length, length), 0) < iota((length, length), 1))
    counted = jnp.concatenate([earlier] + [jnp.ones_like(earlier)] * (tiles - 1), axis=0)
    return dot(jnp.concatenate(shifted, axis=1).astype(BF16), counted).astype(jnp.int32)


def find(local, tiles, cap, g_dev):
    mine = (local >= 0) & (local < g_dev)
    key = jnp.where(mine, ranks(mine, tiles), -1)
    rows, length = local.shape
    slot = iota((cap, length), 0)
    found = []
    for r in range(0, rows, tiles):
        total = jnp.zeros((cap, length), jnp.int32)
        for t in range(r, r + tiles):
            total = total + jnp.where(key[t : t + 1, :] == slot, local[t : t + 1, :], 0)
        found.append(jnp.sum(total, axis=1, keepdims=True))
    return jnp.concatenate(found, axis=0)


def pick_kernel(tiles, cap, lists_ref, params_ref, picked_ref):
    width, g_dev = params_ref.shape
    where = find(lists_ref[...] - lax.axis_index("gauss") * g_dev, tiles, cap, g_dev)
    hot = one_hot(where == iota((where.shape[0], g_dev), 1))
    wide = jnp.concatenate([params_ref[...], jnp.zeros((LANES - width, g_dev), BF16)], axis=0)
    picked_ref[...] = dot(hot, wide, 1, 1).astype(BF16)


def pick_pair_kernel(cap, peers, *refs):
    lists_refs, refs = refs[:peers], refs[peers:]
    own_ref, other_ref = refs[:2]
    picked_refs, refs = refs[2 : 2 + peers], refs[2 + peers :]
    lists_scratch, picked_scratch = refs
    tiles, length = lists_refs[0].shape
    g_dev = own_ref.shape[1]
    me = lax.axis_index("gauss")
    first = me % 2 == 0
    for k in range(peers):
        lists_scratch[(me // 2) ^ k] = lists_refs[k][...]
    ids = lists_scratch[...].reshape(peers * tiles, length)
    local = jnp.concatenate([ids - me * g_dev, ids - (me ^ 1) * g_dev], axis=0)
    where = find(local, tiles, cap, g_dev)
    where_own, where_other = where[: peers * cap], where[peers * cap :]
    lanes = iota((peers * cap, g_dev), 1)
    of_own = dot(own_ref[...], one_hot(where_own == lanes), 1, 1)
    of_other = dot(other_ref[...], one_hot(where_other == lanes), 1, 1)
    of_even = jnp.where(first, of_own, of_other)
    of_odd = jnp.where(first, of_other, of_own)
    for p in range(peers):
        block = slice(p * cap, (p + 1) * cap)
        picked_scratch[p] = jnp.concatenate(
            [of_even[:, block], of_odd[:, block]], axis=1
        ).astype(BF16)
    for k in range(peers):
        picked_refs[peers - 1 - k][...] = picked_scratch[(me // 2) ^ k]


def by_tile(values, row):
    out = jnp.full(row.shape, values[-1])
    for t in range(len(values) - 1):
        out = jnp.where(row == t, values[t], out)
    return out


def prepare_kernel(
    tile_pos_ref, cam_index_ref, cams_ref, params_ref, copy_ref, cam_ref, pixel_ref
):
    copy_ref[...] = params_ref[...]
    values, tiles, length = cam_ref.shape
    share = LANES // tiles
    depth = SIDE * SIDE // share
    cam_ids = [cam_index_ref[t] for t in range(tiles)]
    tile_row = iota((tiles, length), 0)
    for j in range(values):
        cam_ref[j] = by_tile([cams_ref[cam_ids[t], j] for t in range(tiles)], tile_row)
    pos = [tile_pos_ref[t] for t in range(tiles)]
    lane = iota((depth, LANES), 1)
    origin_x = [(SIDE * (lax.rem(p, WIN) - WIN // 2)).astype(F32) + 0.5 for p in pos]
    pixel_ref[0] = by_tile(origin_x, lane // share) + (lane % SIDE).astype(F32)
    origin_y = [(SIDE * (lax.div(p, WIN) - WIN // 2)).astype(F32) + 0.5 for p in pos]
    pixel_row = iota((depth, LANES), 0) * (share // SIDE) + (lane % share) // SIDE
    pixel_ref[1] = by_tile(origin_y, lane // share) + pixel_row.astype(F32)


def place_kernel(owners, cap, g_dev, lists_ref, after_ref, hot_ref, local_ref):
    tiles, length = lists_ref.shape
    slots = owners * cap
    ids = lists_ref[...]
    masks = [(ids >= o * g_dev) & (ids < (o + 1) * g_dev) for o in range(owners)]
    rank = ranks(jnp.concatenate([m.astype(jnp.int32) for m in masks], axis=0) > 0, tiles)
    place = jnp.full((tiles, length), -1, jnp.int32)
    local = jnp.zeros((tiles, length), jnp.int32)
    for o in range(owners):
        place = jnp.where(masks[o], rank[o * tiles : (o + 1) * tiles] + o * cap, place)
        local = jnp.where(masks[o], ids - o * g_dev, local)
    slot_iota = iota((slots, length), 0)
    hot_ref[...] = jnp.concatenate(
        [one_hot(slot_iota == place[t : t + 1, :]) for t in range(tiles)], axis=1
    )
    local_ref[...] = local.astype(F32)


def render_kernel(pieces, width, *refs):
    recv_refs, refs = refs[:pieces], refs[pieces:]
    lists_ref, hot_ref, local_ref, cam_ref, pixel_ref, targets_ref = refs[:6]
    pictures_ref, send_ref, rows_ref, table_ref, alpha_ref, weight_ref, part_ref = refs[6:13]
    tiles, length = lists_ref.shape
    share = LANES // tiles
    depth = SIDE * SIDE // share
    live = lists_ref[...] >= 0
    hot = hot_ref[...]

    if pieces == 1:
        listed = dot(recv_refs[0][...].reshape(-1, LANES), hot, 0, 0)[:width]
    else:
        (recv_scratch,) = refs[13:]
        place = lax.axis_index("gauss") // 2
        for k in range(pieces):
            recv_scratch[place ^ k] = recv_refs[pieces - 1 - k][...]
        received = jnp.concatenate([recv_scratch[p] for p in range(pieces)], axis=1)
        listed = dot(received, hot)
    for t in range(tiles):
        rows_ref[t * width : (t + 1) * width, :] = listed[:, t * length : (t + 1) * length]
    rows = [rows_ref[pl.ds(f, tiles, stride=width), :] for f in range(width)]

    cam = [cam_ref[j] for j in range(cam_ref.shape[0])]
    outs, pullback, rays = jax.vjp(lambda r: project(r, cam, live), rows[:10], has_aux=True)
    terms = outs[5:]
    colors = []
    for k in range(3):
        base = 11 + 16 * k
        shade = 0.5 + rows[base]
        for b in range(15):
            shade = shade + rows[base + 1 + b] * terms[b]
        for j in range(5):
            shade = shade + rows[59 + j] * cam[13 + 3 * j + k]
        colors.append(shade)
    opacity = jax.nn.sigmoid(rows[10])
    con_a, con_b, con_c = outs[2], outs[3], outs[4]

    attrs = [
        outs[0],
        outs[1],
        (-0.5 * LOG2E) * con_a,
        -LOG2E * con_b,
        (-0.5 * LOG2E) * con_c,
        jnp.where(live, opacity, 0.0),
    ] + colors
    count = len(attrs)
    blocks = []
    for value in attrs:
        parts = [p.astype(F32) for p in split(value, 3)]
        parts.append(jnp.zeros((16 - 3 * tiles, length), F32))
        blocks.append(jnp.concatenate(parts, axis=0))
    stacked = jnp.concatenate(blocks, axis=1)
    lane_tile = iota((16, LANES), 1) // share
    row_index = iota((16, LANES), 0)
    spread = one_hot((row_index % tiles == lane_tile) & (row_index < 3 * tiles))
    table = dot(stacked.T.astype(BF16), spread)
    pixel_x, pixel_y = pixel_ref[0, :1, :], pixel_ref[1]
    dx = pixel_x - table[:length]
    table_ref[0:length, :] = table[2 * length : 3 * length] * dx * dx
    table_ref[length : 2 * length, :] = table[3 * length : 4 * length] * dx
    table_ref[2 * length : 3 * length, :] = table[length : 2 * length]
    table_ref[3 * length :, :] = table[4 * length :]

    def row(index, l):
        return table_ref[index * length + l : index * length + l + 1, :]

    zero = jnp.zeros((depth, LANES), F32)
    through = jnp.ones((depth, LANES), F32)
    red, green, blue = zero, zero, zero
    for l in range(length):
        dy = pixel_y - row(2, l)
        power = row(0, l) + dy * (row(1, l) + row(3, l) * dy)
        alpha = row(4, l) * jnp.exp2(power)
        weight = through * alpha
        red = red + weight * row(5, l)
        green = green + weight * row(6, l)
        blue = blue + weight * row(7, l)
        through = through - weight
        at = slice(l * depth, (l + 1) * depth)
        alpha_ref[at, :] = alpha
        weight_ref[at, :] = weight
    pictures_ref[0] = red
    pictures_ref[1] = green
    pictures_ref[2] = blue
    res = [red - targets_ref[0], green - targets_ref[1], blue - targets_ref[2]]

    behind = zero
    for l in reversed(range(length)):
        at = slice(l * depth, (l + 1) * depth)
        alpha = alpha_ref[at, :]
        weight = weight_ref[at, :]
        dy = pixel_y - row(2, l)
        seen = row(5, l) * res[0] + row(6, l) * res[1] + row(7, l) * res[2]
        gap = seen - behind
        behind = behind + alpha * gap
        g = weight * gap
        gy = g * dy
        part_ref[0, at, :] = g
        part_ref[1, at, :] = gy
        part_ref[2, at, :] = gy * dy
        for k in range(3):
            part_ref[3 + k, at, :] = weight * res[k]

    def down(index):
        blocks = []
        for first in range(0, length, 8):
            parts = [
                part_ref[index, pl.ds(first * depth + s, 8, stride=depth), :] for s in range(depth)
            ]
            while len(parts) > 1:
                parts = [a + b for a, b in zip(parts[::2], parts[1::2])]
            blocks.append(parts[0])
        return jnp.concatenate(blocks, axis=0)

    sums = [down(index) for index in range(6)]
    g_x = sums[0] * dx
    sums = sums + [g_x, g_x * dx, sums[1] * dx]
    wide = jnp.concatenate([jnp.concatenate(split(s, 2), axis=1) for s in sums], axis=0)
    gather = one_hot(iota((8, 2 * LANES), 0) == (iota((8, 2 * LANES), 1) % LANES) // share)
    reduced = dot(gather, wide, 1, 1)
    g_0, g_y, g_yy, s_0, s_1, s_2, g_x, g_xx, g_xy = [
        reduced[:tiles, q * length : (q + 1) * length] for q in range(len(sums))
    ]

    d_colors = [s_0, s_1, s_2]
    d_terms = []
    for b in range(15):
        d_terms.append(sum(d_colors[k] * rows[12 + 16 * k + b] for k in range(3)))
    d_geometry = [
        con_a * g_x + con_b * g_y,
        con_b * g_x + con_c * g_y,
        -0.5 * g_xx,
        -g_xy,
        -0.5 * g_yy,
    ]
    (d_rows,) = pullback(d_geometry + d_terms)
    values = list(d_rows)
    values.append(g_0 * (1.0 - opacity))
    values.extend(d_colors)
    values.extend(rays)
    for j in range(5):
        values.append(sum(d_colors[k] * cam[13 + 3 * j + k] for k in range(3)))
    values.append(local_ref[...])
    values.extend([jnp.zeros((tiles, length), F32)] * (SENT - len(values)))
    for v in range(SENT):
        rows_ref[pl.ds(v, tiles, stride=width), :] = values[v]
    by_slot = jnp.concatenate(
        [
            jnp.concatenate(split(rows_ref[t * width : t * width + SENT, :], 3), axis=0)
            for t in range(tiles)
        ],
        axis=1,
    )
    by_slot = dot(by_slot, hot, 1, 1)
    by_slot = by_slot[:SENT] + by_slot[SENT : 2 * SENT] + by_slot[2 * SENT :]
    owners, copies, high, _ = send_ref.shape
    cap = hot.shape[0] // owners
    for o in range(owners):
        block = jnp.concatenate(
            [by_slot[r : r + high, o * cap : (o + 1) * cap] for r in range(0, SENT, high)], axis=1
        )
        for c in range(copies):
            send_ref[o, c] = block


def entry_rows(cap, recv_ref):
    blocks, high, _ = recv_ref.shape
    values = jnp.concatenate(
        [
            jnp.concatenate(
                [recv_ref[b, :, first : first + cap] for b in range(blocks)], axis=1
            )
            for first in range(0, SENT * cap // high, cap)
        ],
        axis=0,
    )
    ray_x, ray_y = values[14:15], values[15:16]
    dir_z = lax.rsqrt(ray_x * ray_x + ray_y * ray_y + 1.0)
    terms = sh_terms(ray_x * dir_z, ray_y * dir_z, dir_z)
    terms = jnp.concatenate([jnp.ones_like(dir_z)] + terms, axis=0)
    rows = [values] + [terms * values[11 + k : 12 + k] for k in range(3)]
    parts = split(jnp.concatenate(rows, axis=0), 2)
    return jnp.concatenate(parts, axis=0), values[21:22].astype(jnp.int32)


def scatter(rows, where, first, count):
    hot = one_hot(iota((count, where.shape[1]), 0) + first == where)
    total = dot(rows, hot, 1, 1)
    half = total.shape[0] // 2
    return total[:half] + total[half:]


def in_order(total):
    return jnp.concatenate([total[:11], total[SENT:], total[16:21]], axis=0)


def scatter_kernel(cap, recv_ref, out_ref):
    rows, where = entry_rows(cap, recv_ref)
    out_ref[...] = in_order(scatter(rows, where, 0, out_ref.shape[1]))


def first_kernel(cap, recv_ref, out_ref):
    rows, where = entry_rows(cap, recv_ref)
    out_ref[...] = scatter(rows, where, 0, out_ref.shape[1])


def last_kernel(
    cap, recv_ref, sum_ref, spread_ref, out_ref, pictures_ref, sums, pictures, out_sem, picture_sem
):
    _, tiles, _ = pictures.shape
    depth = spread_ref.shape[1]
    share = LANES // tiles
    lane_block = iota((depth, LANES), 1) // share
    row = iota((depth, LANES), 0) % tiles
    for k in range(3):
        spread = spread_ref[k]
        whole = spread
        for d in range(1, tiles):
            down = pltpu.roll(spread, d, 0)
            up = pltpu.roll(spread, depth + d - tiles, 0)
            moved = pltpu.roll(jnp.where(row >= d, down, up), LANES - d * share, 1)
            whole = jnp.where((row - lane_block) % tiles == d, moved, whole)
        for h in range(depth // tiles):
            pictures[k, :, h * LANES : (h + 1) * LANES] = whole[h * tiles : (h + 1) * tiles]
    copies = [pltpu.make_async_copy(pictures, pictures_ref, picture_sem)]
    copies[0].start()
    rows, where = entry_rows(cap, recv_ref)
    blocks, _, count = sums.shape
    for b in range(blocks):
        columns = slice(b * count, (b + 1) * count)
        sums[b] = in_order(sum_ref[:, columns] + scatter(rows, where, b * count, count))
        copies.append(
            pltpu.make_async_copy(
                sums.at[b], out_ref.at[:, pl.ds(b * count, count)], out_sem.at[b]
            )
        )
        copies[-1].start()
    for copy in copies:
        copy.wait()


def call(kernel, out_shape, args, scalars=0, left=0, out_left=False, scratch=()):
    in_specs = [pl.BlockSpec(memory_space=pltpu.SMEM)] * scalars
    in_specs += [pl.BlockSpec(memory_space=pltpu.VMEM)] * (len(args) - scalars - left)
    in_specs += [pl.BlockSpec(memory_space=pl.ANY)] * left
    many = isinstance(out_shape, (list, tuple))
    spec = pl.BlockSpec(memory_space=pl.ANY if out_left else pltpu.VMEM)
    return pl.pallas_call(
        kernel,
        out_shape=out_shape,
        in_specs=in_specs,
        out_specs=[spec] * len(out_shape) if many else spec,
        scratch_shapes=list(scratch),
        compiler_params=pltpu.CompilerParams(vmem_limit_bytes=VMEM_LIMIT),
    )(*args)


def swap(x, axis, k):
    return lax.ppermute(x, axis, [(i, i ^ k) for i in range(lax.axis_size(axis))])


def crossed(owner, owners):
    return int(owner >= owners // 2)


def far_first(blocks):
    owners, views = lax.axis_size("gauss"), lax.axis_size("view")
    last = len(blocks) - 1
    out = []
    for i, block in enumerate(blocks):
        k = 2 * (last - i)
        pairs = []
        for g in range(owners):
            flip = k // 2 % 2 if views % 2 == 0 else 0
            pairs += [(g * views + v, (g ^ k) * views + (v ^ flip)) for v in range(views)]
        out.append(lax.ppermute(block, ("gauss", "view"), pairs) if k else block)
    return out


def exchange(x):
    return lax.all_to_all(x, "gauss", split_axis=0, concat_axis=0, tiled=True)


def exchange_wide(x):
    owners, views = lax.axis_size("gauss"), lax.axis_size("view")
    blocks = x.reshape(owners * views // 2, *x.shape[2:])
    groups = [
        [
            g * views + v
            for g in range(owners)
            for v in range(views)
            if v % 2 == c ^ crossed(g, owners)
        ]
        for c in range(2)
    ]
    return lax.all_to_all(
        blocks,
        ("gauss", "view"),
        split_axis=0,
        concat_axis=0,
        axis_index_groups=groups,
        tiled=True,
    )


def power_of_two(n):
    return n & (n - 1) == 0


def shape(dims, dtype):
    return jax.ShapeDtypeStruct(dims, dtype)


def on_device(params, lists, tile_pos, cam_index, cams, targets):
    owners = lax.axis_size("gauss")
    views = lax.axis_size("view")
    width, g_dev = params.shape
    tiles, length = lists.shape
    cap = max(tiles * length // owners, 16)
    slots = owners * cap
    share = LANES // tiles
    depth = SIDE * SIDE // share
    paired = 2 <= owners <= 16 and power_of_two(owners) and LANES == 2 * width
    peers = owners // 2 if paired else 1
    wide = views % 2 == 0 and owners * views <= 32

    if paired:
        other = swap(params, "gauss", 1)
        all_lists = far_first([lists] * peers)
    params_copy, cam, pixel = call(
        prepare_kernel,
        [
            shape((width, g_dev), BF16),
            shape((cams.shape[0], tiles, length), F32),
            shape((2, depth, LANES), F32),
        ],
        (tile_pos, cam_index, cams.T, params),
        scalars=3,
    )
    if paired:
        picked = call(
            functools.partial(pick_pair_kernel, cap, peers),
            [shape((width, 2 * cap), BF16)] * peers,
            (*all_lists[::-1], params_copy, other),
            scratch=(
                pltpu.VMEM((peers, tiles, length), jnp.int32),
                pltpu.VMEM((peers, width, 2 * cap), BF16),
            ),
        )
        returned = far_first(picked)
        after = picked[-1]
    else:
        all_lists = exchange(jnp.broadcast_to(lists[None], (owners, tiles, length)))
        picked = call(
            functools.partial(pick_kernel, tiles, cap),
            shape((slots, LANES), BF16),
            (all_lists.reshape(owners * tiles, length), params_copy),
        )
        returned = [exchange(picked.reshape(owners, cap, LANES))]
        after = picked
    hot, local = call(
        functools.partial(place_kernel, owners, cap, g_dev),
        [shape((slots, tiles * length), BF16), shape((tiles, length), F32)],
        (lists, after),
        left=1,
    )
    spread_targets = (
        targets.reshape(3, tiles, depth, share).transpose(0, 2, 1, 3).reshape(3, depth, LANES)
    )
    copies = views // 2 if wide else 1
    high = SENT * cap // LANES
    pictures, sent = call(
        functools.partial(render_kernel, peers, width),
        [shape((3, depth, LANES), F32), shape((owners, copies, high, LANES), F32)],
        (*returned, lists, hot, local, cam, pixel, spread_targets),
        scratch=(
            pltpu.VMEM((tiles * width, length), F32),
            pltpu.VMEM((8 * length, LANES), F32),
            pltpu.VMEM((length * depth, LANES), F32),
            pltpu.VMEM((length * depth, LANES), F32),
            pltpu.VMEM((6, length * depth, LANES), F32),
            pltpu.VMEM((peers, *returned[0].shape[-2:]), BF16),
        ),
    )
    if wide:
        received = exchange_wide(sent)
        other = swap(received, "view", 1)
        total = call(
            functools.partial(first_kernel, cap), shape((SENT + 48, g_dev), F32), (received,)
        )
        parts = 4
        grads, pictures = call(
            functools.partial(last_kernel, cap),
            [shape((width, g_dev), F32), shape(targets.shape, F32)],
            (other, total, pictures),
            out_left=True,
            scratch=(
                pltpu.VMEM((parts, width, g_dev // parts), F32),
                pltpu.VMEM(targets.shape, F32),
                pltpu.SemaphoreType.DMA((parts,)),
                pltpu.SemaphoreType.DMA,
            ),
        )
        return (pictures, grads)
    pictures = (
        pictures.reshape(3, depth, tiles, share)
        .transpose(0, 2, 1, 3)
        .reshape(3, tiles, SIDE * SIDE)
    )
    received = exchange(sent[:, 0])
    grads = call(
        functools.partial(scatter_kernel, cap), shape((width, g_dev), F32), (received,)
    )
    return (pictures, lax.psum(grads, "view"))


def solution(mesh):
    return jax.shard_map(
        on_device,
        mesh=mesh,
        in_specs=(
            P(None, "gauss"),
            P(("gauss", "view"), None),
            P(("gauss", "view")),
            P(("gauss", "view")),
            P(),
            P(None, ("gauss", "view"), None),
        ),
        out_specs=(P(None, ("gauss", "view"), None), P(None, "gauss")),
        check_vma=False,
    )
```

```python
import functools
import math

import jax
import jax.numpy as jnp
from jax import lax
from jax.experimental import pallas as pl
from jax.experimental.pallas import tpu as pltpu
from jax.sharding import PartitionSpec as P

WIN = 16
SIDE = 16
LANES = 128
LOG2E = math.log2(math.e)
F32 = jnp.float32
BF16 = jnp.bfloat16
VMEM_LIMIT = 24 * 2**20
SENT = 32


def sh_terms(x, y, z):
    xx, yy, zz = x * x, y * y, z * z
    xy = x * y
    diff = xx - yy
    five = 5.0 * zz - 1.0
    return [
        x,
        y,
        z,
        xy,
        y * z,
        x * z,
        diff,
        3.0 * zz - 1.0,
        x * (xx - 3.0 * yy),
        xy * z,
        y * (3.0 * xx - yy),
        z * diff,
        x * five,
        y * five,
        z * (5.0 * zz - 3.0),
    ]


def project(rows, cam, live):
    mx, my, mz = rows[0], rows[1], rows[2]
    cam_x = cam[0] * mx + cam[1] * my + cam[2] * mz + cam[9]
    cam_y = cam[3] * mx + cam[4] * my + cam[5] * mz + cam[10]
    cam_z = cam[6] * mx + cam[7] * my + cam[8] * mz + cam[11]
    cam_z = jnp.where(live, cam_z, 1.0)
    inv_z = 1.0 / cam_z
    qw, qx, qy, qz = rows[6], rows[7], rows[8], rows[9]
    qw = jnp.where(live, qw, 1.0)
    inv_q = lax.rsqrt(qw * qw + qx * qx + qy * qy + qz * qz)
    qw, qx, qy, qz = qw * inv_q, qx * inv_q, qy * inv_q, qz * inv_q
    rot = [
        [
            1.0 - 2.0 * (qy * qy + qz * qz),
            2.0 * (qx * qy - qw * qz),
            2.0 * (qx * qz + qw * qy),
        ],
        [
            2.0 * (qx * qy + qw * qz),
            1.0 - 2.0 * (qx * qx + qz * qz),
            2.0 * (qy * qz - qw * qx),
        ],
        [
            2.0 * (qx * qz - qw * qy),
            2.0 * (qy * qz + qw * qx),
            1.0 - 2.0 * (qx * qx + qy * qy),
        ],
    ]
    mixed = [
        [
            cam[3 * i] * rot[0][k] + cam[3 * i + 1] * rot[1][k] + cam[3 * i + 2] * rot[2][k]
            for k in range(3)
        ]
        for i in range(3)
    ]
    scale = cam[12] * inv_z
    ray_x, ray_y = cam_x * inv_z, cam_y * inv_z
    proj_u = [scale * (mixed[0][k] - ray_x * mixed[2][k]) for k in range(3)]
    proj_v = [scale * (mixed[1][k] - ray_y * mixed[2][k]) for k in range(3)]
    var = [jnp.exp(2.0 * rows[3 + k]) for k in range(3)]
    uv = [proj_u[k] * var[k] for k in range(3)]
    cov_a = sum(uv[k] * proj_u[k] for k in range(3)) + 0.3
    cov_b = sum(uv[k] * proj_v[k] for k in range(3))
    cov_c = sum(proj_v[k] * proj_v[k] * var[k] for k in range(3)) + 0.3
    inv_det = 1.0 / (cov_a * cov_c - cov_b * cov_b)
    inv_dist = lax.rsqrt(cam_x * cam_x + cam_y * cam_y + cam_z * cam_z)
    terms = sh_terms(cam_x * inv_dist, cam_y * inv_dist, cam_z * inv_dist)
    geometry = [cam_x * scale, cam_y * scale, cov_c * inv_det, -cov_b * inv_det, cov_a * inv_det]
    return geometry + terms, (ray_x, ray_y)


def iota(shape, dim):
    return lax.broadcasted_iota(jnp.int32, shape, dim)


def one_hot(mask):
    return jnp.where(mask, 1.0, 0.0).astype(BF16)


def dot(lhs, rhs, lhs_dim=1, rhs_dim=0):
    return lax.dot_general(
        lhs, rhs, (((lhs_dim,), (rhs_dim,)), ((), ())), preferred_element_type=F32
    )


def split(x, parts):
    out = []
    for _ in range(parts):
        head = x.astype(BF16)
        out.append(head)
        x = x - head.astype(F32)
    return out


def ranks(mask, tiles):
    rows, length = mask.shape
    bits = jnp.where(mask, 1.0, 0.0)
    place = iota((rows, length), 0) % tiles
    shifted = [bits] + [
        jnp.where(place >= d, pltpu.roll(bits, d, 0), 0.0) for d in range(1, tiles)
    ]
    earlier = one_hot(iota((length, length), 0) < iota((length, length), 1))
    counted = jnp.concatenate([earlier] + [jnp.ones_like(earlier)] * (tiles - 1), axis=0)
    return dot(jnp.concatenate(shifted, axis=1).astype(BF16), counted).astype(jnp.int32)


def find(local, tiles, cap, g_dev):
    mine = (local >= 0) & (local < g_dev)
    key = jnp.where(mine, ranks(mine, tiles), -1)
    rows, length = local.shape
    slot = iota((cap, length), 0)
    found = []
    for r in range(0, rows, tiles):
        total = jnp.zeros((cap, length), jnp.int32)
        for t in range(r, r + tiles):
            total = total + jnp.where(key[t : t + 1, :] == slot, local[t : t + 1, :], 0)
        found.append(jnp.sum(total, axis=1, keepdims=True))
    return jnp.concatenate(found, axis=0)


def pick_kernel(tiles, cap, lists_ref, params_ref, picked_ref):
    width, g_dev = params_ref.shape
    where = find(lists_ref[...] - lax.axis_index("gauss") * g_dev, tiles, cap, g_dev)
    hot = one_hot(where == iota((where.shape[0], g_dev), 1))
    wide = jnp.concatenate([params_ref[...], jnp.zeros((LANES - width, g_dev), BF16)], axis=0)
    picked_ref[...] = dot(hot, wide, 1, 1).astype(BF16)


def pick_pair_kernel(cap, peers, *refs):
    lists_refs, refs = refs[:peers], refs[peers:]
    own_ref, other_ref = refs[:2]
    picked_refs, refs = refs[2 : 2 + peers], refs[2 + peers :]
    lists_scratch, picked_scratch = refs
    tiles, length = lists_refs[0].shape
    g_dev = own_ref.shape[1]
    me = lax.axis_index("gauss")
    first = me % 2 == 0
    for k in range(peers):
        lists_scratch[(me // 2) ^ k] = lists_refs[k][...]
    ids = lists_scratch[...].reshape(peers * tiles, length)
    local = jnp.concatenate([ids - me * g_dev, ids - (me ^ 1) * g_dev], axis=0)
    where = find(local, tiles, cap, g_dev)
    where_own, where_other = where[: peers * cap], where[peers * cap :]
    lanes = iota((peers * cap, g_dev), 1)
    of_own = dot(own_ref[...], one_hot(where_own == lanes), 1, 1)
    of_other = dot(other_ref[...], one_hot(where_other == lanes), 1, 1)
    of_even = jnp.where(first, of_own, of_other)
    of_odd = jnp.where(first, of_other, of_own)
    for p in range(peers):
        block = slice(p * cap, (p + 1) * cap)
        picked_scratch[p] = jnp.concatenate(
            [of_even[:, block], of_odd[:, block]], axis=1
        ).astype(BF16)
    for k in range(peers):
        picked_refs[peers - 1 - k][...] = picked_scratch[(me // 2) ^ k]


def by_tile(values, row):
    out = jnp.full(row.shape, values[-1])
    for t in range(len(values) - 1):
        out = jnp.where(row == t, values[t], out)
    return out


def prepare_kernel(
    tile_pos_ref, cam_index_ref, cams_ref, params_ref, copy_ref, cam_ref, pixel_ref
):
    copy_ref[...] = params_ref[...]
    values, tiles, length = cam_ref.shape
    share = LANES // tiles
    depth = SIDE * SIDE // share
    cam_ids = [cam_index_ref[t] for t in range(tiles)]
    tile_row = iota((tiles, length), 0)
    for j in range(values):
        cam_ref[j] = by_tile([cams_ref[cam_ids[t], j] for t in range(tiles)], tile_row)
    pos = [tile_pos_ref[t] for t in range(tiles)]
    lane = iota((depth, LANES), 1)
    origin_x = [(SIDE * (lax.rem(p, WIN) - WIN // 2)).astype(F32) + 0.5 for p in pos]
    pixel_ref[0] = by_tile(origin_x, lane // share) + (lane % SIDE).astype(F32)
    origin_y = [(SIDE * (lax.div(p, WIN) - WIN // 2)).astype(F32) + 0.5 for p in pos]
    pixel_row = iota((depth, LANES), 0) * (share // SIDE) + (lane % share) // SIDE
    pixel_ref[1] = by_tile(origin_y, lane // share) + pixel_row.astype(F32)


def place_kernel(owners, cap, g_dev, lists_ref, after_ref, hot_ref, local_ref):
    tiles, length = lists_ref.shape
    slots = owners * cap
    ids = lists_ref[...]
    masks = [(ids >= o * g_dev) & (ids < (o + 1) * g_dev) for o in range(owners)]
    rank = ranks(jnp.concatenate([m.astype(jnp.int32) for m in masks], axis=0) > 0, tiles)
    place = jnp.full((tiles, length), -1, jnp.int32)
    local = jnp.zeros((tiles, length), jnp.int32)
    for o in range(owners):
        place = jnp.where(masks[o], rank[o * tiles : (o + 1) * tiles] + o * cap, place)
        local = jnp.where(masks[o], ids - o * g_dev, local)
    slot_iota = iota((slots, length), 0)
    hot_ref[...] = jnp.concatenate(
        [one_hot(slot_iota == place[t : t + 1, :]) for t in range(tiles)], axis=1
    )
    local_ref[...] = local.astype(F32)


def render_kernel(pieces, width, *refs):
    recv_refs, refs = refs[:pieces], refs[pieces:]
    lists_ref, hot_ref, local_ref, cam_ref, pixel_ref, targets_ref = refs[:6]
    pictures_ref, send_ref, rows_ref, table_ref, alpha_ref, weight_ref, part_ref = refs[6:13]
    tiles, length = lists_ref.shape
    share = LANES // tiles
    depth = SIDE * SIDE // share
    live = lists_ref[...] >= 0
    hot = hot_ref[...]

    if pieces == 1:
        listed = dot(recv_refs[0][...].reshape(-1, LANES), hot, 0, 0)[:width]
    else:
        (recv_scratch,) = refs[13:]
        place = lax.axis_index("gauss") // 2
        for k in range(pieces):
            recv_scratch[place ^ k] = recv_refs[pieces - 1 - k][...]
        received = jnp.concatenate([recv_scratch[p] for p in range(pieces)], axis=1)
        listed = dot(received, hot)
    for t in range(tiles):
        rows_ref[t * width : (t + 1) * width, :] = listed[:, t * length : (t + 1) * length]
    rows = [rows_ref[pl.ds(f, tiles, stride=width), :] for f in range(width)]

    cam = [cam_ref[j] for j in range(cam_ref.shape[0])]
    outs, pullback, rays = jax.vjp(lambda r: project(r, cam, live), rows[:10], has_aux=True)
    terms = outs[5:]
    colors = []
    for k in range(3):
        base = 11 + 16 * k
        shade = 0.5 + rows[base]
        for b in range(15):
            shade = shade + rows[base + 1 + b] * terms[b]
        for j in range(5):
            shade = shade + rows[59 + j] * cam[13 + 3 * j + k]
        colors.append(shade)
    opacity = jax.nn.sigmoid(rows[10])
    con_a, con_b, con_c = outs[2], outs[3], outs[4]

    attrs = [
        outs[0],
        outs[1],
        (-0.5 * LOG2E) * con_a,
        -LOG2E * con_b,
        (-0.5 * LOG2E) * con_c,
        jnp.where(live, opacity, 0.0),
    ] + colors
    count = len(attrs)
    blocks = []
    for value in attrs:
        parts = [p.astype(F32) for p in split(value, 3)]
        parts.append(jnp.zeros((16 - 3 * tiles, length), F32))
        blocks.append(jnp.concatenate(parts, axis=0))
    stacked = jnp.concatenate(blocks, axis=1)
    lane_tile = iota((16, LANES), 1) // share
    row_index = iota((16, LANES), 0)
    spread = one_hot((row_index % tiles == lane_tile) & (row_index < 3 * tiles))
    table = dot(stacked.T.astype(BF16), spread)
    pixel_x, pixel_y = pixel_ref[0, :1, :], pixel_ref[1]
    dx = pixel_x - table[:length]
    table_ref[0:length, :] = table[2 * length : 3 * length] * dx * dx
    table_ref[length : 2 * length, :] = table[3 * length : 4 * length] * dx
    table_ref[2 * length : 3 * length, :] = table[length : 2 * length]
    table_ref[3 * length :, :] = table[4 * length :]

    def row(index, l):
        return table_ref[index * length + l : index * length + l + 1, :]

    zero = jnp.zeros((depth, LANES), F32)
    through = jnp.ones((depth, LANES), F32)
    red, green, blue = zero, zero, zero
    for l in range(length):
        dy = pixel_y - row(2, l)
        power = row(0, l) + dy * (row(1, l) + row(3, l) * dy)
        alpha = row(4, l) * jnp.exp2(power)
        weight = through * alpha
        red = red + weight * row(5, l)
        green = green + weight * row(6, l)
        blue = blue + weight * row(7, l)
        through = through - weight
        at = slice(l * depth, (l + 1) * depth)
        alpha_ref[at, :] = alpha
        weight_ref[at, :] = weight
    pictures_ref[0] = red
    pictures_ref[1] = green
    pictures_ref[2] = blue
    res = [red - targets_ref[0], green - targets_ref[1], blue - targets_ref[2]]

    behind = zero
    for l in reversed(range(length)):
        at = slice(l * depth, (l + 1) * depth)
        alpha = alpha_ref[at, :]
        weight = weight_ref[at, :]
        dy = pixel_y - row(2, l)
        seen = row(5, l) * res[0] + row(6, l) * res[1] + row(7, l) * res[2]
        gap = seen - behind
        behind = behind + alpha * gap
        g = weight * gap
        gy = g * dy
        part_ref[0, at, :] = g
        part_ref[1, at, :] = gy
        part_ref[2, at, :] = gy * dy
        for k in range(3):
            part_ref[3 + k, at, :] = weight * res[k]

    def down(index):
        blocks = []
        for first in range(0, length, 8):
            parts = [
                part_ref[index, pl.ds(first * depth + s, 8, stride=depth), :] for s in range(depth)
            ]
            while len(parts) > 1:
                parts = [a + b for a, b in zip(parts[::2], parts[1::2])]
            blocks.append(parts[0])
        return jnp.concatenate(blocks, axis=0)

    sums = [down(index) for index in range(6)]
    g_x = sums[0] * dx
    sums = sums + [g_x, g_x * dx, sums[1] * dx]
    wide = jnp.concatenate([jnp.concatenate(split(s, 2), axis=1) for s in sums], axis=0)
    gather = one_hot(iota((8, 2 * LANES), 0) == (iota((8, 2 * LANES), 1) % LANES) // share)
    reduced = dot(gather, wide, 1, 1)
    g_0, g_y, g_yy, s_0, s_1, s_2, g_x, g_xx, g_xy = [
        reduced[:tiles, q * length : (q + 1) * length] for q in range(len(sums))
    ]

    d_colors = [s_0, s_1, s_2]
    d_terms = []
    for b in range(15):
        d_terms.append(sum(d_colors[k] * rows[12 + 16 * k + b] for k in range(3)))
    d_geometry = [
        con_a * g_x + con_b * g_y,
        con_b * g_x + con_c * g_y,
        -0.5 * g_xx,
        -g_xy,
        -0.5 * g_yy,
    ]
    (d_rows,) = pullback(d_geometry + d_terms)
    values = list(d_rows)
    values.append(g_0 * (1.0 - opacity))
    values.extend(d_colors)
    values.extend(rays)
    for j in range(5):
        values.append(sum(d_colors[k] * cam[13 + 3 * j + k] for k in range(3)))
    values.append(local_ref[...])
    values.extend([jnp.zeros((tiles, length), F32)] * (SENT - len(values)))
    for v in range(SENT):
        rows_ref[pl.ds(v, tiles, stride=width), :] = values[v]
    by_slot = jnp.concatenate(
        [
            jnp.concatenate(split(rows_ref[t * width : t * width + SENT, :], 3), axis=0)
            for t in range(tiles)
        ],
        axis=1,
    )
    by_slot = dot(by_slot, hot, 1, 1)
    by_slot = by_slot[:SENT] + by_slot[SENT : 2 * SENT] + by_slot[2 * SENT :]
    owners, copies, high, _ = send_ref.shape
    cap = hot.shape[0] // owners
    for o in range(owners):
        block = jnp.concatenate(
            [by_slot[r : r + high, o * cap : (o + 1) * cap] for r in range(0, SENT, high)], axis=1
        )
        for c in range(copies):
            send_ref[o, c] = block


def entry_rows(cap, recv_ref):
    blocks, high, _ = recv_ref.shape
    values = jnp.concatenate(
        [
            jnp.concatenate(
                [recv_ref[b, :, first : first + cap] for b in range(blocks)], axis=1
            )
            for first in range(0, SENT * cap // high, cap)
        ],
        axis=0,
    )
    ray_x, ray_y = values[14:15], values[15:16]
    dir_z = lax.rsqrt(ray_x * ray_x + ray_y * ray_y + 1.0)
    terms = sh_terms(ray_x * dir_z, ray_y * dir_z, dir_z)
    terms = jnp.concatenate([jnp.ones_like(dir_z)] + terms, axis=0)
    rows = [values] + [terms * values[11 + k : 12 + k] for k in range(3)]
    parts = split(jnp.concatenate(rows, axis=0), 2)
    first = 21 // high * cap
    names = recv_ref[:, 21 % high, first : first + cap].T
    names = jnp.concatenate([names[:, b : b + 1] for b in range(blocks)], axis=0)
    return jnp.concatenate(parts, axis=0), names.astype(jnp.int32)


def scatter(rows, where, first, count):
    hot = one_hot(iota((where.shape[0], count), 1) + first == where)
    total = dot(rows, hot)
    half = total.shape[0] // 2
    return total[:half] + total[half:]


def in_order(total):
    return jnp.concatenate([total[:11], total[SENT:], total[16:21]], axis=0)


def scatter_kernel(cap, recv_ref, out_ref):
    rows, where = entry_rows(cap, recv_ref)
    out_ref[...] = in_order(scatter(rows, where, 0, out_ref.shape[1]))


def first_kernel(cap, recv_ref, out_ref):
    rows, where = entry_rows(cap, recv_ref)
    out_ref[...] = scatter(rows, where, 0, out_ref.shape[1])


def last_kernel(
    cap, recv_ref, sum_ref, spread_ref, out_ref, pictures_ref, sums, pictures, out_sem, picture_sem
):
    _, tiles, _ = pictures.shape
    depth = spread_ref.shape[1]
    share = LANES // tiles
    lane_block = iota((depth, LANES), 1) // share
    row = iota((depth, LANES), 0) % tiles
    for k in range(3):
        spread = spread_ref[k]
        whole = spread
        for d in range(1, tiles):
            down = pltpu.roll(spread, d, 0)
            up = pltpu.roll(spread, depth + d - tiles, 0)
            moved = pltpu.roll(jnp.where(row >= d, down, up), LANES - d * share, 1)
            whole = jnp.where((row - lane_block) % tiles == d, moved, whole)
        for h in range(depth // tiles):
            pictures[k, :, h * LANES : (h + 1) * LANES] = whole[h * tiles : (h + 1) * tiles]
    copies = [pltpu.make_async_copy(pictures, pictures_ref, picture_sem)]
    copies[0].start()
    rows, where = entry_rows(cap, recv_ref)
    blocks, _, count = sums.shape
    for b in range(blocks):
        columns = slice(b * count, (b + 1) * count)
        sums[b] = in_order(sum_ref[:, columns] + scatter(rows, where, b * count, count))
        copies.append(
            pltpu.make_async_copy(
                sums.at[b], out_ref.at[:, pl.ds(b * count, count)], out_sem.at[b]
            )
        )
        copies[-1].start()
    for copy in copies:
        copy.wait()


def call(kernel, out_shape, args, scalars=0, left=0, out_left=False, scratch=()):
    in_specs = [pl.BlockSpec(memory_space=pltpu.SMEM)] * scalars
    in_specs += [pl.BlockSpec(memory_space=pltpu.VMEM)] * (len(args) - scalars - left)
    in_specs += [pl.BlockSpec(memory_space=pl.ANY)] * left
    many = isinstance(out_shape, (list, tuple))
    spec = pl.BlockSpec(memory_space=pl.ANY if out_left else pltpu.VMEM)
    return pl.pallas_call(
        kernel,
        out_shape=out_shape,
        in_specs=in_specs,
        out_specs=[spec] * len(out_shape) if many else spec,
        scratch_shapes=list(scratch),
        compiler_params=pltpu.CompilerParams(vmem_limit_bytes=VMEM_LIMIT),
    )(*args)


def swap(x, axis, k):
    return lax.ppermute(x, axis, [(i, i ^ k) for i in range(lax.axis_size(axis))])


def crossed(owner, owners):
    return int(owner >= owners // 2)


def reach(x, step, flip):
    owners, views = lax.axis_size("gauss"), lax.axis_size("view")
    flip = flip if views % 2 == 0 else 0
    pairs = [
        (g * views + v, (g ^ step) * views + (v ^ flip))
        for g in range(owners)
        for v in range(views)
    ]
    return lax.ppermute(x, ("gauss", "view"), pairs)


def far_first(blocks):
    last = len(blocks) - 1
    peers = range(last, 0, -1)
    return [reach(b, 2 * k, k % 2) for b, k in zip(blocks, peers)] + [blocks[last]]


def exchange(x):
    return lax.all_to_all(x, "gauss", split_axis=0, concat_axis=0, tiled=True)


def exchange_wide(x):
    owners, views = lax.axis_size("gauss"), lax.axis_size("view")
    blocks = x.reshape(owners * views // 2, *x.shape[2:])
    groups = [
        [
            g * views + v
            for g in range(owners)
            for v in range(views)
            if v % 2 == c ^ crossed(g, owners)
        ]
        for c in range(2)
    ]
    return lax.all_to_all(
        blocks,
        ("gauss", "view"),
        split_axis=0,
        concat_axis=0,
        axis_index_groups=groups,
        tiled=True,
    )


def power_of_two(n):
    return n & (n - 1) == 0


def shape(dims, dtype):
    return jax.ShapeDtypeStruct(dims, dtype)


def on_device(params, lists, tile_pos, cam_index, cams, targets):
    owners = lax.axis_size("gauss")
    views = lax.axis_size("view")
    width, g_dev = params.shape
    tiles, length = lists.shape
    cap = max(tiles * length // owners, 16)
    slots = owners * cap
    share = LANES // tiles
    depth = SIDE * SIDE // share
    paired = 2 <= owners <= 16 and power_of_two(owners) and LANES == 2 * width
    peers = owners // 2 if paired else 1
    wide = views % 2 == 0 and owners * views <= 32

    if paired:
        other = reach(params, 1, 1)
        all_lists = far_first([lists] * peers)
    params_copy, cam, pixel = call(
        prepare_kernel,
        [
            shape((width, g_dev), BF16),
            shape((cams.shape[0], tiles, length), F32),
            shape((2, depth, LANES), F32),
        ],
        (tile_pos, cam_index, cams.T, params),
        scalars=3,
    )
    if paired:
        picked = call(
            functools.partial(pick_pair_kernel, cap, peers),
            [shape((width, 2 * cap), BF16)] * peers,
            (*all_lists[::-1], params_copy, other),
            scratch=(
                pltpu.VMEM((peers, tiles, length), jnp.int32),
                pltpu.VMEM((peers, width, 2 * cap), BF16),
            ),
        )
        returned = far_first(picked)
        after = picked[-1]
    else:
        all_lists = exchange(jnp.broadcast_to(lists[None], (owners, tiles, length)))
        picked = call(
            functools.partial(pick_kernel, tiles, cap),
            shape((slots, LANES), BF16),
            (all_lists.reshape(owners * tiles, length), params_copy),
        )
        returned = [exchange(picked.reshape(owners, cap, LANES))]
        after = picked
    hot, local = call(
        functools.partial(place_kernel, owners, cap, g_dev),
        [shape((slots, tiles * length), BF16), shape((tiles, length), F32)],
        (lists, after),
        left=1,
    )
    spread_targets = (
        targets.reshape(3, tiles, depth, share).transpose(0, 2, 1, 3).reshape(3, depth, LANES)
    )
    copies = views // 2 if wide else 1
    high = SENT * cap // LANES
    pictures, sent = call(
        functools.partial(render_kernel, peers, width),
        [shape((3, depth, LANES), F32), shape((owners, copies, high, LANES), F32)],
        (*returned, lists, hot, local, cam, pixel, spread_targets),
        scratch=(
            pltpu.VMEM((tiles * width, length), F32),
            pltpu.VMEM((8 * length, LANES), F32),
            pltpu.VMEM((length * depth, LANES), F32),
            pltpu.VMEM((length * depth, LANES), F32),
            pltpu.VMEM((6, length * depth, LANES), F32),
            pltpu.VMEM((peers, *returned[0].shape[-2:]), BF16),
        ),
    )
    if wide:
        received = exchange_wide(sent)
        other = swap(received, "view", 1)
        total = call(
            functools.partial(first_kernel, cap), shape((SENT + 48, g_dev), F32), (received,)
        )
        parts = 4
        grads, pictures = call(
            functools.partial(last_kernel, cap),
            [shape((width, g_dev), F32), shape(targets.shape, F32)],
            (other, total, pictures),
            out_left=True,
            scratch=(
                pltpu.VMEM((parts, width, g_dev // parts), F32),
                pltpu.VMEM(targets.shape, F32),
                pltpu.SemaphoreType.DMA((parts,)),
                pltpu.SemaphoreType.DMA,
            ),
        )
        return (pictures, grads)
    pictures = (
        pictures.reshape(3, depth, tiles, share)
        .transpose(0, 2, 1, 3)
        .reshape(3, tiles, SIDE * SIDE)
    )
    received = exchange(sent[:, 0])
    grads = call(
        functools.partial(scatter_kernel, cap), shape((width, g_dev), F32), (received,)
    )
    return (pictures, lax.psum(grads, "view"))


def solution(mesh):
    return jax.shard_map(
        on_device,
        mesh=mesh,
        in_specs=(
            P(None, "gauss"),
            P(("gauss", "view"), None),
            P(("gauss", "view")),
            P(("gauss", "view")),
            P(),
            P(None, ("gauss", "view"), None),
        ),
        out_specs=(P(None, ("gauss", "view"), None), P(None, "gauss")),
        check_vma=False,
    )
```

```python
import functools
import math

import jax
import jax.numpy as jnp
from jax import lax
from jax.experimental import pallas as pl
from jax.experimental.pallas import tpu as pltpu
from jax.sharding import PartitionSpec as P

WIN = 16
SIDE = 16
LANES = 128
LOG2E = math.log2(math.e)
F32 = jnp.float32
BF16 = jnp.bfloat16
VMEM_LIMIT = 24 * 2**20
SENT = 32


def sh_terms(x, y, z):
    xx, yy, zz = x * x, y * y, z * z
    xy = x * y
    diff = xx - yy
    five = 5.0 * zz - 1.0
    return [
        x,
        y,
        z,
        xy,
        y * z,
        x * z,
        diff,
        3.0 * zz - 1.0,
        x * (xx - 3.0 * yy),
        xy * z,
        y * (3.0 * xx - yy),
        z * diff,
        x * five,
        y * five,
        z * (5.0 * zz - 3.0),
    ]


def project(rows, cam, live):
    mx, my, mz = rows[0], rows[1], rows[2]
    cam_x = cam[0] * mx + cam[1] * my + cam[2] * mz + cam[9]
    cam_y = cam[3] * mx + cam[4] * my + cam[5] * mz + cam[10]
    cam_z = cam[6] * mx + cam[7] * my + cam[8] * mz + cam[11]
    cam_z = jnp.where(live, cam_z, 1.0)
    inv_z = 1.0 / cam_z
    qw, qx, qy, qz = rows[6], rows[7], rows[8], rows[9]
    qw = jnp.where(live, qw, 1.0)
    inv_q = lax.rsqrt(qw * qw + qx * qx + qy * qy + qz * qz)
    qw, qx, qy, qz = qw * inv_q, qx * inv_q, qy * inv_q, qz * inv_q
    rot = [
        [
            1.0 - 2.0 * (qy * qy + qz * qz),
            2.0 * (qx * qy - qw * qz),
            2.0 * (qx * qz + qw * qy),
        ],
        [
            2.0 * (qx * qy + qw * qz),
            1.0 - 2.0 * (qx * qx + qz * qz),
            2.0 * (qy * qz - qw * qx),
        ],
        [
            2.0 * (qx * qz - qw * qy),
            2.0 * (qy * qz + qw * qx),
            1.0 - 2.0 * (qx * qx + qy * qy),
        ],
    ]
    mixed = [
        [
            cam[3 * i] * rot[0][k] + cam[3 * i + 1] * rot[1][k] + cam[3 * i + 2] * rot[2][k]
            for k in range(3)
        ]
        for i in range(3)
    ]
    scale = cam[12] * inv_z
    ray_x, ray_y = cam_x * inv_z, cam_y * inv_z
    proj_u = [scale * (mixed[0][k] - ray_x * mixed[2][k]) for k in range(3)]
    proj_v = [scale * (mixed[1][k] - ray_y * mixed[2][k]) for k in range(3)]
    var = [jnp.exp(2.0 * rows[3 + k]) for k in range(3)]
    uv = [proj_u[k] * var[k] for k in range(3)]
    cov_a = sum(uv[k] * proj_u[k] for k in range(3)) + 0.3
    cov_b = sum(uv[k] * proj_v[k] for k in range(3))
    cov_c = sum(proj_v[k] * proj_v[k] * var[k] for k in range(3)) + 0.3
    inv_det = 1.0 / (cov_a * cov_c - cov_b * cov_b)
    inv_dist = lax.rsqrt(cam_x * cam_x + cam_y * cam_y + cam_z * cam_z)
    terms = sh_terms(cam_x * inv_dist, cam_y * inv_dist, cam_z * inv_dist)
    geometry = [cam_x * scale, cam_y * scale, cov_c * inv_det, -cov_b * inv_det, cov_a * inv_det]
    return geometry + terms, (ray_x, ray_y)


def iota(shape, dim):
    return lax.broadcasted_iota(jnp.int32, shape, dim)


def one_hot(mask):
    return jnp.where(mask, 1.0, 0.0).astype(BF16)


def dot(lhs, rhs, lhs_dim=1, rhs_dim=0):
    return lax.dot_general(
        lhs, rhs, (((lhs_dim,), (rhs_dim,)), ((), ())), preferred_element_type=F32
    )


def split(x, parts):
    out = []
    for _ in range(parts):
        head = x.astype(BF16)
        out.append(head)
        x = x - head.astype(F32)
    return out


def ranks(mask, tiles):
    rows, length = mask.shape
    bits = jnp.where(mask, 1.0, 0.0)
    place = iota((rows, length), 0) % tiles
    shifted = [bits] + [
        jnp.where(place >= d, pltpu.roll(bits, d, 0), 0.0) for d in range(1, tiles)
    ]
    earlier = one_hot(iota((length, length), 0) < iota((length, length), 1))
    counted = jnp.concatenate([earlier] + [jnp.ones_like(earlier)] * (tiles - 1), axis=0)
    return dot(jnp.concatenate(shifted, axis=1).astype(BF16), counted).astype(jnp.int32)


def find(local, tiles, cap, g_dev):
    mine = (local >= 0) & (local < g_dev)
    key = jnp.where(mine, ranks(mine, tiles), -1)
    rows, length = local.shape
    slot = iota((cap, length), 0)
    found = []
    for r in range(0, rows, tiles):
        total = jnp.zeros((cap, length), jnp.int32)
        for t in range(r, r + tiles):
            total = total + jnp.where(key[t : t + 1, :] == slot, local[t : t + 1, :], 0)
        found.append(jnp.sum(total, axis=1, keepdims=True))
    return jnp.concatenate(found, axis=0)


def pick_kernel(tiles, cap, lists_ref, params_ref, picked_ref):
    width, g_dev = params_ref.shape
    where = find(lists_ref[...] - lax.axis_index("gauss") * g_dev, tiles, cap, g_dev)
    hot = one_hot(where == iota((where.shape[0], g_dev), 1))
    wide = jnp.concatenate([params_ref[...], jnp.zeros((LANES - width, g_dev), BF16)], axis=0)
    picked_ref[...] = dot(hot, wide, 1, 1).astype(BF16)


def pick_pair_kernel(cap, peers, *refs):
    lists_refs, refs = refs[:peers], refs[peers:]
    own_ref, other_ref = refs[:2]
    picked_refs, refs = refs[2 : 2 + peers], refs[2 + peers :]
    lists_scratch, picked_scratch = refs
    tiles, length = lists_refs[0].shape
    g_dev = own_ref.shape[1]
    me = lax.axis_index("gauss")
    first = me % 2 == 0
    for k in range(peers):
        lists_scratch[(me // 2) ^ k] = lists_refs[k][...]
    ids = lists_scratch[...].reshape(peers * tiles, length)
    local = jnp.concatenate([ids - me * g_dev, ids - (me ^ 1) * g_dev], axis=0)
    where = find(local, tiles, cap, g_dev)
    where_own, where_other = where[: peers * cap], where[peers * cap :]
    lanes = iota((peers * cap, g_dev), 1)
    of_own = dot(own_ref[...], one_hot(where_own == lanes), 1, 1)
    of_other = dot(other_ref[...], one_hot(where_other == lanes), 1, 1)
    of_even = jnp.where(first, of_own, of_other)
    of_odd = jnp.where(first, of_other, of_own)
    for p in range(peers):
        block = slice(p * cap, (p + 1) * cap)
        picked_scratch[p] = jnp.concatenate(
            [of_even[:, block], of_odd[:, block]], axis=1
        ).astype(BF16)
    for k in range(peers):
        picked_refs[peers - 1 - k][...] = picked_scratch[(me // 2) ^ k]


def by_tile(values, row):
    out = jnp.full(row.shape, values[-1])
    for t in range(len(values) - 1):
        out = jnp.where(row == t, values[t], out)
    return out


def prepare_kernel(
    tile_pos_ref, cam_index_ref, cams_ref, params_ref, copy_ref, cam_ref, pixel_ref
):
    copy_ref[...] = params_ref[...]
    values, tiles, length = cam_ref.shape
    share = LANES // tiles
    depth = SIDE * SIDE // share
    cam_ids = [cam_index_ref[t] for t in range(tiles)]
    tile_row = iota((tiles, length), 0)
    for j in range(values):
        cam_ref[j] = by_tile([cams_ref[cam_ids[t], j] for t in range(tiles)], tile_row)
    pos = [tile_pos_ref[t] for t in range(tiles)]
    lane = iota((depth, LANES), 1)
    origin_x = [(SIDE * (lax.rem(p, WIN) - WIN // 2)).astype(F32) + 0.5 for p in pos]
    pixel_ref[0] = by_tile(origin_x, lane // share) + (lane % SIDE).astype(F32)
    origin_y = [(SIDE * (lax.div(p, WIN) - WIN // 2)).astype(F32) + 0.5 for p in pos]
    pixel_row = iota((depth, LANES), 0) * (share // SIDE) + (lane % share) // SIDE
    pixel_ref[1] = by_tile(origin_y, lane // share) + pixel_row.astype(F32)


def place_kernel(owners, cap, g_dev, lists_ref, after_ref, hot_ref, local_ref):
    tiles, length = lists_ref.shape
    slots = owners * cap
    ids = lists_ref[...]
    masks = [(ids >= o * g_dev) & (ids < (o + 1) * g_dev) for o in range(owners)]
    rank = ranks(jnp.concatenate([m.astype(jnp.int32) for m in masks], axis=0) > 0, tiles)
    place = jnp.full((tiles, length), -1, jnp.int32)
    local = jnp.zeros((tiles, length), jnp.int32)
    for o in range(owners):
        place = jnp.where(masks[o], rank[o * tiles : (o + 1) * tiles] + o * cap, place)
        local = jnp.where(masks[o], ids - o * g_dev, local)
    slot_iota = iota((slots, length), 0)
    hot_ref[...] = jnp.concatenate(
        [one_hot(slot_iota == place[t : t + 1, :]) for t in range(tiles)], axis=1
    )
    local_ref[...] = local.astype(F32)


def render_kernel(pieces, width, *refs):
    recv_refs, refs = refs[:pieces], refs[pieces:]
    lists_ref, hot_ref, local_ref, cam_ref, pixel_ref, targets_ref = refs[:6]
    pictures_ref, send_ref, rows_ref, table_ref, alpha_ref, weight_ref, part_ref = refs[6:13]
    tiles, length = lists_ref.shape
    share = LANES // tiles
    depth = SIDE * SIDE // share
    live = lists_ref[...] >= 0
    hot = hot_ref[...]

    if pieces == 1:
        listed = dot(recv_refs[0][...].reshape(-1, LANES), hot, 0, 0)[:width]
    else:
        (recv_scratch,) = refs[13:]
        place = lax.axis_index("gauss") // 2
        for k in range(pieces):
            recv_scratch[place ^ k] = recv_refs[pieces - 1 - k][...]
        received = jnp.concatenate([recv_scratch[p] for p in range(pieces)], axis=1)
        listed = dot(received, hot)
    for t in range(tiles):
        rows_ref[t * width : (t + 1) * width, :] = listed[:, t * length : (t + 1) * length]
    rows = [rows_ref[pl.ds(f, tiles, stride=width), :] for f in range(width)]

    cam = [cam_ref[j] for j in range(cam_ref.shape[0])]
    outs, pullback, rays = jax.vjp(lambda r: project(r, cam, live), rows[:10], has_aux=True)
    terms = outs[5:]
    colors = []
    for k in range(3):
        base = 11 + 16 * k
        shade = 0.5 + rows[base]
        for b in range(15):
            shade = shade + rows[base + 1 + b] * terms[b]
        for j in range(5):
            shade = shade + rows[59 + j] * cam[13 + 3 * j + k]
        colors.append(shade)
    opacity = jax.nn.sigmoid(rows[10])
    con_a, con_b, con_c = outs[2], outs[3], outs[4]

    attrs = [
        outs[0],
        outs[1],
        (-0.5 * LOG2E) * con_a,
        -LOG2E * con_b,
        (-0.5 * LOG2E) * con_c,
        jnp.where(live, opacity, 0.0),
    ] + colors
    table = [
        jnp.concatenate(
            [jnp.broadcast_to(value[t : t + 1, :], (share, length)) for t in range(tiles)], axis=0
        ).T
        for value in attrs
    ]
    pixel_x, pixel_y = pixel_ref[0, :1, :], pixel_ref[1]
    dx = pixel_x - table[0]
    columns = [table[2] * dx * dx, table[3] * dx, table[1]] + table[4:]
    for index, column in enumerate(columns):
        table_ref[index * length : (index + 1) * length, :] = column

    def row(index, l):
        return table_ref[index * length + l : index * length + l + 1, :]

    zero = jnp.zeros((depth, LANES), F32)
    through = jnp.ones((depth, LANES), F32)
    red, green, blue = zero, zero, zero
    for l in range(length):
        dy = pixel_y - row(2, l)
        power = row(0, l) + dy * (row(1, l) + row(3, l) * dy)
        alpha = row(4, l) * jnp.exp2(power)
        weight = through * alpha
        red = red + weight * row(5, l)
        green = green + weight * row(6, l)
        blue = blue + weight * row(7, l)
        through = through - weight
        at = slice(l * depth, (l + 1) * depth)
        alpha_ref[at, :] = alpha
        weight_ref[at, :] = weight
    pictures_ref[0] = red
    pictures_ref[1] = green
    pictures_ref[2] = blue
    res = [red - targets_ref[0], green - targets_ref[1], blue - targets_ref[2]]

    behind = zero
    for l in reversed(range(length)):
        at = slice(l * depth, (l + 1) * depth)
        alpha = alpha_ref[at, :]
        weight = weight_ref[at, :]
        dy = pixel_y - row(2, l)
        seen = row(5, l) * res[0] + row(6, l) * res[1] + row(7, l) * res[2]
        gap = seen - behind
        behind = behind + alpha * gap
        g = weight * gap
        gy = g * dy
        part_ref[0, at, :] = g
        part_ref[1, at, :] = gy
        part_ref[2, at, :] = gy * dy
        for k in range(3):
            part_ref[3 + k, at, :] = weight * res[k]

    def down(index):
        blocks = []
        for first in range(0, length, 8):
            parts = [
                part_ref[index, pl.ds(first * depth + s, 8, stride=depth), :] for s in range(depth)
            ]
            while len(parts) > 1:
                parts = [a + b for a, b in zip(parts[::2], parts[1::2])]
            blocks.append(parts[0])
        return jnp.concatenate(blocks, axis=0)

    sums = [down(index) for index in range(6)]
    g_x = sums[0] * dx
    sums = sums + [g_x, g_x * dx, sums[1] * dx]
    wide = jnp.concatenate([jnp.concatenate(split(s, 2), axis=1) for s in sums], axis=0)
    gather = one_hot(iota((8, 2 * LANES), 0) == (iota((8, 2 * LANES), 1) % LANES) // share)
    reduced = dot(gather, wide, 1, 1)
    g_0, g_y, g_yy, s_0, s_1, s_2, g_x, g_xx, g_xy = [
        reduced[:tiles, q * length : (q + 1) * length] for q in range(len(sums))
    ]

    d_colors = [s_0, s_1, s_2]
    d_terms = []
    for b in range(15):
        d_terms.append(sum(d_colors[k] * rows[12 + 16 * k + b] for k in range(3)))
    d_geometry = [
        con_a * g_x + con_b * g_y,
        con_b * g_x + con_c * g_y,
        -0.5 * g_xx,
        -g_xy,
        -0.5 * g_yy,
    ]
    (d_rows,) = pullback(d_geometry + d_terms)
    values = list(d_rows)
    values.append(g_0 * (1.0 - opacity))
    values.extend(d_colors)
    values.extend(rays)
    for j in range(5):
        values.append(sum(d_colors[k] * cam[13 + 3 * j + k] for k in range(3)))
    values.append(local_ref[...])
    values.extend([jnp.zeros((tiles, length), F32)] * (SENT - len(values)))
    for v in range(SENT):
        rows_ref[pl.ds(v, tiles, stride=width), :] = values[v]
    by_slot = jnp.concatenate(
        [
            jnp.concatenate(split(rows_ref[t * width : t * width + SENT, :], 3), axis=0)
            for t in range(tiles)
        ],
        axis=1,
    )
    by_slot = dot(by_slot, hot, 1, 1)
    by_slot = by_slot[:SENT] + by_slot[SENT : 2 * SENT] + by_slot[2 * SENT :]
    owners, copies, high, _ = send_ref.shape
    cap = hot.shape[0] // owners
    for o in range(owners):
        block = jnp.concatenate(
            [by_slot[r : r + high, o * cap : (o + 1) * cap] for r in range(0, SENT, high)], axis=1
        )
        for c in range(copies):
            send_ref[o, c] = block


def entry_rows(cap, recv_ref):
    blocks, high, _ = recv_ref.shape
    values = jnp.concatenate(
        [
            jnp.concatenate(
                [recv_ref[b, :, first : first + cap] for b in range(blocks)], axis=1
            )
            for first in range(0, SENT * cap // high, cap)
        ],
        axis=0,
    )
    ray_x, ray_y = values[14:15], values[15:16]
    dir_z = lax.rsqrt(ray_x * ray_x + ray_y * ray_y + 1.0)
    terms = sh_terms(ray_x * dir_z, ray_y * dir_z, dir_z)
    terms = jnp.concatenate([jnp.ones_like(dir_z)] + terms, axis=0)
    rows = [values] + [terms * values[11 + k : 12 + k] for k in range(3)]
    parts = split(jnp.concatenate(rows, axis=0), 2)
    return jnp.concatenate(parts, axis=0), values[21:22].astype(jnp.int32)


def scatter(rows, where, first, count):
    hot = one_hot(iota((count, where.shape[1]), 0) + first == where)
    total = dot(rows, hot, 1, 1)
    half = total.shape[0] // 2
    return total[:half] + total[half:]


def in_order(total):
    return jnp.concatenate([total[:11], total[SENT:], total[16:21]], axis=0)


def scatter_kernel(cap, recv_ref, out_ref):
    rows, where = entry_rows(cap, recv_ref)
    out_ref[...] = in_order(scatter(rows, where, 0, out_ref.shape[1]))


def first_kernel(cap, recv_ref, out_ref):
    rows, where = entry_rows(cap, recv_ref)
    out_ref[...] = scatter(rows, where, 0, out_ref.shape[1])


def last_kernel(
    cap, recv_ref, sum_ref, spread_ref, out_ref, pictures_ref, sums, pictures, out_sem, picture_sem
):
    _, tiles, _ = pictures.shape
    depth = spread_ref.shape[1]
    share = LANES // tiles
    lane_block = iota((depth, LANES), 1) // share
    row = iota((depth, LANES), 0) % tiles
    for k in range(3):
        spread = spread_ref[k]
        whole = spread
        for d in range(1, tiles):
            down = pltpu.roll(spread, d, 0)
            up = pltpu.roll(spread, depth + d - tiles, 0)
            moved = pltpu.roll(jnp.where(row >= d, down, up), LANES - d * share, 1)
            whole = jnp.where((row - lane_block) % tiles == d, moved, whole)
        for h in range(depth // tiles):
            pictures[k, :, h * LANES : (h + 1) * LANES] = whole[h * tiles : (h + 1) * tiles]
    copies = [pltpu.make_async_copy(pictures, pictures_ref, picture_sem)]
    copies[0].start()
    rows, where = entry_rows(cap, recv_ref)
    blocks, _, count = sums.shape
    for b in range(blocks):
        columns = slice(b * count, (b + 1) * count)
        sums[b] = in_order(sum_ref[:, columns] + scatter(rows, where, b * count, count))
        copies.append(
            pltpu.make_async_copy(
                sums.at[b], out_ref.at[:, pl.ds(b * count, count)], out_sem.at[b]
            )
        )
        copies[-1].start()
    for copy in copies:
        copy.wait()


def call(kernel, out_shape, args, scalars=0, left=0, out_left=False, scratch=()):
    in_specs = [pl.BlockSpec(memory_space=pltpu.SMEM)] * scalars
    in_specs += [pl.BlockSpec(memory_space=pltpu.VMEM)] * (len(args) - scalars - left)
    in_specs += [pl.BlockSpec(memory_space=pl.ANY)] * left
    many = isinstance(out_shape, (list, tuple))
    spec = pl.BlockSpec(memory_space=pl.ANY if out_left else pltpu.VMEM)
    return pl.pallas_call(
        kernel,
        out_shape=out_shape,
        in_specs=in_specs,
        out_specs=[spec] * len(out_shape) if many else spec,
        scratch_shapes=list(scratch),
        compiler_params=pltpu.CompilerParams(vmem_limit_bytes=VMEM_LIMIT),
    )(*args)


def swap(x, axis, k):
    return lax.ppermute(x, axis, [(i, i ^ k) for i in range(lax.axis_size(axis))])


def crossed(owner, owners):
    return int(owner >= owners // 2)


def reach(x, step, flip):
    owners, views = lax.axis_size("gauss"), lax.axis_size("view")
    flip = flip if views % 2 == 0 else 0
    pairs = [
        (g * views + v, (g ^ step) * views + (v ^ flip))
        for g in range(owners)
        for v in range(views)
    ]
    return lax.ppermute(x, ("gauss", "view"), pairs)


def far_first(blocks):
    last = len(blocks) - 1
    peers = range(last, 0, -1)
    return [reach(b, 2 * k, k % 2) for b, k in zip(blocks, peers)] + [blocks[last]]


def exchange(x):
    return lax.all_to_all(x, "gauss", split_axis=0, concat_axis=0, tiled=True)


def exchange_wide(x):
    owners, views = lax.axis_size("gauss"), lax.axis_size("view")
    blocks = x.reshape(owners * views // 2, *x.shape[2:])
    groups = [
        [
            g * views + v
            for g in range(owners)
            for v in range(views)
            if v % 2 == c ^ crossed(g, owners)
        ]
        for c in range(2)
    ]
    return lax.all_to_all(
        blocks,
        ("gauss", "view"),
        split_axis=0,
        concat_axis=0,
        axis_index_groups=groups,
        tiled=True,
    )


def power_of_two(n):
    return n & (n - 1) == 0


def shape(dims, dtype):
    return jax.ShapeDtypeStruct(dims, dtype)


def on_device(params, lists, tile_pos, cam_index, cams, targets):
    owners = lax.axis_size("gauss")
    views = lax.axis_size("view")
    width, g_dev = params.shape
    tiles, length = lists.shape
    cap = max(tiles * length // owners, 16)
    slots = owners * cap
    share = LANES // tiles
    depth = SIDE * SIDE // share
    paired = 2 <= owners <= 16 and power_of_two(owners) and LANES == 2 * width
    peers = owners // 2 if paired else 1
    wide = views % 2 == 0 and owners * views <= 32

    if paired:
        other = reach(params, 1, 1)
        all_lists = far_first([lists] * peers)
    params_copy, cam, pixel = call(
        prepare_kernel,
        [
            shape((width, g_dev), BF16),
            shape((cams.shape[0], tiles, length), F32),
            shape((2, depth, LANES), F32),
        ],
        (tile_pos, cam_index, cams.T, params),
        scalars=3,
    )
    if paired:
        picked = call(
            functools.partial(pick_pair_kernel, cap, peers),
            [shape((width, 2 * cap), BF16)] * peers,
            (*all_lists[::-1], params_copy, other),
            scratch=(
                pltpu.VMEM((peers, tiles, length), jnp.int32),
                pltpu.VMEM((peers, width, 2 * cap), BF16),
            ),
        )
        returned = far_first(picked)
        after = picked[-1]
    else:
        all_lists = exchange(jnp.broadcast_to(lists[None], (owners, tiles, length)))
        picked = call(
            functools.partial(pick_kernel, tiles, cap),
            shape((slots, LANES), BF16),
            (all_lists.reshape(owners * tiles, length), params_copy),
        )
        returned = [exchange(picked.reshape(owners, cap, LANES))]
        after = picked
    hot, local = call(
        functools.partial(place_kernel, owners, cap, g_dev),
        [shape((slots, tiles * length), BF16), shape((tiles, length), F32)],
        (lists, after),
        left=1,
    )
    spread_targets = (
        targets.reshape(3, tiles, depth, share).transpose(0, 2, 1, 3).reshape(3, depth, LANES)
    )
    copies = views // 2 if wide else 1
    high = SENT * cap // LANES
    pictures, sent = call(
        functools.partial(render_kernel, peers, width),
        [shape((3, depth, LANES), F32), shape((owners, copies, high, LANES), F32)],
        (*returned, lists, hot, local, cam, pixel, spread_targets),
        scratch=(
            pltpu.VMEM((tiles * width, length), F32),
            pltpu.VMEM((8 * length, LANES), F32),
            pltpu.VMEM((length * depth, LANES), F32),
            pltpu.VMEM((length * depth, LANES), F32),
            pltpu.VMEM((6, length * depth, LANES), F32),
            pltpu.VMEM((peers, *returned[0].shape[-2:]), BF16),
        ),
    )
    if wide:
        received = exchange_wide(sent)
        other = swap(received, "view", 1)
        total = call(
            functools.partial(first_kernel, cap), shape((SENT + 48, g_dev), F32), (received,)
        )
        parts = 4
        grads, pictures = call(
            functools.partial(last_kernel, cap),
            [shape((width, g_dev), F32), shape(targets.shape, F32)],
            (other, total, pictures),
            out_left=True,
            scratch=(
                pltpu.VMEM((parts, width, g_dev // parts), F32),
                pltpu.VMEM(targets.shape, F32),
                pltpu.SemaphoreType.DMA((parts,)),
                pltpu.SemaphoreType.DMA,
            ),
        )
        return (pictures, grads)
    pictures = (
        pictures.reshape(3, depth, tiles, share)
        .transpose(0, 2, 1, 3)
        .reshape(3, tiles, SIDE * SIDE)
    )
    received = exchange(sent[:, 0])
    grads = call(
        functools.partial(scatter_kernel, cap), shape((width, g_dev), F32), (received,)
    )
    return (pictures, lax.psum(grads, "view"))


def solution(mesh):
    return jax.shard_map(
        on_device,
        mesh=mesh,
        in_specs=(
            P(None, "gauss"),
            P(("gauss", "view"), None),
            P(("gauss", "view")),
            P(("gauss", "view")),
            P(),
            P(None, ("gauss", "view"), None),
        ),
        out_specs=(P(None, ("gauss", "view"), None), P(None, "gauss")),
        check_vma=False,
    )
```

```python
import functools
import math

import jax
import jax.numpy as jnp
from jax import lax
from jax.experimental import pallas as pl
from jax.experimental.pallas import tpu as pltpu
from jax.sharding import PartitionSpec as P

WIN = 16
SIDE = 16
LANES = 128
LOG2E = math.log2(math.e)
F32 = jnp.float32
BF16 = jnp.bfloat16
VMEM_LIMIT = 24 * 2**20
SENT = 32


def sh_terms(x, y, z):
    xx, yy, zz = x * x, y * y, z * z
    xy = x * y
    diff = xx - yy
    five = 5.0 * zz - 1.0
    return [
        x,
        y,
        z,
        xy,
        y * z,
        x * z,
        diff,
        3.0 * zz - 1.0,
        x * (xx - 3.0 * yy),
        xy * z,
        y * (3.0 * xx - yy),
        z * diff,
        x * five,
        y * five,
        z * (5.0 * zz - 3.0),
    ]


def project(rows, cam, live):
    mx, my, mz = rows[0], rows[1], rows[2]
    cam_x = cam[0] * mx + cam[1] * my + cam[2] * mz + cam[9]
    cam_y = cam[3] * mx + cam[4] * my + cam[5] * mz + cam[10]
    cam_z = cam[6] * mx + cam[7] * my + cam[8] * mz + cam[11]
    cam_z = jnp.where(live, cam_z, 1.0)
    inv_z = 1.0 / cam_z
    qw, qx, qy, qz = rows[6], rows[7], rows[8], rows[9]
    qw = jnp.where(live, qw, 1.0)
    inv_q = lax.rsqrt(qw * qw + qx * qx + qy * qy + qz * qz)
    qw, qx, qy, qz = qw * inv_q, qx * inv_q, qy * inv_q, qz * inv_q
    rot = [
        [
            1.0 - 2.0 * (qy * qy + qz * qz),
            2.0 * (qx * qy - qw * qz),
            2.0 * (qx * qz + qw * qy),
        ],
        [
            2.0 * (qx * qy + qw * qz),
            1.0 - 2.0 * (qx * qx + qz * qz),
            2.0 * (qy * qz - qw * qx),
        ],
        [
            2.0 * (qx * qz - qw * qy),
            2.0 * (qy * qz + qw * qx),
            1.0 - 2.0 * (qx * qx + qy * qy),
        ],
    ]
    mixed = [
        [
            cam[3 * i] * rot[0][k] + cam[3 * i + 1] * rot[1][k] + cam[3 * i + 2] * rot[2][k]
            for k in range(3)
        ]
        for i in range(3)
    ]
    scale = cam[12] * inv_z
    ray_x, ray_y = cam_x * inv_z, cam_y * inv_z
    proj_u = [scale * (mixed[0][k] - ray_x * mixed[2][k]) for k in range(3)]
    proj_v = [scale * (mixed[1][k] - ray_y * mixed[2][k]) for k in range(3)]
    var = [jnp.exp(2.0 * rows[3 + k]) for k in range(3)]
    uv = [proj_u[k] * var[k] for k in range(3)]
    cov_a = sum(uv[k] * proj_u[k] for k in range(3)) + 0.3
    cov_b = sum(uv[k] * proj_v[k] for k in range(3))
    cov_c = sum(proj_v[k] * proj_v[k] * var[k] for k in range(3)) + 0.3
    inv_det = 1.0 / (cov_a * cov_c - cov_b * cov_b)
    inv_dist = lax.rsqrt(cam_x * cam_x + cam_y * cam_y + cam_z * cam_z)
    terms = sh_terms(cam_x * inv_dist, cam_y * inv_dist, cam_z * inv_dist)
    geometry = [cam_x * scale, cam_y * scale, cov_c * inv_det, -cov_b * inv_det, cov_a * inv_det]
    return geometry + terms, (ray_x, ray_y)


def iota(shape, dim):
    return lax.broadcasted_iota(jnp.int32, shape, dim)


def one_hot(mask):
    return jnp.where(mask, 1.0, 0.0).astype(BF16)


def dot(lhs, rhs, lhs_dim=1, rhs_dim=0):
    return lax.dot_general(
        lhs, rhs, (((lhs_dim,), (rhs_dim,)), ((), ())), preferred_element_type=F32
    )


def split(x, parts):
    out = []
    for _ in range(parts):
        head = x.astype(BF16)
        out.append(head)
        x = x - head.astype(F32)
    return out


def ranks(mask, tiles):
    rows, length = mask.shape
    bits = jnp.where(mask, 1.0, 0.0)
    place = iota((rows, length), 0) % tiles
    shifted = [bits] + [
        jnp.where(place >= d, pltpu.roll(bits, d, 0), 0.0) for d in range(1, tiles)
    ]
    earlier = one_hot(iota((length, length), 0) < iota((length, length), 1))
    counted = jnp.concatenate([earlier] + [jnp.ones_like(earlier)] * (tiles - 1), axis=0)
    return dot(jnp.concatenate(shifted, axis=1).astype(BF16), counted).astype(jnp.int32)


def find(local, tiles, cap, g_dev):
    mine = (local >= 0) & (local < g_dev)
    key = jnp.where(mine, ranks(mine, tiles), -1)
    rows, length = local.shape
    slot = iota((cap, length), 0)
    found = []
    for r in range(0, rows, tiles):
        total = jnp.zeros((cap, length), jnp.int32)
        for t in range(r, r + tiles):
            total = total + jnp.where(key[t : t + 1, :] == slot, local[t : t + 1, :], 0)
        found.append(jnp.sum(total, axis=1, keepdims=True))
    return jnp.concatenate(found, axis=0)


def pick_kernel(tiles, cap, lists_ref, params_ref, picked_ref):
    width, g_dev = params_ref.shape
    where = find(lists_ref[...] - lax.axis_index("gauss") * g_dev, tiles, cap, g_dev)
    hot = one_hot(where == iota((where.shape[0], g_dev), 1))
    wide = jnp.concatenate([params_ref[...], jnp.zeros((LANES - width, g_dev), BF16)], axis=0)
    picked_ref[...] = dot(hot, wide, 1, 1).astype(BF16)


def pick_pair_kernel(cap, peers, *refs):
    lists_refs, refs = refs[:peers], refs[peers:]
    own_ref, other_ref = refs[:2]
    picked_refs, refs = refs[2 : 2 + peers], refs[2 + peers :]
    lists_scratch, picked_scratch = refs
    tiles, length = lists_refs[0].shape
    g_dev = own_ref.shape[1]
    me = lax.axis_index("gauss")
    first = me % 2 == 0
    for k in range(peers):
        lists_scratch[(me // 2) ^ k] = lists_refs[k][...]
    ids = lists_scratch[...].reshape(peers * tiles, length)
    local = jnp.concatenate([ids - me * g_dev, ids - (me ^ 1) * g_dev], axis=0)
    where = find(local, tiles, cap, g_dev)
    where_own, where_other = where[: peers * cap], where[peers * cap :]
    lanes = iota((peers * cap, g_dev), 1)
    of_own = dot(own_ref[...], one_hot(where_own == lanes), 1, 1)
    of_other = dot(other_ref[...], one_hot(where_other == lanes), 1, 1)
    of_even = jnp.where(first, of_own, of_other)
    of_odd = jnp.where(first, of_other, of_own)
    for p in range(peers):
        block = slice(p * cap, (p + 1) * cap)
        picked_scratch[p] = jnp.concatenate(
            [of_even[:, block], of_odd[:, block]], axis=1
        ).astype(BF16)
    for k in range(peers):
        picked_refs[peers - 1 - k][...] = picked_scratch[(me // 2) ^ k]


def by_tile(values, row):
    out = jnp.full(row.shape, values[-1])
    for t in range(len(values) - 1):
        out = jnp.where(row == t, values[t], out)
    return out


def prepare_kernel(
    tile_pos_ref, cam_index_ref, cams_ref, params_ref, copy_ref, cam_ref, pixel_ref
):
    copy_ref[...] = params_ref[...]
    values, tiles, length = cam_ref.shape
    share = LANES // tiles
    depth = SIDE * SIDE // share
    cam_ids = [cam_index_ref[t] for t in range(tiles)]
    tile_row = iota((tiles, length), 0)
    for j in range(values):
        cam_ref[j] = by_tile([cams_ref[cam_ids[t], j] for t in range(tiles)], tile_row)
    pos = [tile_pos_ref[t] for t in range(tiles)]
    lane = iota((depth, LANES), 1)
    origin_x = [(SIDE * (lax.rem(p, WIN) - WIN // 2)).astype(F32) + 0.5 for p in pos]
    pixel_ref[0] = by_tile(origin_x, lane // share) + (lane % SIDE).astype(F32)
    origin_y = [(SIDE * (lax.div(p, WIN) - WIN // 2)).astype(F32) + 0.5 for p in pos]
    pixel_row = iota((depth, LANES), 0) * (share // SIDE) + (lane % share) // SIDE
    pixel_ref[1] = by_tile(origin_y, lane // share) + pixel_row.astype(F32)


def place_kernel(owners, cap, g_dev, lists_ref, after_ref, hot_ref, local_ref):
    tiles, length = lists_ref.shape
    slots = owners * cap
    ids = lists_ref[...]
    masks = [(ids >= o * g_dev) & (ids < (o + 1) * g_dev) for o in range(owners)]
    rank = ranks(jnp.concatenate([m.astype(jnp.int32) for m in masks], axis=0) > 0, tiles)
    place = jnp.full((tiles, length), -1, jnp.int32)
    local = jnp.zeros((tiles, length), jnp.int32)
    for o in range(owners):
        place = jnp.where(masks[o], rank[o * tiles : (o + 1) * tiles] + o * cap, place)
        local = jnp.where(masks[o], ids - o * g_dev, local)
    slot_iota = iota((slots, length), 0)
    hot_ref[...] = jnp.concatenate(
        [one_hot(slot_iota == place[t : t + 1, :]) for t in range(tiles)], axis=1
    )
    local_ref[...] = local.astype(F32)


def render_kernel(pieces, width, *refs):
    recv_refs, refs = refs[:pieces], refs[pieces:]
    lists_ref, hot_ref, local_ref, cam_ref, pixel_ref, targets_ref = refs[:6]
    pictures_ref, send_ref, rows_ref, table_ref, alpha_ref, weight_ref, part_ref = refs[6:13]
    tiles, length = lists_ref.shape
    share = LANES // tiles
    depth = SIDE * SIDE // share
    live = lists_ref[...] >= 0
    hot = hot_ref[...]

    if pieces == 1:
        listed = dot(recv_refs[0][...].reshape(-1, LANES), hot, 0, 0)[:width]
    else:
        (recv_scratch,) = refs[13:]
        place = lax.axis_index("gauss") // 2
        for k in range(pieces):
            recv_scratch[place ^ k] = recv_refs[pieces - 1 - k][...]
        received = jnp.concatenate([recv_scratch[p] for p in range(pieces)], axis=1)
        listed = dot(received, hot)
    for t in range(tiles):
        rows_ref[t * width : (t + 1) * width, :] = listed[:, t * length : (t + 1) * length]
    rows = [rows_ref[pl.ds(f, tiles, stride=width), :] for f in range(width)]

    cam = [cam_ref[j] for j in range(cam_ref.shape[0])]
    outs, pullback, rays = jax.vjp(lambda r: project(r, cam, live), rows[:10], has_aux=True)
    terms = outs[5:]
    colors = []
    for k in range(3):
        base = 11 + 16 * k
        shade = 0.5 + rows[base]
        for b in range(15):
            shade = shade + rows[base + 1 + b] * terms[b]
        for j in range(5):
            shade = shade + rows[59 + j] * cam[13 + 3 * j + k]
        colors.append(shade)
    opacity = jax.nn.sigmoid(rows[10])
    con_a, con_b, con_c = outs[2], outs[3], outs[4]

    attrs = [
        outs[0],
        outs[1],
        (-0.5 * LOG2E) * con_a,
        -LOG2E * con_b,
        (-0.5 * LOG2E) * con_c,
        jnp.where(live, opacity, 0.0),
    ] + colors
    table = [
        jnp.concatenate(
            [jnp.broadcast_to(value[t : t + 1, :], (share, length)) for t in range(tiles)], axis=0
        ).T
        for value in attrs
    ]
    pixel_x, pixel_y = pixel_ref[0, :1, :], pixel_ref[1]
    dx = pixel_x - table[0]
    columns = [table[2] * dx * dx, table[3] * dx, table[1]] + table[4:]
    for index, column in enumerate(columns):
        table_ref[index * length : (index + 1) * length, :] = column

    def row(index, l):
        return table_ref[index * length + l : index * length + l + 1, :]

    zero = jnp.zeros((depth, LANES), F32)
    through = jnp.ones((depth, LANES), F32)
    red, green, blue = zero, zero, zero
    for l in range(length):
        dy = pixel_y - row(2, l)
        power = row(0, l) + dy * (row(1, l) + row(3, l) * dy)
        alpha = row(4, l) * jnp.exp2(power)
        weight = through * alpha
        red = red + weight * row(5, l)
        green = green + weight * row(6, l)
        blue = blue + weight * row(7, l)
        through = through - weight
        at = slice(l * depth, (l + 1) * depth)
        alpha_ref[at, :] = alpha
        weight_ref[at, :] = weight
    pictures_ref[0] = red
    pictures_ref[1] = green
    pictures_ref[2] = blue
    res = [red - targets_ref[0], green - targets_ref[1], blue - targets_ref[2]]

    behind = zero
    for l in reversed(range(length)):
        at = slice(l * depth, (l + 1) * depth)
        alpha = alpha_ref[at, :]
        weight = weight_ref[at, :]
        dy = pixel_y - row(2, l)
        seen = row(5, l) * res[0] + row(6, l) * res[1] + row(7, l) * res[2]
        gap = seen - behind
        behind = behind + alpha * gap
        g = weight * gap
        gy = g * dy
        part_ref[0, at, :] = g
        part_ref[1, at, :] = gy
        part_ref[2, at, :] = gy * dy
        for k in range(3):
            part_ref[3 + k, at, :] = weight * res[k]

    def down(index):
        blocks = []
        for first in range(0, length, 8):
            parts = [
                part_ref[index, pl.ds(first * depth + s, 8, stride=depth), :] for s in range(depth)
            ]
            while len(parts) > 1:
                parts = [a + b for a, b in zip(parts[::2], parts[1::2])]
            blocks.append(parts[0])
        return jnp.concatenate(blocks, axis=0)

    sums = [down(index) for index in range(6)]
    g_x = sums[0] * dx
    sums = sums + [g_x, g_x * dx, sums[1] * dx]
    def over_lanes(x):
        x = x.T
        return jnp.concatenate(
            [
                jnp.sum(x[t * share : (t + 1) * share], axis=0, keepdims=True)
                for t in range(tiles)
            ],
            axis=0,
        )

    g_0, g_y, g_yy, s_0, s_1, s_2, g_x, g_xx, g_xy = [over_lanes(s) for s in sums]

    d_colors = [s_0, s_1, s_2]
    d_terms = []
    for b in range(15):
        d_terms.append(sum(d_colors[k] * rows[12 + 16 * k + b] for k in range(3)))
    d_geometry = [
        con_a * g_x + con_b * g_y,
        con_b * g_x + con_c * g_y,
        -0.5 * g_xx,
        -g_xy,
        -0.5 * g_yy,
    ]
    (d_rows,) = pullback(d_geometry + d_terms)
    values = list(d_rows)
    values.append(g_0 * (1.0 - opacity))
    values.extend(d_colors)
    values.extend(rays)
    for j in range(5):
        values.append(sum(d_colors[k] * cam[13 + 3 * j + k] for k in range(3)))
    values.append(local_ref[...])
    values.extend([jnp.zeros((tiles, length), F32)] * (SENT - len(values)))
    for v in range(SENT):
        rows_ref[pl.ds(v, tiles, stride=width), :] = values[v]
    by_slot = jnp.concatenate(
        [
            jnp.concatenate(split(rows_ref[t * width : t * width + SENT, :], 3), axis=0)
            for t in range(tiles)
        ],
        axis=1,
    )
    by_slot = dot(by_slot, hot, 1, 1)
    by_slot = by_slot[:SENT] + by_slot[SENT : 2 * SENT] + by_slot[2 * SENT :]
    owners, copies, high, _ = send_ref.shape
    cap = hot.shape[0] // owners
    for o in range(owners):
        block = jnp.concatenate(
            [by_slot[r : r + high, o * cap : (o + 1) * cap] for r in range(0, SENT, high)], axis=1
        )
        for c in range(copies):
            send_ref[o, c] = block


def entry_rows(cap, recv_ref):
    blocks, high, _ = recv_ref.shape
    values = jnp.concatenate(
        [
            jnp.concatenate(
                [recv_ref[b, :, first : first + cap] for b in range(blocks)], axis=1
            )
            for first in range(0, SENT * cap // high, cap)
        ],
        axis=0,
    )
    ray_x, ray_y = values[14:15], values[15:16]
    dir_z = lax.rsqrt(ray_x * ray_x + ray_y * ray_y + 1.0)
    terms = sh_terms(ray_x * dir_z, ray_y * dir_z, dir_z)
    terms = jnp.concatenate([jnp.ones_like(dir_z)] + terms, axis=0)
    rows = [values] + [terms * values[11 + k : 12 + k] for k in range(3)]
    parts = split(jnp.concatenate(rows, axis=0), 2)
    return jnp.concatenate(parts, axis=0), values[21:22].astype(jnp.int32)


def scatter(rows, where, first, count):
    hot = one_hot(iota((count, where.shape[1]), 0) + first == where)
    total = dot(rows, hot, 1, 1)
    half = total.shape[0] // 2
    return total[:half] + total[half:]


def in_order(total):
    return jnp.concatenate([total[:11], total[SENT:], total[16:21]], axis=0)


def scatter_kernel(cap, recv_ref, out_ref):
    rows, where = entry_rows(cap, recv_ref)
    out_ref[...] = in_order(scatter(rows, where, 0, out_ref.shape[1]))


def first_kernel(cap, recv_ref, out_ref):
    rows, where = entry_rows(cap, recv_ref)
    out_ref[...] = scatter(rows, where, 0, out_ref.shape[1])


def last_kernel(
    cap, recv_ref, sum_ref, spread_ref, out_ref, pictures_ref, sums, pictures, out_sem, picture_sem
):
    _, tiles, _ = pictures.shape
    depth = spread_ref.shape[1]
    share = LANES // tiles
    lane_block = iota((depth, LANES), 1) // share
    row = iota((depth, LANES), 0) % tiles
    for k in range(3):
        spread = spread_ref[k]
        whole = spread
        for d in range(1, tiles):
            down = pltpu.roll(spread, d, 0)
            up = pltpu.roll(spread, depth + d - tiles, 0)
            moved = pltpu.roll(jnp.where(row >= d, down, up), LANES - d * share, 1)
            whole = jnp.where((row - lane_block) % tiles == d, moved, whole)
        for h in range(depth // tiles):
            pictures[k, :, h * LANES : (h + 1) * LANES] = whole[h * tiles : (h + 1) * tiles]
    copies = [pltpu.make_async_copy(pictures, pictures_ref, picture_sem)]
    copies[0].start()
    rows, where = entry_rows(cap, recv_ref)
    blocks, _, count = sums.shape
    for b in range(blocks):
        columns = slice(b * count, (b + 1) * count)
        sums[b] = in_order(sum_ref[:, columns] + scatter(rows, where, b * count, count))
        copies.append(
            pltpu.make_async_copy(
                sums.at[b], out_ref.at[:, pl.ds(b * count, count)], out_sem.at[b]
            )
        )
        copies[-1].start()
    for copy in copies:
        copy.wait()


def call(kernel, out_shape, args, scalars=0, left=0, out_left=False, scratch=()):
    in_specs = [pl.BlockSpec(memory_space=pltpu.SMEM)] * scalars
    in_specs += [pl.BlockSpec(memory_space=pltpu.VMEM)] * (len(args) - scalars - left)
    in_specs += [pl.BlockSpec(memory_space=pl.ANY)] * left
    many = isinstance(out_shape, (list, tuple))
    spec = pl.BlockSpec(memory_space=pl.ANY if out_left else pltpu.VMEM)
    return pl.pallas_call(
        kernel,
        out_shape=out_shape,
        in_specs=in_specs,
        out_specs=[spec] * len(out_shape) if many else spec,
        scratch_shapes=list(scratch),
        compiler_params=pltpu.CompilerParams(vmem_limit_bytes=VMEM_LIMIT),
    )(*args)


def swap(x, axis, k):
    return lax.ppermute(x, axis, [(i, i ^ k) for i in range(lax.axis_size(axis))])


def crossed(owner, owners):
    return int(owner >= owners // 2)


def reach(x, step, flip):
    owners, views = lax.axis_size("gauss"), lax.axis_size("view")
    flip = flip if views % 2 == 0 else 0
    pairs = [
        (g * views + v, (g ^ step) * views + (v ^ flip))
        for g in range(owners)
        for v in range(views)
    ]
    return lax.ppermute(x, ("gauss", "view"), pairs)


def far_first(blocks):
    last = len(blocks) - 1
    peers = range(last, 0, -1)
    return [reach(b, 2 * k, k % 2) for b, k in zip(blocks, peers)] + [blocks[last]]


def exchange(x):
    return lax.all_to_all(x, "gauss", split_axis=0, concat_axis=0, tiled=True)


def exchange_wide(x):
    owners, views = lax.axis_size("gauss"), lax.axis_size("view")
    blocks = x.reshape(owners * views // 2, *x.shape[2:])
    groups = [
        [
            g * views + v
            for g in range(owners)
            for v in range(views)
            if v % 2 == c ^ crossed(g, owners)
        ]
        for c in range(2)
    ]
    return lax.all_to_all(
        blocks,
        ("gauss", "view"),
        split_axis=0,
        concat_axis=0,
        axis_index_groups=groups,
        tiled=True,
    )


def power_of_two(n):
    return n & (n - 1) == 0


def shape(dims, dtype):
    return jax.ShapeDtypeStruct(dims, dtype)


def on_device(params, lists, tile_pos, cam_index, cams, targets):
    owners = lax.axis_size("gauss")
    views = lax.axis_size("view")
    width, g_dev = params.shape
    tiles, length = lists.shape
    cap = max(tiles * length // owners, 16)
    slots = owners * cap
    share = LANES // tiles
    depth = SIDE * SIDE // share
    paired = 2 <= owners <= 16 and power_of_two(owners) and LANES == 2 * width
    peers = owners // 2 if paired else 1
    wide = views % 2 == 0 and owners * views <= 32

    if paired:
        other = reach(params, 1, 1)
        all_lists = far_first([lists] * peers)
    params_copy, cam, pixel = call(
        prepare_kernel,
        [
            shape((width, g_dev), BF16),
            shape((cams.shape[0], tiles, length), F32),
            shape((2, depth, LANES), F32),
        ],
        (tile_pos, cam_index, cams.T, params),
        scalars=3,
    )
    if paired:
        picked = call(
            functools.partial(pick_pair_kernel, cap, peers),
            [shape((width, 2 * cap), BF16)] * peers,
            (*all_lists[::-1], params_copy, other),
            scratch=(
                pltpu.VMEM((peers, tiles, length), jnp.int32),
                pltpu.VMEM((peers, width, 2 * cap), BF16),
            ),
        )
        returned = far_first(picked)
        after = picked[-1]
    else:
        all_lists = exchange(jnp.broadcast_to(lists[None], (owners, tiles, length)))
        picked = call(
            functools.partial(pick_kernel, tiles, cap),
            shape((slots, LANES), BF16),
            (all_lists.reshape(owners * tiles, length), params_copy),
        )
        returned = [exchange(picked.reshape(owners, cap, LANES))]
        after = picked
    hot, local = call(
        functools.partial(place_kernel, owners, cap, g_dev),
        [shape((slots, tiles * length), BF16), shape((tiles, length), F32)],
        (lists, after),
        left=1,
    )
    spread_targets = (
        targets.reshape(3, tiles, depth, share).transpose(0, 2, 1, 3).reshape(3, depth, LANES)
    )
    copies = views // 2 if wide else 1
    high = SENT * cap // LANES
    pictures, sent = call(
        functools.partial(render_kernel, peers, width),
        [shape((3, depth, LANES), F32), shape((owners, copies, high, LANES), F32)],
        (*returned, lists, hot, local, cam, pixel, spread_targets),
        scratch=(
            pltpu.VMEM((tiles * width, length), F32),
            pltpu.VMEM((8 * length, LANES), F32),
            pltpu.VMEM((length * depth, LANES), F32),
            pltpu.VMEM((length * depth, LANES), F32),
            pltpu.VMEM((6, length * depth, LANES), F32),
            pltpu.VMEM((peers, *returned[0].shape[-2:]), BF16),
        ),
    )
    if wide:
        received = exchange_wide(sent)
        other = swap(received, "view", 1)
        total = call(
            functools.partial(first_kernel, cap), shape((SENT + 48, g_dev), F32), (received,)
        )
        parts = 4
        grads, pictures = call(
            functools.partial(last_kernel, cap),
            [shape((width, g_dev), F32), shape(targets.shape, F32)],
            (other, total, pictures),
            out_left=True,
            scratch=(
                pltpu.VMEM((parts, width, g_dev // parts), F32),
                pltpu.VMEM(targets.shape, F32),
                pltpu.SemaphoreType.DMA((parts,)),
                pltpu.SemaphoreType.DMA,
            ),
        )
        return (pictures, grads)
    pictures = (
        pictures.reshape(3, depth, tiles, share)
        .transpose(0, 2, 1, 3)
        .reshape(3, tiles, SIDE * SIDE)
    )
    received = exchange(sent[:, 0])
    grads = call(
        functools.partial(scatter_kernel, cap), shape((width, g_dev), F32), (received,)
    )
    return (pictures, lax.psum(grads, "view"))


def solution(mesh):
    return jax.shard_map(
        on_device,
        mesh=mesh,
        in_specs=(
            P(None, "gauss"),
            P(("gauss", "view"), None),
            P(("gauss", "view")),
            P(("gauss", "view")),
            P(),
            P(None, ("gauss", "view"), None),
        ),
        out_specs=(P(None, ("gauss", "view"), None), P(None, "gauss")),
        check_vma=False,
    )
```

```python
import functools
import math

import jax
import jax.numpy as jnp
from jax import lax
from jax.experimental import pallas as pl
from jax.experimental.pallas import tpu as pltpu
from jax.sharding import PartitionSpec as P

WIN = 16
SIDE = 16
LANES = 128
LOG2E = math.log2(math.e)
F32 = jnp.float32
BF16 = jnp.bfloat16
VMEM_LIMIT = 24 * 2**20
SENT = 32


def sh_terms(x, y, z):
    xx, yy, zz = x * x, y * y, z * z
    xy = x * y
    diff = xx - yy
    five = 5.0 * zz - 1.0
    return [
        x,
        y,
        z,
        xy,
        y * z,
        x * z,
        diff,
        3.0 * zz - 1.0,
        x * (xx - 3.0 * yy),
        xy * z,
        y * (3.0 * xx - yy),
        z * diff,
        x * five,
        y * five,
        z * (5.0 * zz - 3.0),
    ]


def project(rows, cam, live):
    mx, my, mz = rows[0], rows[1], rows[2]
    cam_x = cam[0] * mx + cam[1] * my + cam[2] * mz + cam[9]
    cam_y = cam[3] * mx + cam[4] * my + cam[5] * mz + cam[10]
    cam_z = cam[6] * mx + cam[7] * my + cam[8] * mz + cam[11]
    cam_z = jnp.where(live, cam_z, 1.0)
    inv_z = 1.0 / cam_z
    qw, qx, qy, qz = rows[6], rows[7], rows[8], rows[9]
    qw = jnp.where(live, qw, 1.0)
    inv_q = lax.rsqrt(qw * qw + qx * qx + qy * qy + qz * qz)
    qw, qx, qy, qz = qw * inv_q, qx * inv_q, qy * inv_q, qz * inv_q
    rot = [
        [
            1.0 - 2.0 * (qy * qy + qz * qz),
            2.0 * (qx * qy - qw * qz),
            2.0 * (qx * qz + qw * qy),
        ],
        [
            2.0 * (qx * qy + qw * qz),
            1.0 - 2.0 * (qx * qx + qz * qz),
            2.0 * (qy * qz - qw * qx),
        ],
        [
            2.0 * (qx * qz - qw * qy),
            2.0 * (qy * qz + qw * qx),
            1.0 - 2.0 * (qx * qx + qy * qy),
        ],
    ]
    mixed = [
        [
            cam[3 * i] * rot[0][k] + cam[3 * i + 1] * rot[1][k] + cam[3 * i + 2] * rot[2][k]
            for k in range(3)
        ]
        for i in range(3)
    ]
    scale = cam[12] * inv_z
    ray_x, ray_y = cam_x * inv_z, cam_y * inv_z
    proj_u = [scale * (mixed[0][k] - ray_x * mixed[2][k]) for k in range(3)]
    proj_v = [scale * (mixed[1][k] - ray_y * mixed[2][k]) for k in range(3)]
    var = [jnp.exp(2.0 * rows[3 + k]) for k in range(3)]
    uv = [proj_u[k] * var[k] for k in range(3)]
    cov_a = sum(uv[k] * proj_u[k] for k in range(3)) + 0.3
    cov_b = sum(uv[k] * proj_v[k] for k in range(3))
    cov_c = sum(proj_v[k] * proj_v[k] * var[k] for k in range(3)) + 0.3
    inv_det = 1.0 / (cov_a * cov_c - cov_b * cov_b)
    inv_dist = lax.rsqrt(cam_x * cam_x + cam_y * cam_y + cam_z * cam_z)
    terms = sh_terms(cam_x * inv_dist, cam_y * inv_dist, cam_z * inv_dist)
    geometry = [cam_x * scale, cam_y * scale, cov_c * inv_det, -cov_b * inv_det, cov_a * inv_det]
    return geometry + terms, (ray_x, ray_y)


def iota(shape, dim):
    return lax.broadcasted_iota(jnp.int32, shape, dim)


def one_hot(mask):
    return jnp.where(mask, 1.0, 0.0).astype(BF16)


def dot(lhs, rhs, lhs_dim=1, rhs_dim=0):
    return lax.dot_general(
        lhs, rhs, (((lhs_dim,), (rhs_dim,)), ((), ())), preferred_element_type=F32
    )


def split(x, parts):
    out = []
    for _ in range(parts):
        head = x.astype(BF16)
        out.append(head)
        x = x - head.astype(F32)
    return out


def ranks(mask, tiles):
    rows, length = mask.shape
    bits = jnp.where(mask, 1.0, 0.0)
    place = iota((rows, length), 0) % tiles
    shifted = [bits] + [
        jnp.where(place >= d, pltpu.roll(bits, d, 0), 0.0) for d in range(1, tiles)
    ]
    earlier = one_hot(iota((length, length), 0) < iota((length, length), 1))
    counted = jnp.concatenate([earlier] + [jnp.ones_like(earlier)] * (tiles - 1), axis=0)
    return dot(jnp.concatenate(shifted, axis=1).astype(BF16), counted).astype(jnp.int32)


def find(local, tiles, cap, g_dev):
    mine = (local >= 0) & (local < g_dev)
    key = jnp.where(mine, ranks(mine, tiles), -1)
    rows, length = local.shape
    slot = iota((cap, length), 0)
    found = []
    for r in range(0, rows, tiles):
        total = jnp.zeros((cap, length), jnp.int32)
        for t in range(r, r + tiles):
            total = total + jnp.where(key[t : t + 1, :] == slot, local[t : t + 1, :], 0)
        found.append(jnp.sum(total, axis=1, keepdims=True))
    return jnp.concatenate(found, axis=0)


def pick_kernel(tiles, cap, lists_ref, params_ref, picked_ref):
    width, g_dev = params_ref.shape
    where = find(lists_ref[...] - lax.axis_index("gauss") * g_dev, tiles, cap, g_dev)
    hot = one_hot(where == iota((where.shape[0], g_dev), 1))
    wide = jnp.concatenate([params_ref[...], jnp.zeros((LANES - width, g_dev), BF16)], axis=0)
    picked_ref[...] = dot(hot, wide, 1, 1).astype(BF16)


def pick_pair_kernel(cap, peers, *refs):
    lists_refs, refs = refs[:peers], refs[peers:]
    own_ref, other_ref = refs[:2]
    picked_refs, refs = refs[2 : 2 + peers], refs[2 + peers :]
    lists_scratch, picked_scratch = refs
    tiles, length = lists_refs[0].shape
    g_dev = own_ref.shape[1]
    me = lax.axis_index("gauss")
    first = me % 2 == 0
    for k in range(peers):
        lists_scratch[(me // 2) ^ k] = lists_refs[k][...]
    ids = lists_scratch[...].reshape(peers * tiles, length)
    local = jnp.concatenate([ids - me * g_dev, ids - (me ^ 1) * g_dev], axis=0)
    where = find(local, tiles, cap, g_dev)
    where_own, where_other = where[: peers * cap], where[peers * cap :]
    lanes = iota((peers * cap, g_dev), 1)
    of_own = dot(own_ref[...], one_hot(where_own == lanes), 1, 1)
    of_other = dot(other_ref[...], one_hot(where_other == lanes), 1, 1)
    of_even = jnp.where(first, of_own, of_other)
    of_odd = jnp.where(first, of_other, of_own)
    for p in range(peers):
        block = slice(p * cap, (p + 1) * cap)
        picked_scratch[p] = jnp.concatenate(
            [of_even[:, block], of_odd[:, block]], axis=1
        ).astype(BF16)
    for k in range(peers):
        picked_refs[peers - 1 - k][...] = picked_scratch[(me // 2) ^ k]


def by_tile(values, row):
    out = jnp.full(row.shape, values[-1])
    for t in range(len(values) - 1):
        out = jnp.where(row == t, values[t], out)
    return out


def prepare_kernel(
    tile_pos_ref, cam_index_ref, cams_ref, params_ref, copy_ref, cam_ref, pixel_ref
):
    copy_ref[...] = params_ref[...]
    values, tiles, length = cam_ref.shape
    share = LANES // tiles
    depth = SIDE * SIDE // share
    cam_ids = [cam_index_ref[t] for t in range(tiles)]
    tile_row = iota((tiles, length), 0)
    for j in range(values):
        cam_ref[j] = by_tile([cams_ref[cam_ids[t], j] for t in range(tiles)], tile_row)
    pos = [tile_pos_ref[t] for t in range(tiles)]
    lane = iota((depth, LANES), 1)
    origin_x = [(SIDE * (lax.rem(p, WIN) - WIN // 2)).astype(F32) + 0.5 for p in pos]
    pixel_ref[0] = by_tile(origin_x, lane // share) + (lane % SIDE).astype(F32)
    origin_y = [(SIDE * (lax.div(p, WIN) - WIN // 2)).astype(F32) + 0.5 for p in pos]
    pixel_row = iota((depth, LANES), 0) * (share // SIDE) + (lane % share) // SIDE
    pixel_ref[1] = by_tile(origin_y, lane // share) + pixel_row.astype(F32)


def place_kernel(owners, cap, g_dev, lists_ref, after_ref, hot_ref, local_ref):
    tiles, length = lists_ref.shape
    slots = owners * cap
    ids = lists_ref[...]
    masks = [(ids >= o * g_dev) & (ids < (o + 1) * g_dev) for o in range(owners)]
    rank = ranks(jnp.concatenate([m.astype(jnp.int32) for m in masks], axis=0) > 0, tiles)
    place = jnp.full((tiles, length), -1, jnp.int32)
    local = jnp.zeros((tiles, length), jnp.int32)
    for o in range(owners):
        place = jnp.where(masks[o], rank[o * tiles : (o + 1) * tiles] + o * cap, place)
        local = jnp.where(masks[o], ids - o * g_dev, local)
    slot_iota = iota((slots, length), 0)
    hot_ref[...] = jnp.concatenate(
        [one_hot(slot_iota == place[t : t + 1, :]) for t in range(tiles)], axis=1
    )
    local_ref[...] = local.astype(F32)


def render_kernel(pieces, width, *refs):
    recv_refs, refs = refs[:pieces], refs[pieces:]
    lists_ref, hot_ref, local_ref, cam_ref, pixel_ref, targets_ref = refs[:6]
    pictures_ref, send_ref, rows_ref, table_ref, alpha_ref, weight_ref, part_ref = refs[6:13]
    tiles, length = lists_ref.shape
    share = LANES // tiles
    depth = SIDE * SIDE // share
    live = lists_ref[...] >= 0
    hot = hot_ref[...]

    if pieces == 1:
        listed = dot(recv_refs[0][...].reshape(-1, LANES), hot, 0, 0)[:width]
    else:
        (recv_scratch,) = refs[13:]
        place = lax.axis_index("gauss") // 2
        for k in range(pieces):
            recv_scratch[place ^ k] = recv_refs[pieces - 1 - k][...]
        received = jnp.concatenate([recv_scratch[p] for p in range(pieces)], axis=1)
        listed = dot(received, hot)
    for t in range(tiles):
        rows_ref[t * width : (t + 1) * width, :] = listed[:, t * length : (t + 1) * length]
    rows = [rows_ref[pl.ds(f, tiles, stride=width), :] for f in range(width)]

    cam = [cam_ref[j] for j in range(cam_ref.shape[0])]
    outs, pullback, rays = jax.vjp(lambda r: project(r, cam, live), rows[:10], has_aux=True)
    terms = outs[5:]
    colors = []
    for k in range(3):
        base = 11 + 16 * k
        shade = 0.5 + rows[base]
        for b in range(15):
            shade = shade + rows[base + 1 + b] * terms[b]
        for j in range(5):
            shade = shade + rows[59 + j] * cam[13 + 3 * j + k]
        colors.append(shade)
    opacity = jax.nn.sigmoid(rows[10])
    con_a, con_b, con_c = outs[2], outs[3], outs[4]

    attrs = [
        outs[0],
        outs[1],
        (-0.5 * LOG2E) * con_a,
        -LOG2E * con_b,
        (-0.5 * LOG2E) * con_c,
        jnp.where(live, opacity, 0.0),
    ] + colors
    table = [
        jnp.concatenate(
            [jnp.broadcast_to(value[t : t + 1, :], (share, length)) for t in range(tiles)], axis=0
        ).T
        for value in attrs
    ]
    pixel_x, pixel_y = pixel_ref[0, :1, :], pixel_ref[1]
    dx = pixel_x - table[0]
    columns = [table[2] * dx * dx, table[3] * dx, table[1]] + table[4:]
    for index, column in enumerate(columns):
        table_ref[index * length : (index + 1) * length, :] = column

    def row(index, l):
        return table_ref[index * length + l : index * length + l + 1, :]

    zero = jnp.zeros((depth, LANES), F32)
    through = jnp.ones((depth, LANES), F32)
    red, green, blue = zero, zero, zero
    for l in range(length):
        dy = pixel_y - row(2, l)
        power = row(0, l) + dy * (row(1, l) + row(3, l) * dy)
        alpha = row(4, l) * jnp.exp2(power)
        weight = through * alpha
        red = red + weight * row(5, l)
        green = green + weight * row(6, l)
        blue = blue + weight * row(7, l)
        through = through - weight
        at = slice(l * depth, (l + 1) * depth)
        alpha_ref[at, :] = alpha
        weight_ref[at, :] = weight
    pictures_ref[0] = red
    pictures_ref[1] = green
    pictures_ref[2] = blue
    res = [red - targets_ref[0], green - targets_ref[1], blue - targets_ref[2]]

    behind = zero
    for l in reversed(range(length)):
        at = slice(l * depth, (l + 1) * depth)
        alpha = alpha_ref[at, :]
        weight = weight_ref[at, :]
        dy = pixel_y - row(2, l)
        seen = row(5, l) * res[0] + row(6, l) * res[1] + row(7, l) * res[2]
        gap = seen - behind
        behind = behind + alpha * gap
        g = weight * gap
        gy = g * dy
        part_ref[0, at, :] = g
        part_ref[1, at, :] = gy
        part_ref[2, at, :] = gy * dy
        for k in range(3):
            part_ref[3 + k, at, :] = weight * res[k]

    def down(index):
        blocks = []
        for first in range(0, length, 8):
            parts = [
                part_ref[index, pl.ds(first * depth + s, 8, stride=depth), :] for s in range(depth)
            ]
            while len(parts) > 1:
                parts = [a + b for a, b in zip(parts[::2], parts[1::2])]
            blocks.append(parts[0])
        return jnp.concatenate(blocks, axis=0)

    sums = [down(index) for index in range(6)]
    g_x = sums[0] * dx
    sums = sums + [g_x, g_x * dx, sums[1] * dx]
    def over_lanes(x):
        x = x.T
        return jnp.concatenate(
            [
                jnp.sum(x[t * share : (t + 1) * share], axis=0, keepdims=True)
                for t in range(tiles)
            ],
            axis=0,
        )

    g_0, g_y, g_yy, s_0, s_1, s_2, g_x, g_xx, g_xy = [over_lanes(s) for s in sums]

    d_colors = [s_0, s_1, s_2]
    d_terms = []
    for b in range(15):
        d_terms.append(sum(d_colors[k] * rows[12 + 16 * k + b] for k in range(3)))
    d_geometry = [
        con_a * g_x + con_b * g_y,
        con_b * g_x + con_c * g_y,
        -0.5 * g_xx,
        -g_xy,
        -0.5 * g_yy,
    ]
    (d_rows,) = pullback(d_geometry + d_terms)
    values = list(d_rows)
    values.append(g_0 * (1.0 - opacity))
    values.extend(d_colors)
    values.extend(rays)
    for j in range(5):
        values.append(sum(d_colors[k] * cam[13 + 3 * j + k] for k in range(3)))
    values.append(local_ref[...])
    values.extend([jnp.zeros((tiles, length), F32)] * (SENT - len(values)))
    for v in range(SENT):
        rows_ref[pl.ds(v, tiles, stride=width), :] = values[v]
    by_slot = jnp.concatenate(
        [
            jnp.concatenate(split(rows_ref[t * width : t * width + SENT, :], 2), axis=0)
            for t in range(tiles)
        ],
        axis=1,
    )
    by_slot = dot(by_slot, hot, 1, 1)
    by_slot = by_slot[:SENT] + by_slot[SENT:]
    owners, copies, high, _ = send_ref.shape
    cap = hot.shape[0] // owners
    for o in range(owners):
        block = jnp.concatenate(
            [by_slot[r : r + high, o * cap : (o + 1) * cap] for r in range(0, SENT, high)], axis=1
        )
        for c in range(copies):
            send_ref[o, c] = block


def entry_rows(cap, recv_ref):
    blocks, high, _ = recv_ref.shape
    values = jnp.concatenate(
        [
            jnp.concatenate(
                [recv_ref[b, :, first : first + cap] for b in range(blocks)], axis=1
            )
            for first in range(0, SENT * cap // high, cap)
        ],
        axis=0,
    )
    ray_x, ray_y = values[14:15], values[15:16]
    dir_z = lax.rsqrt(ray_x * ray_x + ray_y * ray_y + 1.0)
    terms = sh_terms(ray_x * dir_z, ray_y * dir_z, dir_z)
    terms = jnp.concatenate([jnp.ones_like(dir_z)] + terms, axis=0)
    rows = [values] + [terms * values[11 + k : 12 + k] for k in range(3)]
    parts = split(jnp.concatenate(rows, axis=0), 2)
    return jnp.concatenate(parts, axis=0), values[21:22].astype(jnp.int32)


def scatter(rows, where, first, count):
    hot = one_hot(iota((count, where.shape[1]), 0) + first == where)
    total = dot(rows, hot, 1, 1)
    half = total.shape[0] // 2
    return total[:half] + total[half:]


def in_order(total):
    return jnp.concatenate([total[:11], total[SENT:], total[16:21]], axis=0)


def scatter_kernel(cap, recv_ref, out_ref):
    rows, where = entry_rows(cap, recv_ref)
    out_ref[...] = in_order(scatter(rows, where, 0, out_ref.shape[1]))


def first_kernel(cap, recv_ref, out_ref):
    rows, where = entry_rows(cap, recv_ref)
    out_ref[...] = scatter(rows, where, 0, out_ref.shape[1])


def last_kernel(
    cap, recv_ref, sum_ref, spread_ref, out_ref, pictures_ref, sums, pictures, out_sem, picture_sem
):
    _, tiles, _ = pictures.shape
    depth = spread_ref.shape[1]
    share = LANES // tiles
    lane_block = iota((depth, LANES), 1) // share
    row = iota((depth, LANES), 0) % tiles
    for k in range(3):
        spread = spread_ref[k]
        whole = spread
        for d in range(1, tiles):
            down = pltpu.roll(spread, d, 0)
            up = pltpu.roll(spread, depth + d - tiles, 0)
            moved = pltpu.roll(jnp.where(row >= d, down, up), LANES - d * share, 1)
            whole = jnp.where((row - lane_block) % tiles == d, moved, whole)
        for h in range(depth // tiles):
            pictures[k, :, h * LANES : (h + 1) * LANES] = whole[h * tiles : (h + 1) * tiles]
    copies = [pltpu.make_async_copy(pictures, pictures_ref, picture_sem)]
    copies[0].start()
    rows, where = entry_rows(cap, recv_ref)
    blocks, _, count = sums.shape
    for b in range(blocks):
        columns = slice(b * count, (b + 1) * count)
        sums[b] = in_order(sum_ref[:, columns] + scatter(rows, where, b * count, count))
        copies.append(
            pltpu.make_async_copy(
                sums.at[b], out_ref.at[:, pl.ds(b * count, count)], out_sem.at[b]
            )
        )
        copies[-1].start()
    for copy in copies:
        copy.wait()


def call(kernel, out_shape, args, scalars=0, left=0, out_left=False, scratch=()):
    in_specs = [pl.BlockSpec(memory_space=pltpu.SMEM)] * scalars
    in_specs += [pl.BlockSpec(memory_space=pltpu.VMEM)] * (len(args) - scalars - left)
    in_specs += [pl.BlockSpec(memory_space=pl.ANY)] * left
    many = isinstance(out_shape, (list, tuple))
    spec = pl.BlockSpec(memory_space=pl.ANY if out_left else pltpu.VMEM)
    return pl.pallas_call(
        kernel,
        out_shape=out_shape,
        in_specs=in_specs,
        out_specs=[spec] * len(out_shape) if many else spec,
        scratch_shapes=list(scratch),
        compiler_params=pltpu.CompilerParams(vmem_limit_bytes=VMEM_LIMIT),
    )(*args)


def swap(x, axis, k):
    return lax.ppermute(x, axis, [(i, i ^ k) for i in range(lax.axis_size(axis))])


def crossed(owner, owners):
    return int(owner >= owners // 2)


def reach(x, step, flip):
    owners, views = lax.axis_size("gauss"), lax.axis_size("view")
    flip = flip if views % 2 == 0 else 0
    pairs = [
        (g * views + v, (g ^ step) * views + (v ^ flip))
        for g in range(owners)
        for v in range(views)
    ]
    return lax.ppermute(x, ("gauss", "view"), pairs)


def far_first(blocks):
    last = len(blocks) - 1
    peers = range(last, 0, -1)
    return [reach(b, 2 * k, k % 2) for b, k in zip(blocks, peers)] + [blocks[last]]


def exchange(x):
    return lax.all_to_all(x, "gauss", split_axis=0, concat_axis=0, tiled=True)


def exchange_wide(x):
    owners, views = lax.axis_size("gauss"), lax.axis_size("view")
    blocks = x.reshape(owners * views // 2, *x.shape[2:])
    groups = [
        [
            g * views + v
            for g in range(owners)
            for v in range(views)
            if v % 2 == c ^ crossed(g, owners)
        ]
        for c in range(2)
    ]
    return lax.all_to_all(
        blocks,
        ("gauss", "view"),
        split_axis=0,
        concat_axis=0,
        axis_index_groups=groups,
        tiled=True,
    )


def power_of_two(n):
    return n & (n - 1) == 0


def shape(dims, dtype):
    return jax.ShapeDtypeStruct(dims, dtype)


def on_device(params, lists, tile_pos, cam_index, cams, targets):
    owners = lax.axis_size("gauss")
    views = lax.axis_size("view")
    width, g_dev = params.shape
    tiles, length = lists.shape
    cap = max(tiles * length // owners, 16)
    slots = owners * cap
    share = LANES // tiles
    depth = SIDE * SIDE // share
    paired = 2 <= owners <= 16 and power_of_two(owners) and LANES == 2 * width
    peers = owners // 2 if paired else 1
    wide = views % 2 == 0 and owners * views <= 32

    if paired:
        other = reach(params, 1, 1)
        all_lists = far_first([lists] * peers)
    params_copy, cam, pixel = call(
        prepare_kernel,
        [
            shape((width, g_dev), BF16),
            shape((cams.shape[0], tiles, length), F32),
            shape((2, depth, LANES), F32),
        ],
        (tile_pos, cam_index, cams.T, params),
        scalars=3,
    )
    if paired:
        picked = call(
            functools.partial(pick_pair_kernel, cap, peers),
            [shape((width, 2 * cap), BF16)] * peers,
            (*all_lists[::-1], params_copy, other),
            scratch=(
                pltpu.VMEM((peers, tiles, length), jnp.int32),
                pltpu.VMEM((peers, width, 2 * cap), BF16),
            ),
        )
        returned = far_first(picked)
        after = picked[-1]
    else:
        all_lists = exchange(jnp.broadcast_to(lists[None], (owners, tiles, length)))
        picked = call(
            functools.partial(pick_kernel, tiles, cap),
            shape((slots, LANES), BF16),
            (all_lists.reshape(owners * tiles, length), params_copy),
        )
        returned = [exchange(picked.reshape(owners, cap, LANES))]
        after = picked
    hot, local = call(
        functools.partial(place_kernel, owners, cap, g_dev),
        [shape((slots, tiles * length), BF16), shape((tiles, length), F32)],
        (lists, after),
        left=1,
    )
    spread_targets = (
        targets.reshape(3, tiles, depth, share).transpose(0, 2, 1, 3).reshape(3, depth, LANES)
    )
    copies = views // 2 if wide else 1
    high = SENT * cap // LANES
    pictures, sent = call(
        functools.partial(render_kernel, peers, width),
        [shape((3, depth, LANES), F32), shape((owners, copies, high, LANES), F32)],
        (*returned, lists, hot, local, cam, pixel, spread_targets),
        scratch=(
            pltpu.VMEM((tiles * width, length), F32),
            pltpu.VMEM((8 * length, LANES), F32),
            pltpu.VMEM((length * depth, LANES), F32),
            pltpu.VMEM((length * depth, LANES), F32),
            pltpu.VMEM((6, length * depth, LANES), F32),
            pltpu.VMEM((peers, *returned[0].shape[-2:]), BF16),
        ),
    )
    if wide:
        received = exchange_wide(sent)
        other = swap(received, "view", 1)
        total = call(
            functools.partial(first_kernel, cap), shape((SENT + 48, g_dev), F32), (received,)
        )
        parts = 2
        grads, pictures = call(
            functools.partial(last_kernel, cap),
            [shape((width, g_dev), F32), shape(targets.shape, F32)],
            (other, total, pictures),
            out_left=True,
            scratch=(
                pltpu.VMEM((parts, width, g_dev // parts), F32),
                pltpu.VMEM(targets.shape, F32),
                pltpu.SemaphoreType.DMA((parts,)),
                pltpu.SemaphoreType.DMA,
            ),
        )
        return (pictures, grads)
    pictures = (
        pictures.reshape(3, depth, tiles, share)
        .transpose(0, 2, 1, 3)
        .reshape(3, tiles, SIDE * SIDE)
    )
    received = exchange(sent[:, 0])
    grads = call(
        functools.partial(scatter_kernel, cap), shape((width, g_dev), F32), (received,)
    )
    return (pictures, lax.psum(grads, "view"))


def solution(mesh):
    return jax.shard_map(
        on_device,
        mesh=mesh,
        in_specs=(
            P(None, "gauss"),
            P(("gauss", "view"), None),
            P(("gauss", "view")),
            P(("gauss", "view")),
            P(),
            P(None, ("gauss", "view"), None),
        ),
        out_specs=(P(None, ("gauss", "view"), None), P(None, "gauss")),
        check_vma=False,
    )
```
